32 devices in a mesh: dp: 8 (over y, x, core), pair: 4 (over z).
Axes of the slice: x: 2, y: 2, z: 4, core: 2. Of those that a mesh axis runs over, the one named last changes fastest.
Arguments:
- question_tokens: bfloat16 [256, 64, 768], P(('dp', 'pair')), may hold values from -6 to 6
- passage_tokens: bfloat16 [64, 256, 768], P(('dp', 'pair')), may hold values from -6 to 6
- passage_lengths: int32 [64, 4], P(('dp', 'pair')), may hold values from 1 to 128, 256 in all within a row
- positives: int32 [256], P(('dp', 'pair')), may hold values from 0 to 255
- attn_weight: float32 [2, 768, 3072], P(None, ('dp', 'pair'))
- attn_first: float32 [2, 768, 3072], P(None, ('dp', 'pair')), may hold values from -0.375 to 0.375
- attn_second: float32 [2, 768, 3072], P(None, ('dp', 'pair')), may hold values from 2.56e-05 to 0.0004096
- ffn_in_weight: float32 [2, 768, 3072], P(None, ('dp', 'pair')), may hold values from -0.21875 to 0.21875
- ffn_in_first: float32 [2, 768, 3072], P(None, ('dp', 'pair')), may hold values from -0.21875 to 0.21875
- ffn_in_second: float32 [2, 768, 3072], P(None, ('dp', 'pair')), may hold values from 9.216e-06 to 0.000147456
- ffn_out_weight: float32 [2, 3072, 768], P(None, ('dp', 'pair')), may hold values from -0.109375 to 0.109375
- ffn_out_first: float32 [2, 3072, 768], P(None, ('dp', 'pair')), may hold values from -0.5 to 0.5
- ffn_out_second: float32 [2, 3072, 768], P(None, ('dp', 'pair')), may hold values from 5.76e-05 to 0.0009216
- small_params: float32 [2, 9216], P(None, ('dp', 'pair'))
- small_first: float32 [2, 9216], P(None, ('dp', 'pair')), may hold values from -0.75 to 0.75
- small_second: float32 [2, 9216], P(None, ('dp', 'pair')), may hold values from 0.0001024 to 0.0016384
Outputs:
- attn_first_new: float32 [2, 768, 3072], P(None, ('dp', 'pair'))
- attn_second_new: float32 [2, 768, 3072], P(None, ('dp', 'pair'))
- attn_new: float32 [2, 768, 3072], P(None, ('dp', 'pair'))
- ffn_in_first_new: float32 [2, 768, 3072], P(None, ('dp', 'pair'))
- ffn_in_second_new: float32 [2, 768, 3072], P(None, ('dp', 'pair'))
- ffn_in_new: float32 [2, 768, 3072], P(None, ('dp', 'pair'))
- ffn_out_first_new: float32 [2, 3072, 768], P(None, ('dp', 'pair'))
- ffn_out_second_new: float32 [2, 3072, 768], P(None, ('dp', 'pair'))
- ffn_out_new: float32 [2, 3072, 768], P(None, ('dp', 'pair'))
- small_first_new: float32 [2, 9216], P(None, ('dp', 'pair'))
- small_second_new: float32 [2, 9216], P(None, ('dp', 'pair'))
- small_new: float32 [2, 9216], P(None, ('dp', 'pair'))
- question_grad: float32 [256, 64, 768], P(('dp', 'pair'))
- passage_grad: float32 [64, 256, 768], P(('dp', 'pair'))
The draws below stay inside these ranges and needn't reach their ends.
Inputs may be any that keep to these rules, and one draw needn't show every extreme that they name: `passage_lengths`: each row's 4 passage lengths sum to 256, the longest in every row is 128.
All inputs are finite; a program needn't handle non-finite values.
Results may differ from the reference program's by a relative error of at most 0.014.
The reference program's roundings to bfloat16 on the way count: a program that leaves them out, or rounds other values in their place, can miss the bound.
Values may be sent and summed in bfloat16 or wider, within the bound.
A program may use at most 256 MiB of HBM per device.

```python
import math
import jax
import jax.numpy as jnp
import numpy as np
from jax import lax

D = 768
HD = 64
FF = 3072
QLEN = 64
ROW_LEN = 256
PPR = 4
STEP = 5
LEN_MOST = 128
SMALL = 9216
NQ = 256
ROWS = 64
NP = 256
CLSN = 512


def draw_attn_weight(key, part):
    key = jax.random.fold_in(key, 11)
    normal_draw = jnp.clip(jax.random.normal(key, (2, D, 4 * D), jnp.float32), -5.0, 5.0) * D ** (-0.5)
    columns = jnp.arange(4 * D)
    return normal_draw * jnp.where(columns >= 3 * D, 4.0, 1.0)


def draw_small_params(key, part):
    key = jax.random.fold_in(key, 23)
    key_normal, key_gain = jax.random.split(key)
    biases = jnp.clip(jax.random.normal(key_normal, (2, 8 * D + FF), jnp.float32), -4.0, 4.0) * 0.3
    gains = jax.random.uniform(key_gain, (2, 8 * D + FF), jnp.float32, 0.7, 1.3)
    columns = jnp.arange(8 * D + FF)
    gain_one = (columns >= 3 * D) & (columns < 4 * D)
    gain_two = (columns >= 6 * D + FF) & (columns < 7 * D + FF)
    return jnp.where(gain_one | gain_two, gains, biases)


def set_ends(drawn, stream_key, smallest, top_value):
    longest = drawn.shape.index(max(drawn.shape))
    spots = []
    for shift in (0, 1):
        where = [jax.random.randint(jax.random.fold_in(stream_key, axis), (), 0, length) for axis, length in enumerate(drawn.shape)]
        where[longest] = (where[longest] + shift) % drawn.shape[longest]
        spots.append(tuple(where))
    return drawn.at[spots[0]].set(smallest).at[spots[1]].set(top_value)


def shard_levels(rng, extent, cuts, low, high):
    factor_of, own = 1.0, jax.random.fold_in(rng, 6)
    for axis_at, blocks in cuts:
        steps = jnp.exp(jax.random.uniform(jax.random.fold_in(own, axis_at), (blocks,), jnp.float32, low / len(cuts), high / len(cuts)))
        factor_of = factor_of * jnp.repeat(steps, extent[axis_at] // blocks).reshape([-1 if axis == axis_at else 1 for axis in range(len(extent))])
    return factor_of


def profile(count, total, limit, skew):
    portions = [(1 << 20) // math.isqrt(grade ** skew) + 1 for grade in range(2, count + 1)]
    rest, given = total - limit - (count - 1), [1] * (count - 1)
    while rest > 0:
        movable = [i for i in range(count - 1) if given[i] < limit]
        pool, left = sum([portions[i] for i in movable]), rest
        for i in movable:
            more = min(limit - given[i], max(1, left * portions[i] // pool), rest)
            given[i] = given[i] + more
            rest = rest - more
    return np.array([limit] + given)


def ragged_sizes(rng, count, total, reach, skew):
    if count == 2:
        one = jax.random.randint(rng, (), max(1, total - reach), min(reach, total - 1) + 1)
        return jnp.stack([one, total - one])
    tallies = jnp.asarray(profile(count, total, reach, skew), jnp.int32)
    couples = (count - 1) // 2
    donor, sink = tallies[1:1 + 2 * couples:2], tallies[2:2 + 2 * couples:2]
    room = jnp.minimum(donor - 1, reach - sink)
    shifted = jax.random.randint(jax.random.fold_in(rng, 1), (couples,), 0, 1 << 20) % (room + 1)
    tallies = tallies.at[1:1 + 2 * couples:2].set(donor - shifted).at[2:2 + 2 * couples:2].set(sink + shifted)
    return tallies[jax.random.permutation(jax.random.fold_in(rng, 2), count)]


def noise(own_key, extent, width, limit, cuts=(), held_as=jnp.bfloat16):
    factor_of = shard_levels(own_key, extent, cuts, -0.22, 0.18) if cuts else 1.0
    drawn = jax.random.normal(own_key, extent, jnp.float32) * width * factor_of
    return jnp.minimum(jnp.maximum(drawn, -limit), limit).astype(held_as)


def setup_inputs(seed: int = 0) -> dict:
    streams_of = jax.random.split(jax.random.key(seed), 17)
    return {
        "question_tokens": noise(streams_of[0], (NQ, QLEN, D), 1.0, 6.0, ((0, 32),)),
        "passage_tokens": noise(streams_of[1], (ROWS, ROW_LEN, D), 1.0, 6.0, ((0, 32),)),
        "passage_lengths": jax.vmap(lambda own: ragged_sizes(own, PPR, ROW_LEN, LEN_MOST, 2))(jax.random.split(streams_of[2], ROWS)).reshape((ROWS, PPR)).astype(jnp.int32),
        "positives": set_ends(jax.random.randint(streams_of[3], (NQ,), 0, NP), jax.random.fold_in(streams_of[3], 1), 0, NP - 1).astype(jnp.int32),
        "attn_weight": draw_attn_weight(jax.random.fold_in(streams_of[16], 71), 0),
        "attn_first": noise(streams_of[5], (2, D, 4 * D), (0.0011 * CLSN ** 0.5), 0.375, ((1, 32),), jnp.float32),
        "attn_second": jnp.clip(jnp.exp(math.log(0.0004096) - 2.7725887 * jax.random.uniform(streams_of[6], (2, D, 4 * D), jnp.float32) ** shard_levels(streams_of[6], (2, D, 4 * D), ((1, 32),), -0.2, 0.2)), 2.5600000299164094e-05, 0.0004096),
        "ffn_in_weight": noise(streams_of[7], (2, D, FF), D ** -0.5, 0.21875, ((1, 32),), jnp.float32),
        "ffn_in_first": noise(streams_of[8], (2, D, FF), (0.00067 * CLSN ** 0.5), 0.21875, ((1, 32),), jnp.float32),
        "ffn_in_second": jnp.clip(jnp.exp(math.log(0.000147456) - 2.7725887 * jax.random.uniform(streams_of[9], (2, D, FF), jnp.float32) ** shard_levels(streams_of[9], (2, D, FF), ((1, 32),), -0.2, 0.2)), 9.215999853040557e-06, 0.000147456),
        "ffn_out_weight": noise(streams_of[10], (2, FF, D), FF ** -0.5, 0.109375, ((1, 32),), jnp.float32),
        "ffn_out_first": noise(streams_of[11], (2, FF, D), (0.00167 * CLSN ** 0.5), 0.5, ((1, 32),), jnp.float32),
        "ffn_out_second": jnp.clip(jnp.exp(math.log(0.0009216) - 2.7725887 * jax.random.uniform(streams_of[12], (2, FF, D), jnp.float32) ** shard_levels(streams_of[12], (2, FF, D), ((1, 32),), -0.2, 0.2)), 5.759999839938246e-05, 0.0009216),
        "small_params": draw_small_params(jax.random.fold_in(streams_of[16], 71), 0),
        "small_first": noise(streams_of[14], (2, SMALL), (0.0022 * CLSN ** 0.5), 0.75, ((1, 32),), jnp.float32),
        "small_second": jnp.clip(jnp.exp(math.log(0.0016384) - 2.7725887 * jax.random.uniform(streams_of[15], (2, SMALL), jnp.float32) ** shard_levels(streams_of[15], (2, SMALL), ((1, 32),), -0.2, 0.2)), 0.0001024, 0.0016384),
    }


@jax.custom_vjp
def low(v):
    return lax.optimization_barrier(v.astype(jnp.bfloat16)).astype(jnp.float32)

@jax.custom_vjp
def low_back(v):
    return v

def low_keep(v):
    return (low(v), None)

def low_pass(kept, grad):
    return (grad,)

def back_keep(v):
    return (v, None)

def back_low(kept, grad):
    return (low(grad),)
low.defvjp(low_keep, low_pass)
low_back.defvjp(back_keep, back_low)
BETA_ONE = 0.9
BETA_TWO = 0.999
ADAM_EPS = 1e-08
NORM_EPS = 1e-06
RATE_MATRIX = 0.05
RATE_SMALL = 0.3
DECAY_MATRIX = 0.01
HIGH = lax.Precision.HIGHEST

def matmul(left_rows, right_rows):
    return jnp.dot(left_rows, right_rows, precision=HIGH)

def layer_norm(values, norm_gain, norm_shift):
    row_mean = lax.optimization_barrier(jnp.mean(values, axis=-1, keepdims=True))
    centred = values - row_mean
    spread = lax.optimization_barrier(jnp.mean(centred * centred, axis=-1, keepdims=True))
    return centred * lax.rsqrt(spread + NORM_EPS) * norm_gain + norm_shift

def unpack(small_vec, model_width, hidden_width):
    widths = [model_width] * 5 + [hidden_width] + [model_width] * 3
    pieces = []
    offset = 0
    for length in widths:
        pieces.append(small_vec[offset:offset + length])
        offset = offset + length
    return pieces

def encode(tokens, segment, attn_weights, inner_weight, outer_weight, small_vec):
    batch_size, length, model_width = tokens.shape
    head_count = model_width // HD
    flat_rows = tokens.reshape(batch_size * length, model_width)
    bias_query, bias_value, bias_out, gain_one, shift_one, bias_inner, bias_outer, gain_two, shift_two = unpack(small_vec, model_width, inner_weight.shape[1])
    queries = low_back(low(matmul(flat_rows, attn_weights[:, :model_width]) + bias_query))
    key_rows = low_back(low(matmul(flat_rows, attn_weights[:, model_width:2 * model_width])))
    value_rows = low_back(low(matmul(flat_rows, attn_weights[:, 2 * model_width:3 * model_width]) + bias_value))
    head_shape = (batch_size, length, head_count, HD)
    scores = jnp.einsum('blhe,bmhe->bhlm', queries.reshape(head_shape), key_rows.reshape(head_shape), precision=HIGH)
    scores = low_back(scores * HD ** (-0.5))
    allowed = (segment[:, :, None] == segment[:, None, :])[:, None]
    scores = jnp.where(allowed, scores, -1000000000.0)
    top_score = lax.optimization_barrier(jnp.max(scores, axis=-1, keepdims=True))
    raised = jnp.exp(scores - top_score)
    attn_probs = raised / lax.optimization_barrier(jnp.sum(raised, axis=-1, keepdims=True))
    mixed_heads = jnp.einsum('bhlm,bmhe->blhe', low(attn_probs), value_rows.reshape(head_shape), precision=HIGH)
    mixed_heads = low_back(low(mixed_heads.reshape(batch_size * length, model_width)))
    attn_out = low_back(matmul(mixed_heads, attn_weights[:, 3 * model_width:]) + bias_out)
    normed_one = layer_norm(flat_rows + attn_out, gain_one, shift_one)
    pre_act = low_back(matmul(low(normed_one), inner_weight) + bias_inner)
    activated = low(jax.nn.gelu(pre_act, approximate=False))
    branch = low_back(matmul(activated, outer_weight) + bias_outer)
    result = layer_norm(normed_one + branch, gain_two, shift_two)
    return result.reshape(batch_size, length, model_width)

def divisor_up_to(amount, ceiling):
    chosen = 1
    for option in range(1, min(amount, ceiling) + 1):
        if amount % option == 0:
            chosen = option
    return chosen

def adam_update(weight, first_moment, second, gradient, step_rate, decay_rate):
    first_new = BETA_ONE * first_moment + (1.0 - BETA_ONE) * gradient
    second_new = BETA_TWO * second + (1.0 - BETA_TWO) * gradient * gradient
    fix_one = 1.0 - BETA_ONE ** STEP
    fix_two = 1.0 - BETA_TWO ** STEP
    update = first_new / fix_one / (jnp.sqrt(second_new / fix_two) + ADAM_EPS)
    return (first_new, second_new, weight - step_rate * (update + decay_rate * weight))

def reference(question_tokens, passage_tokens, passage_lengths, positives, attn_weight, attn_first, attn_second, ffn_in_weight, ffn_in_first, ffn_in_second, ffn_out_weight, ffn_out_first, ffn_out_second, small_params, small_first, small_second):
    seg_ends = jnp.cumsum(passage_lengths, axis=1).astype(jnp.int32)
    seg_starts = (seg_ends - passage_lengths).astype(jnp.int32)
    positions = jnp.arange(passage_tokens.shape[1], dtype=jnp.int32)
    segment = lax.optimization_barrier(jnp.sum((positions[None, :, None] >= seg_ends[:, None, :]).astype(jnp.int32), axis=2)).astype(jnp.int32)
    question_count, question_len, model_width = question_tokens.shape
    row_count, row_len, _ = passage_tokens.shape
    group_questions = divisor_up_to(question_count, max(1, 4096 // question_len))
    group_rows = divisor_up_to(row_count, max(1, 4096 // row_len))

    def total_loss(question_in, passage_in, attn_full, inner_full, outer_full, small_full):
        attn_low = low(attn_full)
        inner_low = low(inner_full)
        outer_low = low(outer_full)
        small_low = low(small_full)

        def encode_questions(tokens):
            zero_seg = jnp.zeros(tokens.shape[:2], jnp.int32)
            result = encode(tokens, zero_seg, attn_low[0], inner_low[0], outer_low[0], small_low[0])
            return result[:, 0]

        def encode_passages(block_in):
            tokens, row_seg, begins = block_in
            result = encode(tokens, row_seg, attn_low[1], inner_low[1], outer_low[1], small_low[1])
            return jnp.take_along_axis(result, begins[:, :, None], axis=1)
        question_cls = lax.map(jax.checkpoint(encode_questions), question_in.reshape(-1, group_questions, question_len, model_width)).reshape(-1, model_width)
        passage_cls = lax.map(jax.checkpoint(encode_passages), (passage_in.reshape(-1, group_rows, row_len, model_width), segment.reshape(-1, group_rows, row_len), seg_starts.reshape(-1, group_rows, seg_starts.shape[1]))).reshape(-1, model_width)
        scores = low_back(matmul(low(question_cls), low(passage_cls).T) * model_width ** (-0.5))
        top_score = lax.optimization_barrier(jnp.max(scores, axis=1, keepdims=True))
        log_total = top_score[:, 0] + jnp.log(lax.optimization_barrier(jnp.sum(jnp.exp(scores - top_score), axis=1)))
        picked = jnp.take_along_axis(scores, positives[:, None].astype(jnp.int32), axis=1)[:, 0]
        return jnp.sum(log_total - picked)
    primal = (question_tokens.astype(jnp.float32), passage_tokens.astype(jnp.float32), attn_weight, ffn_in_weight, ffn_out_weight, small_params)
    loss_value, backward = jax.vjp(total_loss, *primal)
    grad_question, grad_passage, grad_attn, grad_inner, grad_outer, grad_small = backward(jnp.ones((), jnp.float32))
    attn_m, attn_v, attn_w = adam_update(attn_weight, attn_first, attn_second, grad_attn, RATE_MATRIX, DECAY_MATRIX)
    inner_m, inner_v, inner_w = adam_update(ffn_in_weight, ffn_in_first, ffn_in_second, grad_inner, RATE_MATRIX, DECAY_MATRIX)
    outer_m, outer_v, outer_w = adam_update(ffn_out_weight, ffn_out_first, ffn_out_second, grad_outer, RATE_MATRIX, DECAY_MATRIX)
    small_m, small_v, small_w = adam_update(small_params, small_first, small_second, grad_small, RATE_SMALL, 0.0)
    return (attn_m, attn_v, attn_w, inner_m, inner_v, inner_w, outer_m, outer_v, outer_w, small_m, small_v, small_w, grad_question, grad_passage)
```

```python
import math

import jax
import jax.numpy as jnp
from jax import lax
from jax.experimental import pallas as pl
from jax.experimental.pallas import tpu as pltpu
from jax.sharding import PartitionSpec as P

HD = 64
STEP = 5


BETA_ONE = 0.9
BETA_TWO = 0.999
ADAM_EPS = 1e-08
NORM_EPS = 1e-06
RATE_MATRIX = 0.05
RATE_SMALL = 0.3
DECAY_MATRIX = 0.01


def layer_norm(values, norm_gain, norm_shift):
    row_mean = jnp.mean(values, axis=-1, keepdims=True)
    centred = values - row_mean
    spread = jnp.mean(centred * centred, axis=-1, keepdims=True)
    return centred * lax.rsqrt(spread + NORM_EPS) * norm_gain + norm_shift


def gelu_exact(values):
    return jax.nn.gelu(values, approximate=False)


def unpack(small_vec, model_width, hidden_width):
    widths = [model_width] * 5 + [hidden_width] + [model_width] * 3
    pieces = []
    offset = 0
    for length in widths:
        pieces.append(small_vec[offset : offset + length])
        offset = offset + length
    return pieces


def masked_scores(queries, key_rows, segment):
    scores = jnp.einsum(
        "blhe,bmhe->bhlm", queries, key_rows, preferred_element_type=jnp.float32
    ) * HD ** (-0.5)
    allowed = (segment[:, :, None] == segment[:, None, :])[:, None]
    return jnp.where(allowed, scores, -1000000000.0)


def encoder_forward(tokens, segment, attn_weights, inner_weight, outer_weight, small_vec):
    batch_size, length, model_width = tokens.shape
    head_count = model_width // HD
    flat_rows = tokens.reshape(batch_size * length, model_width)
    (
        bias_query,
        bias_value,
        bias_out,
        gain_one,
        shift_one,
        bias_inner,
        bias_outer,
        gain_two,
        shift_two,
    ) = unpack(small_vec, model_width, inner_weight.shape[1])
    bias_proj = jnp.concatenate([bias_query, jnp.zeros_like(bias_query), bias_value])
    projected = (
        jnp.dot(flat_rows, attn_weights[:, : 3 * model_width], preferred_element_type=jnp.float32)
        + bias_proj
    )
    projected = projected.astype(jnp.bfloat16).reshape(batch_size, length, 3, head_count, HD)
    queries = projected[:, :, 0]
    key_rows = projected[:, :, 1]
    value_rows = projected[:, :, 2]
    scores = masked_scores(queries, key_rows, segment)
    top_score = jnp.max(scores, axis=-1, keepdims=True)
    raised = jnp.exp(scores - top_score)
    totals = jnp.sum(raised, axis=-1, keepdims=True)
    attn_probs = (raised / totals).astype(jnp.bfloat16)
    log_total = top_score + jnp.log(totals)
    mixed_heads = jnp.einsum(
        "bhlm,bmhe->blhe", attn_probs, value_rows, preferred_element_type=jnp.float32
    )
    mixed_flat = mixed_heads.astype(jnp.bfloat16).reshape(batch_size * length, model_width)
    attn_out = (
        jnp.dot(mixed_flat, attn_weights[:, 3 * model_width :], preferred_element_type=jnp.float32)
        + bias_out
    )
    residual_one = flat_rows.astype(jnp.float32) + attn_out
    normed_one = layer_norm(residual_one, gain_one, shift_one)
    pre_act = (
        jnp.dot(normed_one.astype(jnp.bfloat16), inner_weight, preferred_element_type=jnp.float32)
        + bias_inner
    )
    activated = gelu_exact(pre_act).astype(jnp.bfloat16)
    branch = jnp.dot(activated, outer_weight, preferred_element_type=jnp.float32) + bias_outer
    residual_two = normed_one + branch
    result = layer_norm(residual_two, gain_two, shift_two).reshape(batch_size, length, model_width)
    kept_values = (
        queries,
        key_rows,
        value_rows,
        log_total,
        mixed_flat,
        residual_one,
        normed_one,
        pre_act,
        activated,
        residual_two,
    )
    return (result, kept_values)


def encoder_backward(
    tokens, segment, attn_weights, inner_weight, outer_weight, small_vec, kept_values, grad_result
):
    batch_size, length, model_width = tokens.shape
    head_count = model_width // HD
    flat_rows = tokens.reshape(batch_size * length, model_width)
    (
        queries,
        key_rows,
        value_rows,
        log_total,
        mixed_flat,
        residual_one,
        normed_one,
        pre_act,
        activated,
        residual_two,
    ) = kept_values
    (
        bias_query,
        bias_value,
        bias_out,
        gain_one,
        shift_one,
        bias_inner,
        bias_outer,
        gain_two,
        shift_two,
    ) = unpack(small_vec, model_width, inner_weight.shape[1])
    grad_flat = grad_result.reshape(batch_size * length, model_width)
    unused_two, norm_two_back = jax.vjp(layer_norm, residual_two, gain_two, shift_two)
    grad_two, grad_gain_two, grad_shift_two = norm_two_back(grad_flat)
    grad_branch = grad_two.astype(jnp.bfloat16)
    grad_bias_outer = jnp.sum(grad_branch, axis=0, dtype=jnp.float32)
    grad_outer = jnp.dot(activated.T, grad_branch, preferred_element_type=jnp.float32)
    grad_act = jnp.dot(grad_branch, outer_weight.T, preferred_element_type=jnp.float32)
    unused_act, gelu_back = jax.vjp(gelu_exact, pre_act)
    grad_pre = gelu_back(grad_act)[0].astype(jnp.bfloat16)
    grad_bias_inner = jnp.sum(grad_pre, axis=0, dtype=jnp.float32)
    grad_inner = jnp.dot(
        normed_one.astype(jnp.bfloat16).T, grad_pre, preferred_element_type=jnp.float32
    )
    grad_normed = grad_two + jnp.dot(grad_pre, inner_weight.T, preferred_element_type=jnp.float32)
    unused_one, norm_one_back = jax.vjp(layer_norm, residual_one, gain_one, shift_one)
    grad_one, grad_gain_one, grad_shift_one = norm_one_back(grad_normed)
    grad_attn_out = grad_one.astype(jnp.bfloat16)
    grad_bias_out = jnp.sum(grad_attn_out, axis=0, dtype=jnp.float32)
    grad_out_proj = jnp.dot(mixed_flat.T, grad_attn_out, preferred_element_type=jnp.float32)
    grad_mixed = jnp.dot(
        grad_attn_out, attn_weights[:, 3 * model_width :].T, preferred_element_type=jnp.float32
    )
    grad_mixed = grad_mixed.astype(jnp.bfloat16).reshape(batch_size, length, head_count, HD)
    scores = masked_scores(queries, key_rows, segment)
    attn_probs = jnp.exp(scores - log_total)
    grad_probs = jnp.einsum(
        "blhe,bmhe->bhlm", grad_mixed, value_rows, preferred_element_type=jnp.float32
    )
    inner_dot = jnp.sum(attn_probs * grad_probs, axis=-1, keepdims=True)
    grad_scores = (attn_probs * (grad_probs - inner_dot)).astype(jnp.bfloat16)
    grad_values = jnp.einsum(
        "bhlm,blhe->bmhe",
        attn_probs.astype(jnp.bfloat16),
        grad_mixed,
        preferred_element_type=jnp.float32,
    )
    grad_queries = jnp.einsum(
        "bhlm,bmhe->blhe", grad_scores, key_rows, preferred_element_type=jnp.float32
    ) * HD ** (-0.5)
    grad_keys = jnp.einsum(
        "bhlm,blhe->bmhe", grad_scores, queries, preferred_element_type=jnp.float32
    ) * HD ** (-0.5)
    row_total = batch_size * length
    grad_proj = jnp.concatenate(
        [
            grad_queries.reshape(row_total, model_width),
            grad_keys.reshape(row_total, model_width),
            grad_values.reshape(row_total, model_width),
        ],
        axis=1,
    ).astype(jnp.bfloat16)
    grad_bias_query = jnp.sum(grad_proj[:, :model_width], axis=0, dtype=jnp.float32)
    grad_bias_value = jnp.sum(grad_proj[:, 2 * model_width :], axis=0, dtype=jnp.float32)
    grad_proj_weight = jnp.dot(flat_rows.T, grad_proj, preferred_element_type=jnp.float32)
    grad_tokens = grad_one + jnp.dot(
        grad_proj, attn_weights[:, : 3 * model_width].T, preferred_element_type=jnp.float32
    )
    grad_attn = jnp.concatenate([grad_proj_weight, grad_out_proj], axis=1)
    grad_small = jnp.concatenate(
        [
            grad_bias_query,
            grad_bias_value,
            grad_bias_out,
            grad_gain_one,
            grad_shift_one,
            grad_bias_inner,
            grad_bias_outer,
            grad_gain_two,
            grad_shift_two,
        ]
    )
    return (
        grad_tokens.reshape(batch_size, length, model_width),
        grad_attn,
        grad_inner,
        grad_outer,
        grad_small,
    )


def rows_term(stacked, count):
    return jnp.moveaxis(stacked, 0, 1).reshape(count, -1)


def unfold_rows(summed, encoders):
    owned = summed.shape[0]
    return jnp.moveaxis(summed.reshape(owned, encoders, -1), 1, 0)


def adam_update(weight, first_moment, second, gradient, step_rate, decay_rate):
    first_new = BETA_ONE * first_moment + (1.0 - BETA_ONE) * gradient
    second_new = BETA_TWO * second + (1.0 - BETA_TWO) * gradient * gradient
    fix_one = 1.0 - BETA_ONE**STEP
    fix_two = 1.0 - BETA_TWO**STEP
    update = first_new / fix_one / (jnp.sqrt(second_new / fix_two) + ADAM_EPS)
    return (first_new, second_new, weight - step_rate * (update + decay_rate * weight))


def local(
    question_tokens,
    passage_tokens,
    passage_lengths,
    positives,
    attn_weight,
    attn_first,
    attn_second,
    ffn_in_weight,
    ffn_in_first,
    ffn_in_second,
    ffn_out_weight,
    ffn_out_first,
    ffn_out_second,
    small_params,
    small_first,
    small_second,
):
    gathered = (
        lax.all_gather(attn_weight.astype(jnp.bfloat16), ("dp", "pair"), axis=1, tiled=True),
        lax.all_gather(ffn_in_weight.astype(jnp.bfloat16), ("dp", "pair"), axis=1, tiled=True),
        lax.all_gather(ffn_out_weight.astype(jnp.bfloat16), ("dp", "pair"), axis=1, tiled=True),
        lax.all_gather(small_params.astype(jnp.bfloat16), ("dp", "pair"), axis=1, tiled=True),
    )
    attn_all, inner_all, outer_all, small_low = gathered
    small_all = small_low.astype(jnp.float32)
    question_count, question_len, model_width = question_tokens.shape
    row_count, row_len, unused_width = passage_tokens.shape
    attn_cols = attn_weight.shape[2]
    front_rows = attn_weight.shape[1]
    back_rows = ffn_out_weight.shape[1]
    seg_ends = jnp.cumsum(passage_lengths, axis=1)
    seg_starts = seg_ends - passage_lengths
    positions = jnp.arange(row_len, dtype=jnp.int32)
    passage_seg = jnp.sum(
        (positions[None, :, None] >= seg_ends[:, None, :]).astype(jnp.int32), axis=2
    )
    question_seg = jnp.zeros((question_count, question_len), jnp.int32)
    question_out, question_kept = encoder_forward(
        question_tokens, question_seg, attn_all[0], inner_all[0], outer_all[0], small_all[0]
    )
    passage_out, passage_kept = encoder_forward(
        passage_tokens, passage_seg, attn_all[1], inner_all[1], outer_all[1], small_all[1]
    )
    question_cls = question_out[:, 0].astype(jnp.bfloat16)
    passage_cls = (
        jnp.take_along_axis(passage_out, seg_starts[:, :, None], axis=1)
        .reshape(-1, model_width)
        .astype(jnp.bfloat16)
    )
    every_cls = lax.all_gather(passage_cls, ("dp", "pair"), axis=0, tiled=True)
    score_scale = model_width ** (-0.5)
    scores = jnp.dot(question_cls, every_cls.T, preferred_element_type=jnp.float32) * score_scale
    top_score = jnp.max(scores, axis=1, keepdims=True)
    raised = jnp.exp(scores - top_score)
    soft_scores = raised / jnp.sum(raised, axis=1, keepdims=True)
    columns = jnp.arange(every_cls.shape[0], dtype=jnp.int32)
    target = (columns[None, :] == positives[:, None]).astype(jnp.float32)
    grad_scores = (soft_scores - target).astype(jnp.bfloat16)
    grad_qcls = jnp.dot(grad_scores, every_cls, preferred_element_type=jnp.float32) * score_scale
    grad_pcls = lax.psum_scatter(
        jnp.dot(grad_scores.T, question_cls, preferred_element_type=jnp.float32) * score_scale,
        ("dp", "pair"),
        scatter_dimension=0,
        tiled=True,
    )
    grad_question_out = jnp.zeros_like(question_out).at[:, 0].set(grad_qcls)
    row_index = jnp.arange(row_count, dtype=jnp.int32)[:, None]
    grad_passage_out = (
        jnp.zeros_like(passage_out)
        .at[row_index, seg_starts]
        .set(grad_pcls.reshape(row_count, -1, model_width))
    )
    question_grad, q_attn, q_inner, q_outer, q_small = encoder_backward(
        question_tokens,
        question_seg,
        attn_all[0],
        inner_all[0],
        outer_all[0],
        small_all[0],
        question_kept,
        grad_question_out,
    )
    passage_grad, p_attn, p_inner, p_outer, p_small = encoder_backward(
        passage_tokens,
        passage_seg,
        attn_all[1],
        inner_all[1],
        outer_all[1],
        small_all[1],
        passage_kept,
        grad_passage_out,
    )
    front_stack = jnp.stack(
        [jnp.concatenate([q_attn, q_inner], axis=1), jnp.concatenate([p_attn, p_inner], axis=1)]
    )
    front_owned = lax.psum_scatter(
        rows_term(front_stack, front_rows * lax.axis_size(("dp", "pair"))),
        ("dp", "pair"),
        scatter_dimension=0,
        tiled=True,
    )
    back_owned = lax.psum_scatter(
        rows_term(jnp.stack([q_outer, p_outer]), back_rows * lax.axis_size(("dp", "pair"))),
        ("dp", "pair"),
        scatter_dimension=0,
        tiled=True,
    )
    small_sum = lax.psum_scatter(
        jnp.stack([q_small, p_small]), ("dp", "pair"), scatter_dimension=1, tiled=True
    )
    front_sum = unfold_rows(front_owned, 2)
    back_sum = unfold_rows(back_owned, 2)
    attn_sum = front_sum[:, :, :attn_cols]
    inner_sum = front_sum[:, :, attn_cols:]
    attn_m, attn_v, attn_w = adam_update(
        attn_weight, attn_first, attn_second, attn_sum, RATE_MATRIX, DECAY_MATRIX
    )
    inner_m, inner_v, inner_w = adam_update(
        ffn_in_weight, ffn_in_first, ffn_in_second, inner_sum, RATE_MATRIX, DECAY_MATRIX
    )
    outer_m, outer_v, outer_w = adam_update(
        ffn_out_weight, ffn_out_first, ffn_out_second, back_sum, RATE_MATRIX, DECAY_MATRIX
    )
    small_m, small_v, small_w = adam_update(
        small_params, small_first, small_second, small_sum, RATE_SMALL, 0.0
    )
    return (
        attn_m,
        attn_v,
        attn_w,
        inner_m,
        inner_v,
        inner_w,
        outer_m,
        outer_v,
        outer_w,
        small_m,
        small_v,
        small_w,
        question_grad,
        passage_grad,
    )


MESH_ID = pl.DeviceIdType.MESH
LOW = jnp.bfloat16
F32 = jnp.float32


def dot_nn(a, b):
    return jnp.dot(a, b, preferred_element_type=F32)


def dot_nt(a, b):
    return lax.dot_general(a, b, (((1,), (1,)), ((), ())), preferred_element_type=F32)


def dot_tn(a, b):
    return lax.dot_general(a, b, (((0,), (0,)), ((), ())), preferred_element_type=F32)


def expand_heads(rows):
    head_of = lax.broadcasted_iota(jnp.int32, rows.shape, 1) // HD
    heads = rows.shape[1] // HD
    return jnp.concatenate(
        [jnp.where(head_of == h, rows, jnp.zeros_like(rows)) for h in range(heads)], axis=0
    )


def pick_heads(stacked):
    width = stacked.shape[1]
    heads = width // HD
    head_of = lax.broadcasted_iota(jnp.int32, (16, width), 1) // HD
    total = jnp.zeros((16, width), F32)
    for h in range(heads):
        total = total + jnp.where(head_of == h, stacked[16 * h : 16 * h + 16], 0.0)
    return total


def split_low(values):
    high = values.astype(LOW)
    return high, (values - high.astype(F32)).astype(LOW)


def gelu_parts(values):
    cdf = 0.5 * (1.0 + lax.erf(values * (0.5**0.5)))
    density = jnp.exp(-0.5 * values * values) * (0.5 / math.pi) ** 0.5
    return values * cdf, cdf + values * density


def step_kernel(
    qt_ref, pt_ref, attn_ref, ffi_ref, ffo_ref, small_ref, bnd_ref,
    ga_ref, gi_ref, go_ref, gs_ref, dxq_ref, dxp_ref,
    X, slabA, slabI, slabO, smb, bndb, R, WN, sn, sno, ST, Pf, Pb, DSb, Emat, b1p,
    w1s_, w1r, W1, W2, Yb, P2s, P2r, XH, Dout, dZb, Gb, Act, P3s, P3r, Qb, dAb, dUb, dQb,
    m1s, m1r, m2s, m2r, dws, dwr, sgs, sgr, GS, GSw, GA, GI, GO, DX, qsb, vtb, ybf,
    loc, sib_s, sib_r, at_s, at_r, ag_s, ag_z, ag_p, aa_s, aa_r, out_l, out_s, out_r,
):
    dp, z = lax.axis_index("dp"), lax.axis_index("pair")
    core = lax.rem(dp, 2)
    y, x = dp // 4, lax.rem(dp // 2, 2)
    own = y * 8 + x * 4 + z
    line = y * 8 + x * 4

    def dev(slot, k):
        return ((slot // 8) * 4 + lax.rem(slot // 4, 2) * 2 + k, lax.rem(slot, 4))

    sibling = dev(own, 1 - core)
    slot_x = y * 8 + (1 - x) * 4 + z
    slot_y = (1 - y) * 8 + x * 4 + z
    slot_d = (1 - y) * 8 + (1 - x) * 4 + z

    def remote(src, dst, ssem, rsem, target):
        return pltpu.make_async_remote_copy(
            src_ref=src, dst_ref=dst, send_sem=ssem, recv_sem=rsem,
            device_id=target, device_id_type=MESH_ID,
        )

    def done(ref, sem):
        pltpu.make_async_copy(ref, ref, sem).wait()

    barrier = pltpu.get_barrier_semaphore()

    def greet(r, c):
        pl.semaphore_signal(
            barrier, inc=1, device_id=dev(lax.rem(own + r, 16), core), device_id_type=MESH_ID
        )
        return c

    lax.fori_loop(1, 16, greet, 0)
    pl.semaphore_signal(barrier, inc=1, device_id=sibling, device_id_type=MESH_ID)

    rows = pl.ds(pl.multiple_of(512 * core, 512), 512)
    pltpu.make_async_copy(attn_ref.at[core], slabA.at[core], loc.at[0]).start()
    pltpu.make_async_copy(small_ref.at[core], smb.at[own, core], loc.at[1]).start()
    pltpu.make_async_copy(bnd_ref.at[core], bndb.at[core], loc.at[2]).start()

    @pl.when(core == 0)
    def _():
        pltpu.make_async_copy(qt_ref, X.at[rows], loc.at[3]).start()

    @pl.when(core == 1)
    def _():
        pltpu.make_async_copy(pt_ref, X.at[rows], loc.at[3]).start()

    pltpu.make_async_copy(ffi_ref.at[core], slabI.at[core], loc.at[4]).start()
    pltpu.make_async_copy(ffo_ref.at[core], slabO.at[core], loc.at[5]).start()
    pl.semaphore_wait(barrier, 16)

    other = 1 - core
    remote(attn_ref.at[other], slabA.at[core], sib_s.at[0], sib_r.at[0], sibling).start()
    remote(small_ref.at[other], smb.at[own, core], sib_s.at[1], sib_r.at[1], sibling).start()
    remote(bnd_ref.at[other], bndb.at[core], sib_s.at[2], sib_r.at[2], sibling).start()

    @pl.when(core == 0)
    def _():
        remote(pt_ref, X.at[rows], sib_s.at[3], sib_r.at[3], sibling).start()

    @pl.when(core == 1)
    def _():
        remote(qt_ref, X.at[rows], sib_s.at[3], sib_r.at[3], sibling).start()

    remote(ffi_ref.at[other], slabI.at[core], sib_s.at[4], sib_r.at[4], sibling).start()
    remote(ffo_ref.at[other], slabO.at[core], sib_s.at[5], sib_r.at[5], sibling).start()

    done(slabA.at[core], loc.at[0])
    done(slabA.at[other], sib_r.at[0])
    for m in range(4):
        cols = slice(768 * m, 768 * m + 768)
        R[own, m] = jnp.concatenate([slabA[0, :, cols], slabA[1, :, cols]], axis=0).astype(LOW)
        for target in (slot_x, slot_y):
            remote(R.at[own, m], R.at[own, m], at_s.at[m], at_r.at[own, m, 0], dev(target, core)).start()

        def along_z(r, c):
            target = line + lax.rem(z + r, 4)
            remote(R.at[own, m], R.at[own, m], at_s.at[m], at_r.at[own, m, 0], dev(target, core)).start()
            return c

        lax.fori_loop(1, 4, along_z, 0)

    done(smb.at[own, core], loc.at[1])
    done(smb.at[own, other], sib_r.at[1])

    def direct(src_of, dst, ssem, rsem):
        def body(r, c):
            target = lax.rem(own + r, 16)
            remote(src_of(target), dst.at[own], ssem, rsem, dev(target, core)).start()
            return c

        lax.fori_loop(1, 16, body, 0)

    def direct_done(dst, rsem):
        done(dst.at[pl.ds(0, 15)], rsem)

    direct(lambda t: smb.at[own], smb, aa_s.at[0], aa_r.at[0])

    def relay(m):
        def from_z(r, c):
            slot = line + lax.rem(z + r, 4)
            done(R.at[slot, m], at_r.at[slot, m, 0])
            for target in (slot_x, slot_y):
                remote(R.at[slot, m], R.at[slot, m], at_s.at[m], at_r.at[slot, m, 0], dev(target, core)).start()
            return c

        lax.fori_loop(1, 4, from_z, 0)

        def from_plane(r, c):
            zz = lax.rem(z + r, 4)
            for base, target, half in (
                (y * 8 + (1 - x) * 4, slot_y, 0),
                ((1 - y) * 8 + x * 4, slot_x, 1),
            ):
                slot = base + zz
                done(R.at[slot, m], at_r.at[slot, m, 0])
                part = R.at[slot, m, :, pl.ds(384 * half, 384)]
                remote(part, part, at_s.at[m], at_r.at[slot, m, half], dev(target, core)).start()
            return c

        lax.fori_loop(0, 4, from_plane, 0)

    def from_slots(read, write):
        def body(g, c):
            got = [read(4 * g + i).astype(F32) for i in range(4)]
            natural = jnp.concatenate([v[0:24] for v in got] + [v[24:48] for v in got], axis=0)
            write(pl.ds(pl.multiple_of(192 * g, 64), 192), natural.astype(LOW))
            return c

        lax.fori_loop(0, 4, body, 0)

    def to_slots(read, write):
        def body(g, c):
            v = read(pl.ds(pl.multiple_of(192 * g, 64), 192))
            for i in range(4):
                part = jnp.concatenate(
                    [v[24 * i : 24 * i + 24], v[96 + 24 * i : 96 + 24 * i + 24]], axis=0
                )
                write(4 * g + i, part.astype(LOW))
            return c

        lax.fori_loop(0, 4, body, 0)

    def arrive(m):
        def body(zz, c):
            slot = (1 - y) * 8 + (1 - x) * 4 + zz
            for half in range(2):
                done(R.at[slot, m, :, pl.ds(384 * half, 384)], at_r.at[slot, m, half])
            return c

        lax.fori_loop(0, 4, body, 0)

        def write(where, v):
            WN[m, where, :] = v

        from_slots(lambda s: R[s, m], write)

    def gather_start(buf, n):
        def body(r, c):
            target = line + lax.rem(z + r, 4)
            remote(buf.at[own], buf.at[own], ag_s.at[n], ag_z.at[n], dev(target, core)).start()
            return c

        lax.fori_loop(1, 4, body, 0)

    def gather_forward(buf, n):
        done(buf.at[pl.ds(0, 3)], ag_z.at[n])
        block = buf.at[pl.ds(line, 4)]
        for target in (slot_x, slot_y, slot_d):
            remote(block, block, ag_s.at[n], ag_p.at[n], dev(target, core)).start()

    def gather_done(buf, n):
        done(buf.at[pl.ds(0, 12)], ag_p.at[n])

    def prepare_ffn():
        row = lax.broadcasted_iota(jnp.int32, (384, 512), 0)
        col = lax.broadcasted_iota(jnp.int32, (384, 512), 1)
        Emat[...] = jnp.where(col == 128 * (row // 96) + lax.rem(row, 96), 1.0, 0.0).astype(LOW)
        done(slabI.at[core], loc.at[4])
        done(slabI.at[other], sib_r.at[4])
        for g in range(8):
            cols = slice(384 * g, 384 * g + 384)
            part = jnp.concatenate([slabI[0, :, cols], slabI[1, :, cols]], axis=0).astype(LOW)
            wide = dot_nn(part, Emat[...]).astype(LOW)
            for i in range(4):
                w1s_[4 * (g // 2) + i, :, 128 * (g % 2) : 128 * (g % 2) + 128] = wide[
                    :, 128 * i : 128 * i + 128
                ]
        direct(lambda t: w1s_.at[t], w1r, aa_s.at[1], aa_r.at[1])
        w1r[own] = w1s_[own]
        done(slabO.at[core], loc.at[5])
        done(slabO.at[other], sib_r.at[5])
        gap = jnp.zeros((32, 768), F32)
        W2[...] = jnp.concatenate([slabO[0], gap, slabO[1], gap], axis=0).astype(LOW)

    def natural_small():
        direct_done(smb, aa_r.at[0])
        for g in range(8):
            parts = [smb[4 * (g // 2) + i, g % 2] for i in range(4)]
            lines = [parts[0][0:1], parts[0][1:2]]
            for i in range(1, 4):
                lines += [parts[i - 1][2:3] + parts[i][0:1], parts[i][1:2]]
            lines += [parts[3][2:3]]
            sn[9 * g : 9 * g + 9, :] = jnp.concatenate(lines, axis=0)
        remote(sn, sno, sib_s.at[6], sib_r.at[6], sibling).start()

    def vec(row, count=6, ref=sn):
        return jnp.concatenate([ref[row + i : row + i + 1, :] for i in range(count)], axis=1)

    relay(0)
    done(bndb.at[core], loc.at[2])
    done(bndb.at[other], sib_r.at[2])
    done(X.at[pl.ds(0, 512)], loc.at[3])
    done(X.at[pl.ds(0, 512)], sib_r.at[3])
    starts = jnp.concatenate([bndb[0, 0:8], bndb[1, 0:8] + 512], axis=0)[:, 0:1]
    ends = jnp.concatenate([bndb[0, 8:16], bndb[1, 8:16] + 512], axis=0)[:, 0:1]
    token = lax.broadcasted_iota(jnp.int32, (16, 1024), 1)
    inside = jnp.logical_and(token >= starts, token < ends)
    first = jnp.where(token == starts, 1.0, 0.0).astype(LOW)
    cls_in = dot_nn(first, X[...])
    cls_low = cls_in.astype(LOW)
    natural_small()
    relay(1)
    arrive(0)
    queries = (dot_nn(cls_low, WN[0]) + vec(0)).astype(LOW)
    Qb[own] = queries
    relay(2)
    arrive(1)
    qsb[...] = (dot_nt(expand_heads(queries), WN[1]) * (HD**-0.5)).astype(LOW)
    ST[...] = dot_nt(qsb[...], X[...])

    def soften(h, c):
        at = pl.ds(pl.multiple_of(16 * h, 16), 16)
        s = jnp.where(inside, ST[at, :], -1000000000.0)
        e = jnp.exp(s - jnp.max(s, axis=1, keepdims=True))
        p = e / jnp.sum(e, axis=1, keepdims=True)
        Pf[at, :] = p
        Pb[at, :] = p.astype(LOW)
        return c

    lax.fori_loop(0, 12, soften, 0)
    relay(3)
    ybf[...] = dot_nn(Pb[...], X[...]).astype(LOW)
    prepare_ffn()
    arrive(2)
    mixed = (pick_heads(dot_nn(ybf[...], WN[2])) + vec(6)).astype(LOW)
    arrive(3)
    lifted = cls_in + dot_nn(mixed, WN[3]) + vec(12)
    centred = lifted - jnp.mean(lifted, axis=1, keepdims=True)
    rstd_one = lax.rsqrt(jnp.mean(centred * centred, axis=1, keepdims=True) + NORM_EPS)
    hat_one = centred * rstd_one
    normed = hat_one * vec(18) + vec(24)
    Yb[own] = normed.astype(LOW)
    gather_start(Yb, 0)
    gather_start(Qb, 1)

    early = jnp.concatenate(
        [ybf[...].astype(F32), cls_in, mixed.astype(F32), jnp.zeros((32, 768), F32)], axis=0
    )
    DX[0:768, 0:256] = early.T

    def write_m1(slot, v):
        m1s[slot] = v

    to_slots(lambda w: DX[w, 0:256], write_m1)
    m1r[own] = m1s[own]
    gather_forward(Yb, 0)

    b1 = jnp.concatenate([vec(30 + 3 * g, 3) for g in range(8)], axis=0).astype(LOW)
    b1_wide = dot_nn(b1, Emat[...])
    for g in range(8):
        b1p[g] = jnp.broadcast_to(b1_wide[g : g + 1], (8, 512))
    group = pl.multiple_of(128 * z, 128)
    gy = 4 * y + 2 * x
    b1_row = jnp.concatenate(
        [b1p[gy, 0:1, pl.ds(group, 128)], b1p[gy + 1, 0:1, pl.ds(group, 128)]], axis=1
    )
    direct_done(w1r, aa_r.at[1])

    def write_w1(where, v):
        W1[where, :] = v

    from_slots(lambda s: w1r[s], write_w1)
    gather_done(Yb, 0)
    all_y = Yb[...].reshape(256, 768)
    act = dot_nn(all_y, W1[...]) + b1_row
    Act[...] = act
    hidden, unused = gelu_parts(act)
    Gb[...] = hidden.astype(LOW)
    P2s[...] = dot_nn(Gb[...], W2[...]).astype(LOW).reshape(16, 16, 768)
    direct(lambda t: P2s.at[t], P2r, aa_s.at[2], aa_r.at[2])
    P2r[own] = P2s[own]
    gather_forward(Qb, 1)
    direct_done(P2r, aa_r.at[2])
    direct(lambda t: m1s.at[t], m1r, aa_s.at[3], aa_r.at[3])
    second = normed + jnp.sum(P2r[...].astype(F32), axis=0) + vec(54)
    centred = second - jnp.mean(second, axis=1, keepdims=True)
    rstd_two = lax.rsqrt(jnp.mean(centred * centred, axis=1, keepdims=True) + NORM_EPS)
    hat_two = centred * rstd_two
    rstd_high, rstd_low = split_low(rstd_two)
    lane = lax.broadcasted_iota(jnp.int32, (16, 128), 1)
    positive = jnp.concatenate([bndb[0, 16:24], bndb[1, 16:24]], axis=0).astype(F32)
    extra = jnp.where(
        lane == 0, rstd_high.astype(F32),
        jnp.where(lane == 1, rstd_low.astype(F32), jnp.where(lane == 2, positive, 0.0)),
    )
    XH[core, own] = jnp.concatenate([hat_two, extra], axis=1).astype(LOW)
    mine = XH.at[core]
    gather_start(mine, 2)
    gather_forward(mine, 2)
    gather_done(mine, 2)
    remote(XH.at[core], XH.at[core], sib_s.at[7], sib_r.at[7], sibling).start()
    done(sno, sib_r.at[6])
    done(XH.at[other], sib_r.at[7])

    def vec_of(encoder, row):
        return jnp.where(core == encoder, vec(row), vec(row, 6, sno))

    xq = XH[0].reshape(256, 896).astype(F32)
    xp = XH[1].reshape(256, 896).astype(F32)
    qc = (xq[:, 0:768] * vec_of(0, 60) + vec_of(0, 66)).astype(LOW)
    pc = (xp[:, 0:768] * vec_of(1, 60) + vec_of(1, 66)).astype(LOW)
    scale = 768 ** (-0.5)
    scores = dot_nt(qc, pc) * scale
    raised = jnp.exp(scores - jnp.max(scores, axis=1, keepdims=True))
    soft = raised / jnp.sum(raised, axis=1, keepdims=True)
    place = lax.broadcasted_iota(jnp.int32, (256, 256), 1)
    slot_of = place // 16
    owner_of = (
        16 * (slot_of // 8) + 8 * lax.rem(slot_of // 4, 2)
        + 4 * (lax.rem(place, 16) // 8) + lax.rem(slot_of, 4)
    )
    passage = (8 * owner_of + lax.rem(place, 8)).astype(F32)
    target = jnp.where(passage == xq[:, 770:771], 1.0, 0.0)
    grad_scores = (soft - target).astype(LOW)

    @pl.when(core == 0)
    def _():
        Dout[...] = dot_nn(grad_scores, pc) * scale

    @pl.when(core == 1)
    def _():
        Dout[...] = dot_tn(grad_scores, qc) * scale

    dout = Dout[...]
    block = XH[core].reshape(256, 896).astype(F32)
    hat = block[:, 0:768]
    rstd = block[:, 768:769] + block[:, 769:770]
    inner = dout * vec(60)
    grad_two = rstd * (
        inner - jnp.mean(inner, axis=1, keepdims=True)
        - hat * jnp.mean(inner * hat, axis=1, keepdims=True)
    )
    dg2 = jnp.sum(dout * hat, axis=0, keepdims=True)
    ds2 = jnp.sum(dout, axis=0, keepdims=True)
    Dout[...] = grad_two
    dZb[...] = grad_two.astype(LOW)
    db2 = jnp.sum(dZb[...].astype(F32), axis=0, keepdims=True)
    unused, slope = gelu_parts(Act[...])
    da = (dot_nt(dZb[...], W2[...]) * slope).astype(LOW)
    P3s[...] = dot_nt(da, W1[...]).astype(LOW).reshape(16, 16, 768)
    direct(lambda t: P3s.at[t], P3r, aa_s.at[4], aa_r.at[4])
    P3r[own] = P3s[own]
    db1 = jnp.sum(da.astype(F32), axis=0, keepdims=True)
    dw2 = dot_tn(Gb[...], dZb[...])
    GO[0] = dw2[0:96]
    GO[1] = dw2[128:224]
    pltpu.make_async_copy(GO.at[core], go_ref.at[core], out_l.at[0]).start()
    remote(GO.at[other], go_ref.at[core], out_s.at[0], out_r.at[0], sibling).start()
    DX[0:768, 0:256] = dot_tn(all_y, da)

    def write_dw(slot, v):
        dws[slot] = v

    to_slots(lambda w: DX[w, 0:256], write_dw)
    dwr[own] = dws[own]
    own_rows = pl.ds(pl.multiple_of(16 * own, 16), 16)
    direct_done(P3r, aa_r.at[4])

    grad_normed = Dout[own_rows, :] + jnp.sum(P3r[...].astype(F32), axis=0)
    inner = grad_normed * vec(18)
    grad_one = rstd_one * (
        inner - jnp.mean(inner, axis=1, keepdims=True)
        - hat_one * jnp.mean(inner * hat_one, axis=1, keepdims=True)
    )
    grad_lift = grad_one.astype(LOW)
    grad_mixed = dot_nt(grad_lift, WN[3]).astype(LOW)
    dUb[own] = grad_lift
    dAb[own] = grad_mixed
    gather_start(dUb, 3)
    gather_start(dAb, 4)
    direct(lambda t: dws.at[t], dwr, aa_s.at[5], aa_r.at[5])
    dg1 = jnp.sum(grad_normed * hat_one, axis=0, keepdims=True)
    ds1 = jnp.sum(grad_normed, axis=0, keepdims=True)
    sgs[...] = jnp.concatenate(
        [dg1[:, 128 * i : 128 * i + 128] for i in range(6)]
        + [ds1[:, 128 * i : 128 * i + 128] for i in range(6)]
        + [db1[:, 0:128], db1[:, 128:256], jnp.zeros((2, 128), F32)], axis=0,
    )
    direct(lambda t: sgs, sgr, aa_s.at[6], aa_r.at[6])
    sgr[own] = sgs[...]
    spread = expand_heads(grad_mixed)
    vtb[...] = dot_nt(spread, WN[2]).astype(LOW)
    constant = jnp.sum(spread.astype(F32) * vec(6), axis=1, keepdims=True)
    ST[...] = dot_nt(vtb[...], X[...]) + constant

    def harden(h, c):
        at = pl.ds(pl.multiple_of(16 * h, 16), 16)
        p, dprob = Pf[at, :], ST[at, :]
        total = jnp.sum(p * dprob, axis=1, keepdims=True)
        DSb[at, :] = (p * (dprob - total)).astype(LOW)
        return c

    lax.fori_loop(0, 12, harden, 0)
    late = (dot_nn(DSb[...], X[...]) * (HD**-0.5)).astype(LOW)
    DX[0:768, 0:256] = jnp.concatenate(
        [late.astype(F32), jnp.zeros((64, 768), F32)], axis=0
    ).T

    def write_m2(slot, v):
        m2s[slot] = v

    to_slots(lambda w: DX[w, 0:256], write_m2)
    direct(lambda t: m2s.at[t], m2r, aa_s.at[7], aa_r.at[7])
    m2r[own] = m2s[own]
    grad_query = pick_heads(dot_nn(late, WN[1])).astype(LOW)
    dQb[own] = grad_query
    gather_start(dQb, 5)
    gather_forward(dUb, 3)
    gather_forward(dAb, 4)
    gather_forward(dQb, 5)

    grad_cls = grad_one + dot_nt(grad_query, WN[0])
    cls_high, cls_rest = split_low(grad_cls)
    right = jnp.concatenate([qsb[...], vtb[...], cls_high, cls_rest], axis=0)
    for k in range(2):
        part = slice(512 * k, 512 * k + 512)
        left = jnp.concatenate([DSb[:, part], Pb[:, part], first[:, part], first[:, part]], axis=0)
        DX[part, :] = dot_tn(left, right)
    other_rows = pl.ds(pl.multiple_of(512 * other, 512), 512)

    @pl.when(core == 0)
    def _():
        pltpu.make_async_copy(DX.at[rows], dxq_ref, out_l.at[1]).start()
        remote(DX.at[other_rows], dxq_ref, out_s.at[1], out_r.at[1], sibling).start()

    @pl.when(core == 1)
    def _():
        pltpu.make_async_copy(DX.at[rows], dxp_ref, out_l.at[1]).start()
        remote(DX.at[other_rows], dxp_ref, out_s.at[1], out_r.at[1], sibling).start()

    direct_done(dwr, aa_r.at[5])
    for g in range(8):
        wide = jnp.concatenate(
            [dwr[4 * (g // 2) + i, :, 128 * (g % 2) : 128 * (g % 2) + 128] for i in range(4)], axis=1
        )
        narrow = dot_nt(wide, Emat[...])
        GI[0, :, 384 * g : 384 * g + 384] = narrow[0:24]
        GI[1, :, 384 * g : 384 * g + 384] = narrow[24:48]
    pltpu.make_async_copy(GI.at[core], gi_ref.at[core], out_l.at[2]).start()
    remote(GI.at[other], gi_ref.at[core], out_s.at[2], out_r.at[2], sibling).start()

    def put(m, v):
        GA[0, :, 768 * m : 768 * m + 768] = v[0:24]
        GA[1, :, 768 * m : 768 * m + 768] = v[24:48]

    def factor_sum(messages, columns):
        def body(s, total):
            wide = jnp.concatenate(
                [expand_heads(columns[s]), jnp.zeros((64, 768), LOW)], axis=0
            )
            return total + dot_nn(messages[s], wide)

        return lax.fori_loop(0, 16, body, jnp.zeros((48, 768), F32))

    gather_done(Qb, 1)
    gather_done(dAb, 4)
    direct_done(m1r, aa_r.at[3])
    put(2, factor_sum(m1r, dAb))
    gather_done(dUb, 3)

    def columns_of(at):
        return jnp.concatenate(
            [m1r[s, :, at : at + 16].astype(F32) for s in range(16)], axis=1
        ).astype(LOW)

    all_du = dUb[...].reshape(256, 768)
    put(3, dot_nn(columns_of(208), all_du))
    direct_done(m2r, aa_r.at[7])
    put(1, factor_sum(m2r, Qb))
    gather_done(dQb, 5)
    all_dq = dQb[...].reshape(256, 768)
    put(0, dot_nn(columns_of(192), all_dq))
    pltpu.make_async_copy(GA.at[core], ga_ref.at[core], out_l.at[3]).start()
    remote(GA.at[other], ga_ref.at[core], out_s.at[3], out_r.at[3], sibling).start()

    direct_done(sgr, aa_r.at[6])
    sums = jnp.sum(sgr[...], axis=0)
    hidden_rows = []
    for g in range(8):
        wide = jnp.concatenate(
            [sgr[4 * (g // 2) + i, 12 + g % 2 : 13 + g % 2, :] for i in range(4)], axis=1
        )
        hidden_rows.append(wide)
    wide = jnp.concatenate(hidden_rows, axis=0)
    high, rest = split_low(wide)
    rest, last = split_low(wide - high.astype(F32))
    narrow = dot_nt(high, Emat[...]) + dot_nt(rest, Emat[...]) + dot_nt(last, Emat[...])

    def six(v):
        return [v[:, 128 * i : 128 * i + 128] for i in range(6)]

    lines = six(jnp.sum(all_dq.astype(F32), axis=0, keepdims=True))
    lines += six(jnp.sum(dAb[...].reshape(256, 768).astype(F32), axis=0, keepdims=True))
    lines += six(jnp.sum(all_du.astype(F32), axis=0, keepdims=True))
    lines += [sums[0:12]]
    for g in range(8):
        lines += [narrow[g : g + 1, 128 * i : 128 * i + 128] for i in range(3)]
    lines += six(db2) + six(dg2) + six(ds2) + [jnp.zeros((8, 128), F32)]
    packed = jnp.concatenate(lines, axis=0)
    for g in range(8):
        for i in range(4):
            at = 9 * g + 9 * i // 4
            GS[g, i] = packed[at : at + 8]
    for k in range(2):
        GSw[k] = GS[gy + k, z]
    pltpu.make_async_copy(GSw.at[core], gs_ref.at[core], out_l.at[4]).start()
    remote(GSw.at[other], gs_ref.at[core], out_s.at[4], out_r.at[4], sibling).start()

    for n, (mine_ref, theirs) in enumerate(
        ((GO.at[0], GO.at[0]), (DX.at[rows], DX.at[rows]), (GI.at[0], GI.at[0]),
         (GA.at[0], GA.at[0]), (GSw.at[0], GSw.at[0]))
    ):
        done(mine_ref, out_l.at[n])
        done(theirs, out_s.at[n])
        done(theirs, out_r.at[n])
    for n, ref in enumerate(
        (slabA.at[0], smb.at[0, 0], bndb.at[0], X.at[rows], slabI.at[0], slabO.at[0], sn, XH.at[0])
    ):
        done(ref, sib_s.at[n])
    for m in range(4):
        done(R.at[pl.ds(0, 15), m], at_s.at[m])
    for n, ref in enumerate((Yb, Qb, XH.at[0], dUb, dAb, dQb)):
        done(ref.at[pl.ds(0, 15)], ag_s.at[n])
    for n, ref in enumerate((smb, w1r, P2r, m1r, P3r, dwr, sgr, m2r)):
        done(ref.at[pl.ds(0, 15)], aa_s.at[n])


def kernel_call(qt, pt, attn, ffi, ffo, small, bnd):
    any_space = pl.BlockSpec(memory_space=pl.ANY)
    vmem = pl.BlockSpec(memory_space=pltpu.VMEM)
    V = pltpu.VMEM
    dma = pltpu.SemaphoreType.DMA
    scratch = [
        V((1024, 768), LOW), V((2, 24, 3072), F32), V((2, 24, 3072), F32), V((2, 96, 768), F32),
        V((16, 2, 8, 128), F32), V((2, 24, 128), jnp.int32), V((16, 4, 48, 768), LOW),
        V((4, 768, 768), LOW), V((72, 128), F32), V((72, 128), F32), V((192, 1024), F32),
        V((192, 1024), F32), V((192, 1024), LOW), V((192, 1024), LOW), V((384, 512), LOW),
        V((8, 8, 512), F32),
        V((16, 48, 256), LOW), V((16, 48, 256), LOW), V((768, 256), LOW), V((256, 768), LOW),
        V((16, 16, 768), LOW), V((16, 16, 768), LOW), V((16, 16, 768), LOW),
        V((2, 16, 16, 896), LOW), V((256, 768), F32), V((256, 768), LOW), V((256, 256), LOW),
        V((256, 256), F32), V((16, 16, 768), LOW), V((16, 16, 768), LOW), V((16, 16, 768), LOW),
        V((16, 16, 768), LOW), V((16, 16, 768), LOW), V((16, 16, 768), LOW),
        V((16, 48, 256), LOW), V((16, 48, 256), LOW), V((16, 48, 256), LOW), V((16, 48, 256), LOW),
        V((16, 48, 256), LOW), V((16, 48, 256), LOW), V((16, 128), F32), V((16, 16, 128), F32),
        V((8, 4, 8, 128), F32), V((2, 8, 128), F32), V((2, 24, 3072), F32), V((2, 24, 3072), F32),
        V((2, 96, 768), F32), V((1024, 768), F32), V((192, 768), LOW), V((192, 768), LOW),
        V((192, 768), LOW),
        dma((6,)), dma((8,)), dma((8,)), dma((4,)), dma((16, 4, 2)), dma((6,)), dma((6,)),
        dma((6,)), dma((8,)), dma((8,)), dma((5,)), dma((5,)), dma((5,)),
    ]
    shapes = (
        (2, 24, 3072), (2, 24, 3072), (2, 96, 768), (2, 8, 128), (512, 768), (512, 768)
    )
    return pl.pallas_call(
        step_kernel,
        out_shape=[jax.ShapeDtypeStruct(s, F32) for s in shapes],
        in_specs=[any_space] * 5 + [vmem] * 2,
        out_specs=[any_space] * 6,
        scratch_shapes=scratch,
        compiler_params=pltpu.CompilerParams(
            collective_id=0, has_side_effects=True, vmem_limit_bytes=56 << 20
        ),
    )(qt, pt, attn, ffi, ffo, small, bnd)


def local_kernel(
    question_tokens, passage_tokens, passage_lengths, positives,
    attn_weight, attn_first, attn_second, ffn_in_weight, ffn_in_first, ffn_in_second,
    ffn_out_weight, ffn_out_first, ffn_out_second, small_params, small_first, small_second,
):
    pair = lax.axis_index("pair")
    zero = jnp.zeros((), jnp.int32)
    low_small = small_params.astype(LOW).astype(F32)
    window = lax.dynamic_update_slice(jnp.zeros((2, 1024), F32), low_small, (zero, 32 * pair))
    ends = jnp.cumsum(passage_lengths, axis=1)
    base = jnp.array([[0], [256]], jnp.int32)
    passage_ends = (ends + base).reshape(8)
    passage_starts = (ends - passage_lengths + base).reshape(8)
    question_starts = jnp.arange(8, dtype=jnp.int32) * 64
    marks = jnp.stack(
        [
            jnp.concatenate([question_starts, question_starts + 64, positives]),
            jnp.concatenate([passage_starts, passage_ends, positives]),
        ]
    )
    bounds = jnp.broadcast_to(marks[:, :, None], (2, 24, 128))
    grads = kernel_call(
        question_tokens.reshape(512, 768), passage_tokens.reshape(512, 768),
        attn_weight, ffn_in_weight, ffn_out_weight, window.reshape(2, 8, 128), bounds,
    )
    attn_sum, inner_sum, outer_sum, small_window, grad_question, grad_passage = grads
    small_sum = lax.dynamic_slice(small_window.reshape(2, 1024), (zero, 32 * pair), (2, 288))
    return (
        *adam_update(attn_weight, attn_first, attn_second, attn_sum, RATE_MATRIX, DECAY_MATRIX),
        *adam_update(ffn_in_weight, ffn_in_first, ffn_in_second, inner_sum, RATE_MATRIX, DECAY_MATRIX),
        *adam_update(ffn_out_weight, ffn_out_first, ffn_out_second, outer_sum, RATE_MATRIX, DECAY_MATRIX),
        *adam_update(small_params, small_first, small_second, small_sum, RATE_SMALL, 0.0),
        grad_question.reshape(question_tokens.shape),
        grad_passage.reshape(passage_tokens.shape),
    )


def fits_kernel(mesh):
    return mesh.shape["dp"] == 8 and mesh.shape["pair"] == 4


def solution(mesh):
    in_specs = (
        P(("dp", "pair"), None, None),
        P(("dp", "pair"), None, None),
        P(("dp", "pair"), None),
        P(("dp", "pair")),
        P(None, ("dp", "pair"), None),
        P(None, ("dp", "pair"), None),
        P(None, ("dp", "pair"), None),
        P(None, ("dp", "pair"), None),
        P(None, ("dp", "pair"), None),
        P(None, ("dp", "pair"), None),
        P(None, ("dp", "pair"), None),
        P(None, ("dp", "pair"), None),
        P(None, ("dp", "pair"), None),
        P(None, ("dp", "pair")),
        P(None, ("dp", "pair")),
        P(None, ("dp", "pair")),
    )
    out_specs = (
        P(None, ("dp", "pair"), None),
        P(None, ("dp", "pair"), None),
        P(None, ("dp", "pair"), None),
        P(None, ("dp", "pair"), None),
        P(None, ("dp", "pair"), None),
        P(None, ("dp", "pair"), None),
        P(None, ("dp", "pair"), None),
        P(None, ("dp", "pair"), None),
        P(None, ("dp", "pair"), None),
        P(None, ("dp", "pair")),
        P(None, ("dp", "pair")),
        P(None, ("dp", "pair")),
        P(("dp", "pair"), None, None),
        P(("dp", "pair"), None, None),
    )
    body = local_kernel if fits_kernel(mesh) else local
    return jax.shard_map(body, mesh=mesh, in_specs=in_specs, out_specs=out_specs, check_vma=False)
```

```python
import math

import jax
import jax.numpy as jnp
from jax import lax
from jax.experimental import pallas as pl
from jax.experimental.pallas import tpu as pltpu
from jax.sharding import PartitionSpec as P

HD = 64
STEP = 5


BETA_ONE = 0.9
BETA_TWO = 0.999
ADAM_EPS = 1e-08
NORM_EPS = 1e-06
RATE_MATRIX = 0.05
RATE_SMALL = 0.3
DECAY_MATRIX = 0.01


def layer_norm(values, norm_gain, norm_shift):
    row_mean = jnp.mean(values, axis=-1, keepdims=True)
    centred = values - row_mean
    spread = jnp.mean(centred * centred, axis=-1, keepdims=True)
    return centred * lax.rsqrt(spread + NORM_EPS) * norm_gain + norm_shift


def gelu_exact(values):
    return jax.nn.gelu(values, approximate=False)


def unpack(small_vec, model_width, hidden_width):
    widths = [model_width] * 5 + [hidden_width] + [model_width] * 3
    pieces = []
    offset = 0
    for length in widths:
        pieces.append(small_vec[offset : offset + length])
        offset = offset + length
    return pieces


def masked_scores(queries, key_rows, segment):
    scores = jnp.einsum(
        "blhe,bmhe->bhlm", queries, key_rows, preferred_element_type=jnp.float32
    ) * HD ** (-0.5)
    allowed = (segment[:, :, None] == segment[:, None, :])[:, None]
    return jnp.where(allowed, scores, -1000000000.0)


def encoder_forward(tokens, segment, attn_weights, inner_weight, outer_weight, small_vec):
    batch_size, length, model_width = tokens.shape
    head_count = model_width // HD
    flat_rows = tokens.reshape(batch_size * length, model_width)
    (
        bias_query,
        bias_value,
        bias_out,
        gain_one,
        shift_one,
        bias_inner,
        bias_outer,
        gain_two,
        shift_two,
    ) = unpack(small_vec, model_width, inner_weight.shape[1])
    bias_proj = jnp.concatenate([bias_query, jnp.zeros_like(bias_query), bias_value])
    projected = (
        jnp.dot(flat_rows, attn_weights[:, : 3 * model_width], preferred_element_type=jnp.float32)
        + bias_proj
    )
    projected = projected.astype(jnp.bfloat16).reshape(batch_size, length, 3, head_count, HD)
    queries = projected[:, :, 0]
    key_rows = projected[:, :, 1]
    value_rows = projected[:, :, 2]
    scores = masked_scores(queries, key_rows, segment)
    top_score = jnp.max(scores, axis=-1, keepdims=True)
    raised = jnp.exp(scores - top_score)
    totals = jnp.sum(raised, axis=-1, keepdims=True)
    attn_probs = (raised / totals).astype(jnp.bfloat16)
    log_total = top_score + jnp.log(totals)
    mixed_heads = jnp.einsum(
        "bhlm,bmhe->blhe", attn_probs, value_rows, preferred_element_type=jnp.float32
    )
    mixed_flat = mixed_heads.astype(jnp.bfloat16).reshape(batch_size * length, model_width)
    attn_out = (
        jnp.dot(mixed_flat, attn_weights[:, 3 * model_width :], preferred_element_type=jnp.float32)
        + bias_out
    )
    residual_one = flat_rows.astype(jnp.float32) + attn_out
    normed_one = layer_norm(residual_one, gain_one, shift_one)
    pre_act = (
        jnp.dot(normed_one.astype(jnp.bfloat16), inner_weight, preferred_element_type=jnp.float32)
        + bias_inner
    )
    activated = gelu_exact(pre_act).astype(jnp.bfloat16)
    branch = jnp.dot(activated, outer_weight, preferred_element_type=jnp.float32) + bias_outer
    residual_two = normed_one + branch
    result = layer_norm(residual_two, gain_two, shift_two).reshape(batch_size, length, model_width)
    kept_values = (
        queries,
        key_rows,
        value_rows,
        log_total,
        mixed_flat,
        residual_one,
        normed_one,
        pre_act,
        activated,
        residual_two,
    )
    return (result, kept_values)


def encoder_backward(
    tokens, segment, attn_weights, inner_weight, outer_weight, small_vec, kept_values, grad_result
):
    batch_size, length, model_width = tokens.shape
    head_count = model_width // HD
    flat_rows = tokens.reshape(batch_size * length, model_width)
    (
        queries,
        key_rows,
        value_rows,
        log_total,
        mixed_flat,
        residual_one,
        normed_one,
        pre_act,
        activated,
        residual_two,
    ) = kept_values
    (
        bias_query,
        bias_value,
        bias_out,
        gain_one,
        shift_one,
        bias_inner,
        bias_outer,
        gain_two,
        shift_two,
    ) = unpack(small_vec, model_width, inner_weight.shape[1])
    grad_flat = grad_result.reshape(batch_size * length, model_width)
    unused_two, norm_two_back = jax.vjp(layer_norm, residual_two, gain_two, shift_two)
    grad_two, grad_gain_two, grad_shift_two = norm_two_back(grad_flat)
    grad_branch = grad_two.astype(jnp.bfloat16)
    grad_bias_outer = jnp.sum(grad_branch, axis=0, dtype=jnp.float32)
    grad_outer = jnp.dot(activated.T, grad_branch, preferred_element_type=jnp.float32)
    grad_act = jnp.dot(grad_branch, outer_weight.T, preferred_element_type=jnp.float32)
    unused_act, gelu_back = jax.vjp(gelu_exact, pre_act)
    grad_pre = gelu_back(grad_act)[0].astype(jnp.bfloat16)
    grad_bias_inner = jnp.sum(grad_pre, axis=0, dtype=jnp.float32)
    grad_inner = jnp.dot(
        normed_one.astype(jnp.bfloat16).T, grad_pre, preferred_element_type=jnp.float32
    )
    grad_normed = grad_two + jnp.dot(grad_pre, inner_weight.T, preferred_element_type=jnp.float32)
    unused_one, norm_one_back = jax.vjp(layer_norm, residual_one, gain_one, shift_one)
    grad_one, grad_gain_one, grad_shift_one = norm_one_back(grad_normed)
    grad_attn_out = grad_one.astype(jnp.bfloat16)
    grad_bias_out = jnp.sum(grad_attn_out, axis=0, dtype=jnp.float32)
    grad_out_proj = jnp.dot(mixed_flat.T, grad_attn_out, preferred_element_type=jnp.float32)
    grad_mixed = jnp.dot(
        grad_attn_out, attn_weights[:, 3 * model_width :].T, preferred_element_type=jnp.float32
    )
    grad_mixed = grad_mixed.astype(jnp.bfloat16).reshape(batch_size, length, head_count, HD)
    scores = masked_scores(queries, key_rows, segment)
    attn_probs = jnp.exp(scores - log_total)
    grad_probs = jnp.einsum(
        "blhe,bmhe->bhlm", grad_mixed, value_rows, preferred_element_type=jnp.float32
    )
    inner_dot = jnp.sum(attn_probs * grad_probs, axis=-1, keepdims=True)
    grad_scores = (attn_probs * (grad_probs - inner_dot)).astype(jnp.bfloat16)
    grad_values = jnp.einsum(
        "bhlm,blhe->bmhe",
        attn_probs.astype(jnp.bfloat16),
        grad_mixed,
        preferred_element_type=jnp.float32,
    )
    grad_queries = jnp.einsum(
        "bhlm,bmhe->blhe", grad_scores, key_rows, preferred_element_type=jnp.float32
    ) * HD ** (-0.5)
    grad_keys = jnp.einsum(
        "bhlm,blhe->bmhe", grad_scores, queries, preferred_element_type=jnp.float32
    ) * HD ** (-0.5)
    row_total = batch_size * length
    grad_proj = jnp.concatenate(
        [
            grad_queries.reshape(row_total, model_width),
            grad_keys.reshape(row_total, model_width),
            grad_values.reshape(row_total, model_width),
        ],
        axis=1,
    ).astype(jnp.bfloat16)
    grad_bias_query = jnp.sum(grad_proj[:, :model_width], axis=0, dtype=jnp.float32)
    grad_bias_value = jnp.sum(grad_proj[:, 2 * model_width :], axis=0, dtype=jnp.float32)
    grad_proj_weight = jnp.dot(flat_rows.T, grad_proj, preferred_element_type=jnp.float32)
    grad_tokens = grad_one + jnp.dot(
        grad_proj, attn_weights[:, : 3 * model_width].T, preferred_element_type=jnp.float32
    )
    grad_attn = jnp.concatenate([grad_proj_weight, grad_out_proj], axis=1)
    grad_small = jnp.concatenate(
        [
            grad_bias_query,
            grad_bias_value,
            grad_bias_out,
            grad_gain_one,
            grad_shift_one,
            grad_bias_inner,
            grad_bias_outer,
            grad_gain_two,
            grad_shift_two,
        ]
    )
    return (
        grad_tokens.reshape(batch_size, length, model_width),
        grad_attn,
        grad_inner,
        grad_outer,
        grad_small,
    )


def rows_term(stacked, count):
    return jnp.moveaxis(stacked, 0, 1).reshape(count, -1)


def unfold_rows(summed, encoders):
    owned = summed.shape[0]
    return jnp.moveaxis(summed.reshape(owned, encoders, -1), 1, 0)


def adam_update(weight, first_moment, second, gradient, step_rate, decay_rate):
    first_new = BETA_ONE * first_moment + (1.0 - BETA_ONE) * gradient
    second_new = BETA_TWO * second + (1.0 - BETA_TWO) * gradient * gradient
    fix_one = 1.0 - BETA_ONE**STEP
    fix_two = 1.0 - BETA_TWO**STEP
    update = first_new / fix_one / (jnp.sqrt(second_new / fix_two) + ADAM_EPS)
    return (first_new, second_new, weight - step_rate * (update + decay_rate * weight))


def local(
    question_tokens,
    passage_tokens,
    passage_lengths,
    positives,
    attn_weight,
    attn_first,
    attn_second,
    ffn_in_weight,
    ffn_in_first,
    ffn_in_second,
    ffn_out_weight,
    ffn_out_first,
    ffn_out_second,
    small_params,
    small_first,
    small_second,
):
    gathered = (
        lax.all_gather(attn_weight.astype(jnp.bfloat16), ("dp", "pair"), axis=1, tiled=True),
        lax.all_gather(ffn_in_weight.astype(jnp.bfloat16), ("dp", "pair"), axis=1, tiled=True),
        lax.all_gather(ffn_out_weight.astype(jnp.bfloat16), ("dp", "pair"), axis=1, tiled=True),
        lax.all_gather(small_params.astype(jnp.bfloat16), ("dp", "pair"), axis=1, tiled=True),
    )
    attn_all, inner_all, outer_all, small_low = gathered
    small_all = small_low.astype(jnp.float32)
    question_count, question_len, model_width = question_tokens.shape
    row_count, row_len, unused_width = passage_tokens.shape
    attn_cols = attn_weight.shape[2]
    front_rows = attn_weight.shape[1]
    back_rows = ffn_out_weight.shape[1]
    seg_ends = jnp.cumsum(passage_lengths, axis=1)
    seg_starts = seg_ends - passage_lengths
    positions = jnp.arange(row_len, dtype=jnp.int32)
    passage_seg = jnp.sum(
        (positions[None, :, None] >= seg_ends[:, None, :]).astype(jnp.int32), axis=2
    )
    question_seg = jnp.zeros((question_count, question_len), jnp.int32)
    question_out, question_kept = encoder_forward(
        question_tokens, question_seg, attn_all[0], inner_all[0], outer_all[0], small_all[0]
    )
    passage_out, passage_kept = encoder_forward(
        passage_tokens, passage_seg, attn_all[1], inner_all[1], outer_all[1], small_all[1]
    )
    question_cls = question_out[:, 0].astype(jnp.bfloat16)
    passage_cls = (
        jnp.take_along_axis(passage_out, seg_starts[:, :, None], axis=1)
        .reshape(-1, model_width)
        .astype(jnp.bfloat16)
    )
    every_cls = lax.all_gather(passage_cls, ("dp", "pair"), axis=0, tiled=True)
    score_scale = model_width ** (-0.5)
    scores = jnp.dot(question_cls, every_cls.T, preferred_element_type=jnp.float32) * score_scale
    top_score = jnp.max(scores, axis=1, keepdims=True)
    raised = jnp.exp(scores - top_score)
    soft_scores = raised / jnp.sum(raised, axis=1, keepdims=True)
    columns = jnp.arange(every_cls.shape[0], dtype=jnp.int32)
    target = (columns[None, :] == positives[:, None]).astype(jnp.float32)
    grad_scores = (soft_scores - target).astype(jnp.bfloat16)
    grad_qcls = jnp.dot(grad_scores, every_cls, preferred_element_type=jnp.float32) * score_scale
    grad_pcls = lax.psum_scatter(
        jnp.dot(grad_scores.T, question_cls, preferred_element_type=jnp.float32) * score_scale,
        ("dp", "pair"),
        scatter_dimension=0,
        tiled=True,
    )
    grad_question_out = jnp.zeros_like(question_out).at[:, 0].set(grad_qcls)
    row_index = jnp.arange(row_count, dtype=jnp.int32)[:, None]
    grad_passage_out = (
        jnp.zeros_like(passage_out)
        .at[row_index, seg_starts]
        .set(grad_pcls.reshape(row_count, -1, model_width))
    )
    question_grad, q_attn, q_inner, q_outer, q_small = encoder_backward(
        question_tokens,
        question_seg,
        attn_all[0],
        inner_all[0],
        outer_all[0],
        small_all[0],
        question_kept,
        grad_question_out,
    )
    passage_grad, p_attn, p_inner, p_outer, p_small = encoder_backward(
        passage_tokens,
        passage_seg,
        attn_all[1],
        inner_all[1],
        outer_all[1],
        small_all[1],
        passage_kept,
        grad_passage_out,
    )
    front_stack = jnp.stack(
        [jnp.concatenate([q_attn, q_inner], axis=1), jnp.concatenate([p_attn, p_inner], axis=1)]
    )
    front_owned = lax.psum_scatter(
        rows_term(front_stack, front_rows * lax.axis_size(("dp", "pair"))),
        ("dp", "pair"),
        scatter_dimension=0,
        tiled=True,
    )
    back_owned = lax.psum_scatter(
        rows_term(jnp.stack([q_outer, p_outer]), back_rows * lax.axis_size(("dp", "pair"))),
        ("dp", "pair"),
        scatter_dimension=0,
        tiled=True,
    )
    small_sum = lax.psum_scatter(
        jnp.stack([q_small, p_small]), ("dp", "pair"), scatter_dimension=1, tiled=True
    )
    front_sum = unfold_rows(front_owned, 2)
    back_sum = unfold_rows(back_owned, 2)
    attn_sum = front_sum[:, :, :attn_cols]
    inner_sum = front_sum[:, :, attn_cols:]
    attn_m, attn_v, attn_w = adam_update(
        attn_weight, attn_first, attn_second, attn_sum, RATE_MATRIX, DECAY_MATRIX
    )
    inner_m, inner_v, inner_w = adam_update(
        ffn_in_weight, ffn_in_first, ffn_in_second, inner_sum, RATE_MATRIX, DECAY_MATRIX
    )
    outer_m, outer_v, outer_w = adam_update(
        ffn_out_weight, ffn_out_first, ffn_out_second, back_sum, RATE_MATRIX, DECAY_MATRIX
    )
    small_m, small_v, small_w = adam_update(
        small_params, small_first, small_second, small_sum, RATE_SMALL, 0.0
    )
    return (
        attn_m,
        attn_v,
        attn_w,
        inner_m,
        inner_v,
        inner_w,
        outer_m,
        outer_v,
        outer_w,
        small_m,
        small_v,
        small_w,
        question_grad,
        passage_grad,
    )


MESH_ID = pl.DeviceIdType.MESH
LOW = jnp.bfloat16
F32 = jnp.float32


def dot_nn(a, b):
    return jnp.dot(a, b, preferred_element_type=F32)


def dot_nt(a, b):
    return lax.dot_general(a, b, (((1,), (1,)), ((), ())), preferred_element_type=F32)


def dot_tn(a, b):
    return lax.dot_general(a, b, (((0,), (0,)), ((), ())), preferred_element_type=F32)


def expand_heads(rows):
    head_of = lax.broadcasted_iota(jnp.int32, rows.shape, 1) // HD
    heads = rows.shape[1] // HD
    return jnp.concatenate(
        [jnp.where(head_of == h, rows, jnp.zeros_like(rows)) for h in range(heads)], axis=0
    )


def pick_heads(stacked):
    width = stacked.shape[1]
    heads = width // HD
    head_of = lax.broadcasted_iota(jnp.int32, (16, width), 1) // HD
    total = jnp.zeros((16, width), F32)
    for h in range(heads):
        total = total + jnp.where(head_of == h, stacked[16 * h : 16 * h + 16], 0.0)
    return total


def split_low(values):
    high = values.astype(LOW)
    return high, (values - high.astype(F32)).astype(LOW)


def gelu_parts(values):
    cdf = 0.5 * (1.0 + lax.erf(values * (0.5**0.5)))
    density = jnp.exp(-0.5 * values * values) * (0.5 / math.pi) ** 0.5
    return values * cdf, cdf + values * density


def step_kernel(
    qt_ref, pt_ref, attn_ref, ffi_ref, ffo_ref, small_ref, len_ref, pos_ref,
    ga_ref, gi_ref, go_ref, gs_ref, dxq_ref, dxp_ref,
    X, slabA, slabI, slabO, smw, sm2, smb, bndo, bndb, R, WN, sn, sno, ST, Pf, Pb, DSb, Emat, b1p,
    w1s_, w1r, W1, W2, Yb, P2s, P2r, XH, Dout, dZb, Gb, Act, P3s, P3r, Qb, dAb, dUb, dQb,
    m1s, m1r, m2s, m2r, dws, dwr, sgr, GS, GSw, GA, GI, GO, DX, qsb, vtb, ybf,
    loc, sib_s, sib_r, at_s, at_r, ag_s, ag_z, ag_p, aa_s, aa_r, out_l, out_s, out_r,
):
    dp, z = lax.axis_index("dp"), lax.axis_index("pair")
    core = lax.rem(dp, 2)
    y, x = dp // 4, lax.rem(dp // 2, 2)
    own = y * 8 + x * 4 + z
    line = y * 8 + x * 4

    def dev(slot, k):
        return ((slot // 8) * 4 + lax.rem(slot // 4, 2) * 2 + k, lax.rem(slot, 4))

    sibling = dev(own, 1 - core)
    slot_x = y * 8 + (1 - x) * 4 + z
    slot_y = (1 - y) * 8 + x * 4 + z
    slot_d = (1 - y) * 8 + (1 - x) * 4 + z

    def remote(src, dst, ssem, rsem, target):
        return pltpu.make_async_remote_copy(
            src_ref=src, dst_ref=dst, send_sem=ssem, recv_sem=rsem,
            device_id=target, device_id_type=MESH_ID,
        )

    def done(ref, sem):
        pltpu.make_async_copy(ref, ref, sem).wait()

    barrier = pltpu.get_barrier_semaphore()
    other = 1 - core
    rows = pl.ds(pl.multiple_of(512 * core, 512), 512)
    pltpu.make_async_copy(attn_ref.at[core], slabA.at[core], loc.at[0]).start()

    def greet(r, c):
        pl.semaphore_signal(
            barrier, inc=1, device_id=dev(lax.rem(own + r, 16), core), device_id_type=MESH_ID
        )
        return c

    pl.semaphore_signal(barrier, inc=1, device_id=sibling, device_id_type=MESH_ID)
    lax.fori_loop(1, 16, greet, 0)

    @pl.when(core == 0)
    def _():
        pltpu.make_async_copy(qt_ref, X.at[rows], loc.at[1]).start()

    @pl.when(core == 1)
    def _():
        pltpu.make_async_copy(pt_ref, X.at[rows], loc.at[1]).start()

    pltpu.make_async_copy(ffi_ref.at[core], slabI.at[core], loc.at[2]).start()
    pltpu.make_async_copy(ffo_ref.at[core], slabO.at[core], loc.at[3]).start()

    narrow = small_ref[...].astype(LOW).astype(F32)
    window = jnp.zeros((2, 384), F32)
    for i in range(4):
        gaps = [jnp.zeros((2, n), F32) for n in (32 * i, 96 - 32 * i) if n]
        placed = jnp.concatenate(([gaps[0]] if i else []) + [narrow] + ([gaps[-1]] if i < 3 else []), axis=1)
        window = jnp.where(z == i, placed, window)
    for k in range(2):
        smw[k] = jnp.concatenate(
            [window[k : k + 1, 128 * i : 128 * i + 128] for i in range(3)]
            + [jnp.zeros((5, 128), F32)], axis=0,
        )
    sm2[core] = smw[core]

    lengths = len_ref[...].astype(F32)
    spans = jnp.concatenate(
        [jnp.broadcast_to(lengths[i : i + 1], (4, 4)) for i in range(2)], axis=0
    )
    at_row = lax.broadcasted_iota(jnp.int32, (8, 4), 0)
    at_lane = lax.broadcasted_iota(jnp.int32, (8, 4), 1)
    upto = at_lane <= lax.rem(at_row, 4)
    here = at_lane == lax.rem(at_row, 4)
    line_of = lax.broadcasted_iota(jnp.int32, (8, 1), 0)
    base = jnp.where(line_of >= 4, 256.0, 0.0)
    passage_end = jnp.sum(jnp.where(upto, spans, 0.0), axis=1, keepdims=True) + base
    passage_start = passage_end - jnp.sum(jnp.where(here, spans, 0.0), axis=1, keepdims=True)
    question_start = line_of.astype(F32) * 64.0
    eye = lax.broadcasted_iota(jnp.int32, (8, 8), 0) == lax.broadcasted_iota(jnp.int32, (8, 8), 1)
    goal = jnp.broadcast_to(pos_ref[...].astype(F32), (8, 8))
    goal = jnp.sum(jnp.where(eye, goal, 0.0), axis=1, keepdims=True)
    of_questions = jnp.concatenate([question_start, question_start + 64.0, goal], axis=0)
    of_passages = jnp.concatenate([passage_start, passage_end, goal], axis=0)
    bndb[core] = jnp.broadcast_to(jnp.where(core == 0, of_questions, of_passages), (24, 128))
    bndo[...] = jnp.broadcast_to(jnp.where(core == 0, of_passages, of_questions), (24, 128))
    pl.semaphore_wait(barrier, 16)

    remote(smw.at[other], sm2.at[core], sib_s.at[1], sib_r.at[1], sibling).start()
    remote(attn_ref.at[other], slabA.at[core], sib_s.at[0], sib_r.at[0], sibling).start()
    remote(bndo, bndb.at[core], sib_s.at[2], sib_r.at[2], sibling).start()

    @pl.when(core == 0)
    def _():
        remote(pt_ref, X.at[rows], sib_s.at[3], sib_r.at[3], sibling).start()

    @pl.when(core == 1)
    def _():
        remote(qt_ref, X.at[rows], sib_s.at[3], sib_r.at[3], sibling).start()

    remote(ffi_ref.at[other], slabI.at[core], sib_s.at[4], sib_r.at[4], sibling).start()
    remote(ffo_ref.at[other], slabO.at[core], sib_s.at[5], sib_r.at[5], sibling).start()

    done(sm2.at[other], sib_r.at[1])
    smb[own] = jnp.concatenate([sm2[0], sm2[1]], axis=0).astype(LOW)

    exchanged = (smb, w1r, P2r, m1r, P3r, dwr, m2r)
    gathered = (Yb, Qb, XH.at[core], dUb, dAb, dQb, sgr)
    passed = ((slabA.at[0], slabA.at[0]), (sm2.at[0], sm2.at[0]), (bndb.at[0], bndb.at[0]),
              (X.at[rows], X.at[rows]), (slabI.at[0], slabI.at[0]), (slabO.at[0], slabO.at[0]),
              (sn, sno), (XH.at[0], XH.at[0]))
    written = (GO.at[0], DX.at[rows], GI.at[0], GA.at[0], GSw.at[0])
    state = {("pass", n): int(n < 2) for n in range(6)}

    def direct(n, src_of):
        def body(r, c):
            target = lax.rem(own + r, 16)
            remote(src_of(target), exchanged[n].at[own], aa_s.at[n], aa_r.at[n], dev(target, core)).start()
            return c

        lax.fori_loop(1, 16, body, 0)
        state["direct", n] = 0

    def direct_done(n):
        done(exchanged[n].at[pl.ds(0, 15)], aa_r.at[n])
        state["direct", n] = 1

    def pass_done(n):
        done(passed[n][1], sib_r.at[n])
        state["pass", n] = 1

    direct(0, lambda t: smb.at[own])

    def push(slot, m, target):
        remote(R.at[slot, m], R.at[slot, m], at_s.at[m], at_r.at[slot, m, 0], dev(target, core)).start()

    def near(f, nearest=1):
        for d in range(nearest, 4):
            for dz in (d, -d) if d else (0,):
                @pl.when(jnp.logical_and(z + dz >= 0, z + dz <= 3))
                def _():
                    f(dz)

    def got(slot, m):
        done(R.at[slot, m], at_r.at[slot, m, 0])

    done(slabA.at[core], loc.at[0])
    done(slabA.at[other], sib_r.at[0])
    for m in (0, 3, 1, 2):
        cols = slice(768 * m, 768 * m + 768)
        R[own, m] = jnp.concatenate([slabA[0, :, cols], slabA[1, :, cols]], axis=0).astype(LOW)
        for target in (slot_x, slot_y) if m < 3 else (slot_x, slot_y, slot_d):
            push(own, m, target)
        if m < 3:
            near(lambda dz: push(own, m, own + dz))

    def hop(d):
        for i in range(4):
            slot = 4 * i + z
            if d == 0:
                @pl.when(4 * i != line)
                def _():
                    got(slot, 3)

                @pl.when(z < 3)
                def _():
                    push(slot, 3, own + 1)

                @pl.when(z > 0)
                def _():
                    push(slot, 3, own - 1)
            else:
                @pl.when(z - d >= 0)
                def _():
                    got(slot - d, 3)

                    @pl.when(z < 3)
                    def _():
                        push(slot - d, 3, own + 1)

                @pl.when(z + d <= 3)
                def _():
                    got(slot + d, 3)

                    @pl.when(z > 0)
                    def _():
                        push(slot + d, 3, own - 1)

    def finish():
        for kind, n in list(state):
            if kind == "gather" and state[kind, n] == 0:
                gather_forward(n)
            if kind == "gather" and state[kind, n] == 1:
                gather_done(n)
            if kind == "direct" and state[kind, n] == 0:
                direct_done(n)
            if kind == "pass" and state[kind, n] == 0:
                pass_done(n)
            if kind == "gather":
                done(gathered[n].at[pl.ds(0, 15)], ag_s.at[n])
            if kind == "direct":
                done(exchanged[n].at[pl.ds(0, 15)], aa_s.at[n])
            if kind == "pass":
                done(passed[n][0], sib_s.at[n])
            if kind == "out":
                done(written[n], out_l.at[n])
                done(written[n], out_s.at[n])
                done(written[n], out_r.at[n])
        for m in range(3):
            done(R.at[pl.ds(0, 15), m], at_s.at[m])
        done(R.at[pl.ds(0, 7), 3], at_s.at[3])

        @pl.when(jnp.logical_and(z > 0, z < 3))
        def _():
            done(R.at[pl.ds(0, 16), 3], at_s.at[3])

    def relay(m):
        def from_z(dz):
            got(own + dz, m)
            for target in (slot_x, slot_y):
                push(own + dz, m, target)

        near(from_z)

        def from_plane(dz):
            for slot, target, half in ((slot_x + dz, slot_y, 0), (slot_y + dz, slot_x, 1)):
                got(slot, m)
                part = R.at[slot, m, :, pl.ds(384 * half, 384)]
                remote(part, part, at_s.at[m], at_r.at[slot, m, half], dev(target, core)).start()

        near(from_plane, 0)

    def from_slots(read, write):
        def body(g, c):
            got = [read(4 * g + i).astype(F32) for i in range(4)]
            natural = jnp.concatenate([v[0:24] for v in got] + [v[24:48] for v in got], axis=0)
            write(pl.ds(pl.multiple_of(192 * g, 64), 192), natural.astype(LOW))
            return c

        lax.fori_loop(0, 4, body, 0)

    def to_slots(read, write):
        def body(g, c):
            v = read(pl.ds(pl.multiple_of(192 * g, 64), 192))
            for i in range(4):
                part = jnp.concatenate(
                    [v[24 * i : 24 * i + 24], v[96 + 24 * i : 96 + 24 * i + 24]], axis=0
                )
                write(4 * g + i, part.astype(LOW))
            return c

        lax.fori_loop(0, 4, body, 0)

    def arrive(m):
        def body(zz, c):
            slot = (1 - y) * 8 + (1 - x) * 4 + zz
            for half in range(2):
                done(R.at[slot, m, :, pl.ds(384 * half, 384)], at_r.at[slot, m, half])
            return c

        if m < 3:
            lax.fori_loop(0, 4, body, 0)

        def write(where, v):
            WN[m, where, :] = v

        from_slots(lambda s: R[s, m], write)

    def gather_start(n):
        buf = gathered[n]
        state["gather", n] = 0

        def give(dz):
            remote(buf.at[own], buf.at[own], ag_s.at[n], ag_z.at[n, z], dev(own + dz, core)).start()

        near(give)
        for target in (slot_x, slot_y, slot_d):
            remote(buf.at[own], buf.at[own], ag_s.at[n], ag_p.at[n], dev(target, core)).start()

    def gather_forward(n):
        buf = gathered[n]
        state["gather", n] = 1

        def pass_on(dz):
            block = buf.at[own + dz]
            done(block, ag_z.at[n, z + dz])
            for target in (slot_x, slot_y, slot_d):
                remote(block, block, ag_s.at[n], ag_p.at[n], dev(target, core)).start()

        near(pass_on)

    def gather_done(n):
        state["gather", n] = 2
        done(gathered[n].at[pl.ds(0, 12)], ag_p.at[n])

    def prepare_ffn():
        row = lax.broadcasted_iota(jnp.int32, (384, 512), 0)
        col = lax.broadcasted_iota(jnp.int32, (384, 512), 1)
        Emat[...] = jnp.where(col == 128 * (row // 96) + lax.rem(row, 96), 1.0, 0.0).astype(LOW)
        done(slabI.at[core], loc.at[2])
        pass_done(4)
        for g in range(8):
            cols = slice(384 * g, 384 * g + 384)
            part = jnp.concatenate([slabI[0, :, cols], slabI[1, :, cols]], axis=0).astype(LOW)
            wide = dot_nn(part, Emat[...]).astype(LOW)
            for i in range(4):
                w1s_[4 * (g // 2) + i, :, 128 * (g % 2) : 128 * (g % 2) + 128] = wide[
                    :, 128 * i : 128 * i + 128
                ]
        w1r[own] = w1s_[own]
        done(slabO.at[core], loc.at[3])
        pass_done(5)
        gap = jnp.zeros((32, 768), F32)
        W2[...] = jnp.concatenate([slabO[0], gap, slabO[1], gap], axis=0).astype(LOW)

    def natural_small():
        direct_done(0)
        for g in range(8):
            parts = [
                smb[4 * (g // 2) + i].astype(F32)[8 * (g % 2) : 8 * (g % 2) + 8] for i in range(4)
            ]
            lines = [parts[0][0:1], parts[0][1:2]]
            for i in range(1, 4):
                lines += [parts[i - 1][2:3] + parts[i][0:1], parts[i][1:2]]
            lines += [parts[3][2:3]]
            sn[9 * g : 9 * g + 9, :] = jnp.concatenate(lines, axis=0)
        remote(sn, sno, sib_s.at[6], sib_r.at[6], sibling).start()
        state["pass", 6] = 0

    def vec(row, count=6, ref=sn):
        return jnp.concatenate([ref[row + i : row + i + 1, :] for i in range(count)], axis=1)

    relay(0)
    hop(0)
    pass_done(2)
    done(X.at[pl.ds(0, 512)], loc.at[1])
    pass_done(3)
    starts = jnp.concatenate([bndb[0, 0:8], bndb[1, 0:8] + 512.0], axis=0)[:, 0:1]
    ends = jnp.concatenate([bndb[0, 8:16], bndb[1, 8:16] + 512.0], axis=0)[:, 0:1]
    token = lax.broadcasted_iota(jnp.int32, (16, 1024), 1).astype(F32)
    inside = jnp.logical_and(token >= starts, token < ends)
    first = jnp.where(token == starts, 1.0, 0.0).astype(LOW)
    cls_in = dot_nn(first, X[...])
    cls_low = cls_in.astype(LOW)
    natural_small()
    prepare_ffn()
    relay(1)
    hop(1)
    arrive(0)
    queries = (dot_nn(cls_low, WN[0]) + vec(0)).astype(LOW)
    Qb[own] = queries
    relay(2)
    hop(2)
    direct(1, lambda t: w1s_.at[t])
    gather_start(1)
    arrive(1)
    qsb[...] = (dot_nt(expand_heads(queries), WN[1]) * (HD**-0.5)).astype(LOW)
    ST[...] = dot_nt(qsb[...], X[...])

    def soften(h, c):
        at = pl.ds(pl.multiple_of(16 * h, 16), 16)
        s = jnp.where(inside, ST[at, :], -1000000000.0)
        e = jnp.exp(s - jnp.max(s, axis=1, keepdims=True))
        p = e / jnp.sum(e, axis=1, keepdims=True)
        Pf[at, :] = p
        Pb[at, :] = p.astype(LOW)
        return c

    lax.fori_loop(0, 12, soften, 0)
    ybf[...] = dot_nn(Pb[...], X[...]).astype(LOW)
    arrive(2)
    mixed = (pick_heads(dot_nn(ybf[...], WN[2])) + vec(6)).astype(LOW)
    hop(3)
    arrive(3)
    lifted = cls_in + dot_nn(mixed, WN[3]) + vec(12)
    centred = lifted - jnp.mean(lifted, axis=1, keepdims=True)
    rstd_one = lax.rsqrt(jnp.mean(centred * centred, axis=1, keepdims=True) + NORM_EPS)
    hat_one = centred * rstd_one
    normed = hat_one * vec(18) + vec(24)
    Yb[own] = normed.astype(LOW)
    gather_start(0)

    early = jnp.concatenate(
        [ybf[...].astype(F32), cls_in, mixed.astype(F32), jnp.zeros((32, 768), F32)], axis=0
    )
    DX[0:768, 0:256] = early.T

    def write_m1(slot, v):
        m1s[slot] = v

    to_slots(lambda w: DX[w, 0:256], write_m1)
    m1r[own] = m1s[own]
    gather_forward(0)

    b1 = jnp.concatenate([vec(30 + 3 * g, 3) for g in range(8)], axis=0).astype(LOW)
    b1_wide = dot_nn(b1, Emat[...])
    for g in range(8):
        b1p[g] = jnp.broadcast_to(b1_wide[g : g + 1], (8, 512))
    group = pl.multiple_of(128 * z, 128)
    gy = 4 * y + 2 * x
    b1_row = jnp.concatenate(
        [b1p[gy, 0:1, pl.ds(group, 128)], b1p[gy + 1, 0:1, pl.ds(group, 128)]], axis=1
    )
    direct_done(1)

    def write_w1(where, v):
        W1[where, :] = v

    from_slots(lambda s: w1r[s], write_w1)
    gather_done(0)
    all_y = Yb[...].reshape(256, 768)
    act = dot_nn(all_y, W1[...]) + b1_row
    Act[...] = act
    hidden, unused = gelu_parts(act)
    Gb[...] = hidden.astype(LOW)
    P2s[...] = dot_nn(Gb[...], W2[...]).astype(LOW).reshape(16, 16, 768)
    direct(2, lambda t: P2s.at[t])
    P2r[own] = P2s[own]
    gather_forward(1)
    direct_done(2)
    second = normed + jnp.sum(P2r[...].astype(F32), axis=0) + vec(54)
    centred = second - jnp.mean(second, axis=1, keepdims=True)
    rstd_two = lax.rsqrt(jnp.mean(centred * centred, axis=1, keepdims=True) + NORM_EPS)
    hat_two = centred * rstd_two
    rstd_high, rstd_low = split_low(rstd_two)
    lane = lax.broadcasted_iota(jnp.int32, (16, 128), 1)
    positive = jnp.concatenate([bndb[0, 16:24], bndb[1, 16:24]], axis=0)
    extra = jnp.where(
        lane == 0, rstd_high.astype(F32),
        jnp.where(lane == 1, rstd_low.astype(F32), jnp.where(lane == 2, positive, 0.0)),
    )
    XH[core, own] = jnp.concatenate([hat_two, extra], axis=1).astype(LOW)
    gather_start(2)
    gather_forward(2)
    direct(3, lambda t: m1s.at[t])
    gather_done(2)
    remote(XH.at[core], XH.at[core], sib_s.at[7], sib_r.at[7], sibling).start()
    state["pass", 7] = 0
    pass_done(6)
    pass_done(7)

    def vec_of(encoder, row):
        return jnp.where(core == encoder, vec(row), vec(row, 6, sno))

    xq = XH[0].reshape(256, 896).astype(F32)
    xp = XH[1].reshape(256, 896).astype(F32)
    qc = (xq[:, 0:768] * vec_of(0, 60) + vec_of(0, 66)).astype(LOW)
    pc = (xp[:, 0:768] * vec_of(1, 60) + vec_of(1, 66)).astype(LOW)
    scale = 768 ** (-0.5)
    scores = dot_nt(qc, pc) * scale
    raised = jnp.exp(scores - jnp.max(scores, axis=1, keepdims=True))
    soft = raised / jnp.sum(raised, axis=1, keepdims=True)
    place = lax.broadcasted_iota(jnp.int32, (256, 256), 1)
    slot_of = place // 16
    owner_of = (
        16 * (slot_of // 8) + 8 * lax.rem(slot_of // 4, 2)
        + 4 * (lax.rem(place, 16) // 8) + lax.rem(slot_of, 4)
    )
    passage = (8 * owner_of + lax.rem(place, 8)).astype(F32)
    target = jnp.where(passage == xq[:, 770:771], 1.0, 0.0)
    grad_scores = (soft - target).astype(LOW)

    @pl.when(core == 0)
    def _():
        Dout[...] = dot_nn(grad_scores, pc) * scale

    @pl.when(core == 1)
    def _():
        Dout[...] = dot_tn(grad_scores, qc) * scale

    dout = Dout[...]
    block = XH[core].reshape(256, 896).astype(F32)
    hat = block[:, 0:768]
    rstd = block[:, 768:769] + block[:, 769:770]
    inner = dout * vec(60)
    grad_two = rstd * (
        inner - jnp.mean(inner, axis=1, keepdims=True)
        - hat * jnp.mean(inner * hat, axis=1, keepdims=True)
    )
    dg2 = jnp.sum(dout * hat, axis=0, keepdims=True)
    ds2 = jnp.sum(dout, axis=0, keepdims=True)
    Dout[...] = grad_two
    dZb[...] = grad_two.astype(LOW)
    db2 = jnp.sum(dZb[...].astype(F32), axis=0, keepdims=True)
    unused, slope = gelu_parts(Act[...])
    da = (dot_nt(dZb[...], W2[...]) * slope).astype(LOW)
    P3s[...] = dot_nt(da, W1[...]).astype(LOW).reshape(16, 16, 768)
    direct(4, lambda t: P3s.at[t])
    P3r[own] = P3s[own]
    DX[0:768, 0:256] = dot_tn(all_y, da)

    def write_dw(slot, v):
        dws[slot] = v

    to_slots(lambda w: DX[w, 0:256], write_dw)
    direct(5, lambda t: dws.at[t])
    dwr[own] = dws[own]
    db1 = jnp.sum(da.astype(F32), axis=0, keepdims=True)
    dw2 = dot_tn(Gb[...], dZb[...])
    GO[0] = dw2[0:96]
    GO[1] = dw2[128:224]
    pltpu.make_async_copy(GO.at[core], go_ref.at[core], out_l.at[0]).start()
    remote(GO.at[other], go_ref.at[core], out_s.at[0], out_r.at[0], sibling).start()
    state["out", 0] = 0
    own_rows = pl.ds(pl.multiple_of(16 * own, 16), 16)
    direct_done(4)

    grad_normed = Dout[own_rows, :] + jnp.sum(P3r[...].astype(F32), axis=0)
    inner = grad_normed * vec(18)
    grad_one = rstd_one * (
        inner - jnp.mean(inner, axis=1, keepdims=True)
        - hat_one * jnp.mean(inner * hat_one, axis=1, keepdims=True)
    )
    grad_lift = grad_one.astype(LOW)
    grad_mixed = dot_nt(grad_lift, WN[3]).astype(LOW)
    dUb[own] = grad_lift
    dAb[own] = grad_mixed
    gather_start(3)
    gather_start(4)
    dg1 = jnp.sum(grad_normed * hat_one, axis=0, keepdims=True)
    ds1 = jnp.sum(grad_normed, axis=0, keepdims=True)
    sgr[own] = jnp.concatenate(
        [dg1[:, 128 * i : 128 * i + 128] for i in range(6)]
        + [ds1[:, 128 * i : 128 * i + 128] for i in range(6)]
        + [db1[:, 0:128], db1[:, 128:256], jnp.zeros((2, 128), F32)], axis=0,
    )
    gather_start(6)
    spread = expand_heads(grad_mixed)
    vtb[...] = dot_nt(spread, WN[2]).astype(LOW)
    constant = jnp.sum(spread.astype(F32) * vec(6), axis=1, keepdims=True)
    ST[...] = dot_nt(vtb[...], X[...]) + constant
    gather_forward(3)
    gather_forward(4)
    gather_forward(6)

    def harden(h, c):
        at = pl.ds(pl.multiple_of(16 * h, 16), 16)
        p, dprob = Pf[at, :], ST[at, :]
        total = jnp.sum(p * dprob, axis=1, keepdims=True)
        DSb[at, :] = (p * (dprob - total)).astype(LOW)
        return c

    lax.fori_loop(0, 12, harden, 0)
    late = (dot_nn(DSb[...], X[...]) * (HD**-0.5)).astype(LOW)
    DX[0:768, 0:256] = jnp.concatenate(
        [late.astype(F32), jnp.zeros((64, 768), F32)], axis=0
    ).T

    def write_m2(slot, v):
        m2s[slot] = v

    to_slots(lambda w: DX[w, 0:256], write_m2)
    direct(6, lambda t: m2s.at[t])
    m2r[own] = m2s[own]
    grad_query = pick_heads(dot_nn(late, WN[1])).astype(LOW)
    dQb[own] = grad_query
    gather_start(5)

    grad_cls = grad_one + dot_nt(grad_query, WN[0])
    cls_high, cls_rest = split_low(grad_cls)
    right = jnp.concatenate([qsb[...], vtb[...], cls_high, cls_rest], axis=0)
    for k in range(2):
        part = slice(512 * k, 512 * k + 512)
        left = jnp.concatenate([DSb[:, part], Pb[:, part], first[:, part], first[:, part]], axis=0)
        DX[part, :] = dot_tn(left, right)
    gather_forward(5)
    other_rows = pl.ds(pl.multiple_of(512 * other, 512), 512)

    @pl.when(core == 0)
    def _():
        pltpu.make_async_copy(DX.at[rows], dxq_ref, out_l.at[1]).start()
        remote(DX.at[other_rows], dxq_ref, out_s.at[1], out_r.at[1], sibling).start()

    @pl.when(core == 1)
    def _():
        pltpu.make_async_copy(DX.at[rows], dxp_ref, out_l.at[1]).start()
        remote(DX.at[other_rows], dxp_ref, out_s.at[1], out_r.at[1], sibling).start()

    state["out", 1] = 0

    direct_done(5)
    for g in range(8):
        wide = jnp.concatenate(
            [dwr[4 * (g // 2) + i, :, 128 * (g % 2) : 128 * (g % 2) + 128] for i in range(4)], axis=1
        )
        narrow = dot_nt(wide, Emat[...])
        GI[0, :, 384 * g : 384 * g + 384] = narrow[0:24]
        GI[1, :, 384 * g : 384 * g + 384] = narrow[24:48]
    pltpu.make_async_copy(GI.at[core], gi_ref.at[core], out_l.at[2]).start()
    remote(GI.at[other], gi_ref.at[core], out_s.at[2], out_r.at[2], sibling).start()
    state["out", 2] = 0

    def put(m, v):
        GA[0, :, 768 * m : 768 * m + 768] = v[0:24]
        GA[1, :, 768 * m : 768 * m + 768] = v[24:48]

    def factor_sum(messages, columns):
        def body(s, total):
            wide = jnp.concatenate(
                [expand_heads(columns[s]), jnp.zeros((64, 768), LOW)], axis=0
            )
            return total + dot_nn(messages[s], wide)

        return lax.fori_loop(0, 16, body, jnp.zeros((48, 768), F32))

    gather_done(1)
    gather_done(4)
    direct_done(3)
    put(2, factor_sum(m1r, dAb))
    gather_done(3)

    def columns_of(at):
        return jnp.concatenate(
            [m1r[s, :, at : at + 16].astype(F32) for s in range(16)], axis=1
        ).astype(LOW)

    all_du = dUb[...].reshape(256, 768)
    put(3, dot_nn(columns_of(208), all_du))
    direct_done(6)
    put(1, factor_sum(m2r, Qb))
    gather_done(5)
    all_dq = dQb[...].reshape(256, 768)
    put(0, dot_nn(columns_of(192), all_dq))
    pltpu.make_async_copy(GA.at[core], ga_ref.at[core], out_l.at[3]).start()
    remote(GA.at[other], ga_ref.at[core], out_s.at[3], out_r.at[3], sibling).start()
    state["out", 3] = 0

    gather_done(6)
    sums = jnp.sum(sgr[...], axis=0)
    hidden_rows = []
    for g in range(8):
        wide = jnp.concatenate(
            [sgr[4 * (g // 2) + i, 12 + g % 2 : 13 + g % 2, :] for i in range(4)], axis=1
        )
        hidden_rows.append(wide)
    wide = jnp.concatenate(hidden_rows, axis=0)
    high, rest = split_low(wide)
    rest, last = split_low(wide - high.astype(F32))
    narrow = dot_nt(high, Emat[...]) + dot_nt(rest, Emat[...]) + dot_nt(last, Emat[...])

    def six(v):
        return [v[:, 128 * i : 128 * i + 128] for i in range(6)]

    lines = six(jnp.sum(all_dq.astype(F32), axis=0, keepdims=True))
    lines += six(jnp.sum(dAb[...].reshape(256, 768).astype(F32), axis=0, keepdims=True))
    lines += six(jnp.sum(all_du.astype(F32), axis=0, keepdims=True))
    lines += [sums[0:12]]
    for g in range(8):
        lines += [narrow[g : g + 1, 128 * i : 128 * i + 128] for i in range(3)]
    lines += six(db2) + six(dg2) + six(ds2) + [jnp.zeros((8, 128), F32)]
    packed = jnp.concatenate(lines, axis=0)
    for g in range(8):
        for i in range(4):
            at = 9 * g + 9 * i // 4
            GS[g, i] = packed[at : at + 8]
    for k in range(2):
        GSw[k] = GS[gy + k, z]
    pltpu.make_async_copy(GSw.at[core], gs_ref.at[core], out_l.at[4]).start()
    remote(GSw.at[other], gs_ref.at[core], out_s.at[4], out_r.at[4], sibling).start()
    state["out", 4] = 0

    finish()


def kernel_call(qt, pt, attn, ffi, ffo, small, lengths, positives):
    any_space = pl.BlockSpec(memory_space=pl.ANY)
    vmem = pl.BlockSpec(memory_space=pltpu.VMEM)
    V = pltpu.VMEM
    dma = pltpu.SemaphoreType.DMA
    scratch = [
        V((1024, 768), LOW), V((2, 24, 3072), F32), V((2, 24, 3072), F32), V((2, 96, 768), F32),
        V((2, 8, 128), F32), V((2, 8, 128), F32), V((16, 16, 128), LOW),
        V((24, 128), F32), V((2, 24, 128), F32), V((16, 4, 48, 768), LOW),
        V((4, 768, 768), LOW), V((72, 128), F32), V((72, 128), F32), V((192, 1024), F32),
        V((192, 1024), F32), V((192, 1024), LOW), V((192, 1024), LOW), V((384, 512), LOW),
        V((8, 8, 512), F32),
        V((16, 48, 256), LOW), V((16, 48, 256), LOW), V((768, 256), LOW), V((256, 768), LOW),
        V((16, 16, 768), LOW), V((16, 16, 768), LOW), V((16, 16, 768), LOW),
        V((2, 16, 16, 896), LOW), V((256, 768), F32), V((256, 768), LOW), V((256, 256), LOW),
        V((256, 256), F32), V((16, 16, 768), LOW), V((16, 16, 768), LOW), V((16, 16, 768), LOW),
        V((16, 16, 768), LOW), V((16, 16, 768), LOW), V((16, 16, 768), LOW),
        V((16, 48, 256), LOW), V((16, 48, 256), LOW), V((16, 48, 256), LOW), V((16, 48, 256), LOW),
        V((16, 48, 256), LOW), V((16, 48, 256), LOW), V((16, 16, 128), F32),
        V((8, 4, 8, 128), F32), V((2, 8, 128), F32), V((2, 24, 3072), F32), V((2, 24, 3072), F32),
        V((2, 96, 768), F32), V((1024, 768), F32), V((192, 768), LOW), V((192, 768), LOW),
        V((192, 768), LOW),
        dma((4,)), dma((8,)), dma((8,)), dma((4,)), dma((16, 4, 2)), dma((7,)), dma((7, 4)),
        dma((7,)), dma((7,)), dma((7,)), dma((5,)), dma((5,)), dma((5,)),
    ]
    shapes = (
        (2, 24, 3072), (2, 24, 3072), (2, 96, 768), (2, 8, 128), (512, 768), (512, 768)
    )
    return pl.pallas_call(
        step_kernel,
        out_shape=[jax.ShapeDtypeStruct(s, F32) for s in shapes],
        in_specs=[any_space] * 5 + [vmem] * 3,
        out_specs=[any_space] * 6,
        scratch_shapes=scratch,
        compiler_params=pltpu.CompilerParams(
            collective_id=0, has_side_effects=True, vmem_limit_bytes=56 << 20
        ),
    )(qt, pt, attn, ffi, ffo, small, lengths, positives)


def update_kernel(*refs):
    ins, outs = refs[:18], refs[18:]
    for n in range(3):
        weight, first, second, grad = (r[...] for r in ins[4 * n : 4 * n + 4])
        new = adam_update(weight, first, second, grad, RATE_MATRIX, DECAY_MATRIX)
        for ref, value in zip(outs[3 * n : 3 * n + 3], new):
            ref[...] = value

    @pl.when(pl.program_id(0) == 0)
    def _():
        z = lax.axis_index("pair")
        weight, first, second, window = ins[12:16]
        lines = []
        for e in range(2):
            row = jnp.concatenate([window[e, i : i + 1, :] for i in range(3)], axis=1)
            picked = row[:, 0:288]
            for i in range(1, 4):
                picked = jnp.where(z == i, row[:, 32 * i : 32 * i + 288], picked)
            lines.append(picked)
        grad = jnp.concatenate(lines, axis=0)
        new = adam_update(weight[...], first[...], second[...], grad, RATE_SMALL, 0.0)
        for ref, value in zip(outs[9:12], new):
            ref[...] = value

    outs[12][...] = ins[16][...]
    outs[13][...] = ins[17][...]


def update_call(attn, inner, outer, small, grad_question, grad_passage):
    wide = pl.BlockSpec((1, 24, 768), lambda i: (i // 4, 0, i % 4))
    tall = pl.BlockSpec((1, 24, 768), lambda i: (i // 4, i % 4, 0))
    vector = pl.BlockSpec((2, 288), lambda i: (0, 0))
    window = pl.BlockSpec((2, 8, 128), lambda i: (0, 0, 0))
    token = pl.BlockSpec((64, 768), lambda i: (i, 0))

    def like(a):
        return jax.ShapeDtypeStruct(a.shape, F32)

    return pl.pallas_call(
        update_kernel,
        grid=(8,),
        out_shape=[like(g[0]) for g in (attn, inner, outer, small) for _ in range(3)]
        + [like(grad_question), like(grad_passage)],
        in_specs=[wide] * 8 + [tall] * 4 + [vector] * 3 + [window, token, token],
        out_specs=[wide] * 6 + [tall] * 3 + [vector] * 3 + [token, token],
    )(*attn, *inner, *outer, *small, grad_question, grad_passage)


def local_kernel(
    question_tokens, passage_tokens, passage_lengths, positives,
    attn_weight, attn_first, attn_second, ffn_in_weight, ffn_in_first, ffn_in_second,
    ffn_out_weight, ffn_out_first, ffn_out_second, small_params, small_first, small_second,
):
    grads = kernel_call(
        question_tokens.reshape(512, 768), passage_tokens.reshape(512, 768),
        attn_weight, ffn_in_weight, ffn_out_weight, small_params,
        passage_lengths, positives.reshape(1, 8),
    )
    attn_sum, inner_sum, outer_sum, small_window, grad_question, grad_passage = grads
    results = update_call(
        (attn_weight, attn_first, attn_second, attn_sum),
        (ffn_in_weight, ffn_in_first, ffn_in_second, inner_sum),
        (ffn_out_weight, ffn_out_first, ffn_out_second, outer_sum),
        (small_params, small_first, small_second, small_window),
        grad_question, grad_passage,
    )
    return (
        *results[:12],
        results[12].reshape(question_tokens.shape),
        results[13].reshape(passage_tokens.shape),
    )


def fits_kernel(mesh):
    return mesh.shape["dp"] == 8 and mesh.shape["pair"] == 4


def solution(mesh):
    in_specs = (
        P(("dp", "pair"), None, None),
        P(("dp", "pair"), None, None),
        P(("dp", "pair"), None),
        P(("dp", "pair")),
        P(None, ("dp", "pair"), None),
        P(None, ("dp", "pair"), None),
        P(None, ("dp", "pair"), None),
        P(None, ("dp", "pair"), None),
        P(None, ("dp", "pair"), None),
        P(None, ("dp", "pair"), None),
        P(None, ("dp", "pair"), None),
        P(None, ("dp", "pair"), None),
        P(None, ("dp", "pair"), None),
        P(None, ("dp", "pair")),
        P(None, ("dp", "pair")),
        P(None, ("dp", "pair")),
    )
    out_specs = (
        P(None, ("dp", "pair"), None),
        P(None, ("dp", "pair"), None),
        P(None, ("dp", "pair"), None),
        P(None, ("dp", "pair"), None),
        P(None, ("dp", "pair"), None),
        P(None, ("dp", "pair"), None),
        P(None, ("dp", "pair"), None),
        P(None, ("dp", "pair"), None),
        P(None, ("dp", "pair"), None),
        P(None, ("dp", "pair")),
        P(None, ("dp", "pair")),
        P(None, ("dp", "pair")),
        P(("dp", "pair"), None, None),
        P(("dp", "pair"), None, None),
    )
    body = local_kernel if fits_kernel(mesh) else local
    return jax.shard_map(body, mesh=mesh, in_specs=in_specs, out_specs=out_specs, check_vma=False)
```

```python
import math

import jax
import jax.numpy as jnp
from jax import lax
from jax.experimental import pallas as pl
from jax.experimental.pallas import tpu as pltpu
from jax.sharding import PartitionSpec as P

HD = 64
STEP = 5


BETA_ONE = 0.9
BETA_TWO = 0.999
ADAM_EPS = 1e-08
NORM_EPS = 1e-06
RATE_MATRIX = 0.05
RATE_SMALL = 0.3
DECAY_MATRIX = 0.01


def layer_norm(values, norm_gain, norm_shift):
    row_mean = jnp.mean(values, axis=-1, keepdims=True)
    centred = values - row_mean
    spread = jnp.mean(centred * centred, axis=-1, keepdims=True)
    return centred * lax.rsqrt(spread + NORM_EPS) * norm_gain + norm_shift


def gelu_exact(values):
    return jax.nn.gelu(values, approximate=False)


def unpack(small_vec, model_width, hidden_width):
    widths = [model_width] * 5 + [hidden_width] + [model_width] * 3
    pieces = []
    offset = 0
    for length in widths:
        pieces.append(small_vec[offset : offset + length])
        offset = offset + length
    return pieces


def masked_scores(queries, key_rows, segment):
    scores = jnp.einsum(
        "blhe,bmhe->bhlm", queries, key_rows, preferred_element_type=jnp.float32
    ) * HD ** (-0.5)
    allowed = (segment[:, :, None] == segment[:, None, :])[:, None]
    return jnp.where(allowed, scores, -1000000000.0)


def encoder_forward(tokens, segment, attn_weights, inner_weight, outer_weight, small_vec):
    batch_size, length, model_width = tokens.shape
    head_count = model_width // HD
    flat_rows = tokens.reshape(batch_size * length, model_width)
    (
        bias_query,
        bias_value,
        bias_out,
        gain_one,
        shift_one,
        bias_inner,
        bias_outer,
        gain_two,
        shift_two,
    ) = unpack(small_vec, model_width, inner_weight.shape[1])
    bias_proj = jnp.concatenate([bias_query, jnp.zeros_like(bias_query), bias_value])
    projected = (
        jnp.dot(flat_rows, attn_weights[:, : 3 * model_width], preferred_element_type=jnp.float32)
        + bias_proj
    )
    projected = projected.astype(jnp.bfloat16).reshape(batch_size, length, 3, head_count, HD)
    queries = projected[:, :, 0]
    key_rows = projected[:, :, 1]
    value_rows = projected[:, :, 2]
    scores = masked_scores(queries, key_rows, segment)
    top_score = jnp.max(scores, axis=-1, keepdims=True)
    raised = jnp.exp(scores - top_score)
    totals = jnp.sum(raised, axis=-1, keepdims=True)
    attn_probs = (raised / totals).astype(jnp.bfloat16)
    log_total = top_score + jnp.log(totals)
    mixed_heads = jnp.einsum(
        "bhlm,bmhe->blhe", attn_probs, value_rows, preferred_element_type=jnp.float32
    )
    mixed_flat = mixed_heads.astype(jnp.bfloat16).reshape(batch_size * length, model_width)
    attn_out = (
        jnp.dot(mixed_flat, attn_weights[:, 3 * model_width :], preferred_element_type=jnp.float32)
        + bias_out
    )
    residual_one = flat_rows.astype(jnp.float32) + attn_out
    normed_one = layer_norm(residual_one, gain_one, shift_one)
    pre_act = (
        jnp.dot(normed_one.astype(jnp.bfloat16), inner_weight, preferred_element_type=jnp.float32)
        + bias_inner
    )
    activated = gelu_exact(pre_act).astype(jnp.bfloat16)
    branch = jnp.dot(activated, outer_weight, preferred_element_type=jnp.float32) + bias_outer
    residual_two = normed_one + branch
    result = layer_norm(residual_two, gain_two, shift_two).reshape(batch_size, length, model_width)
    kept_values = (
        queries,
        key_rows,
        value_rows,
        log_total,
        mixed_flat,
        residual_one,
        normed_one,
        pre_act,
        activated,
        residual_two,
    )
    return (result, kept_values)


def encoder_backward(
    tokens, segment, attn_weights, inner_weight, outer_weight, small_vec, kept_values, grad_result
):
    batch_size, length, model_width = tokens.shape
    head_count = model_width // HD
    flat_rows = tokens.reshape(batch_size * length, model_width)
    (
        queries,
        key_rows,
        value_rows,
        log_total,
        mixed_flat,
        residual_one,
        normed_one,
        pre_act,
        activated,
        residual_two,
    ) = kept_values
    (
        bias_query,
        bias_value,
        bias_out,
        gain_one,
        shift_one,
        bias_inner,
        bias_outer,
        gain_two,
        shift_two,
    ) = unpack(small_vec, model_width, inner_weight.shape[1])
    grad_flat = grad_result.reshape(batch_size * length, model_width)
    unused_two, norm_two_back = jax.vjp(layer_norm, residual_two, gain_two, shift_two)
    grad_two, grad_gain_two, grad_shift_two = norm_two_back(grad_flat)
    grad_branch = grad_two.astype(jnp.bfloat16)
    grad_bias_outer = jnp.sum(grad_branch, axis=0, dtype=jnp.float32)
    grad_outer = jnp.dot(activated.T, grad_branch, preferred_element_type=jnp.float32)
    grad_act = jnp.dot(grad_branch, outer_weight.T, preferred_element_type=jnp.float32)
    unused_act, gelu_back = jax.vjp(gelu_exact, pre_act)
    grad_pre = gelu_back(grad_act)[0].astype(jnp.bfloat16)
    grad_bias_inner = jnp.sum(grad_pre, axis=0, dtype=jnp.float32)
    grad_inner = jnp.dot(
        normed_one.astype(jnp.bfloat16).T, grad_pre, preferred_element_type=jnp.float32
    )
    grad_normed = grad_two + jnp.dot(grad_pre, inner_weight.T, preferred_element_type=jnp.float32)
    unused_one, norm_one_back = jax.vjp(layer_norm, residual_one, gain_one, shift_one)
    grad_one, grad_gain_one, grad_shift_one = norm_one_back(grad_normed)
    grad_attn_out = grad_one.astype(jnp.bfloat16)
    grad_bias_out = jnp.sum(grad_attn_out, axis=0, dtype=jnp.float32)
    grad_out_proj = jnp.dot(mixed_flat.T, grad_attn_out, preferred_element_type=jnp.float32)
    grad_mixed = jnp.dot(
        grad_attn_out, attn_weights[:, 3 * model_width :].T, preferred_element_type=jnp.float32
    )
    grad_mixed = grad_mixed.astype(jnp.bfloat16).reshape(batch_size, length, head_count, HD)
    scores = masked_scores(queries, key_rows, segment)
    attn_probs = jnp.exp(scores - log_total)
    grad_probs = jnp.einsum(
        "blhe,bmhe->bhlm", grad_mixed, value_rows, preferred_element_type=jnp.float32
    )
    inner_dot = jnp.sum(attn_probs * grad_probs, axis=-1, keepdims=True)
    grad_scores = (attn_probs * (grad_probs - inner_dot)).astype(jnp.bfloat16)
    grad_values = jnp.einsum(
        "bhlm,blhe->bmhe",
        attn_probs.astype(jnp.bfloat16),
        grad_mixed,
        preferred_element_type=jnp.float32,
    )
    grad_queries = jnp.einsum(
        "bhlm,bmhe->blhe", grad_scores, key_rows, preferred_element_type=jnp.float32
    ) * HD ** (-0.5)
    grad_keys = jnp.einsum(
        "bhlm,blhe->bmhe", grad_scores, queries, preferred_element_type=jnp.float32
    ) * HD ** (-0.5)
    row_total = batch_size * length
    grad_proj = jnp.concatenate(
        [
            grad_queries.reshape(row_total, model_width),
            grad_keys.reshape(row_total, model_width),
            grad_values.reshape(row_total, model_width),
        ],
        axis=1,
    ).astype(jnp.bfloat16)
    grad_bias_query = jnp.sum(grad_proj[:, :model_width], axis=0, dtype=jnp.float32)
    grad_bias_value = jnp.sum(grad_proj[:, 2 * model_width :], axis=0, dtype=jnp.float32)
    grad_proj_weight = jnp.dot(flat_rows.T, grad_proj, preferred_element_type=jnp.float32)
    grad_tokens = grad_one + jnp.dot(
        grad_proj, attn_weights[:, : 3 * model_width].T, preferred_element_type=jnp.float32
    )
    grad_attn = jnp.concatenate([grad_proj_weight, grad_out_proj], axis=1)
    grad_small = jnp.concatenate(
        [
            grad_bias_query,
            grad_bias_value,
            grad_bias_out,
            grad_gain_one,
            grad_shift_one,
            grad_bias_inner,
            grad_bias_outer,
            grad_gain_two,
            grad_shift_two,
        ]
    )
    return (
        grad_tokens.reshape(batch_size, length, model_width),
        grad_attn,
        grad_inner,
        grad_outer,
        grad_small,
    )


def rows_term(stacked, count):
    return jnp.moveaxis(stacked, 0, 1).reshape(count, -1)


def unfold_rows(summed, encoders):
    owned = summed.shape[0]
    return jnp.moveaxis(summed.reshape(owned, encoders, -1), 1, 0)


def adam_update(weight, first_moment, second, gradient, step_rate, decay_rate):
    first_new = BETA_ONE * first_moment + (1.0 - BETA_ONE) * gradient
    second_new = BETA_TWO * second + (1.0 - BETA_TWO) * gradient * gradient
    fix_one = 1.0 - BETA_ONE**STEP
    fix_two = 1.0 - BETA_TWO**STEP
    update = first_new / fix_one / (jnp.sqrt(second_new / fix_two) + ADAM_EPS)
    return (first_new, second_new, weight - step_rate * (update + decay_rate * weight))


def local(
    question_tokens,
    passage_tokens,
    passage_lengths,
    positives,
    attn_weight,
    attn_first,
    attn_second,
    ffn_in_weight,
    ffn_in_first,
    ffn_in_second,
    ffn_out_weight,
    ffn_out_first,
    ffn_out_second,
    small_params,
    small_first,
    small_second,
):
    gathered = (
        lax.all_gather(attn_weight.astype(jnp.bfloat16), ("dp", "pair"), axis=1, tiled=True),
        lax.all_gather(ffn_in_weight.astype(jnp.bfloat16), ("dp", "pair"), axis=1, tiled=True),
        lax.all_gather(ffn_out_weight.astype(jnp.bfloat16), ("dp", "pair"), axis=1, tiled=True),
        lax.all_gather(small_params.astype(jnp.bfloat16), ("dp", "pair"), axis=1, tiled=True),
    )
    attn_all, inner_all, outer_all, small_low = gathered
    small_all = small_low.astype(jnp.float32)
    question_count, question_len, model_width = question_tokens.shape
    row_count, row_len, unused_width = passage_tokens.shape
    attn_cols = attn_weight.shape[2]
    front_rows = attn_weight.shape[1]
    back_rows = ffn_out_weight.shape[1]
    seg_ends = jnp.cumsum(passage_lengths, axis=1)
    seg_starts = seg_ends - passage_lengths
    positions = jnp.arange(row_len, dtype=jnp.int32)
    passage_seg = jnp.sum(
        (positions[None, :, None] >= seg_ends[:, None, :]).astype(jnp.int32), axis=2
    )
    question_seg = jnp.zeros((question_count, question_len), jnp.int32)
    question_out, question_kept = encoder_forward(
        question_tokens, question_seg, attn_all[0], inner_all[0], outer_all[0], small_all[0]
    )
    passage_out, passage_kept = encoder_forward(
        passage_tokens, passage_seg, attn_all[1], inner_all[1], outer_all[1], small_all[1]
    )
    question_cls = question_out[:, 0].astype(jnp.bfloat16)
    passage_cls = (
        jnp.take_along_axis(passage_out, seg_starts[:, :, None], axis=1)
        .reshape(-1, model_width)
        .astype(jnp.bfloat16)
    )
    every_cls = lax.all_gather(passage_cls, ("dp", "pair"), axis=0, tiled=True)
    score_scale = model_width ** (-0.5)
    scores = jnp.dot(question_cls, every_cls.T, preferred_element_type=jnp.float32) * score_scale
    top_score = jnp.max(scores, axis=1, keepdims=True)
    raised = jnp.exp(scores - top_score)
    soft_scores = raised / jnp.sum(raised, axis=1, keepdims=True)
    columns = jnp.arange(every_cls.shape[0], dtype=jnp.int32)
    target = (columns[None, :] == positives[:, None]).astype(jnp.float32)
    grad_scores = (soft_scores - target).astype(jnp.bfloat16)
    grad_qcls = jnp.dot(grad_scores, every_cls, preferred_element_type=jnp.float32) * score_scale
    grad_pcls = lax.psum_scatter(
        jnp.dot(grad_scores.T, question_cls, preferred_element_type=jnp.float32) * score_scale,
        ("dp", "pair"),
        scatter_dimension=0,
        tiled=True,
    )
    grad_question_out = jnp.zeros_like(question_out).at[:, 0].set(grad_qcls)
    row_index = jnp.arange(row_count, dtype=jnp.int32)[:, None]
    grad_passage_out = (
        jnp.zeros_like(passage_out)
        .at[row_index, seg_starts]
        .set(grad_pcls.reshape(row_count, -1, model_width))
    )
    question_grad, q_attn, q_inner, q_outer, q_small = encoder_backward(
        question_tokens,
        question_seg,
        attn_all[0],
        inner_all[0],
        outer_all[0],
        small_all[0],
        question_kept,
        grad_question_out,
    )
    passage_grad, p_attn, p_inner, p_outer, p_small = encoder_backward(
        passage_tokens,
        passage_seg,
        attn_all[1],
        inner_all[1],
        outer_all[1],
        small_all[1],
        passage_kept,
        grad_passage_out,
    )
    front_stack = jnp.stack(
        [jnp.concatenate([q_attn, q_inner], axis=1), jnp.concatenate([p_attn, p_inner], axis=1)]
    )
    front_owned = lax.psum_scatter(
        rows_term(front_stack, front_rows * lax.axis_size(("dp", "pair"))),
        ("dp", "pair"),
        scatter_dimension=0,
        tiled=True,
    )
    back_owned = lax.psum_scatter(
        rows_term(jnp.stack([q_outer, p_outer]), back_rows * lax.axis_size(("dp", "pair"))),
        ("dp", "pair"),
        scatter_dimension=0,
        tiled=True,
    )
    small_sum = lax.psum_scatter(
        jnp.stack([q_small, p_small]), ("dp", "pair"), scatter_dimension=1, tiled=True
    )
    front_sum = unfold_rows(front_owned, 2)
    back_sum = unfold_rows(back_owned, 2)
    attn_sum = front_sum[:, :, :attn_cols]
    inner_sum = front_sum[:, :, attn_cols:]
    attn_m, attn_v, attn_w = adam_update(
        attn_weight, attn_first, attn_second, attn_sum, RATE_MATRIX, DECAY_MATRIX
    )
    inner_m, inner_v, inner_w = adam_update(
        ffn_in_weight, ffn_in_first, ffn_in_second, inner_sum, RATE_MATRIX, DECAY_MATRIX
    )
    outer_m, outer_v, outer_w = adam_update(
        ffn_out_weight, ffn_out_first, ffn_out_second, back_sum, RATE_MATRIX, DECAY_MATRIX
    )
    small_m, small_v, small_w = adam_update(
        small_params, small_first, small_second, small_sum, RATE_SMALL, 0.0
    )
    return (
        attn_m,
        attn_v,
        attn_w,
        inner_m,
        inner_v,
        inner_w,
        outer_m,
        outer_v,
        outer_w,
        small_m,
        small_v,
        small_w,
        question_grad,
        passage_grad,
    )


MESH_ID = pl.DeviceIdType.MESH
LOW = jnp.bfloat16
F32 = jnp.float32


def dot_nn(a, b):
    return jnp.dot(a, b, preferred_element_type=F32)


def dot_nt(a, b):
    return lax.dot_general(a, b, (((1,), (1,)), ((), ())), preferred_element_type=F32)


def dot_tn(a, b):
    return lax.dot_general(a, b, (((0,), (0,)), ((), ())), preferred_element_type=F32)


def expand_heads(rows):
    head_of = lax.broadcasted_iota(jnp.int32, rows.shape, 1) // HD
    heads = rows.shape[1] // HD
    return jnp.concatenate(
        [jnp.where(head_of == h, rows, jnp.zeros_like(rows)) for h in range(heads)], axis=0
    )


def pick_heads(stacked):
    width = stacked.shape[1]
    heads = width // HD
    head_of = lax.broadcasted_iota(jnp.int32, (16, width), 1) // HD
    total = jnp.zeros((16, width), F32)
    for h in range(heads):
        total = total + jnp.where(head_of == h, stacked[16 * h : 16 * h + 16], 0.0)
    return total


def split_low(values):
    high = values.astype(LOW)
    return high, (values - high.astype(F32)).astype(LOW)


def gelu_parts(values):
    cdf = 0.5 * (1.0 + lax.erf(values * (0.5**0.5)))
    density = jnp.exp(-0.5 * values * values) * (0.5 / math.pi) ** 0.5
    return values * cdf, cdf + values * density


def step_kernel(
    qt_ref, pt_ref, attn_ref, ffi_ref, ffo_ref, small_ref, len_ref, pos_ref,
    ga_ref, gi_ref, go_ref, gs_ref, dxq_ref, dxp_ref,
    X, slabA, slabI, slabO, smw, sm2, smb, bndo, bndb, R, WN, sn, sno, ST, Pf, Pb, DSb, Emat, b1p,
    w1s_, w1r, W1, W2, Yb, P2s, P2a, P2b, P2c, XH, Dout, dZb, Gb, Act, P3s, P3a, P3b, P3c, Qb, dAb, dUb, dQb,
    m1s, m1r, m2s, m2r, dws, dwr, GP, GS, GSw, GA, GI, GO, DX, qsb, vtb, ybf,
    loc, sib_s, sib_r, at_s, at_r, ag_s, ag_z, ag_p, aa_s, aa_r, rs_s, rs_p, rs_z, out_l, out_s, out_r,
):
    dp, z = lax.axis_index("dp"), lax.axis_index("pair")
    core = lax.rem(dp, 2)
    y, x = dp // 4, lax.rem(dp // 2, 2)
    own = y * 8 + x * 4 + z
    line = y * 8 + x * 4

    def dev(slot, k):
        return ((slot // 8) * 4 + lax.rem(slot // 4, 2) * 2 + k, lax.rem(slot, 4))

    sibling = dev(own, 1 - core)
    slot_x = y * 8 + (1 - x) * 4 + z
    slot_y = (1 - y) * 8 + x * 4 + z
    slot_d = (1 - y) * 8 + (1 - x) * 4 + z

    def remote(src, dst, ssem, rsem, target):
        return pltpu.make_async_remote_copy(
            src_ref=src, dst_ref=dst, send_sem=ssem, recv_sem=rsem,
            device_id=target, device_id_type=MESH_ID,
        )

    def done(ref, sem):
        pltpu.make_async_copy(ref, ref, sem).wait()

    barrier = pltpu.get_barrier_semaphore()
    other = 1 - core
    rows = pl.ds(pl.multiple_of(512 * core, 512), 512)
    pltpu.make_async_copy(attn_ref.at[core], slabA.at[core], loc.at[0]).start()

    def greet(r, c):
        pl.semaphore_signal(
            barrier, inc=1, device_id=dev(lax.rem(own + r, 16), core), device_id_type=MESH_ID
        )
        return c

    pl.semaphore_signal(barrier, inc=1, device_id=sibling, device_id_type=MESH_ID)
    lax.fori_loop(1, 16, greet, 0)

    @pl.when(core == 0)
    def _():
        pltpu.make_async_copy(qt_ref, X.at[rows], loc.at[1]).start()

    @pl.when(core == 1)
    def _():
        pltpu.make_async_copy(pt_ref, X.at[rows], loc.at[1]).start()

    pltpu.make_async_copy(ffi_ref.at[core], slabI.at[core], loc.at[2]).start()
    pltpu.make_async_copy(ffo_ref.at[core], slabO.at[core], loc.at[3]).start()

    narrow = small_ref[...].astype(LOW).astype(F32)
    window = jnp.zeros((2, 384), F32)
    for i in range(4):
        gaps = [jnp.zeros((2, n), F32) for n in (32 * i, 96 - 32 * i) if n]
        placed = jnp.concatenate(([gaps[0]] if i else []) + [narrow] + ([gaps[-1]] if i < 3 else []), axis=1)
        window = jnp.where(z == i, placed, window)
    for k in range(2):
        smw[k] = jnp.concatenate(
            [window[k : k + 1, 128 * i : 128 * i + 128] for i in range(3)]
            + [jnp.zeros((5, 128), F32)], axis=0,
        )
    sm2[core] = smw[core]

    lengths = len_ref[...].astype(F32)
    spans = jnp.concatenate(
        [jnp.broadcast_to(lengths[i : i + 1], (4, 4)) for i in range(2)], axis=0
    )
    at_row = lax.broadcasted_iota(jnp.int32, (8, 4), 0)
    at_lane = lax.broadcasted_iota(jnp.int32, (8, 4), 1)
    upto = at_lane <= lax.rem(at_row, 4)
    here = at_lane == lax.rem(at_row, 4)
    line_of = lax.broadcasted_iota(jnp.int32, (8, 1), 0)
    base = jnp.where(line_of >= 4, 256.0, 0.0)
    passage_end = jnp.sum(jnp.where(upto, spans, 0.0), axis=1, keepdims=True) + base
    passage_start = passage_end - jnp.sum(jnp.where(here, spans, 0.0), axis=1, keepdims=True)
    question_start = line_of.astype(F32) * 64.0
    eye = lax.broadcasted_iota(jnp.int32, (8, 8), 0) == lax.broadcasted_iota(jnp.int32, (8, 8), 1)
    goal = jnp.broadcast_to(pos_ref[...].astype(F32), (8, 8))
    goal = jnp.sum(jnp.where(eye, goal, 0.0), axis=1, keepdims=True)
    of_questions = jnp.concatenate([question_start, question_start + 64.0, goal], axis=0)
    of_passages = jnp.concatenate([passage_start, passage_end, goal], axis=0)
    bndb[core] = jnp.broadcast_to(jnp.where(core == 0, of_questions, of_passages), (24, 128))
    bndo[...] = jnp.broadcast_to(jnp.where(core == 0, of_passages, of_questions), (24, 128))
    pl.semaphore_wait(barrier, 16)

    remote(smw.at[other], sm2.at[core], sib_s.at[1], sib_r.at[1], sibling).start()
    remote(attn_ref.at[other], slabA.at[core], sib_s.at[0], sib_r.at[0], sibling).start()
    remote(bndo, bndb.at[core], sib_s.at[2], sib_r.at[2], sibling).start()

    @pl.when(core == 0)
    def _():
        remote(pt_ref, X.at[rows], sib_s.at[3], sib_r.at[3], sibling).start()

    @pl.when(core == 1)
    def _():
        remote(qt_ref, X.at[rows], sib_s.at[3], sib_r.at[3], sibling).start()

    remote(ffi_ref.at[other], slabI.at[core], sib_s.at[4], sib_r.at[4], sibling).start()
    remote(ffo_ref.at[other], slabO.at[core], sib_s.at[5], sib_r.at[5], sibling).start()

    done(sm2.at[other], sib_r.at[1])
    smb[own] = jnp.concatenate([sm2[0], sm2[1]], axis=0).astype(LOW)

    exchanged = (smb, w1r, None, m1r, None, dwr, m2r)
    gathered = (Yb, Qb, XH.at[core], dUb, None, dQb)
    summed = ((P2s, P2a, P2b, P2c), (P3s, P3a, P3b, P3c))
    passed = ((slabA.at[0], slabA.at[0]), (sm2.at[0], sm2.at[0]), (bndb.at[0], bndb.at[0]),
              (X.at[rows], X.at[rows]), (slabI.at[0], slabI.at[0]), (slabO.at[0], slabO.at[0]),
              (sn, sno), (XH.at[0], XH.at[0]))
    written = [[ref] * 3 for ref in (GO.at[0], DX.at[rows], GI.at[0], GA.at[0, 0], GSw.at[0], GA.at[0, 0])]
    state = {("pass", n): int(n < 2) for n in range(6)}
    state["attn", 0] = 1

    def direct(n, src_of):
        def body(r, c):
            target = lax.rem(own + r, 16)
            remote(src_of(target), exchanged[n].at[own], aa_s.at[n], aa_r.at[n], dev(target, core)).start()
            return c

        lax.fori_loop(1, 16, body, 0)
        state["direct", n] = 0

    def direct_done(n):
        done(exchanged[n].at[pl.ds(0, 15)], aa_r.at[n])
        state["direct", n] = 1

    def pass_done(n):
        done(passed[n][1], sib_r.at[n])
        state["pass", n] = 1

    direct(0, lambda t: smb.at[own])

    def push(slot, m, target):
        remote(R.at[slot, m], R.at[slot, m], at_s.at[m], at_r.at[slot, m, 0], dev(target, core)).start()

    def near(f, nearest=1):
        for d in range(nearest, 4):
            for dz in (d, -d) if d else (0,):
                @pl.when(jnp.logical_and(z + dz >= 0, z + dz <= 3))
                def _():
                    f(dz)

    def got(slot, m):
        done(R.at[slot, m], at_r.at[slot, m, 0])

    done(slabA.at[core], loc.at[0])
    done(slabA.at[other], sib_r.at[0])
    for m in (0, 3, 1, 2):
        cols = slice(768 * m, 768 * m + 768)
        R[own, m] = jnp.concatenate([slabA[0, :, cols], slabA[1, :, cols]], axis=0).astype(LOW)
        for target in (slot_x, slot_y) if m < 3 else (slot_x, slot_y, slot_d):
            push(own, m, target)
        if m < 3:
            near(lambda dz: push(own, m, own + dz))

    def hop(d):
        for i in range(4):
            slot = 4 * i + z
            if d == 0:
                @pl.when(4 * i != line)
                def _():
                    got(slot, 3)

                @pl.when(z < 3)
                def _():
                    push(slot, 3, own + 1)

                @pl.when(z > 0)
                def _():
                    push(slot, 3, own - 1)
            else:
                @pl.when(z - d >= 0)
                def _():
                    got(slot - d, 3)

                    @pl.when(z < 3)
                    def _():
                        push(slot - d, 3, own + 1)

                @pl.when(z + d <= 3)
                def _():
                    got(slot + d, 3)

                    @pl.when(z > 0)
                    def _():
                        push(slot + d, 3, own - 1)

    def settle(last=True):
        for kind, n in list(state):
            at = state[kind, n]
            if last and kind == "gather" and at == 0:
                gather_forward(n)
            if last and kind == "gather" and at < 2:
                gather_done(n)
            if last and kind == "sum" and at == 0:
                sum_forward(n)
            if last and kind == "sum" and at < 2:
                sum_done(n)
            if last and kind == "direct" and at == 0:
                direct_done(n)
            if last and kind == "pass" and at == 0:
                pass_done(n)
            if kind == "gather" and (last or at == 2):
                done(gathered[n].at[pl.ds(0, 15)], ag_s.at[n])
            elif kind == "direct" and (last or at == 1):
                done(exchanged[n].at[pl.ds(0, 15)], aa_s.at[n])
            elif kind == "sum" and (last or at == 2):
                done(summed[n][1].at[pl.ds(0, 3)], rs_s.at[n, 0])
                done(summed[n][3].at[pl.ds(0, 3)], rs_s.at[n, 1])
            elif kind == "pass" and (last or at == 1):
                done(passed[n][0], sib_s.at[n])
            elif kind == "out" and last:
                for ref, sem in zip(written[n], (out_l, out_s, out_r)):
                    done(ref, sem.at[n])
            elif kind == "attn":
                for m in range(3):
                    done(R.at[pl.ds(0, 15), m], at_s.at[m])
                done(R.at[pl.ds(0, 7), 3], at_s.at[3])

                @pl.when(jnp.logical_and(z > 0, z < 3))
                def _():
                    done(R.at[pl.ds(0, 16), 3], at_s.at[3])
            else:
                continue
            del state[kind, n]

    def finish():
        settle()

    def relay(m):
        def from_z(dz):
            got(own + dz, m)
            for target in (slot_x, slot_y):
                push(own + dz, m, target)

        near(from_z)

        def from_plane(dz):
            for slot, target, half in ((slot_x + dz, slot_y, 0), (slot_y + dz, slot_x, 1)):
                got(slot, m)
                part = R.at[slot, m, :, pl.ds(384 * half, 384)]
                remote(part, part, at_s.at[m], at_r.at[slot, m, half], dev(target, core)).start()

        near(from_plane, 0)

    def from_slots(read, write):
        def body(g, c):
            got = [read(4 * g + i).astype(F32) for i in range(4)]
            natural = jnp.concatenate([v[0:24] for v in got] + [v[24:48] for v in got], axis=0)
            write(pl.ds(pl.multiple_of(192 * g, 64), 192), natural.astype(LOW))
            return c

        lax.fori_loop(0, 4, body, 0)

    def to_slots(read, write):
        def body(g, c):
            v = read(pl.ds(pl.multiple_of(192 * g, 64), 192))
            for i in range(4):
                part = jnp.concatenate(
                    [v[24 * i : 24 * i + 24], v[96 + 24 * i : 96 + 24 * i + 24]], axis=0
                )
                write(4 * g + i, part.astype(LOW))
            return c

        lax.fori_loop(0, 4, body, 0)

    def arrive(m):
        def body(zz, c):
            slot = (1 - y) * 8 + (1 - x) * 4 + zz
            for half in range(2):
                done(R.at[slot, m, :, pl.ds(384 * half, 384)], at_r.at[slot, m, half])
            return c

        if m < 3:
            lax.fori_loop(0, 4, body, 0)

        def write(where, v):
            WN[m, where, :] = v

        from_slots(lambda s: R[s, m], write)

    early_own = (0, 2, 5)

    def gather_start(n):
        buf = gathered[n]
        state["gather", n] = 0

        def give(dz):
            remote(buf.at[own], buf.at[own], ag_s.at[n], ag_z.at[n, z], dev(own + dz, core)).start()

        near(give)
        if n in early_own:
            for target in (slot_x, slot_y, slot_d):
                remote(buf.at[own], buf.at[own], ag_s.at[n], ag_p.at[n], dev(target, core)).start()

    def gather_forward(n):
        buf = gathered[n]
        state["gather", n] = 1

        def pass_on(dz):
            block = buf.at[own + dz]
            done(block, ag_z.at[n, z + dz])
            if n in early_own:
                for target in (slot_x, slot_y, slot_d):
                    remote(block, block, ag_s.at[n], ag_p.at[n], dev(target, core)).start()

        near(pass_on)
        if n not in early_own:
            block = buf.at[pl.ds(line, 4)]
            for target in (slot_x, slot_y, slot_d):
                remote(block, block, ag_s.at[n], ag_p.at[n], dev(target, core)).start()

    def gather_done(n):
        state["gather", n] = 2
        done(gathered[n].at[pl.ds(0, 12)], ag_p.at[n])

    def sum_start(n):
        source, plane, unused, unused = summed[n]
        state["sum", n] = 0
        for target in (slot_x, slot_y, slot_d):
            remote(
                source.at[pl.ds(target - z, 4)], plane.at[line // 4],
                rs_s.at[n, 0], rs_p.at[n], dev(target, core),
            ).start()
        plane[line // 4] = source[pl.ds(line, 4)]

    def sum_forward(n):
        unused, plane, along, final = summed[n]
        state["sum", n] = 1
        done(plane.at[pl.ds(0, 3)], rs_p.at[n])
        along[...] = jnp.sum(plane[...].astype(F32), axis=0).astype(LOW)

        def give(dz):
            remote(
                along.at[z + dz], final.at[z], rs_s.at[n, 1], rs_z.at[n], dev(own + dz, core)
            ).start()

        near(give)
        final[z] = along[z]

    def sum_done(n):
        final = summed[n][3]
        state["sum", n] = 2
        done(final.at[pl.ds(0, 3)], rs_z.at[n])
        return jnp.sum(final[...].astype(F32), axis=0)

    def prepare_ffn():
        row = lax.broadcasted_iota(jnp.int32, (384, 512), 0)
        col = lax.broadcasted_iota(jnp.int32, (384, 512), 1)
        Emat[...] = jnp.where(col == 128 * (row // 96) + lax.rem(row, 96), 1.0, 0.0).astype(LOW)
        done(slabI.at[core], loc.at[2])
        pass_done(4)
        for g in range(8):
            cols = slice(384 * g, 384 * g + 384)
            part = jnp.concatenate([slabI[0, :, cols], slabI[1, :, cols]], axis=0).astype(LOW)
            wide = dot_nn(part, Emat[...]).astype(LOW)
            for i in range(4):
                w1s_[4 * (g // 2) + i, :, 128 * (g % 2) : 128 * (g % 2) + 128] = wide[
                    :, 128 * i : 128 * i + 128
                ]
        w1r[own] = w1s_[own]
        done(slabO.at[core], loc.at[3])
        pass_done(5)
        gap = jnp.zeros((32, 768), F32)
        W2[...] = jnp.concatenate([slabO[0], gap, slabO[1], gap], axis=0).astype(LOW)

    def natural_small():
        direct_done(0)
        for g in range(8):
            parts = [
                smb[4 * (g // 2) + i].astype(F32)[8 * (g % 2) : 8 * (g % 2) + 8] for i in range(4)
            ]
            lines = [parts[0][0:1], parts[0][1:2]]
            for i in range(1, 4):
                lines += [parts[i - 1][2:3] + parts[i][0:1], parts[i][1:2]]
            lines += [parts[3][2:3]]
            sn[9 * g : 9 * g + 9, :] = jnp.concatenate(lines, axis=0)
        remote(sn, sno, sib_s.at[6], sib_r.at[6], sibling).start()
        state["pass", 6] = 0

    def vec(row, count=6, ref=sn):
        return jnp.concatenate([ref[row + i : row + i + 1, :] for i in range(count)], axis=1)

    relay(0)
    hop(0)
    pass_done(2)
    done(X.at[pl.ds(0, 512)], loc.at[1])
    pass_done(3)
    starts = jnp.concatenate([bndb[0, 0:8], bndb[1, 0:8] + 512.0], axis=0)[:, 0:1]
    ends = jnp.concatenate([bndb[0, 8:16], bndb[1, 8:16] + 512.0], axis=0)[:, 0:1]
    token = lax.broadcasted_iota(jnp.int32, (16, 1024), 1).astype(F32)
    inside = jnp.logical_and(token >= starts, token < ends)
    first = jnp.where(token == starts, 1.0, 0.0).astype(LOW)
    cls_in = dot_nn(first, X[...])
    cls_low = cls_in.astype(LOW)
    natural_small()
    prepare_ffn()
    relay(1)
    hop(1)
    arrive(0)
    queries = (dot_nn(cls_low, WN[0]) + vec(0)).astype(LOW)
    Qb[own] = queries
    gather_start(1)
    relay(2)
    hop(2)
    arrive(1)
    qsb[...] = (dot_nt(expand_heads(queries), WN[1]) * (HD**-0.5)).astype(LOW)
    ST[...] = dot_nt(qsb[...], X[...])

    def soften(h, c):
        at = pl.ds(pl.multiple_of(16 * h, 16), 16)
        s = jnp.where(inside, ST[at, :], -1000000000.0)
        e = jnp.exp(s - jnp.max(s, axis=1, keepdims=True))
        p = e / jnp.sum(e, axis=1, keepdims=True)
        Pf[at, :] = p
        Pb[at, :] = p.astype(LOW)
        return c

    lax.fori_loop(0, 12, soften, 0, unroll=4)
    ybf[...] = dot_nn(Pb[...], X[...]).astype(LOW)
    arrive(2)
    mixed = (pick_heads(dot_nn(ybf[...], WN[2])) + vec(6)).astype(LOW)
    hop(3)
    arrive(3)
    lifted = cls_in + dot_nn(mixed, WN[3]) + vec(12)
    centred = lifted - jnp.mean(lifted, axis=1, keepdims=True)
    rstd_one = lax.rsqrt(jnp.mean(centred * centred, axis=1, keepdims=True) + NORM_EPS)
    hat_one = centred * rstd_one
    normed = hat_one * vec(18) + vec(24)
    Yb[own] = normed.astype(LOW)
    gather_start(0)
    direct(1, lambda t: w1s_.at[t])

    early = jnp.concatenate(
        [ybf[...].astype(F32), cls_in, mixed.astype(F32), jnp.zeros((32, 768), F32)], axis=0
    )
    DX[0:768, 0:256] = early.T

    def write_m1(slot, v):
        m1s[slot] = v

    to_slots(lambda w: DX[w, 0:256], write_m1)
    m1r[own] = m1s[own]
    gather_forward(0)

    b1 = jnp.concatenate([vec(30 + 3 * g, 3) for g in range(8)], axis=0).astype(LOW)
    b1_wide = dot_nn(b1, Emat[...])
    for g in range(8):
        b1p[g] = jnp.broadcast_to(b1_wide[g : g + 1], (8, 512))
    group = pl.multiple_of(128 * z, 128)
    gy = 4 * y + 2 * x
    b1_row = jnp.concatenate(
        [b1p[gy, 0:1, pl.ds(group, 128)], b1p[gy + 1, 0:1, pl.ds(group, 128)]], axis=1
    )
    direct_done(1)

    def write_w1(where, v):
        W1[where, :] = v

    from_slots(lambda s: w1r[s], write_w1)
    gather_done(0)
    all_y = Yb[...].reshape(256, 768)
    act = dot_nn(all_y, W1[...]) + b1_row
    Act[...] = act
    hidden, unused = gelu_parts(act)
    Gb[...] = hidden.astype(LOW)
    P2s[...] = dot_nn(Gb[...], W2[...]).astype(LOW).reshape(16, 16, 768)
    sum_start(0)
    direct(3, lambda t: m1s.at[t])
    sum_forward(0)
    hidden_sum = sum_done(0)
    second = normed + hidden_sum + vec(54)
    centred = second - jnp.mean(second, axis=1, keepdims=True)
    rstd_two = lax.rsqrt(jnp.mean(centred * centred, axis=1, keepdims=True) + NORM_EPS)
    hat_two = centred * rstd_two
    rstd_high, rstd_low = split_low(rstd_two)
    lane = lax.broadcasted_iota(jnp.int32, (16, 128), 1)
    positive = jnp.concatenate([bndb[0, 16:24], bndb[1, 16:24]], axis=0)
    extra = jnp.where(
        lane == 0, rstd_high.astype(F32),
        jnp.where(lane == 1, rstd_low.astype(F32), jnp.where(lane == 2, positive, 0.0)),
    )
    XH[core, own] = jnp.concatenate([hat_two, extra], axis=1).astype(LOW)
    gather_start(2)
    gather_forward(2)
    gather_forward(1)
    gather_done(2)
    remote(XH.at[core], XH.at[core], sib_s.at[7], sib_r.at[7], sibling).start()
    state["pass", 7] = 0
    pass_done(6)
    pass_done(7)

    def vec_of(encoder, row):
        return jnp.where(core == encoder, vec(row), vec(row, 6, sno))

    xq = XH[0].reshape(256, 896).astype(F32)
    xp = XH[1].reshape(256, 896).astype(F32)
    qc = (xq[:, 0:768] * vec_of(0, 60) + vec_of(0, 66)).astype(LOW)
    pc = (xp[:, 0:768] * vec_of(1, 60) + vec_of(1, 66)).astype(LOW)
    scale = 768 ** (-0.5)
    scores = dot_nt(qc, pc) * scale
    raised = jnp.exp(scores - jnp.max(scores, axis=1, keepdims=True))
    soft = raised / jnp.sum(raised, axis=1, keepdims=True)
    place = lax.broadcasted_iota(jnp.int32, (256, 256), 1)
    slot_of = place // 16
    owner_of = (
        16 * (slot_of // 8) + 8 * lax.rem(slot_of // 4, 2)
        + 4 * (lax.rem(place, 16) // 8) + lax.rem(slot_of, 4)
    )
    passage = (8 * owner_of + lax.rem(place, 8)).astype(F32)
    target = jnp.where(passage == xq[:, 770:771], 1.0, 0.0)
    grad_scores = (soft - target).astype(LOW)

    @pl.when(core == 0)
    def _():
        Dout[...] = dot_nn(grad_scores, pc) * scale

    @pl.when(core == 1)
    def _():
        Dout[...] = dot_tn(grad_scores, qc) * scale

    dout = Dout[...]
    block = XH[core].reshape(256, 896).astype(F32)
    hat = block[:, 0:768]
    rstd = block[:, 768:769] + block[:, 769:770]
    inner = dout * vec(60)
    grad_two = rstd * (
        inner - jnp.mean(inner, axis=1, keepdims=True)
        - hat * jnp.mean(inner * hat, axis=1, keepdims=True)
    )
    dg2 = jnp.sum(dout * hat, axis=0, keepdims=True)
    ds2 = jnp.sum(dout, axis=0, keepdims=True)
    Dout[...] = grad_two
    dZb[...] = grad_two.astype(LOW)
    db2 = jnp.sum(dZb[...].astype(F32), axis=0, keepdims=True)
    unused, slope = gelu_parts(Act[...])
    da = (dot_nt(dZb[...], W2[...]) * slope).astype(LOW)
    P3s[...] = dot_nt(da, W1[...]).astype(LOW).reshape(16, 16, 768)
    sum_start(1)
    DX[0:768, 0:256] = dot_tn(all_y, da)

    def write_dw(slot, v):
        dws[slot] = v

    to_slots(lambda w: DX[w, 0:256], write_dw)
    direct(5, lambda t: dws.at[t])
    sum_forward(1)
    dwr[own] = dws[own]
    db1 = jnp.sum(da.astype(F32), axis=0, keepdims=True)
    dw2 = dot_tn(Gb[...], dZb[...])
    GO[0] = dw2[0:96]
    GO[1] = dw2[128:224]
    pltpu.make_async_copy(GO.at[core], go_ref.at[core], out_l.at[0]).start()
    remote(GO.at[other], go_ref.at[core], out_s.at[0], out_r.at[0], sibling).start()
    state["out", 0] = 0
    own_rows = pl.ds(pl.multiple_of(16 * own, 16), 16)
    normed_sum = sum_done(1)

    grad_normed = Dout[own_rows, :] + normed_sum
    inner = grad_normed * vec(18)
    grad_one = rstd_one * (
        inner - jnp.mean(inner, axis=1, keepdims=True)
        - hat_one * jnp.mean(inner * hat_one, axis=1, keepdims=True)
    )
    grad_lift = grad_one.astype(LOW)
    grad_mixed = dot_nt(grad_lift, WN[3]).astype(LOW)
    dg1 = jnp.sum(grad_normed * hat_one, axis=0, keepdims=True)
    ds1 = jnp.sum(grad_normed, axis=0, keepdims=True)
    partial_sums = jnp.concatenate(
        [dg1[:, 128 * i : 128 * i + 128] for i in range(6)]
        + [ds1[:, 128 * i : 128 * i + 128] for i in range(6)]
        + [db1[:, 0:128], db1[:, 128:256], jnp.zeros((2, 128), F32)], axis=0,
    )
    dUb[own] = jnp.concatenate([grad_one, partial_sums], axis=1).astype(LOW)
    gather_start(3)
    spread = expand_heads(grad_mixed)
    vtb[...] = dot_nt(spread, WN[2]).astype(LOW)
    constant = jnp.sum(spread.astype(F32) * vec(6), axis=1, keepdims=True)
    ST[...] = dot_nt(vtb[...], X[...]) + constant

    def harden(h, c):
        at = pl.ds(pl.multiple_of(16 * h, 16), 16)
        p, dprob = Pf[at, :], ST[at, :]
        total = jnp.sum(p * dprob, axis=1, keepdims=True)
        DSb[at, :] = (p * (dprob - total)).astype(LOW)
        return c

    lax.fori_loop(0, 12, harden, 0, unroll=4)
    late = (dot_nn(DSb[...], X[...]) * (HD**-0.5)).astype(LOW)
    grad_query = pick_heads(dot_nn(late, WN[1])).astype(LOW)
    dQb[own] = grad_query
    gather_start(5)
    DX[0:768, 0:256] = jnp.concatenate(
        [late.astype(F32), jnp.zeros((64, 768), F32)], axis=0
    ).T

    def write_m2(slot, v):
        m2s[slot] = v

    to_slots(lambda w: DX[w, 0:256], write_m2)
    direct(6, lambda t: m2s.at[t])
    m2r[own] = m2s[own]
    gather_forward(3)

    grad_cls = grad_one + dot_nt(grad_query, WN[0])
    cls_high, cls_rest = split_low(grad_cls)
    right = jnp.concatenate([qsb[...], vtb[...], cls_high, cls_rest], axis=0)
    for k in range(2):
        part = slice(512 * k, 512 * k + 512)
        left = jnp.concatenate([DSb[:, part], Pb[:, part], first[:, part], first[:, part]], axis=0)
        DX[part, :] = dot_tn(left, right)
    gather_forward(5)
    other_rows = pl.ds(pl.multiple_of(512 * other, 512), 512)

    @pl.when(core == 0)
    def _():
        pltpu.make_async_copy(DX.at[rows], dxq_ref, out_l.at[1]).start()
        remote(DX.at[other_rows], dxq_ref, out_s.at[1], out_r.at[1], sibling).start()

    @pl.when(core == 1)
    def _():
        pltpu.make_async_copy(DX.at[rows], dxp_ref, out_l.at[1]).start()
        remote(DX.at[other_rows], dxp_ref, out_s.at[1], out_r.at[1], sibling).start()

    state["out", 1] = 0

    direct_done(5)
    for g in range(8):
        wide = jnp.concatenate(
            [dwr[4 * (g // 2) + i, :, 128 * (g % 2) : 128 * (g % 2) + 128] for i in range(4)], axis=1
        )
        narrow = dot_nt(wide, Emat[...])
        GI[0, :, 384 * g : 384 * g + 384] = narrow[0:24]
        GI[1, :, 384 * g : 384 * g + 384] = narrow[24:48]
    pltpu.make_async_copy(GI.at[core], gi_ref.at[core], out_l.at[2]).start()
    remote(GI.at[other], gi_ref.at[core], out_s.at[2], out_r.at[2], sibling).start()
    state["out", 2] = 0

    def put(m, v):
        GA[m // 2, 0, :, 768 * (m % 2) : 768 * (m % 2) + 768] = v[0:24]
        GA[m // 2, 1, :, 768 * (m % 2) : 768 * (m % 2) + 768] = v[24:48]

    def hand_out(half, n):
        part = ga_ref.at[core, :, pl.ds(1536 * half, 1536)]
        pltpu.make_async_copy(GA.at[half, core], part, out_l.at[n]).start()
        remote(GA.at[half, other], part, out_s.at[n], out_r.at[n], sibling).start()
        state["out", n] = 0

    def factor_sum(messages, columns):
        def body(s, total):
            wide = jnp.concatenate(
                [expand_heads(columns[s]), jnp.zeros((64, 768), LOW)], axis=0
            )
            return total + dot_nn(messages[s], wide)

        return lax.fori_loop(0, 16, body, jnp.zeros((48, 768), F32), unroll=4)

    def columns_of(at):
        return jnp.concatenate(
            [m1r[s, :, at : at + 16].astype(F32) for s in range(16)], axis=1
        ).astype(LOW)

    gather_done(3)
    all_du = dUb[...].reshape(256, 896)[:, 0:768]
    all_da = dot_nt(all_du, WN[3]).astype(LOW)
    dAb[...] = all_da.reshape(16, 16, 768)
    direct_done(3)
    put(2, factor_sum(m1r, dAb))
    put(3, dot_nn(columns_of(208), all_du))
    hand_out(1, 5)
    cls_columns = columns_of(192)

    parts = [dUb[i, :, 768:896].astype(F32) for i in range(16)]
    sums = parts[0]
    for part in parts[1:]:
        sums = sums + part
    hidden_rows = []
    for g in range(8):
        hidden_rows.append(
            jnp.concatenate(
                [parts[4 * (g // 2) + i][12 + g % 2 : 13 + g % 2] for i in range(4)], axis=1
            )
        )
    wide = jnp.concatenate(hidden_rows, axis=0)
    narrow = dot_nt(wide.astype(LOW), Emat[...])

    def six(v):
        return [v[:, 128 * i : 128 * i + 128] for i in range(6)]

    lines = six(jnp.sum(all_da.astype(F32), axis=0, keepdims=True))
    lines += six(jnp.sum(all_du.astype(F32), axis=0, keepdims=True))
    lines += [sums[0:12]]
    for g in range(8):
        lines += [narrow[g : g + 1, 128 * i : 128 * i + 128] for i in range(3)]
    lines += six(db2) + six(dg2) + six(ds2) + [jnp.zeros((8, 128), F32)]
    GP[6:80] = jnp.concatenate(lines, axis=0)
    for g in range(8):
        for i in range(4):
            at = 9 * g + 9 * i // 4
            if at > 5:
                GS[g, i] = GP[at : at + 8]
    gather_done(1)
    settle(False)
    direct_done(6)
    put(1, factor_sum(m2r, Qb))
    gather_done(5)
    all_dq = dQb[...].reshape(256, 768)
    put(0, dot_nn(cls_columns, all_dq))
    hand_out(0, 3)
    GP[0:6] = jnp.concatenate(six(jnp.sum(all_dq.astype(F32), axis=0, keepdims=True)), axis=0)
    for i in range(3):
        GS[0, i] = GP[9 * i // 4 : 9 * i // 4 + 8]
    for k in range(2):
        GSw[k] = GS[gy + k, z]
    pltpu.make_async_copy(GSw.at[core], gs_ref.at[core], out_l.at[4]).start()
    remote(GSw.at[other], gs_ref.at[core], out_s.at[4], out_r.at[4], sibling).start()
    state["out", 4] = 0
    finish()


def kernel_call(qt, pt, attn, ffi, ffo, small, lengths, positives):
    any_space = pl.BlockSpec(memory_space=pl.ANY)
    vmem = pl.BlockSpec(memory_space=pltpu.VMEM)
    V = pltpu.VMEM
    dma = pltpu.SemaphoreType.DMA
    scratch = [
        V((1024, 768), LOW), V((2, 24, 3072), F32), V((2, 24, 3072), F32), V((2, 96, 768), F32),
        V((2, 8, 128), F32), V((2, 8, 128), F32), V((16, 16, 128), LOW),
        V((24, 128), F32), V((2, 24, 128), F32), V((16, 4, 48, 768), LOW),
        V((4, 768, 768), LOW), V((72, 128), F32), V((72, 128), F32), V((192, 1024), F32),
        V((192, 1024), F32), V((192, 1024), LOW), V((192, 1024), LOW), V((384, 512), LOW),
        V((8, 8, 512), F32),
        V((16, 48, 256), LOW), V((16, 48, 256), LOW), V((768, 256), LOW), V((256, 768), LOW),
        V((16, 16, 768), LOW), V((16, 16, 768), LOW), V((4, 4, 16, 768), LOW),
        V((4, 16, 768), LOW), V((4, 16, 768), LOW),
        V((2, 16, 16, 896), LOW), V((256, 768), F32), V((256, 768), LOW), V((256, 256), LOW),
        V((256, 256), F32), V((16, 16, 768), LOW), V((4, 4, 16, 768), LOW),
        V((4, 16, 768), LOW), V((4, 16, 768), LOW), V((16, 16, 768), LOW),
        V((16, 16, 768), LOW), V((16, 16, 896), LOW), V((16, 16, 768), LOW),
        V((16, 48, 256), LOW), V((16, 48, 256), LOW), V((16, 48, 256), LOW), V((16, 48, 256), LOW),
        V((16, 48, 256), LOW), V((16, 48, 256), LOW),
        V((80, 128), F32), V((8, 4, 8, 128), F32), V((2, 8, 128), F32), V((2, 2, 24, 1536), F32), V((2, 24, 3072), F32),
        V((2, 96, 768), F32), V((1024, 768), F32), V((192, 768), LOW), V((192, 768), LOW),
        V((192, 768), LOW),
        dma((4,)), dma((8,)), dma((8,)), dma((4,)), dma((16, 4, 2)), dma((7,)), dma((7, 4)),
        dma((7,)), dma((7,)), dma((7,)), dma((2, 2)), dma((2,)), dma((2,)),
        dma((6,)), dma((6,)), dma((6,)),
    ]
    shapes = (
        (2, 24, 3072), (2, 24, 3072), (2, 96, 768), (2, 8, 128), (512, 768), (512, 768)
    )
    return pl.pallas_call(
        step_kernel,
        out_shape=[jax.ShapeDtypeStruct(s, F32) for s in shapes],
        in_specs=[any_space] * 5 + [vmem] * 3,
        out_specs=[any_space] * 6,
        scratch_shapes=scratch,
        compiler_params=pltpu.CompilerParams(
            collective_id=0, has_side_effects=True, vmem_limit_bytes=56 << 20
        ),
    )(qt, pt, attn, ffi, ffo, small, lengths, positives)


def update_kernel(*refs):
    ins, outs = refs[:18], refs[18:]
    for n in range(3):
        weight, first, second, grad = (r[...] for r in ins[4 * n : 4 * n + 4])
        new = adam_update(weight, first, second, grad, RATE_MATRIX, DECAY_MATRIX)
        for ref, value in zip(outs[3 * n : 3 * n + 3], new):
            ref[...] = value

    @pl.when(pl.program_id(0) == 0)
    def _():
        z = lax.axis_index("pair")
        weight, first, second, window = ins[12:16]
        lines = []
        for e in range(2):
            row = jnp.concatenate([window[e, i : i + 1, :] for i in range(3)], axis=1)
            picked = row[:, 0:288]
            for i in range(1, 4):
                picked = jnp.where(z == i, row[:, 32 * i : 32 * i + 288], picked)
            lines.append(picked)
        grad = jnp.concatenate(lines, axis=0)
        new = adam_update(weight[...], first[...], second[...], grad, RATE_SMALL, 0.0)
        for ref, value in zip(outs[9:12], new):
            ref[...] = value

    outs[12][...] = ins[16][...]
    outs[13][...] = ins[17][...]


def update_call(attn, inner, outer, small, grad_question, grad_passage):
    wide = pl.BlockSpec((1, 24, 3072), lambda i: (i, 0, 0))
    tall = pl.BlockSpec((1, 96, 768), lambda i: (i, 0, 0))
    vector = pl.BlockSpec((2, 288), lambda i: (0, 0))
    window = pl.BlockSpec((2, 8, 128), lambda i: (0, 0, 0))
    token = pl.BlockSpec((256, 768), lambda i: (i, 0))

    def like(a):
        return jax.ShapeDtypeStruct(a.shape, F32)

    return pl.pallas_call(
        update_kernel,
        grid=(2,),
        out_shape=[like(g[0]) for g in (attn, inner, outer, small) for _ in range(3)]
        + [like(grad_question), like(grad_passage)],
        in_specs=[wide] * 8 + [tall] * 4 + [vector] * 3 + [window, token, token],
        out_specs=[wide] * 6 + [tall] * 3 + [vector] * 3 + [token, token],
    )(*attn, *inner, *outer, *small, grad_question, grad_passage)


def local_kernel(
    question_tokens, passage_tokens, passage_lengths, positives,
    attn_weight, attn_first, attn_second, ffn_in_weight, ffn_in_first, ffn_in_second,
    ffn_out_weight, ffn_out_first, ffn_out_second, small_params, small_first, small_second,
):
    grads = kernel_call(
        question_tokens.reshape(512, 768), passage_tokens.reshape(512, 768),
        attn_weight, ffn_in_weight, ffn_out_weight, small_params,
        passage_lengths, positives.reshape(1, 8),
    )
    attn_sum, inner_sum, outer_sum, small_window, grad_question, grad_passage = grads
    results = update_call(
        (attn_weight, attn_first, attn_second, attn_sum),
        (ffn_in_weight, ffn_in_first, ffn_in_second, inner_sum),
        (ffn_out_weight, ffn_out_first, ffn_out_second, outer_sum),
        (small_params, small_first, small_second, small_window),
        grad_question, grad_passage,
    )
    return (
        *results[:12],
        results[12].reshape(question_tokens.shape),
        results[13].reshape(passage_tokens.shape),
    )


def fits_kernel(mesh):
    return mesh.shape["dp"] == 8 and mesh.shape["pair"] == 4


def solution(mesh):
    in_specs = (
        P(("dp", "pair"), None, None),
        P(("dp", "pair"), None, None),
        P(("dp", "pair"), None),
        P(("dp", "pair")),
        P(None, ("dp", "pair"), None),
        P(None, ("dp", "pair"), None),
        P(None, ("dp", "pair"), None),
        P(None, ("dp", "pair"), None),
        P(None, ("dp", "pair"), None),
        P(None, ("dp", "pair"), None),
        P(None, ("dp", "pair"), None),
        P(None, ("dp", "pair"), None),
        P(None, ("dp", "pair"), None),
        P(None, ("dp", "pair")),
        P(None, ("dp", "pair")),
        P(None, ("dp", "pair")),
    )
    out_specs = (
        P(None, ("dp", "pair"), None),
        P(None, ("dp", "pair"), None),
        P(None, ("dp", "pair"), None),
        P(None, ("dp", "pair"), None),
        P(None, ("dp", "pair"), None),
        P(None, ("dp", "pair"), None),
        P(None, ("dp", "pair"), None),
        P(None, ("dp", "pair"), None),
        P(None, ("dp", "pair"), None),
        P(None, ("dp", "pair")),
        P(None, ("dp", "pair")),
        P(None, ("dp", "pair")),
        P(("dp", "pair"), None, None),
        P(("dp", "pair"), None, None),
    )
    body = local_kernel if fits_kernel(mesh) else local
    return jax.shard_map(body, mesh=mesh, in_specs=in_specs, out_specs=out_specs, check_vma=False)
```

```python
import math

import jax
import jax.numpy as jnp
from jax import lax
from jax.experimental import pallas as pl
from jax.experimental.pallas import tpu as pltpu
from jax.sharding import PartitionSpec as P

HD = 64
STEP = 5


BETA_ONE = 0.9
BETA_TWO = 0.999
ADAM_EPS = 1e-08
NORM_EPS = 1e-06
RATE_MATRIX = 0.05
RATE_SMALL = 0.3
DECAY_MATRIX = 0.01


def layer_norm(values, norm_gain, norm_shift):
    row_mean = jnp.mean(values, axis=-1, keepdims=True)
    centred = values - row_mean
    spread = jnp.mean(centred * centred, axis=-1, keepdims=True)
    return centred * lax.rsqrt(spread + NORM_EPS) * norm_gain + norm_shift


def gelu_exact(values):
    return jax.nn.gelu(values, approximate=False)


def unpack(small_vec, model_width, hidden_width):
    widths = [model_width] * 5 + [hidden_width] + [model_width] * 3
    pieces = []
    offset = 0
    for length in widths:
        pieces.append(small_vec[offset : offset + length])
        offset = offset + length
    return pieces


def masked_scores(queries, key_rows, segment):
    scores = jnp.einsum(
        "blhe,bmhe->bhlm", queries, key_rows, preferred_element_type=jnp.float32
    ) * HD ** (-0.5)
    allowed = (segment[:, :, None] == segment[:, None, :])[:, None]
    return jnp.where(allowed, scores, -1000000000.0)


def encoder_forward(tokens, segment, attn_weights, inner_weight, outer_weight, small_vec):
    batch_size, length, model_width = tokens.shape
    head_count = model_width // HD
    flat_rows = tokens.reshape(batch_size * length, model_width)
    (
        bias_query,
        bias_value,
        bias_out,
        gain_one,
        shift_one,
        bias_inner,
        bias_outer,
        gain_two,
        shift_two,
    ) = unpack(small_vec, model_width, inner_weight.shape[1])
    bias_proj = jnp.concatenate([bias_query, jnp.zeros_like(bias_query), bias_value])
    projected = (
        jnp.dot(flat_rows, attn_weights[:, : 3 * model_width], preferred_element_type=jnp.float32)
        + bias_proj
    )
    projected = projected.astype(jnp.bfloat16).reshape(batch_size, length, 3, head_count, HD)
    queries = projected[:, :, 0]
    key_rows = projected[:, :, 1]
    value_rows = projected[:, :, 2]
    scores = masked_scores(queries, key_rows, segment)
    top_score = jnp.max(scores, axis=-1, keepdims=True)
    raised = jnp.exp(scores - top_score)
    totals = jnp.sum(raised, axis=-1, keepdims=True)
    attn_probs = (raised / totals).astype(jnp.bfloat16)
    log_total = top_score + jnp.log(totals)
    mixed_heads = jnp.einsum(
        "bhlm,bmhe->blhe", attn_probs, value_rows, preferred_element_type=jnp.float32
    )
    mixed_flat = mixed_heads.astype(jnp.bfloat16).reshape(batch_size * length, model_width)
    attn_out = (
        jnp.dot(mixed_flat, attn_weights[:, 3 * model_width :], preferred_element_type=jnp.float32)
        + bias_out
    )
    residual_one = flat_rows.astype(jnp.float32) + attn_out
    normed_one = layer_norm(residual_one, gain_one, shift_one)
    pre_act = (
        jnp.dot(normed_one.astype(jnp.bfloat16), inner_weight, preferred_element_type=jnp.float32)
        + bias_inner
    )
    activated = gelu_exact(pre_act).astype(jnp.bfloat16)
    branch = jnp.dot(activated, outer_weight, preferred_element_type=jnp.float32) + bias_outer
    residual_two = normed_one + branch
    result = layer_norm(residual_two, gain_two, shift_two).reshape(batch_size, length, model_width)
    kept_values = (
        queries,
        key_rows,
        value_rows,
        log_total,
        mixed_flat,
        residual_one,
        normed_one,
        pre_act,
        activated,
        residual_two,
    )
    return (result, kept_values)


def encoder_backward(
    tokens, segment, attn_weights, inner_weight, outer_weight, small_vec, kept_values, grad_result
):
    batch_size, length, model_width = tokens.shape
    head_count = model_width // HD
    flat_rows = tokens.reshape(batch_size * length, model_width)
    (
        queries,
        key_rows,
        value_rows,
        log_total,
        mixed_flat,
        residual_one,
        normed_one,
        pre_act,
        activated,
        residual_two,
    ) = kept_values
    (
        bias_query,
        bias_value,
        bias_out,
        gain_one,
        shift_one,
        bias_inner,
        bias_outer,
        gain_two,
        shift_two,
    ) = unpack(small_vec, model_width, inner_weight.shape[1])
    grad_flat = grad_result.reshape(batch_size * length, model_width)
    unused_two, norm_two_back = jax.vjp(layer_norm, residual_two, gain_two, shift_two)
    grad_two, grad_gain_two, grad_shift_two = norm_two_back(grad_flat)
    grad_branch = grad_two.astype(jnp.bfloat16)
    grad_bias_outer = jnp.sum(grad_branch, axis=0, dtype=jnp.float32)
    grad_outer = jnp.dot(activated.T, grad_branch, preferred_element_type=jnp.float32)
    grad_act = jnp.dot(grad_branch, outer_weight.T, preferred_element_type=jnp.float32)
    unused_act, gelu_back = jax.vjp(gelu_exact, pre_act)
    grad_pre = gelu_back(grad_act)[0].astype(jnp.bfloat16)
    grad_bias_inner = jnp.sum(grad_pre, axis=0, dtype=jnp.float32)
    grad_inner = jnp.dot(
        normed_one.astype(jnp.bfloat16).T, grad_pre, preferred_element_type=jnp.float32
    )
    grad_normed = grad_two + jnp.dot(grad_pre, inner_weight.T, preferred_element_type=jnp.float32)
    unused_one, norm_one_back = jax.vjp(layer_norm, residual_one, gain_one, shift_one)
    grad_one, grad_gain_one, grad_shift_one = norm_one_back(grad_normed)
    grad_attn_out = grad_one.astype(jnp.bfloat16)
    grad_bias_out = jnp.sum(grad_attn_out, axis=0, dtype=jnp.float32)
    grad_out_proj = jnp.dot(mixed_flat.T, grad_attn_out, preferred_element_type=jnp.float32)
    grad_mixed = jnp.dot(
        grad_attn_out, attn_weights[:, 3 * model_width :].T, preferred_element_type=jnp.float32
    )
    grad_mixed = grad_mixed.astype(jnp.bfloat16).reshape(batch_size, length, head_count, HD)
    scores = masked_scores(queries, key_rows, segment)
    attn_probs = jnp.exp(scores - log_total)
    grad_probs = jnp.einsum(
        "blhe,bmhe->bhlm", grad_mixed, value_rows, preferred_element_type=jnp.float32
    )
    inner_dot = jnp.sum(attn_probs * grad_probs, axis=-1, keepdims=True)
    grad_scores = (attn_probs * (grad_probs - inner_dot)).astype(jnp.bfloat16)
    grad_values = jnp.einsum(
        "bhlm,blhe->bmhe",
        attn_probs.astype(jnp.bfloat16),
        grad_mixed,
        preferred_element_type=jnp.float32,
    )
    grad_queries = jnp.einsum(
        "bhlm,bmhe->blhe", grad_scores, key_rows, preferred_element_type=jnp.float32
    ) * HD ** (-0.5)
    grad_keys = jnp.einsum(
        "bhlm,blhe->bmhe", grad_scores, queries, preferred_element_type=jnp.float32
    ) * HD ** (-0.5)
    row_total = batch_size * length
    grad_proj = jnp.concatenate(
        [
            grad_queries.reshape(row_total, model_width),
            grad_keys.reshape(row_total, model_width),
            grad_values.reshape(row_total, model_width),
        ],
        axis=1,
    ).astype(jnp.bfloat16)
    grad_bias_query = jnp.sum(grad_proj[:, :model_width], axis=0, dtype=jnp.float32)
    grad_bias_value = jnp.sum(grad_proj[:, 2 * model_width :], axis=0, dtype=jnp.float32)
    grad_proj_weight = jnp.dot(flat_rows.T, grad_proj, preferred_element_type=jnp.float32)
    grad_tokens = grad_one + jnp.dot(
        grad_proj, attn_weights[:, : 3 * model_width].T, preferred_element_type=jnp.float32
    )
    grad_attn = jnp.concatenate([grad_proj_weight, grad_out_proj], axis=1)
    grad_small = jnp.concatenate(
        [
            grad_bias_query,
            grad_bias_value,
            grad_bias_out,
            grad_gain_one,
            grad_shift_one,
            grad_bias_inner,
            grad_bias_outer,
            grad_gain_two,
            grad_shift_two,
        ]
    )
    return (
        grad_tokens.reshape(batch_size, length, model_width),
        grad_attn,
        grad_inner,
        grad_outer,
        grad_small,
    )


def rows_term(stacked, count):
    return jnp.moveaxis(stacked, 0, 1).reshape(count, -1)


def unfold_rows(summed, encoders):
    owned = summed.shape[0]
    return jnp.moveaxis(summed.reshape(owned, encoders, -1), 1, 0)


def adam_update(weight, first_moment, second, gradient, step_rate, decay_rate):
    first_new = BETA_ONE * first_moment + (1.0 - BETA_ONE) * gradient
    second_new = BETA_TWO * second + (1.0 - BETA_TWO) * gradient * gradient
    fix_one = 1.0 - BETA_ONE**STEP
    fix_two = 1.0 - BETA_TWO**STEP
    update = first_new / fix_one / (jnp.sqrt(second_new / fix_two) + ADAM_EPS)
    return (first_new, second_new, weight - step_rate * (update + decay_rate * weight))


def local(
    question_tokens,
    passage_tokens,
    passage_lengths,
    positives,
    attn_weight,
    attn_first,
    attn_second,
    ffn_in_weight,
    ffn_in_first,
    ffn_in_second,
    ffn_out_weight,
    ffn_out_first,
    ffn_out_second,
    small_params,
    small_first,
    small_second,
):
    gathered = (
        lax.all_gather(attn_weight.astype(jnp.bfloat16), ("dp", "pair"), axis=1, tiled=True),
        lax.all_gather(ffn_in_weight.astype(jnp.bfloat16), ("dp", "pair"), axis=1, tiled=True),
        lax.all_gather(ffn_out_weight.astype(jnp.bfloat16), ("dp", "pair"), axis=1, tiled=True),
        lax.all_gather(small_params.astype(jnp.bfloat16), ("dp", "pair"), axis=1, tiled=True),
    )
    attn_all, inner_all, outer_all, small_low = gathered
    small_all = small_low.astype(jnp.float32)
    question_count, question_len, model_width = question_tokens.shape
    row_count, row_len, unused_width = passage_tokens.shape
    attn_cols = attn_weight.shape[2]
    front_rows = attn_weight.shape[1]
    back_rows = ffn_out_weight.shape[1]
    seg_ends = jnp.cumsum(passage_lengths, axis=1)
    seg_starts = seg_ends - passage_lengths
    positions = jnp.arange(row_len, dtype=jnp.int32)
    passage_seg = jnp.sum(
        (positions[None, :, None] >= seg_ends[:, None, :]).astype(jnp.int32), axis=2
    )
    question_seg = jnp.zeros((question_count, question_len), jnp.int32)
    question_out, question_kept = encoder_forward(
        question_tokens, question_seg, attn_all[0], inner_all[0], outer_all[0], small_all[0]
    )
    passage_out, passage_kept = encoder_forward(
        passage_tokens, passage_seg, attn_all[1], inner_all[1], outer_all[1], small_all[1]
    )
    question_cls = question_out[:, 0].astype(jnp.bfloat16)
    passage_cls = (
        jnp.take_along_axis(passage_out, seg_starts[:, :, None], axis=1)
        .reshape(-1, model_width)
        .astype(jnp.bfloat16)
    )
    every_cls = lax.all_gather(passage_cls, ("dp", "pair"), axis=0, tiled=True)
    score_scale = model_width ** (-0.5)
    scores = jnp.dot(question_cls, every_cls.T, preferred_element_type=jnp.float32) * score_scale
    top_score = jnp.max(scores, axis=1, keepdims=True)
    raised = jnp.exp(scores - top_score)
    soft_scores = raised / jnp.sum(raised, axis=1, keepdims=True)
    columns = jnp.arange(every_cls.shape[0], dtype=jnp.int32)
    target = (columns[None, :] == positives[:, None]).astype(jnp.float32)
    grad_scores = (soft_scores - target).astype(jnp.bfloat16)
    grad_qcls = jnp.dot(grad_scores, every_cls, preferred_element_type=jnp.float32) * score_scale
    grad_pcls = lax.psum_scatter(
        jnp.dot(grad_scores.T, question_cls, preferred_element_type=jnp.float32) * score_scale,
        ("dp", "pair"),
        scatter_dimension=0,
        tiled=True,
    )
    grad_question_out = jnp.zeros_like(question_out).at[:, 0].set(grad_qcls)
    row_index = jnp.arange(row_count, dtype=jnp.int32)[:, None]
    grad_passage_out = (
        jnp.zeros_like(passage_out)
        .at[row_index, seg_starts]
        .set(grad_pcls.reshape(row_count, -1, model_width))
    )
    question_grad, q_attn, q_inner, q_outer, q_small = encoder_backward(
        question_tokens,
        question_seg,
        attn_all[0],
        inner_all[0],
        outer_all[0],
        small_all[0],
        question_kept,
        grad_question_out,
    )
    passage_grad, p_attn, p_inner, p_outer, p_small = encoder_backward(
        passage_tokens,
        passage_seg,
        attn_all[1],
        inner_all[1],
        outer_all[1],
        small_all[1],
        passage_kept,
        grad_passage_out,
    )
    front_stack = jnp.stack(
        [jnp.concatenate([q_attn, q_inner], axis=1), jnp.concatenate([p_attn, p_inner], axis=1)]
    )
    front_owned = lax.psum_scatter(
        rows_term(front_stack, front_rows * lax.axis_size(("dp", "pair"))),
        ("dp", "pair"),
        scatter_dimension=0,
        tiled=True,
    )
    back_owned = lax.psum_scatter(
        rows_term(jnp.stack([q_outer, p_outer]), back_rows * lax.axis_size(("dp", "pair"))),
        ("dp", "pair"),
        scatter_dimension=0,
        tiled=True,
    )
    small_sum = lax.psum_scatter(
        jnp.stack([q_small, p_small]), ("dp", "pair"), scatter_dimension=1, tiled=True
    )
    front_sum = unfold_rows(front_owned, 2)
    back_sum = unfold_rows(back_owned, 2)
    attn_sum = front_sum[:, :, :attn_cols]
    inner_sum = front_sum[:, :, attn_cols:]
    attn_m, attn_v, attn_w = adam_update(
        attn_weight, attn_first, attn_second, attn_sum, RATE_MATRIX, DECAY_MATRIX
    )
    inner_m, inner_v, inner_w = adam_update(
        ffn_in_weight, ffn_in_first, ffn_in_second, inner_sum, RATE_MATRIX, DECAY_MATRIX
    )
    outer_m, outer_v, outer_w = adam_update(
        ffn_out_weight, ffn_out_first, ffn_out_second, back_sum, RATE_MATRIX, DECAY_MATRIX
    )
    small_m, small_v, small_w = adam_update(
        small_params, small_first, small_second, small_sum, RATE_SMALL, 0.0
    )
    return (
        attn_m,
        attn_v,
        attn_w,
        inner_m,
        inner_v,
        inner_w,
        outer_m,
        outer_v,
        outer_w,
        small_m,
        small_v,
        small_w,
        question_grad,
        passage_grad,
    )


MESH_ID = pl.DeviceIdType.MESH
LOW = jnp.bfloat16
F32 = jnp.float32


def dot_nn(a, b):
    return jnp.dot(a, b, preferred_element_type=F32)


def dot_nt(a, b):
    return lax.dot_general(a, b, (((1,), (1,)), ((), ())), preferred_element_type=F32)


def dot_tn(a, b):
    return lax.dot_general(a, b, (((0,), (0,)), ((), ())), preferred_element_type=F32)


def expand_heads(rows):
    head_of = lax.broadcasted_iota(jnp.int32, rows.shape, 1) // HD
    heads = rows.shape[1] // HD
    return jnp.concatenate(
        [jnp.where(head_of == h, rows, jnp.zeros_like(rows)) for h in range(heads)], axis=0
    )


def pick_heads(stacked):
    width = stacked.shape[1]
    heads = width // HD
    head_of = lax.broadcasted_iota(jnp.int32, (16, width), 1) // HD
    total = jnp.zeros((16, width), F32)
    for h in range(heads):
        total = total + jnp.where(head_of == h, stacked[16 * h : 16 * h + 16], 0.0)
    return total


def split_low(values):
    high = values.astype(LOW)
    return high, (values - high.astype(F32)).astype(LOW)


def gelu_parts(values):
    cdf = 0.5 * (1.0 + lax.erf(values * (0.5**0.5)))
    density = jnp.exp(-0.5 * values * values) * (0.5 / math.pi) ** 0.5
    return values * cdf, cdf + values * density


def step_kernel(
    qt_ref, pt_ref, attn_ref, ffi_ref, ffo_ref, small_ref, len_ref, pos_ref,
    ga_ref, gi_ref, go_ref, gs_ref, dxq_ref, dxp_ref,
    X, slabA, slabI, slabO, smw, sm2, smb, bndo, bndb, R, WN, sn, sno, ST, Pf, Pb, DSb, Emat, b1p,
    w1s_, w1r, W1, W2, Yb, P2s, P2a, P2b, P2c, XH, Dout, dZb, Gb, Act, P3s, P3a, P3b, P3c, Qb, dAb, dUb, dQb,
    m1s, m1r, m2s, m2r, dws, dwr, GP, GS, GSw, GA, GI, GO, DX, qsb, vtb, ybf,
    loc, sib_s, sib_r, at_s, at_r, ag_s, ag_z, ag_p, aa_s, aa_r, rs_s, rs_p, rs_z, out_l, out_s, out_r,
):
    dp, z = lax.axis_index("dp"), lax.axis_index("pair")
    core = lax.rem(dp, 2)
    y, x = dp // 4, lax.rem(dp // 2, 2)
    own = y * 8 + x * 4 + z
    line = y * 8 + x * 4

    def dev(slot, k):
        return ((slot // 8) * 4 + lax.rem(slot // 4, 2) * 2 + k, lax.rem(slot, 4))

    sibling = dev(own, 1 - core)
    slot_x = y * 8 + (1 - x) * 4 + z
    slot_y = (1 - y) * 8 + x * 4 + z
    slot_d = (1 - y) * 8 + (1 - x) * 4 + z

    def remote(src, dst, ssem, rsem, target):
        return pltpu.make_async_remote_copy(
            src_ref=src, dst_ref=dst, send_sem=ssem, recv_sem=rsem,
            device_id=target, device_id_type=MESH_ID,
        )

    def done(ref, sem):
        pltpu.make_async_copy(ref, ref, sem).wait()

    barrier = pltpu.get_barrier_semaphore()
    other = 1 - core
    rows = pl.ds(pl.multiple_of(512 * core, 512), 512)
    pltpu.make_async_copy(attn_ref.at[core], slabA.at[core], loc.at[0]).start()

    def greet(r, c):
        pl.semaphore_signal(
            barrier, inc=1, device_id=dev(lax.rem(own + r, 16), core), device_id_type=MESH_ID
        )
        return c

    pl.semaphore_signal(barrier, inc=1, device_id=sibling, device_id_type=MESH_ID)
    lax.fori_loop(1, 16, greet, 0)

    @pl.when(core == 0)
    def _():
        pltpu.make_async_copy(qt_ref, X.at[rows], loc.at[1]).start()

    @pl.when(core == 1)
    def _():
        pltpu.make_async_copy(pt_ref, X.at[rows], loc.at[1]).start()

    pltpu.make_async_copy(ffi_ref.at[core], slabI.at[core], loc.at[2]).start()
    pltpu.make_async_copy(ffo_ref.at[core], slabO.at[core], loc.at[3]).start()

    narrow = small_ref[...].astype(LOW).astype(F32)
    window = jnp.zeros((2, 384), F32)
    for i in range(4):
        gaps = [jnp.zeros((2, n), F32) for n in (32 * i, 96 - 32 * i) if n]
        placed = jnp.concatenate(([gaps[0]] if i else []) + [narrow] + ([gaps[-1]] if i < 3 else []), axis=1)
        window = jnp.where(z == i, placed, window)
    for k in range(2):
        smw[k] = jnp.concatenate(
            [window[k : k + 1, 128 * i : 128 * i + 128] for i in range(3)]
            + [jnp.zeros((5, 128), F32)], axis=0,
        )
    sm2[core] = smw[core]

    lengths = len_ref[...].astype(F32)
    spans = jnp.concatenate(
        [jnp.broadcast_to(lengths[i : i + 1], (4, 4)) for i in range(2)], axis=0
    )
    at_row = lax.broadcasted_iota(jnp.int32, (8, 4), 0)
    at_lane = lax.broadcasted_iota(jnp.int32, (8, 4), 1)
    upto = at_lane <= lax.rem(at_row, 4)
    here = at_lane == lax.rem(at_row, 4)
    line_of = lax.broadcasted_iota(jnp.int32, (8, 1), 0)
    base = jnp.where(line_of >= 4, 256.0, 0.0)
    passage_end = jnp.sum(jnp.where(upto, spans, 0.0), axis=1, keepdims=True) + base
    passage_start = passage_end - jnp.sum(jnp.where(here, spans, 0.0), axis=1, keepdims=True)
    question_start = line_of.astype(F32) * 64.0
    eye = lax.broadcasted_iota(jnp.int32, (8, 8), 0) == lax.broadcasted_iota(jnp.int32, (8, 8), 1)
    goal = jnp.broadcast_to(pos_ref[...].astype(F32), (8, 8))
    goal = jnp.sum(jnp.where(eye, goal, 0.0), axis=1, keepdims=True)
    of_questions = jnp.concatenate([question_start, question_start + 64.0, goal], axis=0)
    of_passages = jnp.concatenate([passage_start, passage_end, goal], axis=0)
    bndb[core] = jnp.broadcast_to(jnp.where(core == 0, of_questions, of_passages), (24, 128))
    bndo[...] = jnp.broadcast_to(jnp.where(core == 0, of_passages, of_questions), (24, 128))
    pl.semaphore_wait(barrier, 16)

    remote(smw.at[other], sm2.at[core], sib_s.at[1], sib_r.at[1], sibling).start()
    remote(attn_ref.at[other], slabA.at[core], sib_s.at[0], sib_r.at[0], sibling).start()
    remote(bndo, bndb.at[core], sib_s.at[2], sib_r.at[2], sibling).start()

    @pl.when(core == 0)
    def _():
        remote(pt_ref, X.at[rows], sib_s.at[3], sib_r.at[3], sibling).start()

    @pl.when(core == 1)
    def _():
        remote(qt_ref, X.at[rows], sib_s.at[3], sib_r.at[3], sibling).start()

    remote(ffi_ref.at[other], slabI.at[core], sib_s.at[4], sib_r.at[4], sibling).start()
    remote(ffo_ref.at[other], slabO.at[core], sib_s.at[5], sib_r.at[5], sibling).start()

    done(sm2.at[other], sib_r.at[1])
    smb[own] = jnp.concatenate([sm2[0], sm2[1]], axis=0).astype(LOW)

    exchanged = (smb, w1r, None, m1r, None, dwr, m2r)
    gathered = (Yb, Qb, XH.at[core], dUb, None, dQb)
    summed = ((P2s, P2a, P2b, P2c), (P3s, P3a, P3b, P3c))
    passed = ((slabA.at[0], slabA.at[0]), (sm2.at[0], sm2.at[0]), (bndb.at[0], bndb.at[0]),
              (X.at[rows], X.at[rows]), (slabI.at[0], slabI.at[0]), (slabO.at[0], slabO.at[0]),
              (sn, sno), (XH.at[0], XH.at[0]))
    written = [[ref] * 3 for ref in (GO.at[0], DX.at[rows], GI.at[0], GA.at[0, 0], GSw.at[0], GA.at[0, 0])]
    state = {("pass", n): int(n < 2) for n in range(6)}
    state["attn", 0] = 1

    def direct(n, src_of):
        def body(r, c):
            target = lax.rem(own + r, 16)
            remote(src_of(target), exchanged[n].at[own], aa_s.at[n], aa_r.at[n], dev(target, core)).start()
            return c

        lax.fori_loop(1, 16, body, 0)
        state["direct", n] = 0

    def direct_done(n):
        done(exchanged[n].at[pl.ds(0, 15)], aa_r.at[n])
        state["direct", n] = 1

    def pass_done(n):
        done(passed[n][1], sib_r.at[n])
        state["pass", n] = 1

    direct(0, lambda t: smb.at[own])

    def push(slot, m, target):
        remote(R.at[slot, m], R.at[slot, m], at_s.at[m], at_r.at[slot, m, 0], dev(target, core)).start()

    def near(f, nearest=1):
        for d in range(nearest, 4):
            for dz in (d, -d) if d else (0,):
                @pl.when(jnp.logical_and(z + dz >= 0, z + dz <= 3))
                def _():
                    f(dz)

    def got(slot, m):
        done(R.at[slot, m], at_r.at[slot, m, 0])

    done(slabA.at[core], loc.at[0])
    done(slabA.at[other], sib_r.at[0])
    for m in (0, 3, 1, 2):
        cols = slice(768 * m, 768 * m + 768)
        R[own, m] = jnp.concatenate([slabA[0, :, cols], slabA[1, :, cols]], axis=0).astype(LOW)
        for target in (slot_x, slot_y) if m < 3 else (slot_x, slot_y, slot_d):
            push(own, m, target)
        if m < 3:
            near(lambda dz: push(own, m, own + dz))

    def hop(d):
        for i in range(4):
            slot = 4 * i + z
            if d == 0:
                @pl.when(4 * i != line)
                def _():
                    got(slot, 3)

                @pl.when(z < 3)
                def _():
                    push(slot, 3, own + 1)

                @pl.when(z > 0)
                def _():
                    push(slot, 3, own - 1)
            else:
                @pl.when(z - d >= 0)
                def _():
                    got(slot - d, 3)

                    @pl.when(z < 3)
                    def _():
                        push(slot - d, 3, own + 1)

                @pl.when(z + d <= 3)
                def _():
                    got(slot + d, 3)

                    @pl.when(z > 0)
                    def _():
                        push(slot + d, 3, own - 1)

    def settle(last=True):
        for kind, n in list(state):
            at = state[kind, n]
            if last and kind == "gather" and at == 0:
                gather_forward(n)
            if last and kind == "gather" and at < 2:
                gather_done(n)
            if last and kind == "sum" and at == 0:
                sum_forward(n)
            if last and kind == "sum" and at < 2:
                sum_done(n)
            if last and kind == "direct" and at == 0:
                direct_done(n)
            if last and kind == "pass" and at == 0:
                pass_done(n)
            if kind == "gather" and (last or at == 2):
                done(gathered[n].at[pl.ds(0, 15)], ag_s.at[n])
            elif kind == "direct" and (last or at == 1):
                done(exchanged[n].at[pl.ds(0, 15)], aa_s.at[n])
            elif kind == "sum" and (last or at == 2):
                done(summed[n][1].at[pl.ds(0, 3)], rs_s.at[n, 0])
                done(summed[n][3].at[pl.ds(0, 3)], rs_s.at[n, 1])
            elif kind == "pass" and (last or at == 1):
                done(passed[n][0], sib_s.at[n])
            elif kind == "out" and last:
                for ref, sem in zip(written[n], (out_l, out_s, out_r)):
                    done(ref, sem.at[n])
            elif kind == "attn":
                for m in range(3):
                    done(R.at[pl.ds(0, 15), m], at_s.at[m])
                done(R.at[pl.ds(0, 7), 3], at_s.at[3])

                @pl.when(jnp.logical_and(z > 0, z < 3))
                def _():
                    done(R.at[pl.ds(0, 16), 3], at_s.at[3])
            else:
                continue
            del state[kind, n]

    def finish():
        settle()

    def relay_z(m):
        def give(dz):
            got(own + dz, m)
            for target in (slot_x, slot_y):
                push(own + dz, m, target)

        near(give)

    def relay_plane(m):
        def give(dz):
            for slot, target, half in ((slot_x + dz, slot_y, 0), (slot_y + dz, slot_x, 1)):
                got(slot, m)
                part = R.at[slot, m, :, pl.ds(384 * half, 384)]
                remote(part, part, at_s.at[m], at_r.at[slot, m, half], dev(target, core)).start()

        near(give, 0)

    def from_slots(read, write):
        def body(g, c):
            got = [read(4 * g + i) for i in range(4)]
            natural = jnp.concatenate([v[0:24] for v in got] + [v[24:48] for v in got], axis=0)
            write(pl.ds(pl.multiple_of(192 * g, 64), 192), natural.astype(LOW))
            return c

        lax.fori_loop(0, 4, body, 0)

    def to_slots(read, write):
        def body(g, c):
            v = read(pl.ds(pl.multiple_of(192 * g, 64), 192))
            for i in range(4):
                part = jnp.concatenate(
                    [v[24 * i : 24 * i + 24], v[96 + 24 * i : 96 + 24 * i + 24]], axis=0
                )
                write(4 * g + i, part)
            return c

        lax.fori_loop(0, 4, body, 0)

    def pack(v):
        tail = jnp.concatenate([v[0:24, 128:192], v[24:48, 128:192]], axis=1)
        return jnp.concatenate([v[:, 0:128], tail, jnp.zeros((8, 128), F32)], axis=0).astype(LOW)

    def unpack(packed):
        v = packed.astype(F32)
        tail = jnp.concatenate([v[48:72, 0:64], v[48:72, 64:128]], axis=0)
        return jnp.concatenate([v[0:48], tail], axis=1)

    def arrive(m):
        def body(zz, c):
            slot = (1 - y) * 8 + (1 - x) * 4 + zz
            for half in range(2):
                done(R.at[slot, m, :, pl.ds(384 * half, 384)], at_r.at[slot, m, half])
            return c

        if m < 3:
            lax.fori_loop(0, 4, body, 0)

        def write(where, v):
            WN[m, where, :] = v

        from_slots(lambda s: R[s, m].astype(F32), write)

    early_own = (0, 2)

    def gather_start(n):
        buf = gathered[n]
        state["gather", n] = 0

        def give(dz):
            remote(buf.at[own], buf.at[own], ag_s.at[n], ag_z.at[n, z], dev(own + dz, core)).start()

        near(give)
        if n in early_own:
            for target in (slot_x, slot_y, slot_d):
                remote(buf.at[own], buf.at[own], ag_s.at[n], ag_p.at[n], dev(target, core)).start()

    def gather_forward(n):
        buf = gathered[n]
        state["gather", n] = 1

        def pass_on(dz):
            block = buf.at[own + dz]
            done(block, ag_z.at[n, z + dz])
            if n in early_own:
                for target in (slot_x, slot_y, slot_d):
                    remote(block, block, ag_s.at[n], ag_p.at[n], dev(target, core)).start()

        near(pass_on)
        if n not in early_own:
            block = buf.at[pl.ds(line, 4)]
            for target in (slot_x, slot_y, slot_d):
                remote(block, block, ag_s.at[n], ag_p.at[n], dev(target, core)).start()

    def gather_done(n):
        state["gather", n] = 2
        done(gathered[n].at[pl.ds(0, 12)], ag_p.at[n])

    def sum_start(n):
        source, plane, unused, unused = summed[n]
        state["sum", n] = 0
        for target in (slot_x, slot_y, slot_d):
            remote(
                source.at[pl.ds(target - z, 4)], plane.at[line // 4],
                rs_s.at[n, 0], rs_p.at[n], dev(target, core),
            ).start()
        plane[line // 4] = source[pl.ds(line, 4)]

    def sum_forward(n):
        unused, plane, along, final = summed[n]
        state["sum", n] = 1
        done(plane.at[pl.ds(0, 3)], rs_p.at[n])
        along[...] = jnp.sum(plane[...].astype(F32), axis=0).astype(LOW)

        def give(dz):
            remote(
                along.at[z + dz], final.at[z], rs_s.at[n, 1], rs_z.at[n], dev(own + dz, core)
            ).start()

        near(give)
        final[z] = along[z]

    def sum_done(n):
        final = summed[n][3]
        state["sum", n] = 2
        done(final.at[pl.ds(0, 3)], rs_z.at[n])
        return jnp.sum(final[...].astype(F32), axis=0)

    def prepare_ffn():
        row = lax.broadcasted_iota(jnp.int32, (384, 512), 0)
        col = lax.broadcasted_iota(jnp.int32, (384, 512), 1)
        Emat[...] = jnp.where(col == 128 * (row // 96) + lax.rem(row, 96), 1.0, 0.0).astype(LOW)
        done(slabI.at[core], loc.at[2])
        pass_done(4)
        for g in range(4):
            halves = []
            for k in range(2):
                cols = slice(768 * g + 384 * k, 768 * g + 384 * k + 384)
                halves.append(jnp.concatenate([slabI[0, :, cols], slabI[1, :, cols]], axis=0))
            for i in range(4):
                lanes = slice(96 * i, 96 * i + 96)
                w1s_[4 * g + i] = pack(jnp.concatenate([half[:, lanes] for half in halves], axis=1))
        w1r[own] = w1s_[own]
        done(slabO.at[core], loc.at[3])
        pass_done(5)
        gap = jnp.zeros((64, 768), F32)
        W2[...] = jnp.concatenate([slabO[0], slabO[1], gap], axis=0).astype(LOW)

    def natural_small():
        direct_done(0)
        for g in range(8):
            parts = [
                smb[4 * (g // 2) + i].astype(F32)[8 * (g % 2) : 8 * (g % 2) + 8] for i in range(4)
            ]
            lines = [parts[0][0:1], parts[0][1:2]]
            for i in range(1, 4):
                lines += [parts[i - 1][2:3] + parts[i][0:1], parts[i][1:2]]
            lines += [parts[3][2:3]]
            sn[9 * g : 9 * g + 9, :] = jnp.concatenate(lines, axis=0)
        remote(sn, sno, sib_s.at[6], sib_r.at[6], sibling).start()
        state["pass", 6] = 0

    def vec(row, count=6, ref=sn):
        return jnp.concatenate([ref[row + i : row + i + 1, :] for i in range(count)], axis=1)

    relay_z(0)
    hop(0)
    pass_done(2)
    done(X.at[pl.ds(0, 512)], loc.at[1])
    pass_done(3)
    starts = jnp.concatenate([bndb[0, 0:8], bndb[1, 0:8] + 512.0], axis=0)[:, 0:1]
    ends = jnp.concatenate([bndb[0, 8:16], bndb[1, 8:16] + 512.0], axis=0)[:, 0:1]
    token = lax.broadcasted_iota(jnp.int32, (16, 1024), 1).astype(F32)
    inside = jnp.logical_and(token >= starts, token < ends)
    first = jnp.where(token == starts, 1.0, 0.0).astype(LOW)
    cls_in = dot_nn(first, X[...])
    cls_low = cls_in.astype(LOW)
    relay_z(1)
    relay_plane(0)
    natural_small()
    prepare_ffn()
    hop(1)
    relay_z(2)
    relay_plane(1)
    arrive(0)
    queries = (dot_nn(cls_low, WN[0]) + vec(0)).astype(LOW)
    Qb[own] = queries
    gather_start(1)
    hop(2)
    relay_plane(2)
    arrive(1)
    qsb[...] = (dot_nt(expand_heads(queries), WN[1]) * (HD**-0.5)).astype(LOW)
    ST[...] = dot_nt(qsb[...], X[...])

    def soften(h, c):
        at = pl.ds(pl.multiple_of(16 * h, 16), 16)
        s = jnp.where(inside, ST[at, :], -1000000000.0)
        e = jnp.exp(s - jnp.max(s, axis=1, keepdims=True))
        p = e / jnp.sum(e, axis=1, keepdims=True)
        Pf[at, :] = p
        Pb[at, :] = p.astype(LOW)
        return c

    lax.fori_loop(0, 12, soften, 0, unroll=4)
    ybf[...] = dot_nn(Pb[...], X[...]).astype(LOW)
    arrive(2)
    mixed = (pick_heads(dot_nn(ybf[...], WN[2])) + vec(6)).astype(LOW)
    hop(3)
    arrive(3)
    lifted = cls_in + dot_nn(mixed, WN[3]) + vec(12)
    centred = lifted - jnp.mean(lifted, axis=1, keepdims=True)
    rstd_one = lax.rsqrt(jnp.mean(centred * centred, axis=1, keepdims=True) + NORM_EPS)
    hat_one = centred * rstd_one
    normed = hat_one * vec(18) + vec(24)
    Yb[own] = normed.astype(LOW)
    gather_start(0)
    direct(1, lambda t: w1s_.at[t])

    early = jnp.concatenate(
        [ybf[...].astype(F32), cls_in, mixed.astype(F32), jnp.zeros((32, 768), F32)], axis=0
    )
    DX[0:768, 0:256] = early.T

    def write_m1(slot, v):
        m1s[slot] = v.astype(LOW)

    to_slots(lambda w: DX[w, 0:256], write_m1)
    m1r[own] = m1s[own]
    gather_forward(0)

    b1 = jnp.concatenate([vec(30 + 3 * g, 3) for g in range(8)], axis=0).astype(LOW)
    b1_wide = dot_nn(b1, Emat[...])
    for g in range(8):
        b1p[g] = jnp.broadcast_to(b1_wide[g : g + 1], (8, 512))
    group = pl.multiple_of(128 * z, 128)
    gy = 4 * y + 2 * x
    b1_row = jnp.concatenate(
        [
            b1p[gy, 0:1, pl.ds(group, 128)][:, 0:96], b1p[gy + 1, 0:1, pl.ds(group, 128)][:, 0:96],
            jnp.zeros((1, 64), F32),
        ], axis=1,
    )
    direct_done(1)

    def write_w1(where, v):
        W1[where, :] = v

    pad = jnp.zeros((48, 64), F32)
    from_slots(lambda s: jnp.concatenate([unpack(w1r[s]), pad], axis=1), write_w1)
    gather_done(0)
    all_y = Yb[...].reshape(256, 768)
    act = dot_nn(all_y, W1[...]) + b1_row
    Act[...] = act
    hidden, unused = gelu_parts(act)
    Gb[...] = hidden.astype(LOW)
    P2s[...] = dot_nn(Gb[...], W2[...]).astype(LOW).reshape(16, 16, 768)
    sum_start(0)
    direct(3, lambda t: m1s.at[t])
    sum_forward(0)
    hidden_sum = sum_done(0)
    second = normed + hidden_sum + vec(54)
    centred = second - jnp.mean(second, axis=1, keepdims=True)
    rstd_two = lax.rsqrt(jnp.mean(centred * centred, axis=1, keepdims=True) + NORM_EPS)
    hat_two = centred * rstd_two
    rstd_high, rstd_low = split_low(rstd_two)
    lane = lax.broadcasted_iota(jnp.int32, (16, 128), 1)
    positive = jnp.concatenate([bndb[0, 16:24], bndb[1, 16:24]], axis=0)
    extra = jnp.where(
        lane == 0, rstd_high.astype(F32),
        jnp.where(lane == 1, rstd_low.astype(F32), jnp.where(lane == 2, positive, 0.0)),
    )
    XH[core, own] = jnp.concatenate([hat_two, extra], axis=1).astype(LOW)
    gather_start(2)
    gather_forward(2)
    gather_forward(1)
    gather_done(2)
    remote(XH.at[core], XH.at[core], sib_s.at[7], sib_r.at[7], sibling).start()
    state["pass", 7] = 0
    pass_done(6)
    pass_done(7)

    def vec_of(encoder, row):
        return jnp.where(core == encoder, vec(row), vec(row, 6, sno))

    xq = XH[0].reshape(256, 896).astype(F32)
    xp = XH[1].reshape(256, 896).astype(F32)
    qc = (xq[:, 0:768] * vec_of(0, 60) + vec_of(0, 66)).astype(LOW)
    pc = (xp[:, 0:768] * vec_of(1, 60) + vec_of(1, 66)).astype(LOW)
    scale = 768 ** (-0.5)
    scores = dot_nt(qc, pc) * scale
    raised = jnp.exp(scores - jnp.max(scores, axis=1, keepdims=True))
    soft = raised / jnp.sum(raised, axis=1, keepdims=True)
    place = lax.broadcasted_iota(jnp.int32, (256, 256), 1)
    slot_of = place // 16
    owner_of = (
        16 * (slot_of // 8) + 8 * lax.rem(slot_of // 4, 2)
        + 4 * (lax.rem(place, 16) // 8) + lax.rem(slot_of, 4)
    )
    passage = (8 * owner_of + lax.rem(place, 8)).astype(F32)
    target = jnp.where(passage == xq[:, 770:771], 1.0, 0.0)
    grad_scores = (soft - target).astype(LOW)

    @pl.when(core == 0)
    def _():
        Dout[...] = dot_nn(grad_scores, pc) * scale

    @pl.when(core == 1)
    def _():
        Dout[...] = dot_tn(grad_scores, qc) * scale

    dout = Dout[...]
    block = XH[core].reshape(256, 896).astype(F32)
    hat = block[:, 0:768]
    rstd = block[:, 768:769] + block[:, 769:770]
    inner = dout * vec(60)
    grad_two = rstd * (
        inner - jnp.mean(inner, axis=1, keepdims=True)
        - hat * jnp.mean(inner * hat, axis=1, keepdims=True)
    )
    dg2 = jnp.sum(dout * hat, axis=0, keepdims=True)
    ds2 = jnp.sum(dout, axis=0, keepdims=True)
    Dout[...] = grad_two
    dZb[...] = grad_two.astype(LOW)
    db2 = jnp.sum(dZb[...].astype(F32), axis=0, keepdims=True)
    unused, slope = gelu_parts(Act[...])
    da = (dot_nt(dZb[...], W2[...]) * slope).astype(LOW)
    P3s[...] = dot_nt(da, W1[...]).astype(LOW).reshape(16, 16, 768)
    sum_start(1)
    DX[0:768, 0:256] = dot_tn(all_y, da)

    def write_dw(slot, v):
        dws[slot] = pack(v)

    to_slots(lambda w: DX[w, 0:256], write_dw)
    direct(5, lambda t: dws.at[t])
    sum_forward(1)
    dwr[own] = dws[own]
    db1 = jnp.sum(da.astype(F32), axis=0, keepdims=True)
    dw2 = dot_tn(Gb[...], dZb[...])
    GO[0] = dw2[0:96]
    GO[1] = dw2[96:192]
    pltpu.make_async_copy(GO.at[core], go_ref.at[core], out_l.at[0]).start()
    remote(GO.at[other], go_ref.at[core], out_s.at[0], out_r.at[0], sibling).start()
    state["out", 0] = 0
    own_rows = pl.ds(pl.multiple_of(16 * own, 16), 16)
    normed_sum = sum_done(1)

    grad_normed = Dout[own_rows, :] + normed_sum
    inner = grad_normed * vec(18)
    grad_one = rstd_one * (
        inner - jnp.mean(inner, axis=1, keepdims=True)
        - hat_one * jnp.mean(inner * hat_one, axis=1, keepdims=True)
    )
    grad_lift = grad_one.astype(LOW)
    grad_mixed = dot_nt(grad_lift, WN[3]).astype(LOW)
    dg1 = jnp.sum(grad_normed * hat_one, axis=0, keepdims=True)
    ds1 = jnp.sum(grad_normed, axis=0, keepdims=True)
    partial_sums = jnp.concatenate(
        [dg1[:, 128 * i : 128 * i + 128] for i in range(6)]
        + [ds1[:, 128 * i : 128 * i + 128] for i in range(6)]
        + [db1[:, 0:128], db1[:, 128:256], jnp.zeros((2, 128), F32)], axis=0,
    )
    dUb[own] = jnp.concatenate([grad_one, partial_sums], axis=1).astype(LOW)
    gather_start(3)
    spread = expand_heads(grad_mixed)
    vtb[...] = dot_nt(spread, WN[2]).astype(LOW)
    constant = jnp.sum(spread.astype(F32) * vec(6), axis=1, keepdims=True)
    ST[...] = dot_nt(vtb[...], X[...]) + constant

    def harden(h, c):
        at = pl.ds(pl.multiple_of(16 * h, 16), 16)
        p, dprob = Pf[at, :], ST[at, :]
        total = jnp.sum(p * dprob, axis=1, keepdims=True)
        DSb[at, :] = (p * (dprob - total)).astype(LOW)
        return c

    lax.fori_loop(0, 12, harden, 0, unroll=4)
    late = (dot_nn(DSb[...], X[...]) * (HD**-0.5)).astype(LOW)
    grad_query = pick_heads(dot_nn(late, WN[1])).astype(LOW)
    dQb[own] = grad_query
    gather_start(5)
    DX[0:768, 0:256] = jnp.concatenate(
        [late.astype(F32), jnp.zeros((64, 768), F32)], axis=0
    ).T

    def write_m2(slot, v):
        m2s[slot] = pack(v)

    to_slots(lambda w: DX[w, 0:256], write_m2)
    direct(6, lambda t: m2s.at[t])
    m2r[own] = m2s[own]
    gather_forward(3)

    grad_cls = grad_one + dot_nt(grad_query, WN[0])
    cls_high, cls_rest = split_low(grad_cls)
    right = jnp.concatenate([qsb[...], vtb[...], cls_high, cls_rest], axis=0)
    for k in range(2):
        part = slice(512 * k, 512 * k + 512)
        left = jnp.concatenate([DSb[:, part], Pb[:, part], first[:, part], first[:, part]], axis=0)
        DX[part, :] = dot_tn(left, right)
    gather_forward(5)
    other_rows = pl.ds(pl.multiple_of(512 * other, 512), 512)

    @pl.when(core == 0)
    def _():
        pltpu.make_async_copy(DX.at[rows], dxq_ref, out_l.at[1]).start()
        remote(DX.at[other_rows], dxq_ref, out_s.at[1], out_r.at[1], sibling).start()

    @pl.when(core == 1)
    def _():
        pltpu.make_async_copy(DX.at[rows], dxp_ref, out_l.at[1]).start()
        remote(DX.at[other_rows], dxp_ref, out_s.at[1], out_r.at[1], sibling).start()

    state["out", 1] = 0

    direct_done(5)
    for g in range(4):
        parts = [unpack(dwr[4 * g + i]) for i in range(4)]
        for k in range(2):
            block = jnp.concatenate([v[:, 96 * k : 96 * k + 96] for v in parts], axis=1)
            cols = slice(768 * g + 384 * k, 768 * g + 384 * k + 384)
            GI[0, :, cols] = block[0:24]
            GI[1, :, cols] = block[24:48]
    pltpu.make_async_copy(GI.at[core], gi_ref.at[core], out_l.at[2]).start()
    remote(GI.at[other], gi_ref.at[core], out_s.at[2], out_r.at[2], sibling).start()
    state["out", 2] = 0

    def put(m, v):
        GA[m // 2, 0, :, 768 * (m % 2) : 768 * (m % 2) + 768] = v[0:24]
        GA[m // 2, 1, :, 768 * (m % 2) : 768 * (m % 2) + 768] = v[24:48]

    def hand_out(half, n):
        part = ga_ref.at[core, :, pl.ds(1536 * half, 1536)]
        pltpu.make_async_copy(GA.at[half, core], part, out_l.at[n]).start()
        remote(GA.at[half, other], part, out_s.at[n], out_r.at[n], sibling).start()
        state["out", n] = 0

    def factor_sum(read, columns):
        def body(s, total):
            return total + dot_nn(read(s), expand_heads(columns[s]))

        return lax.fori_loop(0, 16, body, jnp.zeros((48, 768), F32), unroll=4)

    def columns_of(at):
        return jnp.concatenate(
            [m1r[s, :, at : at + 16].astype(F32) for s in range(16)], axis=1
        ).astype(LOW)

    gather_done(3)
    all_du = dUb[...].reshape(256, 896)[:, 0:768]
    all_da = dot_nt(all_du, WN[3]).astype(LOW)
    dAb[...] = all_da.reshape(16, 16, 768)
    direct_done(3)
    put(2, factor_sum(lambda s: m1r[s, :, 0:192], dAb))
    put(3, dot_nn(columns_of(208), all_du))
    hand_out(1, 5)
    cls_columns = columns_of(192)

    parts = [dUb[i, :, 768:896].astype(F32) for i in range(16)]
    sums = parts[0]
    for part in parts[1:]:
        sums = sums + part
    wide = [jnp.concatenate([part[12:13], part[13:14]], axis=1) for part in parts]
    narrow = jnp.concatenate(
        [
            jnp.concatenate(
                [wide[4 * (g // 2) + i][:, 96 * (g % 2) : 96 * (g % 2) + 96] for i in range(4)], axis=1
            )
            for g in range(8)
        ], axis=0,
    )

    def six(v):
        return [v[:, 128 * i : 128 * i + 128] for i in range(6)]

    lines = six(jnp.sum(all_da.astype(F32), axis=0, keepdims=True))
    lines += six(jnp.sum(all_du.astype(F32), axis=0, keepdims=True))
    lines += [sums[0:12]]
    for g in range(8):
        lines += [narrow[g : g + 1, 128 * i : 128 * i + 128] for i in range(3)]
    lines += six(db2) + six(dg2) + six(ds2) + [jnp.zeros((8, 128), F32)]
    GP[6:80] = jnp.concatenate(lines, axis=0)
    for g in range(8):
        for i in range(4):
            at = 9 * g + 9 * i // 4
            if at > 5:
                GS[g, i] = GP[at : at + 8]
    gather_done(1)
    settle(False)
    direct_done(6)
    put(1, factor_sum(lambda s: unpack(m2r[s]).astype(LOW), Qb))
    gather_done(5)
    all_dq = dQb[...].reshape(256, 768)
    put(0, dot_nn(cls_columns, all_dq))
    hand_out(0, 3)
    GP[0:6] = jnp.concatenate(six(jnp.sum(all_dq.astype(F32), axis=0, keepdims=True)), axis=0)
    for i in range(3):
        GS[0, i] = GP[9 * i // 4 : 9 * i // 4 + 8]
    for k in range(2):
        GSw[k] = GS[gy + k, z]
    pltpu.make_async_copy(GSw.at[core], gs_ref.at[core], out_l.at[4]).start()
    remote(GSw.at[other], gs_ref.at[core], out_s.at[4], out_r.at[4], sibling).start()
    state["out", 4] = 0
    finish()


def kernel_call(qt, pt, attn, ffi, ffo, small, lengths, positives):
    any_space = pl.BlockSpec(memory_space=pl.ANY)
    vmem = pl.BlockSpec(memory_space=pltpu.VMEM)
    V = pltpu.VMEM
    dma = pltpu.SemaphoreType.DMA
    scratch = [
        V((1024, 768), LOW), V((2, 24, 3072), F32), V((2, 24, 3072), F32), V((2, 96, 768), F32),
        V((2, 8, 128), F32), V((2, 8, 128), F32), V((16, 16, 128), LOW),
        V((24, 128), F32), V((2, 24, 128), F32), V((16, 4, 48, 768), LOW),
        V((4, 768, 768), LOW), V((72, 128), F32), V((72, 128), F32), V((192, 1024), F32),
        V((192, 1024), F32), V((192, 1024), LOW), V((192, 1024), LOW), V((384, 512), LOW),
        V((8, 8, 512), F32),
        V((16, 80, 128), LOW), V((16, 80, 128), LOW), V((768, 256), LOW), V((256, 768), LOW),
        V((16, 16, 768), LOW), V((16, 16, 768), LOW), V((4, 4, 16, 768), LOW),
        V((4, 16, 768), LOW), V((4, 16, 768), LOW),
        V((2, 16, 16, 896), LOW), V((256, 768), F32), V((256, 768), LOW), V((256, 256), LOW),
        V((256, 256), F32), V((16, 16, 768), LOW), V((4, 4, 16, 768), LOW),
        V((4, 16, 768), LOW), V((4, 16, 768), LOW), V((16, 16, 768), LOW),
        V((16, 16, 768), LOW), V((16, 16, 896), LOW), V((16, 16, 768), LOW),
        V((16, 48, 256), LOW), V((16, 48, 256), LOW), V((16, 80, 128), LOW), V((16, 80, 128), LOW),
        V((16, 80, 128), LOW), V((16, 80, 128), LOW),
        V((80, 128), F32), V((8, 4, 8, 128), F32), V((2, 8, 128), F32), V((2, 2, 24, 1536), F32), V((2, 24, 3072), F32),
        V((2, 96, 768), F32), V((1024, 768), F32), V((192, 768), LOW), V((192, 768), LOW),
        V((192, 768), LOW),
        dma((4,)), dma((8,)), dma((8,)), dma((4,)), dma((16, 4, 2)), dma((7,)), dma((7, 4)),
        dma((7,)), dma((7,)), dma((7,)), dma((2, 2)), dma((2,)), dma((2,)),
        dma((6,)), dma((6,)), dma((6,)),
    ]
    shapes = (
        (2, 24, 3072), (2, 24, 3072), (2, 96, 768), (2, 8, 128), (512, 768), (512, 768)
    )
    return pl.pallas_call(
        step_kernel,
        out_shape=[jax.ShapeDtypeStruct(s, F32) for s in shapes],
        in_specs=[any_space] * 5 + [vmem] * 3,
        out_specs=[any_space] * 6,
        scratch_shapes=scratch,
        compiler_params=pltpu.CompilerParams(
            collective_id=0, has_side_effects=True, vmem_limit_bytes=56 << 20
        ),
    )(qt, pt, attn, ffi, ffo, small, lengths, positives)


def update_kernel(*refs):
    ins, outs = refs[:18], refs[18:]
    for n in range(3):
        weight, first, second, grad = (r[...] for r in ins[4 * n : 4 * n + 4])
        new = adam_update(weight, first, second, grad, RATE_MATRIX, DECAY_MATRIX)
        for ref, value in zip(outs[3 * n : 3 * n + 3], new):
            ref[...] = value

    @pl.when(pl.program_id(0) == 0)
    def _():
        z = lax.axis_index("pair")
        weight, first, second, window = ins[12:16]
        lines = []
        for e in range(2):
            row = jnp.concatenate([window[e, i : i + 1, :] for i in range(3)], axis=1)
            picked = row[:, 0:288]
            for i in range(1, 4):
                picked = jnp.where(z == i, row[:, 32 * i : 32 * i + 288], picked)
            lines.append(picked)
        grad = jnp.concatenate(lines, axis=0)
        new = adam_update(weight[...], first[...], second[...], grad, RATE_SMALL, 0.0)
        for ref, value in zip(outs[9:12], new):
            ref[...] = value

    outs[12][...] = ins[16][...]
    outs[13][...] = ins[17][...]


def update_call(attn, inner, outer, small, grad_question, grad_passage):
    wide = pl.BlockSpec((1, 24, 3072), lambda i: (i, 0, 0))
    tall = pl.BlockSpec((1, 96, 768), lambda i: (i, 0, 0))
    vector = pl.BlockSpec((2, 288), lambda i: (0, 0))
    window = pl.BlockSpec((2, 8, 128), lambda i: (0, 0, 0))
    token = pl.BlockSpec((256, 768), lambda i: (i, 0))

    def like(a):
        return jax.ShapeDtypeStruct(a.shape, F32)

    return pl.pallas_call(
        update_kernel,
        grid=(2,),
        out_shape=[like(g[0]) for g in (attn, inner, outer, small) for _ in range(3)]
        + [like(grad_question), like(grad_passage)],
        in_specs=[wide] * 8 + [tall] * 4 + [vector] * 3 + [window, token, token],
        out_specs=[wide] * 6 + [tall] * 3 + [vector] * 3 + [token, token],
    )(*attn, *inner, *outer, *small, grad_question, grad_passage)


def local_kernel(
    question_tokens, passage_tokens, passage_lengths, positives,
    attn_weight, attn_first, attn_second, ffn_in_weight, ffn_in_first, ffn_in_second,
    ffn_out_weight, ffn_out_first, ffn_out_second, small_params, small_first, small_second,
):
    grads = kernel_call(
        question_tokens.reshape(512, 768), passage_tokens.reshape(512, 768),
        attn_weight, ffn_in_weight, ffn_out_weight, small_params,
        passage_lengths, positives.reshape(1, 8),
    )
    attn_sum, inner_sum, outer_sum, small_window, grad_question, grad_passage = grads
    results = update_call(
        (attn_weight, attn_first, attn_second, attn_sum),
        (ffn_in_weight, ffn_in_first, ffn_in_second, inner_sum),
        (ffn_out_weight, ffn_out_first, ffn_out_second, outer_sum),
        (small_params, small_first, small_second, small_window),
        grad_question, grad_passage,
    )
    return (
        *results[:12],
        results[12].reshape(question_tokens.shape),
        results[13].reshape(passage_tokens.shape),
    )


def fits_kernel(mesh):
    return mesh.shape["dp"] == 8 and mesh.shape["pair"] == 4


def solution(mesh):
    in_specs = (
        P(("dp", "pair"), None, None),
        P(("dp", "pair"), None, None),
        P(("dp", "pair"), None),
        P(("dp", "pair")),
        P(None, ("dp", "pair"), None),
        P(None, ("dp", "pair"), None),
        P(None, ("dp", "pair"), None),
        P(None, ("dp", "pair"), None),
        P(None, ("dp", "pair"), None),
        P(None, ("dp", "pair"), None),
        P(None, ("dp", "pair"), None),
        P(None, ("dp", "pair"), None),
        P(None, ("dp", "pair"), None),
        P(None, ("dp", "pair")),
        P(None, ("dp", "pair")),
        P(None, ("dp", "pair")),
    )
    out_specs = (
        P(None, ("dp", "pair"), None),
        P(None, ("dp", "pair"), None),
        P(None, ("dp", "pair"), None),
        P(None, ("dp", "pair"), None),
        P(None, ("dp", "pair"), None),
        P(None, ("dp", "pair"), None),
        P(None, ("dp", "pair"), None),
        P(None, ("dp", "pair"), None),
        P(None, ("dp", "pair"), None),
        P(None, ("dp", "pair")),
        P(None, ("dp", "pair")),
        P(None, ("dp", "pair")),
        P(("dp", "pair"), None, None),
        P(("dp", "pair"), None, None),
    )
    body = local_kernel if fits_kernel(mesh) else local
    return jax.shard_map(body, mesh=mesh, in_specs=in_specs, out_specs=out_specs, check_vma=False)
```

```python
import math

import jax
import jax.numpy as jnp
from jax import lax
from jax.experimental import pallas as pl
from jax.experimental.pallas import tpu as pltpu
from jax.sharding import PartitionSpec as P

HD = 64
STEP = 5


BETA_ONE = 0.9
BETA_TWO = 0.999
ADAM_EPS = 1e-08
NORM_EPS = 1e-06
RATE_MATRIX = 0.05
RATE_SMALL = 0.3
DECAY_MATRIX = 0.01


def layer_norm(values, norm_gain, norm_shift):
    row_mean = jnp.mean(values, axis=-1, keepdims=True)
    centred = values - row_mean
    spread = jnp.mean(centred * centred, axis=-1, keepdims=True)
    return centred * lax.rsqrt(spread + NORM_EPS) * norm_gain + norm_shift


def gelu_exact(values):
    return jax.nn.gelu(values, approximate=False)


def unpack(small_vec, model_width, hidden_width):
    widths = [model_width] * 5 + [hidden_width] + [model_width] * 3
    pieces = []
    offset = 0
    for length in widths:
        pieces.append(small_vec[offset : offset + length])
        offset = offset + length
    return pieces


def masked_scores(queries, key_rows, segment):
    scores = jnp.einsum(
        "blhe,bmhe->bhlm", queries, key_rows, preferred_element_type=jnp.float32
    ) * HD ** (-0.5)
    allowed = (segment[:, :, None] == segment[:, None, :])[:, None]
    return jnp.where(allowed, scores, -1000000000.0)


def encoder_forward(tokens, segment, attn_weights, inner_weight, outer_weight, small_vec):
    batch_size, length, model_width = tokens.shape
    head_count = model_width // HD
    flat_rows = tokens.reshape(batch_size * length, model_width)
    (
        bias_query,
        bias_value,
        bias_out,
        gain_one,
        shift_one,
        bias_inner,
        bias_outer,
        gain_two,
        shift_two,
    ) = unpack(small_vec, model_width, inner_weight.shape[1])
    bias_proj = jnp.concatenate([bias_query, jnp.zeros_like(bias_query), bias_value])
    projected = (
        jnp.dot(flat_rows, attn_weights[:, : 3 * model_width], preferred_element_type=jnp.float32)
        + bias_proj
    )
    projected = projected.astype(jnp.bfloat16).reshape(batch_size, length, 3, head_count, HD)
    queries = projected[:, :, 0]
    key_rows = projected[:, :, 1]
    value_rows = projected[:, :, 2]
    scores = masked_scores(queries, key_rows, segment)
    top_score = jnp.max(scores, axis=-1, keepdims=True)
    raised = jnp.exp(scores - top_score)
    totals = jnp.sum(raised, axis=-1, keepdims=True)
    attn_probs = (raised / totals).astype(jnp.bfloat16)
    log_total = top_score + jnp.log(totals)
    mixed_heads = jnp.einsum(
        "bhlm,bmhe->blhe", attn_probs, value_rows, preferred_element_type=jnp.float32
    )
    mixed_flat = mixed_heads.astype(jnp.bfloat16).reshape(batch_size * length, model_width)
    attn_out = (
        jnp.dot(mixed_flat, attn_weights[:, 3 * model_width :], preferred_element_type=jnp.float32)
        + bias_out
    )
    residual_one = flat_rows.astype(jnp.float32) + attn_out
    normed_one = layer_norm(residual_one, gain_one, shift_one)
    pre_act = (
        jnp.dot(normed_one.astype(jnp.bfloat16), inner_weight, preferred_element_type=jnp.float32)
        + bias_inner
    )
    activated = gelu_exact(pre_act).astype(jnp.bfloat16)
    branch = jnp.dot(activated, outer_weight, preferred_element_type=jnp.float32) + bias_outer
    residual_two = normed_one + branch
    result = layer_norm(residual_two, gain_two, shift_two).reshape(batch_size, length, model_width)
    kept_values = (
        queries,
        key_rows,
        value_rows,
        log_total,
        mixed_flat,
        residual_one,
        normed_one,
        pre_act,
        activated,
        residual_two,
    )
    return (result, kept_values)


def encoder_backward(
    tokens, segment, attn_weights, inner_weight, outer_weight, small_vec, kept_values, grad_result
):
    batch_size, length, model_width = tokens.shape
    head_count = model_width // HD
    flat_rows = tokens.reshape(batch_size * length, model_width)
    (
        queries,
        key_rows,
        value_rows,
        log_total,
        mixed_flat,
        residual_one,
        normed_one,
        pre_act,
        activated,
        residual_two,
    ) = kept_values
    (
        bias_query,
        bias_value,
        bias_out,
        gain_one,
        shift_one,
        bias_inner,
        bias_outer,
        gain_two,
        shift_two,
    ) = unpack(small_vec, model_width, inner_weight.shape[1])
    grad_flat = grad_result.reshape(batch_size * length, model_width)
    unused_two, norm_two_back = jax.vjp(layer_norm, residual_two, gain_two, shift_two)
    grad_two, grad_gain_two, grad_shift_two = norm_two_back(grad_flat)
    grad_branch = grad_two.astype(jnp.bfloat16)
    grad_bias_outer = jnp.sum(grad_branch, axis=0, dtype=jnp.float32)
    grad_outer = jnp.dot(activated.T, grad_branch, preferred_element_type=jnp.float32)
    grad_act = jnp.dot(grad_branch, outer_weight.T, preferred_element_type=jnp.float32)
    unused_act, gelu_back = jax.vjp(gelu_exact, pre_act)
    grad_pre = gelu_back(grad_act)[0].astype(jnp.bfloat16)
    grad_bias_inner = jnp.sum(grad_pre, axis=0, dtype=jnp.float32)
    grad_inner = jnp.dot(
        normed_one.astype(jnp.bfloat16).T, grad_pre, preferred_element_type=jnp.float32
    )
    grad_normed = grad_two + jnp.dot(grad_pre, inner_weight.T, preferred_element_type=jnp.float32)
    unused_one, norm_one_back = jax.vjp(layer_norm, residual_one, gain_one, shift_one)
    grad_one, grad_gain_one, grad_shift_one = norm_one_back(grad_normed)
    grad_attn_out = grad_one.astype(jnp.bfloat16)
    grad_bias_out = jnp.sum(grad_attn_out, axis=0, dtype=jnp.float32)
    grad_out_proj = jnp.dot(mixed_flat.T, grad_attn_out, preferred_element_type=jnp.float32)
    grad_mixed = jnp.dot(
        grad_attn_out, attn_weights[:, 3 * model_width :].T, preferred_element_type=jnp.float32
    )
    grad_mixed = grad_mixed.astype(jnp.bfloat16).reshape(batch_size, length, head_count, HD)
    scores = masked_scores(queries, key_rows, segment)
    attn_probs = jnp.exp(scores - log_total)
    grad_probs = jnp.einsum(
        "blhe,bmhe->bhlm", grad_mixed, value_rows, preferred_element_type=jnp.float32
    )
    inner_dot = jnp.sum(attn_probs * grad_probs, axis=-1, keepdims=True)
    grad_scores = (attn_probs * (grad_probs - inner_dot)).astype(jnp.bfloat16)
    grad_values = jnp.einsum(
        "bhlm,blhe->bmhe",
        attn_probs.astype(jnp.bfloat16),
        grad_mixed,
        preferred_element_type=jnp.float32,
    )
    grad_queries = jnp.einsum(
        "bhlm,bmhe->blhe", grad_scores, key_rows, preferred_element_type=jnp.float32
    ) * HD ** (-0.5)
    grad_keys = jnp.einsum(
        "bhlm,blhe->bmhe", grad_scores, queries, preferred_element_type=jnp.float32
    ) * HD ** (-0.5)
    row_total = batch_size * length
    grad_proj = jnp.concatenate(
        [
            grad_queries.reshape(row_total, model_width),
            grad_keys.reshape(row_total, model_width),
            grad_values.reshape(row_total, model_width),
        ],
        axis=1,
    ).astype(jnp.bfloat16)
    grad_bias_query = jnp.sum(grad_proj[:, :model_width], axis=0, dtype=jnp.float32)
    grad_bias_value = jnp.sum(grad_proj[:, 2 * model_width :], axis=0, dtype=jnp.float32)
    grad_proj_weight = jnp.dot(flat_rows.T, grad_proj, preferred_element_type=jnp.float32)
    grad_tokens = grad_one + jnp.dot(
        grad_proj, attn_weights[:, : 3 * model_width].T, preferred_element_type=jnp.float32
    )
    grad_attn = jnp.concatenate([grad_proj_weight, grad_out_proj], axis=1)
    grad_small = jnp.concatenate(
        [
            grad_bias_query,
            grad_bias_value,
            grad_bias_out,
            grad_gain_one,
            grad_shift_one,
            grad_bias_inner,
            grad_bias_outer,
            grad_gain_two,
            grad_shift_two,
        ]
    )
    return (
        grad_tokens.reshape(batch_size, length, model_width),
        grad_attn,
        grad_inner,
        grad_outer,
        grad_small,
    )


def rows_term(stacked, count):
    return jnp.moveaxis(stacked, 0, 1).reshape(count, -1)


def unfold_rows(summed, encoders):
    owned = summed.shape[0]
    return jnp.moveaxis(summed.reshape(owned, encoders, -1), 1, 0)


def adam_update(weight, first_moment, second, gradient, step_rate, decay_rate):
    first_new = BETA_ONE * first_moment + (1.0 - BETA_ONE) * gradient
    second_new = BETA_TWO * second + (1.0 - BETA_TWO) * gradient * gradient
    fix_one = 1.0 - BETA_ONE**STEP
    fix_two = 1.0 - BETA_TWO**STEP
    update = first_new / fix_one / (jnp.sqrt(second_new / fix_two) + ADAM_EPS)
    return (first_new, second_new, weight - step_rate * (update + decay_rate * weight))


def local(
    question_tokens,
    passage_tokens,
    passage_lengths,
    positives,
    attn_weight,
    attn_first,
    attn_second,
    ffn_in_weight,
    ffn_in_first,
    ffn_in_second,
    ffn_out_weight,
    ffn_out_first,
    ffn_out_second,
    small_params,
    small_first,
    small_second,
):
    gathered = (
        lax.all_gather(attn_weight.astype(jnp.bfloat16), ("dp", "pair"), axis=1, tiled=True),
        lax.all_gather(ffn_in_weight.astype(jnp.bfloat16), ("dp", "pair"), axis=1, tiled=True),
        lax.all_gather(ffn_out_weight.astype(jnp.bfloat16), ("dp", "pair"), axis=1, tiled=True),
        lax.all_gather(small_params.astype(jnp.bfloat16), ("dp", "pair"), axis=1, tiled=True),
    )
    attn_all, inner_all, outer_all, small_low = gathered
    small_all = small_low.astype(jnp.float32)
    question_count, question_len, model_width = question_tokens.shape
    row_count, row_len, unused_width = passage_tokens.shape
    attn_cols = attn_weight.shape[2]
    front_rows = attn_weight.shape[1]
    back_rows = ffn_out_weight.shape[1]
    seg_ends = jnp.cumsum(passage_lengths, axis=1)
    seg_starts = seg_ends - passage_lengths
    positions = jnp.arange(row_len, dtype=jnp.int32)
    passage_seg = jnp.sum(
        (positions[None, :, None] >= seg_ends[:, None, :]).astype(jnp.int32), axis=2
    )
    question_seg = jnp.zeros((question_count, question_len), jnp.int32)
    question_out, question_kept = encoder_forward(
        question_tokens, question_seg, attn_all[0], inner_all[0], outer_all[0], small_all[0]
    )
    passage_out, passage_kept = encoder_forward(
        passage_tokens, passage_seg, attn_all[1], inner_all[1], outer_all[1], small_all[1]
    )
    question_cls = question_out[:, 0].astype(jnp.bfloat16)
    passage_cls = (
        jnp.take_along_axis(passage_out, seg_starts[:, :, None], axis=1)
        .reshape(-1, model_width)
        .astype(jnp.bfloat16)
    )
    every_cls = lax.all_gather(passage_cls, ("dp", "pair"), axis=0, tiled=True)
    score_scale = model_width ** (-0.5)
    scores = jnp.dot(question_cls, every_cls.T, preferred_element_type=jnp.float32) * score_scale
    top_score = jnp.max(scores, axis=1, keepdims=True)
    raised = jnp.exp(scores - top_score)
    soft_scores = raised / jnp.sum(raised, axis=1, keepdims=True)
    columns = jnp.arange(every_cls.shape[0], dtype=jnp.int32)
    target = (columns[None, :] == positives[:, None]).astype(jnp.float32)
    grad_scores = (soft_scores - target).astype(jnp.bfloat16)
    grad_qcls = jnp.dot(grad_scores, every_cls, preferred_element_type=jnp.float32) * score_scale
    grad_pcls = lax.psum_scatter(
        jnp.dot(grad_scores.T, question_cls, preferred_element_type=jnp.float32) * score_scale,
        ("dp", "pair"),
        scatter_dimension=0,
        tiled=True,
    )
    grad_question_out = jnp.zeros_like(question_out).at[:, 0].set(grad_qcls)
    row_index = jnp.arange(row_count, dtype=jnp.int32)[:, None]
    grad_passage_out = (
        jnp.zeros_like(passage_out)
        .at[row_index, seg_starts]
        .set(grad_pcls.reshape(row_count, -1, model_width))
    )
    question_grad, q_attn, q_inner, q_outer, q_small = encoder_backward(
        question_tokens,
        question_seg,
        attn_all[0],
        inner_all[0],
        outer_all[0],
        small_all[0],
        question_kept,
        grad_question_out,
    )
    passage_grad, p_attn, p_inner, p_outer, p_small = encoder_backward(
        passage_tokens,
        passage_seg,
        attn_all[1],
        inner_all[1],
        outer_all[1],
        small_all[1],
        passage_kept,
        grad_passage_out,
    )
    front_stack = jnp.stack(
        [jnp.concatenate([q_attn, q_inner], axis=1), jnp.concatenate([p_attn, p_inner], axis=1)]
    )
    front_owned = lax.psum_scatter(
        rows_term(front_stack, front_rows * lax.axis_size(("dp", "pair"))),
        ("dp", "pair"),
        scatter_dimension=0,
        tiled=True,
    )
    back_owned = lax.psum_scatter(
        rows_term(jnp.stack([q_outer, p_outer]), back_rows * lax.axis_size(("dp", "pair"))),
        ("dp", "pair"),
        scatter_dimension=0,
        tiled=True,
    )
    small_sum = lax.psum_scatter(
        jnp.stack([q_small, p_small]), ("dp", "pair"), scatter_dimension=1, tiled=True
    )
    front_sum = unfold_rows(front_owned, 2)
    back_sum = unfold_rows(back_owned, 2)
    attn_sum = front_sum[:, :, :attn_cols]
    inner_sum = front_sum[:, :, attn_cols:]
    attn_m, attn_v, attn_w = adam_update(
        attn_weight, attn_first, attn_second, attn_sum, RATE_MATRIX, DECAY_MATRIX
    )
    inner_m, inner_v, inner_w = adam_update(
        ffn_in_weight, ffn_in_first, ffn_in_second, inner_sum, RATE_MATRIX, DECAY_MATRIX
    )
    outer_m, outer_v, outer_w = adam_update(
        ffn_out_weight, ffn_out_first, ffn_out_second, back_sum, RATE_MATRIX, DECAY_MATRIX
    )
    small_m, small_v, small_w = adam_update(
        small_params, small_first, small_second, small_sum, RATE_SMALL, 0.0
    )
    return (
        attn_m,
        attn_v,
        attn_w,
        inner_m,
        inner_v,
        inner_w,
        outer_m,
        outer_v,
        outer_w,
        small_m,
        small_v,
        small_w,
        question_grad,
        passage_grad,
    )


MESH_ID = pl.DeviceIdType.MESH
LOW = jnp.bfloat16
F32 = jnp.float32


def dot_nn(a, b):
    return jnp.dot(a, b, preferred_element_type=F32)


def dot_nt(a, b):
    return lax.dot_general(a, b, (((1,), (1,)), ((), ())), preferred_element_type=F32)


def dot_tn(a, b):
    return lax.dot_general(a, b, (((0,), (0,)), ((), ())), preferred_element_type=F32)


def expand_heads(rows):
    head_of = lax.broadcasted_iota(jnp.int32, rows.shape, 1) // HD
    heads = rows.shape[1] // HD
    return jnp.concatenate(
        [jnp.where(head_of == h, rows, jnp.zeros_like(rows)) for h in range(heads)], axis=0
    )


def pick_heads(stacked):
    width = stacked.shape[1]
    heads = width // HD
    head_of = lax.broadcasted_iota(jnp.int32, (16, width), 1) // HD
    total = jnp.zeros((16, width), F32)
    for h in range(heads):
        total = total + jnp.where(head_of == h, stacked[16 * h : 16 * h + 16], 0.0)
    return total


def split_low(values):
    high = values.astype(LOW)
    return high, (values - high.astype(F32)).astype(LOW)


def gelu_parts(values):
    cdf = 0.5 * (1.0 + lax.erf(values * (0.5**0.5)))
    density = jnp.exp(-0.5 * values * values) * (0.5 / math.pi) ** 0.5
    return values * cdf, cdf + values * density


def step_kernel(
    qt_ref, pt_ref, attn_ref, ffi_ref, ffo_ref, small_ref, len_ref, pos_ref,
    ga_ref, gi_ref, go_ref, gs_ref, dxq_ref, dxp_ref,
    X, slabA, slabI, slabO, smw, sm2, smb, bndo, bndb, R, WN, sn, sno, ST, Pf, Pb, DSb, Emat, b1p,
    w1s_, w1r, W1, W2, Yb, P2s, P2a, P2b, P2c, XH, Dout, dZb, Gb, Act, P3s, P3a, P3b, P3c, Qb, dAb, dUb, dQb,
    m1s, m1r, m2s, m2r, dws, dwr, GP, GS, GSw, GA, GI, GO, DX, qsb, vtb, ybf,
    loc, sib_s, sib_r, at_s, at_r, ag_s, ag_z, ag_p, aa_s, aa_r, rs_s, rs_p, rs_z, out_l, out_s, out_r,
):
    dp, z = lax.axis_index("dp"), lax.axis_index("pair")
    core = lax.rem(dp, 2)
    y, x = dp // 4, lax.rem(dp // 2, 2)
    own = y * 8 + x * 4 + z
    line = y * 8 + x * 4

    def dev(slot, k):
        return ((slot // 8) * 4 + lax.rem(slot // 4, 2) * 2 + k, lax.rem(slot, 4))

    sibling = dev(own, 1 - core)
    slot_x = y * 8 + (1 - x) * 4 + z
    slot_y = (1 - y) * 8 + x * 4 + z
    slot_d = (1 - y) * 8 + (1 - x) * 4 + z

    def remote(src, dst, ssem, rsem, target):
        return pltpu.make_async_remote_copy(
            src_ref=src, dst_ref=dst, send_sem=ssem, recv_sem=rsem,
            device_id=target, device_id_type=MESH_ID,
        )

    def done(ref, sem):
        pltpu.make_async_copy(ref, ref, sem).wait()

    barrier = pltpu.get_barrier_semaphore()
    other = 1 - core
    rows = pl.ds(pl.multiple_of(512 * core, 512), 512)
    pltpu.make_async_copy(attn_ref.at[core], slabA.at[core], loc.at[0]).start()

    def greet(r, c):
        pl.semaphore_signal(
            barrier, inc=1, device_id=dev(lax.rem(own + r, 16), core), device_id_type=MESH_ID
        )
        return c

    pl.semaphore_signal(barrier, inc=1, device_id=sibling, device_id_type=MESH_ID)
    lax.fori_loop(1, 16, greet, 0)

    @pl.when(core == 0)
    def _():
        pltpu.make_async_copy(qt_ref, X.at[rows], loc.at[1]).start()

    @pl.when(core == 1)
    def _():
        pltpu.make_async_copy(pt_ref, X.at[rows], loc.at[1]).start()

    pltpu.make_async_copy(ffi_ref.at[core], slabI.at[core], loc.at[2]).start()
    pltpu.make_async_copy(ffo_ref.at[core], slabO.at[core], loc.at[3]).start()

    narrow = small_ref[...].astype(LOW).astype(F32)
    window = jnp.zeros((2, 384), F32)
    for i in range(4):
        gaps = [jnp.zeros((2, n), F32) for n in (32 * i, 96 - 32 * i) if n]
        placed = jnp.concatenate(([gaps[0]] if i else []) + [narrow] + ([gaps[-1]] if i < 3 else []), axis=1)
        window = jnp.where(z == i, placed, window)
    for k in range(2):
        smw[k] = jnp.concatenate(
            [window[k : k + 1, 128 * i : 128 * i + 128] for i in range(3)]
            + [jnp.zeros((5, 128), F32)], axis=0,
        )
    sm2[core] = smw[core]

    lengths = len_ref[...].astype(F32)
    spans = jnp.concatenate(
        [jnp.broadcast_to(lengths[i : i + 1], (4, 4)) for i in range(2)], axis=0
    )
    at_row = lax.broadcasted_iota(jnp.int32, (8, 4), 0)
    at_lane = lax.broadcasted_iota(jnp.int32, (8, 4), 1)
    upto = at_lane <= lax.rem(at_row, 4)
    here = at_lane == lax.rem(at_row, 4)
    line_of = lax.broadcasted_iota(jnp.int32, (8, 1), 0)
    base = jnp.where(line_of >= 4, 256.0, 0.0)
    passage_end = jnp.sum(jnp.where(upto, spans, 0.0), axis=1, keepdims=True) + base
    passage_start = passage_end - jnp.sum(jnp.where(here, spans, 0.0), axis=1, keepdims=True)
    question_start = line_of.astype(F32) * 64.0
    eye = lax.broadcasted_iota(jnp.int32, (8, 8), 0) == lax.broadcasted_iota(jnp.int32, (8, 8), 1)
    goal = jnp.broadcast_to(pos_ref[...].astype(F32), (8, 8))
    goal = jnp.sum(jnp.where(eye, goal, 0.0), axis=1, keepdims=True)
    of_questions = jnp.concatenate([question_start, question_start + 64.0, goal], axis=0)
    of_passages = jnp.concatenate([passage_start, passage_end, goal], axis=0)
    bndb[core] = jnp.broadcast_to(jnp.where(core == 0, of_questions, of_passages), (24, 128))
    bndo[...] = jnp.broadcast_to(jnp.where(core == 0, of_passages, of_questions), (24, 128))
    pl.semaphore_wait(barrier, 16)

    remote(smw.at[other], sm2.at[core], sib_s.at[1], sib_r.at[1], sibling).start()
    remote(attn_ref.at[other], slabA.at[core], sib_s.at[0], sib_r.at[0], sibling).start()
    remote(bndo, bndb.at[core], sib_s.at[2], sib_r.at[2], sibling).start()

    @pl.when(core == 0)
    def _():
        remote(pt_ref, X.at[rows], sib_s.at[3], sib_r.at[3], sibling).start()

    @pl.when(core == 1)
    def _():
        remote(qt_ref, X.at[rows], sib_s.at[3], sib_r.at[3], sibling).start()

    remote(ffi_ref.at[other], slabI.at[core], sib_s.at[4], sib_r.at[4], sibling).start()
    remote(ffo_ref.at[other], slabO.at[core], sib_s.at[5], sib_r.at[5], sibling).start()

    done(sm2.at[other], sib_r.at[1])
    smb[own] = jnp.concatenate([sm2[0], sm2[1]], axis=0).astype(LOW)

    exchanged = (smb, w1r, None, m1r, None, dwr, m2r)
    gathered = (Yb, Qb, XH.at[core], dUb, None, dQb)
    summed = ((P2s, P2a, P2b, P2c), (P3s, P3a, P3b, P3c))
    passed = ((slabA.at[0], slabA.at[0]), (sm2.at[0], sm2.at[0]), (bndb.at[0], bndb.at[0]),
              (X.at[rows], X.at[rows]), (slabI.at[0], slabI.at[0]), (slabO.at[0], slabO.at[0]),
              (sn, sno), (XH.at[0], XH.at[0]))
    written = [[ref] * 3 for ref in (GO.at[0], DX.at[rows], GI.at[0], GA.at[0, 0], GSw.at[0], GA.at[0, 0])]
    state = {("pass", n): int(n < 2) for n in range(6)}
    state["attn", 0] = 1

    def direct(n, src_of):
        def body(r, c):
            target = lax.rem(own + r, 16)
            remote(src_of(target), exchanged[n].at[own], aa_s.at[n], aa_r.at[n], dev(target, core)).start()
            return c

        lax.fori_loop(1, 16, body, 0)
        state["direct", n] = 0

    def direct_done(n):
        done(exchanged[n].at[pl.ds(0, 15)], aa_r.at[n])
        state["direct", n] = 1

    def pass_done(n):
        done(passed[n][1], sib_r.at[n])
        state["pass", n] = 1

    direct(0, lambda t: smb.at[own])

    def push(slot, m, target):
        remote(R.at[slot, m], R.at[slot, m], at_s.at[m], at_r.at[slot, m, 0], dev(target, core)).start()

    def near(f, nearest=1):
        for d in range(nearest, 4):
            for dz in (d, -d) if d else (0,):
                @pl.when(jnp.logical_and(z + dz >= 0, z + dz <= 3))
                def _():
                    f(dz)

    def got(slot, m):
        done(R.at[slot, m], at_r.at[slot, m, 0])

    done(slabA.at[core], loc.at[0])
    done(slabA.at[other], sib_r.at[0])
    for m in (0, 3, 1, 2):
        cols = slice(768 * m, 768 * m + 768)
        R[own, m] = jnp.concatenate([slabA[0, :, cols], slabA[1, :, cols]], axis=0).astype(LOW)
        for target in (slot_x, slot_y) if m < 3 else (slot_x, slot_y, slot_d):
            push(own, m, target)
        if m < 3:
            near(lambda dz: push(own, m, own + dz))

    def hop(d):
        for i in range(4):
            slot = 4 * i + z
            if d == 0:
                @pl.when(4 * i != line)
                def _():
                    got(slot, 3)

                @pl.when(z < 3)
                def _():
                    push(slot, 3, own + 1)

                @pl.when(z > 0)
                def _():
                    push(slot, 3, own - 1)
            else:
                @pl.when(z - d >= 0)
                def _():
                    got(slot - d, 3)

                    @pl.when(z < 3)
                    def _():
                        push(slot - d, 3, own + 1)

                @pl.when(z + d <= 3)
                def _():
                    got(slot + d, 3)

                    @pl.when(z > 0)
                    def _():
                        push(slot + d, 3, own - 1)

    def settle(last=True):
        for kind, n in list(state):
            at = state[kind, n]
            if last and kind == "gather" and at == 0:
                gather_forward(n)
            if last and kind == "gather" and at < 2:
                gather_done(n)
            if last and kind == "sum" and at == 0:
                sum_forward(n)
            if last and kind == "sum" and at < 2:
                sum_done(n)
            if last and kind == "direct" and at == 0:
                direct_done(n)
            if last and kind == "pass" and at == 0:
                pass_done(n)
            if kind == "gather" and (last or at == 2):
                done(gathered[n].at[pl.ds(0, 15)], ag_s.at[n])
            elif kind == "direct" and (last or at == 1):
                done(exchanged[n].at[pl.ds(0, 15)], aa_s.at[n])
            elif kind == "sum" and (last or at == 2):
                done(summed[n][1].at[pl.ds(0, 3)], rs_s.at[n, 0])
                done(summed[n][3].at[pl.ds(0, 3)], rs_s.at[n, 1])
            elif kind == "pass" and (last or at == 1):
                done(passed[n][0], sib_s.at[n])
            elif kind == "out" and last:
                for ref, sem in zip(written[n], (out_l, out_s, out_r)):
                    done(ref, sem.at[n])
            elif kind == "attn":
                for m in range(3):
                    done(R.at[pl.ds(0, 15), m], at_s.at[m])
                done(R.at[pl.ds(0, 7), 3], at_s.at[3])

                @pl.when(jnp.logical_and(z > 0, z < 3))
                def _():
                    done(R.at[pl.ds(0, 16), 3], at_s.at[3])
            else:
                continue
            del state[kind, n]

    def finish():
        settle()

    def relay_z(m):
        def give(dz):
            got(own + dz, m)
            for target in (slot_x, slot_y):
                push(own + dz, m, target)

        near(give)

    def relay_plane(m):
        def give(dz):
            for slot, target, half in ((slot_x + dz, slot_y, 0), (slot_y + dz, slot_x, 1)):
                got(slot, m)
                part = R.at[slot, m, :, pl.ds(384 * half, 384)]
                remote(part, part, at_s.at[m], at_r.at[slot, m, half], dev(target, core)).start()

        near(give, 0)

    def from_slots(read, write):
        def body(g, c):
            got = [read(4 * g + i) for i in range(4)]
            natural = jnp.concatenate([v[0:24] for v in got] + [v[24:48] for v in got], axis=0)
            write(pl.ds(pl.multiple_of(192 * g, 64), 192), natural.astype(LOW))
            return c

        lax.fori_loop(0, 4, body, 0)

    def to_slots(read, write):
        def body(g, c):
            v = read(pl.ds(pl.multiple_of(192 * g, 64), 192))
            for i in range(4):
                part = jnp.concatenate(
                    [v[24 * i : 24 * i + 24], v[96 + 24 * i : 96 + 24 * i + 24]], axis=0
                )
                write(4 * g + i, part)
            return c

        lax.fori_loop(0, 4, body, 0)

    def pack(v):
        tail = jnp.concatenate([v[0:24, 128:192], v[24:48, 128:192]], axis=1)
        return jnp.concatenate([v[:, 0:128], tail, jnp.zeros((8, 128), F32)], axis=0).astype(LOW)

    def unpack(packed):
        v = packed.astype(F32)
        tail = jnp.concatenate([v[48:72, 0:64], v[48:72, 64:128]], axis=0)
        return jnp.concatenate([v[0:48], tail], axis=1)

    def arrive(m):
        def body(zz, c):
            slot = (1 - y) * 8 + (1 - x) * 4 + zz
            for half in range(2):
                done(R.at[slot, m, :, pl.ds(384 * half, 384)], at_r.at[slot, m, half])
            return c

        if m < 3:
            lax.fori_loop(0, 4, body, 0)

        def write(where, v):
            WN[m, where, :] = v

        from_slots(lambda s: R[s, m].astype(F32), write)

    early_own = (0, 2, 3)

    def gather_start(n):
        buf = gathered[n]
        state["gather", n] = 0

        def give(dz):
            remote(buf.at[own], buf.at[own], ag_s.at[n], ag_z.at[n, z], dev(own + dz, core)).start()

        near(give)
        if n in early_own:
            for target in (slot_x, slot_y, slot_d):
                remote(buf.at[own], buf.at[own], ag_s.at[n], ag_p.at[n], dev(target, core)).start()

    def gather_forward(n):
        buf = gathered[n]
        state["gather", n] = 1

        def pass_on(dz):
            block = buf.at[own + dz]
            done(block, ag_z.at[n, z + dz])
            if n in early_own:
                for target in (slot_x, slot_y, slot_d):
                    remote(block, block, ag_s.at[n], ag_p.at[n], dev(target, core)).start()

        near(pass_on)
        if n not in early_own:
            block = buf.at[pl.ds(line, 4)]
            for target in (slot_x, slot_y, slot_d):
                remote(block, block, ag_s.at[n], ag_p.at[n], dev(target, core)).start()

    def gather_done(n):
        state["gather", n] = 2
        done(gathered[n].at[pl.ds(0, 12)], ag_p.at[n])

    def each_z(f):
        for d in range(3, -1, -1):
            for dz in (d, -d) if d else (0,):
                @pl.when(jnp.logical_and(z + dz >= 0, z + dz <= 3))
                def _():
                    f(dz)

    def sum_start(n):
        source, plane, unused, unused = summed[n]
        state["sum", n] = 0

        def give(dz):
            for target in (slot_x, slot_y, slot_d):
                remote(
                    source.at[target + dz], plane.at[line // 4, z + dz],
                    rs_s.at[n, 0], rs_p.at[n, z + dz], dev(target, core),
                ).start()

        each_z(give)
        plane[line // 4] = source[pl.ds(line, 4)]

    def sum_forward(n):
        unused, plane, along, final = summed[n]
        state["sum", n] = 1

        def give(dz):
            done(plane.at[pl.ds(0, 3), z + dz], rs_p.at[n, z + dz])
            total = jnp.sum(plane[:, z + dz].astype(F32), axis=0).astype(LOW)
            if dz == 0:
                final[z] = total
            else:
                along[z + dz] = total
                remote(
                    along.at[z + dz], final.at[z], rs_s.at[n, 1], rs_z.at[n], dev(own + dz, core)
                ).start()

        each_z(give)

    def sum_done(n):
        final = summed[n][3]
        state["sum", n] = 2
        done(final.at[pl.ds(0, 3)], rs_z.at[n])
        return jnp.sum(final[...].astype(F32), axis=0)

    def prepare_ffn():
        row = lax.broadcasted_iota(jnp.int32, (384, 512), 0)
        col = lax.broadcasted_iota(jnp.int32, (384, 512), 1)
        Emat[...] = jnp.where(col == 128 * (row // 96) + lax.rem(row, 96), 1.0, 0.0).astype(LOW)
        done(slabI.at[core], loc.at[2])
        pass_done(4)
        for g in range(4):
            halves = []
            for k in range(2):
                cols = slice(768 * g + 384 * k, 768 * g + 384 * k + 384)
                halves.append(jnp.concatenate([slabI[0, :, cols], slabI[1, :, cols]], axis=0))
            for i in range(4):
                lanes = slice(96 * i, 96 * i + 96)
                w1s_[4 * g + i] = pack(jnp.concatenate([half[:, lanes] for half in halves], axis=1))
        w1r[own] = w1s_[own]
        done(slabO.at[core], loc.at[3])
        pass_done(5)
        gap = jnp.zeros((64, 768), F32)
        W2[...] = jnp.concatenate([slabO[0], slabO[1], gap], axis=0).astype(LOW)

    def natural_small():
        direct_done(0)
        for g in range(8):
            parts = [
                smb[4 * (g // 2) + i].astype(F32)[8 * (g % 2) : 8 * (g % 2) + 8] for i in range(4)
            ]
            lines = [parts[0][0:1], parts[0][1:2]]
            for i in range(1, 4):
                lines += [parts[i - 1][2:3] + parts[i][0:1], parts[i][1:2]]
            lines += [parts[3][2:3]]
            sn[9 * g : 9 * g + 9, :] = jnp.concatenate(lines, axis=0)
        remote(sn, sno, sib_s.at[6], sib_r.at[6], sibling).start()
        state["pass", 6] = 0

    def vec(row, count=6, ref=sn):
        return jnp.concatenate([ref[row + i : row + i + 1, :] for i in range(count)], axis=1)

    relay_z(0)
    hop(0)
    pass_done(2)
    done(X.at[pl.ds(0, 512)], loc.at[1])
    pass_done(3)
    starts = jnp.concatenate([bndb[0, 0:8], bndb[1, 0:8] + 512.0], axis=0)[:, 0:1]
    ends = jnp.concatenate([bndb[0, 8:16], bndb[1, 8:16] + 512.0], axis=0)[:, 0:1]
    token = lax.broadcasted_iota(jnp.int32, (16, 1024), 1).astype(F32)
    inside = jnp.logical_and(token >= starts, token < ends)
    first = jnp.where(token == starts, 1.0, 0.0).astype(LOW)
    cls_in = dot_nn(first, X[...])
    cls_low = cls_in.astype(LOW)
    relay_z(1)
    relay_plane(0)
    natural_small()
    prepare_ffn()
    hop(1)
    relay_z(2)
    relay_plane(1)
    arrive(0)
    queries = (dot_nn(cls_low, WN[0]) + vec(0)).astype(LOW)
    Qb[own] = queries
    gather_start(1)
    hop(2)
    relay_plane(2)
    arrive(1)
    qsb[...] = (dot_nt(expand_heads(queries), WN[1]) * (HD**-0.5)).astype(LOW)
    ST[...] = dot_nt(qsb[...], X[...])

    def soften(h, c):
        at = pl.ds(pl.multiple_of(16 * h, 16), 16)
        s = jnp.where(inside, ST[at, :], -1000000000.0)
        e = jnp.exp(s - jnp.max(s, axis=1, keepdims=True))
        p = e / jnp.sum(e, axis=1, keepdims=True)
        Pf[at, :] = p
        Pb[at, :] = p.astype(LOW)
        return c

    lax.fori_loop(0, 12, soften, 0, unroll=12)
    ybf[...] = dot_nn(Pb[...], X[...]).astype(LOW)
    arrive(2)
    mixed = (pick_heads(dot_nn(ybf[...], WN[2])) + vec(6)).astype(LOW)
    hop(3)
    arrive(3)
    lifted = cls_in + dot_nn(mixed, WN[3]) + vec(12)
    centred = lifted - jnp.mean(lifted, axis=1, keepdims=True)
    rstd_one = lax.rsqrt(jnp.mean(centred * centred, axis=1, keepdims=True) + NORM_EPS)
    hat_one = centred * rstd_one
    normed = hat_one * vec(18) + vec(24)
    Yb[own] = normed.astype(LOW)
    gather_start(0)
    direct(1, lambda t: w1s_.at[t])

    early = jnp.concatenate(
        [ybf[...].astype(F32), cls_in, mixed.astype(F32), jnp.zeros((32, 768), F32)], axis=0
    )
    DX[0:768, 0:256] = early.T

    def write_m1(slot, v):
        m1s[slot] = v.astype(LOW)

    to_slots(lambda w: DX[w, 0:256], write_m1)
    m1r[own] = m1s[own]
    gather_forward(0)

    b1 = jnp.concatenate([vec(30 + 3 * g, 3) for g in range(8)], axis=0).astype(LOW)
    b1_wide = dot_nn(b1, Emat[...])
    for g in range(8):
        b1p[g] = jnp.broadcast_to(b1_wide[g : g + 1], (8, 512))
    group = pl.multiple_of(128 * z, 128)
    gy = 4 * y + 2 * x
    b1_row = jnp.concatenate(
        [
            b1p[gy, 0:1, pl.ds(group, 128)][:, 0:96], b1p[gy + 1, 0:1, pl.ds(group, 128)][:, 0:96],
            jnp.zeros((1, 64), F32),
        ], axis=1,
    )
    direct_done(1)

    def write_w1(where, v):
        W1[where, :] = v

    pad = jnp.zeros((48, 64), F32)
    from_slots(lambda s: jnp.concatenate([unpack(w1r[s]), pad], axis=1), write_w1)
    gather_done(0)
    all_y = Yb[...].reshape(256, 768)
    act = dot_nn(all_y, W1[...]) + b1_row
    Act[...] = act
    hidden, unused = gelu_parts(act)
    Gb[...] = hidden.astype(LOW)
    P2s[...] = dot_nn(Gb[...], W2[...]).astype(LOW).reshape(16, 16, 768)
    sum_start(0)
    direct(3, lambda t: m1s.at[t])
    sum_forward(0)
    hidden_sum = sum_done(0)
    second = normed + hidden_sum + vec(54)
    centred = second - jnp.mean(second, axis=1, keepdims=True)
    rstd_two = lax.rsqrt(jnp.mean(centred * centred, axis=1, keepdims=True) + NORM_EPS)
    hat_two = centred * rstd_two
    rstd_high, rstd_low = split_low(rstd_two)
    lane = lax.broadcasted_iota(jnp.int32, (16, 128), 1)
    positive = jnp.concatenate([bndb[0, 16:24], bndb[1, 16:24]], axis=0)
    extra = jnp.where(
        lane == 0, rstd_high.astype(F32),
        jnp.where(lane == 1, rstd_low.astype(F32), jnp.where(lane == 2, positive, 0.0)),
    )
    XH[core, own] = jnp.concatenate([hat_two, extra], axis=1).astype(LOW)
    gather_start(2)
    gather_forward(2)
    gather_forward(1)
    gather_done(2)
    remote(XH.at[core], XH.at[core], sib_s.at[7], sib_r.at[7], sibling).start()
    state["pass", 7] = 0
    pass_done(6)
    pass_done(7)

    def vec_of(encoder, row):
        return jnp.where(core == encoder, vec(row), vec(row, 6, sno))

    xq = XH[0].reshape(256, 896).astype(F32)
    xp = XH[1].reshape(256, 896).astype(F32)
    qc = (xq[:, 0:768] * vec_of(0, 60) + vec_of(0, 66)).astype(LOW)
    pc = (xp[:, 0:768] * vec_of(1, 60) + vec_of(1, 66)).astype(LOW)
    scale = 768 ** (-0.5)
    scores = dot_nt(qc, pc) * scale
    raised = jnp.exp(scores - jnp.max(scores, axis=1, keepdims=True))
    soft = raised / jnp.sum(raised, axis=1, keepdims=True)
    place = lax.broadcasted_iota(jnp.int32, (256, 256), 1)
    slot_of = place // 16
    owner_of = (
        16 * (slot_of // 8) + 8 * lax.rem(slot_of // 4, 2)
        + 4 * (lax.rem(place, 16) // 8) + lax.rem(slot_of, 4)
    )
    passage = (8 * owner_of + lax.rem(place, 8)).astype(F32)
    target = jnp.where(passage == xq[:, 770:771], 1.0, 0.0)
    grad_scores = (soft - target).astype(LOW)

    @pl.when(core == 0)
    def _():
        Dout[...] = dot_nn(grad_scores, pc) * scale

    @pl.when(core == 1)
    def _():
        Dout[...] = dot_tn(grad_scores, qc) * scale

    dout = Dout[...]
    block = XH[core].reshape(256, 896).astype(F32)
    hat = block[:, 0:768]
    rstd = block[:, 768:769] + block[:, 769:770]
    inner = dout * vec(60)
    grad_two = rstd * (
        inner - jnp.mean(inner, axis=1, keepdims=True)
        - hat * jnp.mean(inner * hat, axis=1, keepdims=True)
    )
    dg2 = jnp.sum(dout * hat, axis=0, keepdims=True)
    ds2 = jnp.sum(dout, axis=0, keepdims=True)
    Dout[...] = grad_two
    dZb[...] = grad_two.astype(LOW)
    db2 = jnp.sum(dZb[...].astype(F32), axis=0, keepdims=True)
    unused, slope = gelu_parts(Act[...])
    da = (dot_nt(dZb[...], W2[...]) * slope).astype(LOW)
    P3s[...] = dot_nt(da, W1[...]).astype(LOW).reshape(16, 16, 768)
    sum_start(1)
    DX[0:768, 0:256] = dot_tn(all_y, da)

    def write_dw(slot, v):
        dws[slot] = pack(v)

    to_slots(lambda w: DX[w, 0:256], write_dw)
    direct(5, lambda t: dws.at[t])
    sum_forward(1)
    dwr[own] = dws[own]
    db1 = jnp.sum(da.astype(F32), axis=0, keepdims=True)
    dw2 = dot_tn(Gb[...], dZb[...])
    GO[0] = dw2[0:96]
    GO[1] = dw2[96:192]
    pltpu.make_async_copy(GO.at[core], go_ref.at[core], out_l.at[0]).start()
    remote(GO.at[other], go_ref.at[core], out_s.at[0], out_r.at[0], sibling).start()
    state["out", 0] = 0
    own_rows = pl.ds(pl.multiple_of(16 * own, 16), 16)
    normed_sum = sum_done(1)

    grad_normed = Dout[own_rows, :] + normed_sum
    inner = grad_normed * vec(18)
    grad_one = rstd_one * (
        inner - jnp.mean(inner, axis=1, keepdims=True)
        - hat_one * jnp.mean(inner * hat_one, axis=1, keepdims=True)
    )
    grad_lift = grad_one.astype(LOW)
    grad_mixed = dot_nt(grad_lift, WN[3]).astype(LOW)
    dg1 = jnp.sum(grad_normed * hat_one, axis=0, keepdims=True)
    ds1 = jnp.sum(grad_normed, axis=0, keepdims=True)
    partial_sums = jnp.concatenate(
        [dg1[:, 128 * i : 128 * i + 128] for i in range(6)]
        + [ds1[:, 128 * i : 128 * i + 128] for i in range(6)]
        + [db1[:, 0:128], db1[:, 128:256], jnp.zeros((2, 128), F32)], axis=0,
    )
    dUb[own] = jnp.concatenate([grad_one, partial_sums], axis=1).astype(LOW)
    gather_start(3)
    spread = expand_heads(grad_mixed)
    vtb[...] = dot_nt(spread, WN[2]).astype(LOW)
    constant = jnp.sum(spread.astype(F32) * vec(6), axis=1, keepdims=True)
    ST[...] = dot_nt(vtb[...], X[...]) + constant

    def harden(h, c):
        at = pl.ds(pl.multiple_of(16 * h, 16), 16)
        p, dprob = Pf[at, :], ST[at, :]
        total = jnp.sum(p * dprob, axis=1, keepdims=True)
        DSb[at, :] = (p * (dprob - total)).astype(LOW)
        return c

    lax.fori_loop(0, 12, harden, 0, unroll=12)
    late = (dot_nn(DSb[...], X[...]) * (HD**-0.5)).astype(LOW)
    grad_query = pick_heads(dot_nn(late, WN[1])).astype(LOW)
    dQb[own] = grad_query
    gather_start(5)
    DX[0:768, 0:256] = jnp.concatenate(
        [late.astype(F32), jnp.zeros((64, 768), F32)], axis=0
    ).T

    def write_m2(slot, v):
        m2s[slot] = pack(v)

    to_slots(lambda w: DX[w, 0:256], write_m2)
    direct(6, lambda t: m2s.at[t])
    m2r[own] = m2s[own]
    gather_forward(3)

    grad_cls = grad_one + dot_nt(grad_query, WN[0])
    cls_high, cls_rest = split_low(grad_cls)
    right = jnp.concatenate([qsb[...], vtb[...], cls_high, cls_rest], axis=0)
    for k in range(2):
        part = slice(512 * k, 512 * k + 512)
        left = jnp.concatenate([DSb[:, part], Pb[:, part], first[:, part], first[:, part]], axis=0)
        DX[part, :] = dot_tn(left, right)
    gather_forward(5)
    other_rows = pl.ds(pl.multiple_of(512 * other, 512), 512)

    @pl.when(core == 0)
    def _():
        pltpu.make_async_copy(DX.at[rows], dxq_ref, out_l.at[1]).start()
        remote(DX.at[other_rows], dxq_ref, out_s.at[1], out_r.at[1], sibling).start()

    @pl.when(core == 1)
    def _():
        pltpu.make_async_copy(DX.at[rows], dxp_ref, out_l.at[1]).start()
        remote(DX.at[other_rows], dxp_ref, out_s.at[1], out_r.at[1], sibling).start()

    state["out", 1] = 0

    direct_done(5)
    for g in range(4):
        parts = [unpack(dwr[4 * g + i]) for i in range(4)]
        for k in range(2):
            block = jnp.concatenate([v[:, 96 * k : 96 * k + 96] for v in parts], axis=1)
            cols = slice(768 * g + 384 * k, 768 * g + 384 * k + 384)
            GI[0, :, cols] = block[0:24]
            GI[1, :, cols] = block[24:48]
    pltpu.make_async_copy(GI.at[core], gi_ref.at[core], out_l.at[2]).start()
    remote(GI.at[other], gi_ref.at[core], out_s.at[2], out_r.at[2], sibling).start()
    state["out", 2] = 0

    def put(m, v):
        GA[m // 2, 0, :, 768 * (m % 2) : 768 * (m % 2) + 768] = v[0:24]
        GA[m // 2, 1, :, 768 * (m % 2) : 768 * (m % 2) + 768] = v[24:48]

    def hand_out(half, n):
        part = ga_ref.at[core, :, pl.ds(1536 * half, 1536)]
        pltpu.make_async_copy(GA.at[half, core], part, out_l.at[n]).start()
        remote(GA.at[half, other], part, out_s.at[n], out_r.at[n], sibling).start()
        state["out", n] = 0

    def factor_sum(read, columns):
        def body(s, total):
            return total + dot_nn(read(s), expand_heads(columns[s]))

        return lax.fori_loop(0, 16, body, jnp.zeros((48, 768), F32), unroll=16)

    def columns_of(at):
        return jnp.concatenate(
            [m1r[s, :, at : at + 16].astype(F32) for s in range(16)], axis=1
        ).astype(LOW)

    gather_done(3)
    all_du = dUb[...].reshape(256, 896)[:, 0:768]
    all_da = dot_nt(all_du, WN[3]).astype(LOW)
    dAb[...] = all_da.reshape(16, 16, 768)
    direct_done(3)
    put(2, factor_sum(lambda s: m1r[s, :, 0:192], dAb))
    put(3, dot_nn(columns_of(208), all_du))
    hand_out(1, 5)
    cls_columns = columns_of(192)

    parts = [dUb[i, :, 768:896].astype(F32) for i in range(16)]
    sums = parts[0]
    for part in parts[1:]:
        sums = sums + part
    wide = [jnp.concatenate([part[12:13], part[13:14]], axis=1) for part in parts]
    narrow = jnp.concatenate(
        [
            jnp.concatenate(
                [wide[4 * (g // 2) + i][:, 96 * (g % 2) : 96 * (g % 2) + 96] for i in range(4)], axis=1
            )
            for g in range(8)
        ], axis=0,
    )

    def six(v):
        return [v[:, 128 * i : 128 * i + 128] for i in range(6)]

    lines = six(jnp.sum(all_da.astype(F32), axis=0, keepdims=True))
    lines += six(jnp.sum(all_du.astype(F32), axis=0, keepdims=True))
    lines += [sums[0:12]]
    for g in range(8):
        lines += [narrow[g : g + 1, 128 * i : 128 * i + 128] for i in range(3)]
    lines += six(db2) + six(dg2) + six(ds2) + [jnp.zeros((8, 128), F32)]
    GP[6:80] = jnp.concatenate(lines, axis=0)
    for g in range(8):
        for i in range(4):
            at = 9 * g + 9 * i // 4
            if at > 5:
                GS[g, i] = GP[at : at + 8]
    gather_done(1)
    settle(False)
    direct_done(6)
    put(1, factor_sum(lambda s: unpack(m2r[s]).astype(LOW), Qb))
    gather_done(5)
    all_dq = dQb[...].reshape(256, 768)
    put(0, dot_nn(cls_columns, all_dq))
    hand_out(0, 3)
    GP[0:6] = jnp.concatenate(six(jnp.sum(all_dq.astype(F32), axis=0, keepdims=True)), axis=0)
    for i in range(3):
        GS[0, i] = GP[9 * i // 4 : 9 * i // 4 + 8]
    for k in range(2):
        GSw[k] = GS[gy + k, z]
    pltpu.make_async_copy(GSw.at[core], gs_ref.at[core], out_l.at[4]).start()
    remote(GSw.at[other], gs_ref.at[core], out_s.at[4], out_r.at[4], sibling).start()
    state["out", 4] = 0
    finish()


def kernel_call(qt, pt, attn, ffi, ffo, small, lengths, positives):
    any_space = pl.BlockSpec(memory_space=pl.ANY)
    vmem = pl.BlockSpec(memory_space=pltpu.VMEM)
    V = pltpu.VMEM
    dma = pltpu.SemaphoreType.DMA
    scratch = [
        V((1024, 768), LOW), V((2, 24, 3072), F32), V((2, 24, 3072), F32), V((2, 96, 768), F32),
        V((2, 8, 128), F32), V((2, 8, 128), F32), V((16, 16, 128), LOW),
        V((24, 128), F32), V((2, 24, 128), F32), V((16, 4, 48, 768), LOW),
        V((4, 768, 768), LOW), V((72, 128), F32), V((72, 128), F32), V((192, 1024), F32),
        V((192, 1024), F32), V((192, 1024), LOW), V((192, 1024), LOW), V((384, 512), LOW),
        V((8, 8, 512), F32),
        V((16, 80, 128), LOW), V((16, 80, 128), LOW), V((768, 256), LOW), V((256, 768), LOW),
        V((16, 16, 768), LOW), V((16, 16, 768), LOW), V((4, 4, 16, 768), LOW),
        V((4, 16, 768), LOW), V((4, 16, 768), LOW),
        V((2, 16, 16, 896), LOW), V((256, 768), F32), V((256, 768), LOW), V((256, 256), LOW),
        V((256, 256), F32), V((16, 16, 768), LOW), V((4, 4, 16, 768), LOW),
        V((4, 16, 768), LOW), V((4, 16, 768), LOW), V((16, 16, 768), LOW),
        V((16, 16, 768), LOW), V((16, 16, 896), LOW), V((16, 16, 768), LOW),
        V((16, 48, 256), LOW), V((16, 48, 256), LOW), V((16, 80, 128), LOW), V((16, 80, 128), LOW),
        V((16, 80, 128), LOW), V((16, 80, 128), LOW),
        V((80, 128), F32), V((8, 4, 8, 128), F32), V((2, 8, 128), F32), V((2, 2, 24, 1536), F32), V((2, 24, 3072), F32),
        V((2, 96, 768), F32), V((1024, 768), F32), V((192, 768), LOW), V((192, 768), LOW),
        V((192, 768), LOW),
        dma((4,)), dma((8,)), dma((8,)), dma((4,)), dma((16, 4, 2)), dma((7,)), dma((7, 4)),
        dma((7,)), dma((7,)), dma((7,)), dma((2, 2)), dma((2, 4)), dma((2,)),
        dma((6,)), dma((6,)), dma((6,)),
    ]
    shapes = (
        (2, 24, 3072), (2, 24, 3072), (2, 96, 768), (2, 8, 128), (512, 768), (512, 768)
    )
    return pl.pallas_call(
        step_kernel,
        out_shape=[jax.ShapeDtypeStruct(s, F32) for s in shapes],
        in_specs=[any_space] * 5 + [vmem] * 3,
        out_specs=[any_space] * 6,
        scratch_shapes=scratch,
        compiler_params=pltpu.CompilerParams(
            collective_id=0, has_side_effects=True, vmem_limit_bytes=56 << 20
        ),
    )(qt, pt, attn, ffi, ffo, small, lengths, positives)


def update_kernel(*refs):
    ins, outs = refs[:18], refs[18:]
    for n in range(3):
        weight, first, second, grad = (r[...] for r in ins[4 * n : 4 * n + 4])
        new = adam_update(weight, first, second, grad, RATE_MATRIX, DECAY_MATRIX)
        for ref, value in zip(outs[3 * n : 3 * n + 3], new):
            ref[...] = value

    @pl.when(pl.program_id(0) == 0)
    def _():
        z = lax.axis_index("pair")
        weight, first, second, window = ins[12:16]
        lines = []
        for e in range(2):
            row = jnp.concatenate([window[e, i : i + 1, :] for i in range(3)], axis=1)
            picked = row[:, 0:288]
            for i in range(1, 4):
                picked = jnp.where(z == i, row[:, 32 * i : 32 * i + 288], picked)
            lines.append(picked)
        grad = jnp.concatenate(lines, axis=0)
        new = adam_update(weight[...], first[...], second[...], grad, RATE_SMALL, 0.0)
        for ref, value in zip(outs[9:12], new):
            ref[...] = value

    outs[12][...] = ins[16][...]
    outs[13][...] = ins[17][...]


def update_call(attn, inner, outer, small, grad_question, grad_passage):
    wide = pl.BlockSpec((1, 24, 3072), lambda i: (i, 0, 0))
    tall = pl.BlockSpec((1, 96, 768), lambda i: (i, 0, 0))
    vector = pl.BlockSpec((2, 288), lambda i: (0, 0))
    window = pl.BlockSpec((2, 8, 128), lambda i: (0, 0, 0))
    token = pl.BlockSpec((256, 768), lambda i: (i, 0))

    def like(a):
        return jax.ShapeDtypeStruct(a.shape, F32)

    return pl.pallas_call(
        update_kernel,
        grid=(2,),
        out_shape=[like(g[0]) for g in (attn, inner, outer, small) for _ in range(3)]
        + [like(grad_question), like(grad_passage)],
        in_specs=[wide] * 8 + [tall] * 4 + [vector] * 3 + [window, token, token],
        out_specs=[wide] * 6 + [tall] * 3 + [vector] * 3 + [token, token],
    )(*attn, *inner, *outer, *small, grad_question, grad_passage)


def local_kernel(
    question_tokens, passage_tokens, passage_lengths, positives,
    attn_weight, attn_first, attn_second, ffn_in_weight, ffn_in_first, ffn_in_second,
    ffn_out_weight, ffn_out_first, ffn_out_second, small_params, small_first, small_second,
):
    grads = kernel_call(
        question_tokens.reshape(512, 768), passage_tokens.reshape(512, 768),
        attn_weight, ffn_in_weight, ffn_out_weight, small_params,
        passage_lengths, positives.reshape(1, 8),
    )
    attn_sum, inner_sum, outer_sum, small_window, grad_question, grad_passage = grads
    results = update_call(
        (attn_weight, attn_first, attn_second, attn_sum),
        (ffn_in_weight, ffn_in_first, ffn_in_second, inner_sum),
        (ffn_out_weight, ffn_out_first, ffn_out_second, outer_sum),
        (small_params, small_first, small_second, small_window),
        grad_question, grad_passage,
    )
    return (
        *results[:12],
        results[12].reshape(question_tokens.shape),
        results[13].reshape(passage_tokens.shape),
    )


def fits_kernel(mesh):
    return mesh.shape["dp"] == 8 and mesh.shape["pair"] == 4


def solution(mesh):
    in_specs = (
        P(("dp", "pair"), None, None),
        P(("dp", "pair"), None, None),
        P(("dp", "pair"), None),
        P(("dp", "pair")),
        P(None, ("dp", "pair"), None),
        P(None, ("dp", "pair"), None),
        P(None, ("dp", "pair"), None),
        P(None, ("dp", "pair"), None),
        P(None, ("dp", "pair"), None),
        P(None, ("dp", "pair"), None),
        P(None, ("dp", "pair"), None),
        P(None, ("dp", "pair"), None),
        P(None, ("dp", "pair"), None),
        P(None, ("dp", "pair")),
        P(None, ("dp", "pair")),
        P(None, ("dp", "pair")),
    )
    out_specs = (
        P(None, ("dp", "pair"), None),
        P(None, ("dp", "pair"), None),
        P(None, ("dp", "pair"), None),
        P(None, ("dp", "pair"), None),
        P(None, ("dp", "pair"), None),
        P(None, ("dp", "pair"), None),
        P(None, ("dp", "pair"), None),
        P(None, ("dp", "pair"), None),
        P(None, ("dp", "pair"), None),
        P(None, ("dp", "pair")),
        P(None, ("dp", "pair")),
        P(None, ("dp", "pair")),
        P(("dp", "pair"), None, None),
        P(("dp", "pair"), None, None),
    )
    body = local_kernel if fits_kernel(mesh) else local
    return jax.shard_map(body, mesh=mesh, in_specs=in_specs, out_specs=out_specs, check_vma=False)
```

```python
import math

import jax
import jax.numpy as jnp
from jax import lax
from jax.experimental import pallas as pl
from jax.experimental.pallas import tpu as pltpu
from jax.sharding import PartitionSpec as P

HD = 64
STEP = 5


BETA_ONE = 0.9
BETA_TWO = 0.999
ADAM_EPS = 1e-08
NORM_EPS = 1e-06
RATE_MATRIX = 0.05
RATE_SMALL = 0.3
DECAY_MATRIX = 0.01


def layer_norm(values, norm_gain, norm_shift):
    row_mean = jnp.mean(values, axis=-1, keepdims=True)
    centred = values - row_mean
    spread = jnp.mean(centred * centred, axis=-1, keepdims=True)
    return centred * lax.rsqrt(spread + NORM_EPS) * norm_gain + norm_shift


def gelu_exact(values):
    return jax.nn.gelu(values, approximate=False)


def unpack(small_vec, model_width, hidden_width):
    widths = [model_width] * 5 + [hidden_width] + [model_width] * 3
    pieces = []
    offset = 0
    for length in widths:
        pieces.append(small_vec[offset : offset + length])
        offset = offset + length
    return pieces


def masked_scores(queries, key_rows, segment):
    scores = jnp.einsum(
        "blhe,bmhe->bhlm", queries, key_rows, preferred_element_type=jnp.float32
    ) * HD ** (-0.5)
    allowed = (segment[:, :, None] == segment[:, None, :])[:, None]
    return jnp.where(allowed, scores, -1000000000.0)


def encoder_forward(tokens, segment, attn_weights, inner_weight, outer_weight, small_vec):
    batch_size, length, model_width = tokens.shape
    head_count = model_width // HD
    flat_rows = tokens.reshape(batch_size * length, model_width)
    (
        bias_query,
        bias_value,
        bias_out,
        gain_one,
        shift_one,
        bias_inner,
        bias_outer,
        gain_two,
        shift_two,
    ) = unpack(small_vec, model_width, inner_weight.shape[1])
    bias_proj = jnp.concatenate([bias_query, jnp.zeros_like(bias_query), bias_value])
    projected = (
        jnp.dot(flat_rows, attn_weights[:, : 3 * model_width], preferred_element_type=jnp.float32)
        + bias_proj
    )
    projected = projected.astype(jnp.bfloat16).reshape(batch_size, length, 3, head_count, HD)
    queries = projected[:, :, 0]
    key_rows = projected[:, :, 1]
    value_rows = projected[:, :, 2]
    scores = masked_scores(queries, key_rows, segment)
    top_score = jnp.max(scores, axis=-1, keepdims=True)
    raised = jnp.exp(scores - top_score)
    totals = jnp.sum(raised, axis=-1, keepdims=True)
    attn_probs = (raised / totals).astype(jnp.bfloat16)
    log_total = top_score + jnp.log(totals)
    mixed_heads = jnp.einsum(
        "bhlm,bmhe->blhe", attn_probs, value_rows, preferred_element_type=jnp.float32
    )
    mixed_flat = mixed_heads.astype(jnp.bfloat16).reshape(batch_size * length, model_width)
    attn_out = (
        jnp.dot(mixed_flat, attn_weights[:, 3 * model_width :], preferred_element_type=jnp.float32)
        + bias_out
    )
    residual_one = flat_rows.astype(jnp.float32) + attn_out
    normed_one = layer_norm(residual_one, gain_one, shift_one)
    pre_act = (
        jnp.dot(normed_one.astype(jnp.bfloat16), inner_weight, preferred_element_type=jnp.float32)
        + bias_inner
    )
    activated = gelu_exact(pre_act).astype(jnp.bfloat16)
    branch = jnp.dot(activated, outer_weight, preferred_element_type=jnp.float32) + bias_outer
    residual_two = normed_one + branch
    result = layer_norm(residual_two, gain_two, shift_two).reshape(batch_size, length, model_width)
    kept_values = (
        queries,
        key_rows,
        value_rows,
        log_total,
        mixed_flat,
        residual_one,
        normed_one,
        pre_act,
        activated,
        residual_two,
    )
    return (result, kept_values)


def encoder_backward(
    tokens, segment, attn_weights, inner_weight, outer_weight, small_vec, kept_values, grad_result
):
    batch_size, length, model_width = tokens.shape
    head_count = model_width // HD
    flat_rows = tokens.reshape(batch_size * length, model_width)
    (
        queries,
        key_rows,
        value_rows,
        log_total,
        mixed_flat,
        residual_one,
        normed_one,
        pre_act,
        activated,
        residual_two,
    ) = kept_values
    (
        bias_query,
        bias_value,
        bias_out,
        gain_one,
        shift_one,
        bias_inner,
        bias_outer,
        gain_two,
        shift_two,
    ) = unpack(small_vec, model_width, inner_weight.shape[1])
    grad_flat = grad_result.reshape(batch_size * length, model_width)
    unused_two, norm_two_back = jax.vjp(layer_norm, residual_two, gain_two, shift_two)
    grad_two, grad_gain_two, grad_shift_two = norm_two_back(grad_flat)
    grad_branch = grad_two.astype(jnp.bfloat16)
    grad_bias_outer = jnp.sum(grad_branch, axis=0, dtype=jnp.float32)
    grad_outer = jnp.dot(activated.T, grad_branch, preferred_element_type=jnp.float32)
    grad_act = jnp.dot(grad_branch, outer_weight.T, preferred_element_type=jnp.float32)
    unused_act, gelu_back = jax.vjp(gelu_exact, pre_act)
    grad_pre = gelu_back(grad_act)[0].astype(jnp.bfloat16)
    grad_bias_inner = jnp.sum(grad_pre, axis=0, dtype=jnp.float32)
    grad_inner = jnp.dot(
        normed_one.astype(jnp.bfloat16).T, grad_pre, preferred_element_type=jnp.float32
    )
    grad_normed = grad_two + jnp.dot(grad_pre, inner_weight.T, preferred_element_type=jnp.float32)
    unused_one, norm_one_back = jax.vjp(layer_norm, residual_one, gain_one, shift_one)
    grad_one, grad_gain_one, grad_shift_one = norm_one_back(grad_normed)
    grad_attn_out = grad_one.astype(jnp.bfloat16)
    grad_bias_out = jnp.sum(grad_attn_out, axis=0, dtype=jnp.float32)
    grad_out_proj = jnp.dot(mixed_flat.T, grad_attn_out, preferred_element_type=jnp.float32)
    grad_mixed = jnp.dot(
        grad_attn_out, attn_weights[:, 3 * model_width :].T, preferred_element_type=jnp.float32
    )
    grad_mixed = grad_mixed.astype(jnp.bfloat16).reshape(batch_size, length, head_count, HD)
    scores = masked_scores(queries, key_rows, segment)
    attn_probs = jnp.exp(scores - log_total)
    grad_probs = jnp.einsum(
        "blhe,bmhe->bhlm", grad_mixed, value_rows, preferred_element_type=jnp.float32
    )
    inner_dot = jnp.sum(attn_probs * grad_probs, axis=-1, keepdims=True)
    grad_scores = (attn_probs * (grad_probs - inner_dot)).astype(jnp.bfloat16)
    grad_values = jnp.einsum(
        "bhlm,blhe->bmhe",
        attn_probs.astype(jnp.bfloat16),
        grad_mixed,
        preferred_element_type=jnp.float32,
    )
    grad_queries = jnp.einsum(
        "bhlm,bmhe->blhe", grad_scores, key_rows, preferred_element_type=jnp.float32
    ) * HD ** (-0.5)
    grad_keys = jnp.einsum(
        "bhlm,blhe->bmhe", grad_scores, queries, preferred_element_type=jnp.float32
    ) * HD ** (-0.5)
    row_total = batch_size * length
    grad_proj = jnp.concatenate(
        [
            grad_queries.reshape(row_total, model_width),
            grad_keys.reshape(row_total, model_width),
            grad_values.reshape(row_total, model_width),
        ],
        axis=1,
    ).astype(jnp.bfloat16)
    grad_bias_query = jnp.sum(grad_proj[:, :model_width], axis=0, dtype=jnp.float32)
    grad_bias_value = jnp.sum(grad_proj[:, 2 * model_width :], axis=0, dtype=jnp.float32)
    grad_proj_weight = jnp.dot(flat_rows.T, grad_proj, preferred_element_type=jnp.float32)
    grad_tokens = grad_one + jnp.dot(
        grad_proj, attn_weights[:, : 3 * model_width].T, preferred_element_type=jnp.float32
    )
    grad_attn = jnp.concatenate([grad_proj_weight, grad_out_proj], axis=1)
    grad_small = jnp.concatenate(
        [
            grad_bias_query,
            grad_bias_value,
            grad_bias_out,
            grad_gain_one,
            grad_shift_one,
            grad_bias_inner,
            grad_bias_outer,
            grad_gain_two,
            grad_shift_two,
        ]
    )
    return (
        grad_tokens.reshape(batch_size, length, model_width),
        grad_attn,
        grad_inner,
        grad_outer,
        grad_small,
    )


def rows_term(stacked, count):
    return jnp.moveaxis(stacked, 0, 1).reshape(count, -1)


def unfold_rows(summed, encoders):
    owned = summed.shape[0]
    return jnp.moveaxis(summed.reshape(owned, encoders, -1), 1, 0)


def adam_update(weight, first_moment, second, gradient, step_rate, decay_rate):
    first_new = BETA_ONE * first_moment + (1.0 - BETA_ONE) * gradient
    second_new = BETA_TWO * second + (1.0 - BETA_TWO) * gradient * gradient
    fix_one = 1.0 - BETA_ONE**STEP
    fix_two = 1.0 - BETA_TWO**STEP
    update = first_new / fix_one / (jnp.sqrt(second_new / fix_two) + ADAM_EPS)
    return (first_new, second_new, weight - step_rate * (update + decay_rate * weight))


def local(
    question_tokens,
    passage_tokens,
    passage_lengths,
    positives,
    attn_weight,
    attn_first,
    attn_second,
    ffn_in_weight,
    ffn_in_first,
    ffn_in_second,
    ffn_out_weight,
    ffn_out_first,
    ffn_out_second,
    small_params,
    small_first,
    small_second,
):
    gathered = (
        lax.all_gather(attn_weight.astype(jnp.bfloat16), ("dp", "pair"), axis=1, tiled=True),
        lax.all_gather(ffn_in_weight.astype(jnp.bfloat16), ("dp", "pair"), axis=1, tiled=True),
        lax.all_gather(ffn_out_weight.astype(jnp.bfloat16), ("dp", "pair"), axis=1, tiled=True),
        lax.all_gather(small_params.astype(jnp.bfloat16), ("dp", "pair"), axis=1, tiled=True),
    )
    attn_all, inner_all, outer_all, small_low = gathered
    small_all = small_low.astype(jnp.float32)
    question_count, question_len, model_width = question_tokens.shape
    row_count, row_len, unused_width = passage_tokens.shape
    attn_cols = attn_weight.shape[2]
    front_rows = attn_weight.shape[1]
    back_rows = ffn_out_weight.shape[1]
    seg_ends = jnp.cumsum(passage_lengths, axis=1)
    seg_starts = seg_ends - passage_lengths
    positions = jnp.arange(row_len, dtype=jnp.int32)
    passage_seg = jnp.sum(
        (positions[None, :, None] >= seg_ends[:, None, :]).astype(jnp.int32), axis=2
    )
    question_seg = jnp.zeros((question_count, question_len), jnp.int32)
    question_out, question_kept = encoder_forward(
        question_tokens, question_seg, attn_all[0], inner_all[0], outer_all[0], small_all[0]
    )
    passage_out, passage_kept = encoder_forward(
        passage_tokens, passage_seg, attn_all[1], inner_all[1], outer_all[1], small_all[1]
    )
    question_cls = question_out[:, 0].astype(jnp.bfloat16)
    passage_cls = (
        jnp.take_along_axis(passage_out, seg_starts[:, :, None], axis=1)
        .reshape(-1, model_width)
        .astype(jnp.bfloat16)
    )
    every_cls = lax.all_gather(passage_cls, ("dp", "pair"), axis=0, tiled=True)
    score_scale = model_width ** (-0.5)
    scores = jnp.dot(question_cls, every_cls.T, preferred_element_type=jnp.float32) * score_scale
    top_score = jnp.max(scores, axis=1, keepdims=True)
    raised = jnp.exp(scores - top_score)
    soft_scores = raised / jnp.sum(raised, axis=1, keepdims=True)
    columns = jnp.arange(every_cls.shape[0], dtype=jnp.int32)
    target = (columns[None, :] == positives[:, None]).astype(jnp.float32)
    grad_scores = (soft_scores - target).astype(jnp.bfloat16)
    grad_qcls = jnp.dot(grad_scores, every_cls, preferred_element_type=jnp.float32) * score_scale
    grad_pcls = lax.psum_scatter(
        jnp.dot(grad_scores.T, question_cls, preferred_element_type=jnp.float32) * score_scale,
        ("dp", "pair"),
        scatter_dimension=0,
        tiled=True,
    )
    grad_question_out = jnp.zeros_like(question_out).at[:, 0].set(grad_qcls)
    row_index = jnp.arange(row_count, dtype=jnp.int32)[:, None]
    grad_passage_out = (
        jnp.zeros_like(passage_out)
        .at[row_index, seg_starts]
        .set(grad_pcls.reshape(row_count, -1, model_width))
    )
    question_grad, q_attn, q_inner, q_outer, q_small = encoder_backward(
        question_tokens,
        question_seg,
        attn_all[0],
        inner_all[0],
        outer_all[0],
        small_all[0],
        question_kept,
        grad_question_out,
    )
    passage_grad, p_attn, p_inner, p_outer, p_small = encoder_backward(
        passage_tokens,
        passage_seg,
        attn_all[1],
        inner_all[1],
        outer_all[1],
        small_all[1],
        passage_kept,
        grad_passage_out,
    )
    front_stack = jnp.stack(
        [jnp.concatenate([q_attn, q_inner], axis=1), jnp.concatenate([p_attn, p_inner], axis=1)]
    )
    front_owned = lax.psum_scatter(
        rows_term(front_stack, front_rows * lax.axis_size(("dp", "pair"))),
        ("dp", "pair"),
        scatter_dimension=0,
        tiled=True,
    )
    back_owned = lax.psum_scatter(
        rows_term(jnp.stack([q_outer, p_outer]), back_rows * lax.axis_size(("dp", "pair"))),
        ("dp", "pair"),
        scatter_dimension=0,
        tiled=True,
    )
    small_sum = lax.psum_scatter(
        jnp.stack([q_small, p_small]), ("dp", "pair"), scatter_dimension=1, tiled=True
    )
    front_sum = unfold_rows(front_owned, 2)
    back_sum = unfold_rows(back_owned, 2)
    attn_sum = front_sum[:, :, :attn_cols]
    inner_sum = front_sum[:, :, attn_cols:]
    attn_m, attn_v, attn_w = adam_update(
        attn_weight, attn_first, attn_second, attn_sum, RATE_MATRIX, DECAY_MATRIX
    )
    inner_m, inner_v, inner_w = adam_update(
        ffn_in_weight, ffn_in_first, ffn_in_second, inner_sum, RATE_MATRIX, DECAY_MATRIX
    )
    outer_m, outer_v, outer_w = adam_update(
        ffn_out_weight, ffn_out_first, ffn_out_second, back_sum, RATE_MATRIX, DECAY_MATRIX
    )
    small_m, small_v, small_w = adam_update(
        small_params, small_first, small_second, small_sum, RATE_SMALL, 0.0
    )
    return (
        attn_m,
        attn_v,
        attn_w,
        inner_m,
        inner_v,
        inner_w,
        outer_m,
        outer_v,
        outer_w,
        small_m,
        small_v,
        small_w,
        question_grad,
        passage_grad,
    )


MESH_ID = pl.DeviceIdType.MESH
LOW = jnp.bfloat16
F32 = jnp.float32


def dot_nn(a, b):
    return jnp.dot(a, b, preferred_element_type=F32)


def dot_nt(a, b):
    return lax.dot_general(a, b, (((1,), (1,)), ((), ())), preferred_element_type=F32)


def dot_tn(a, b):
    return lax.dot_general(a, b, (((0,), (0,)), ((), ())), preferred_element_type=F32)


def expand_heads(rows):
    head_of = lax.broadcasted_iota(jnp.int32, rows.shape, 1) // HD
    heads = rows.shape[1] // HD
    return jnp.concatenate(
        [jnp.where(head_of == h, rows, jnp.zeros_like(rows)) for h in range(heads)], axis=0
    )


def pick_heads(stacked):
    width = stacked.shape[1]
    heads = width // HD
    head_of = lax.broadcasted_iota(jnp.int32, (16, width), 1) // HD
    total = jnp.zeros((16, width), F32)
    for h in range(heads):
        total = total + jnp.where(head_of == h, stacked[16 * h : 16 * h + 16], 0.0)
    return total


def split_low(values):
    high = values.astype(LOW)
    return high, (values - high.astype(F32)).astype(LOW)


def gelu_parts(values):
    cdf = 0.5 * (1.0 + lax.erf(values * (0.5**0.5)))
    density = jnp.exp(-0.5 * values * values) * (0.5 / math.pi) ** 0.5
    return values * cdf, cdf + values * density


def step_kernel(
    qt_ref, pt_ref, attn_ref, ffi_ref, ffo_ref, small_ref, len_ref, pos_ref,
    ga_ref, gi_ref, go_ref, gs_ref, dxq_ref, dxp_ref,
    X, slabA, slabI, slabO, smw, sm2, smb, bndo, bndb, R, WN, sn, sno, ST, Pf, Pb, DSb, Emat, b1p,
    w1s_, w1r, W1, W2, Yb, P2s, P2a, P2b, P2c, XH, Dout, dZb, Gb, Act, P3s, P3a, P3b, P3c, Qb, dAb, dUb, dQb,
    m1s, m1r, m2s, m2r, dws, dwr, GP, GS, GSw, GA, GI, GO, DX, qsb, vtb, ybf,
    loc, sib_s, sib_r, at_s, at_r, ag_s, ag_z, ag_p, aa_s, aa_r, rs_s, rs_p, rs_z, out_l, out_s, out_r,
):
    dp, z = lax.axis_index("dp"), lax.axis_index("pair")
    core = lax.rem(dp, 2)
    y, x = dp // 4, lax.rem(dp // 2, 2)
    own = y * 8 + x * 4 + z
    line = y * 8 + x * 4

    def dev(slot, k):
        return ((slot // 8) * 4 + lax.rem(slot // 4, 2) * 2 + k, lax.rem(slot, 4))

    sibling = dev(own, 1 - core)
    slot_x = y * 8 + (1 - x) * 4 + z
    slot_y = (1 - y) * 8 + x * 4 + z
    slot_d = (1 - y) * 8 + (1 - x) * 4 + z

    def remote(src, dst, ssem, rsem, target):
        return pltpu.make_async_remote_copy(
            src_ref=src, dst_ref=dst, send_sem=ssem, recv_sem=rsem,
            device_id=target, device_id_type=MESH_ID,
        )

    def done(ref, sem):
        pltpu.make_async_copy(ref, ref, sem).wait()

    barrier = pltpu.get_barrier_semaphore()
    other = 1 - core
    rows = pl.ds(pl.multiple_of(512 * core, 512), 512)
    pltpu.make_async_copy(attn_ref.at[core], slabA.at[core], loc.at[0]).start()

    def greet(r, c):
        pl.semaphore_signal(
            barrier, inc=1, device_id=dev(lax.rem(own + r, 16), core), device_id_type=MESH_ID
        )
        return c

    pl.semaphore_signal(barrier, inc=1, device_id=sibling, device_id_type=MESH_ID)
    lax.fori_loop(1, 16, greet, 0)

    @pl.when(core == 0)
    def _():
        pltpu.make_async_copy(qt_ref, X.at[rows], loc.at[1]).start()

    @pl.when(core == 1)
    def _():
        pltpu.make_async_copy(pt_ref, X.at[rows], loc.at[1]).start()

    pltpu.make_async_copy(ffi_ref.at[core], slabI.at[core], loc.at[2]).start()
    pltpu.make_async_copy(ffo_ref.at[core], slabO.at[core], loc.at[3]).start()

    narrow = small_ref[...].astype(LOW).astype(F32)
    window = jnp.zeros((2, 384), F32)
    for i in range(4):
        gaps = [jnp.zeros((2, n), F32) for n in (32 * i, 96 - 32 * i) if n]
        placed = jnp.concatenate(([gaps[0]] if i else []) + [narrow] + ([gaps[-1]] if i < 3 else []), axis=1)
        window = jnp.where(z == i, placed, window)
    for k in range(2):
        smw[k] = jnp.concatenate(
            [window[k : k + 1, 128 * i : 128 * i + 128] for i in range(3)]
            + [jnp.zeros((5, 128), F32)], axis=0,
        )
    sm2[core] = smw[core]

    lengths = len_ref[...].astype(F32)
    spans = jnp.concatenate(
        [jnp.broadcast_to(lengths[i : i + 1], (4, 4)) for i in range(2)], axis=0
    )
    at_row = lax.broadcasted_iota(jnp.int32, (8, 4), 0)
    at_lane = lax.broadcasted_iota(jnp.int32, (8, 4), 1)
    upto = at_lane <= lax.rem(at_row, 4)
    here = at_lane == lax.rem(at_row, 4)
    line_of = lax.broadcasted_iota(jnp.int32, (8, 1), 0)
    base = jnp.where(line_of >= 4, 256.0, 0.0)
    passage_end = jnp.sum(jnp.where(upto, spans, 0.0), axis=1, keepdims=True) + base
    passage_start = passage_end - jnp.sum(jnp.where(here, spans, 0.0), axis=1, keepdims=True)
    question_start = line_of.astype(F32) * 64.0
    eye = lax.broadcasted_iota(jnp.int32, (8, 8), 0) == lax.broadcasted_iota(jnp.int32, (8, 8), 1)
    goal = jnp.broadcast_to(pos_ref[...].astype(F32), (8, 8))
    goal = jnp.sum(jnp.where(eye, goal, 0.0), axis=1, keepdims=True)
    of_questions = jnp.concatenate([question_start, question_start + 64.0, goal], axis=0)
    of_passages = jnp.concatenate([passage_start, passage_end, goal], axis=0)
    bndb[core] = jnp.broadcast_to(jnp.where(core == 0, of_questions, of_passages), (24, 128))
    bndo[...] = jnp.broadcast_to(jnp.where(core == 0, of_passages, of_questions), (24, 128))
    pl.semaphore_wait(barrier, 16)

    remote(smw.at[other], sm2.at[core], sib_s.at[1], sib_r.at[1], sibling).start()
    remote(attn_ref.at[other], slabA.at[core], sib_s.at[0], sib_r.at[0], sibling).start()
    remote(bndo, bndb.at[core], sib_s.at[2], sib_r.at[2], sibling).start()

    @pl.when(core == 0)
    def _():
        remote(pt_ref, X.at[rows], sib_s.at[3], sib_r.at[3], sibling).start()

    @pl.when(core == 1)
    def _():
        remote(qt_ref, X.at[rows], sib_s.at[3], sib_r.at[3], sibling).start()

    remote(ffi_ref.at[other], slabI.at[core], sib_s.at[4], sib_r.at[4], sibling).start()
    remote(ffo_ref.at[other], slabO.at[core], sib_s.at[5], sib_r.at[5], sibling).start()

    done(sm2.at[other], sib_r.at[1])
    smb[own] = jnp.concatenate([sm2[0], sm2[1]], axis=0).astype(LOW)

    exchanged = (smb, w1r, None, m1r, None, dwr, m2r)
    gathered = (Yb, Qb, XH.at[core], dUb, None, dQb)
    summed = ((P2s, P2a, P2b, P2c), (P3s, P3a, P3b, P3c))
    passed = ((slabA.at[0], slabA.at[0]), (sm2.at[0], sm2.at[0]), (bndb.at[0], bndb.at[0]),
              (X.at[rows], X.at[rows]), (slabI.at[0], slabI.at[0]), (slabO.at[0], slabO.at[0]),
              (sn, sno), (XH.at[0], XH.at[0]))
    written = [[ref] * 3 for ref in (GO.at[0], DX.at[rows], GI.at[0], GA.at[0, 0], GSw.at[0], GA.at[0, 0])]
    state = {("pass", n): int(n < 2) for n in range(6)}
    state["attn", 0] = 1

    def direct(n, src_of):
        def body(r, c):
            target = lax.rem(own + r, 16)
            remote(src_of(target), exchanged[n].at[own], aa_s.at[n], aa_r.at[n], dev(target, core)).start()
            return c

        lax.fori_loop(1, 16, body, 0)
        state["direct", n] = 0

    def direct_done(n):
        done(exchanged[n].at[pl.ds(0, 15)], aa_r.at[n])
        state["direct", n] = 1

    def pass_done(n):
        done(passed[n][1], sib_r.at[n])
        state["pass", n] = 1

    direct(0, lambda t: smb.at[own])

    def push(slot, m, target):
        remote(R.at[slot, m], R.at[slot, m], at_s.at[m], at_r.at[slot, m, 0], dev(target, core)).start()

    def near(f, nearest=1):
        for d in range(nearest, 4):
            for dz in (d, -d) if d else (0,):
                @pl.when(jnp.logical_and(z + dz >= 0, z + dz <= 3))
                def _():
                    f(dz)

    def got(slot, m):
        done(R.at[slot, m], at_r.at[slot, m, 0])

    done(slabA.at[core], loc.at[0])
    done(slabA.at[other], sib_r.at[0])
    for m in (0, 3, 1, 2):
        cols = slice(768 * m, 768 * m + 768)
        R[own, m] = jnp.concatenate([slabA[0, :, cols], slabA[1, :, cols]], axis=0).astype(LOW)
        for target in (slot_x, slot_y) if m < 3 else (slot_x, slot_y, slot_d):
            push(own, m, target)
        if m < 3:
            near(lambda dz: push(own, m, own + dz))

    def hop(d):
        for i in range(4):
            slot = 4 * i + z
            if d == 0:
                @pl.when(4 * i != line)
                def _():
                    got(slot, 3)

                @pl.when(z < 3)
                def _():
                    push(slot, 3, own + 1)

                @pl.when(z > 0)
                def _():
                    push(slot, 3, own - 1)
            else:
                @pl.when(z - d >= 0)
                def _():
                    got(slot - d, 3)

                    @pl.when(z < 3)
                    def _():
                        push(slot - d, 3, own + 1)

                @pl.when(z + d <= 3)
                def _():
                    got(slot + d, 3)

                    @pl.when(z > 0)
                    def _():
                        push(slot + d, 3, own - 1)

    def settle(last=True):
        for kind, n in list(state):
            at = state[kind, n]
            if last and kind == "gather" and at == 0:
                gather_forward(n)
            if last and kind == "gather" and at < 2:
                gather_done(n)
            if last and kind == "sum" and at == 0:
                sum_forward(n)
            if last and kind == "sum" and at < 2:
                sum_done(n)
            if last and kind == "direct" and at == 0:
                direct_done(n)
            if last and kind == "pass" and at == 0:
                pass_done(n)
            if kind == "gather" and (last or at == 2):
                done(gathered[n].at[pl.ds(0, 15)], ag_s.at[n])
            elif kind == "direct" and (last or at == 1):
                done(exchanged[n].at[pl.ds(0, 15)], aa_s.at[n])
            elif kind == "sum" and (last or at == 2):
                done(summed[n][1].at[pl.ds(0, 3)], rs_s.at[n, 0])
                done(summed[n][3].at[pl.ds(0, 3)], rs_s.at[n, 1])
            elif kind == "pass" and (last or at == 1):
                done(passed[n][0], sib_s.at[n])
            elif kind == "out" and last:
                for ref, sem in zip(written[n], (out_l, out_s, out_r)):
                    done(ref, sem.at[n])
            elif kind == "attn":
                for m in range(3):
                    done(R.at[pl.ds(0, 15), m], at_s.at[m])
                done(R.at[pl.ds(0, 7), 3], at_s.at[3])

                @pl.when(jnp.logical_and(z > 0, z < 3))
                def _():
                    done(R.at[pl.ds(0, 16), 3], at_s.at[3])
            else:
                continue
            del state[kind, n]

    def finish():
        settle()

    def relay_z(m):
        def give(dz):
            got(own + dz, m)
            for target in (slot_x, slot_y):
                push(own + dz, m, target)

        near(give)

    def relay_plane(m):
        def give(dz):
            for slot, target, half in ((slot_x + dz, slot_y, 0), (slot_y + dz, slot_x, 1)):
                got(slot, m)
                part = R.at[slot, m, :, pl.ds(384 * half, 384)]
                remote(part, part, at_s.at[m], at_r.at[slot, m, half], dev(target, core)).start()

        near(give, 0)

    def from_slots(read, write):
        def body(g, c):
            got = [read(4 * g + i) for i in range(4)]
            natural = jnp.concatenate([v[0:24] for v in got] + [v[24:48] for v in got], axis=0)
            write(pl.ds(pl.multiple_of(192 * g, 64), 192), natural.astype(LOW))
            return c

        lax.fori_loop(0, 4, body, 0)

    def to_slots(read, write):
        def body(g, c):
            v = read(pl.ds(pl.multiple_of(192 * g, 64), 192))
            for i in range(4):
                part = jnp.concatenate(
                    [v[24 * i : 24 * i + 24], v[96 + 24 * i : 96 + 24 * i + 24]], axis=0
                )
                write(4 * g + i, part)
            return c

        lax.fori_loop(0, 4, body, 0)

    def pack(v):
        tail = jnp.concatenate([v[0:24, 128:192], v[24:48, 128:192]], axis=1)
        return jnp.concatenate([v[:, 0:128], tail, jnp.zeros((8, 128), F32)], axis=0).astype(LOW)

    def unpack(packed):
        v = packed.astype(F32)
        tail = jnp.concatenate([v[48:72, 0:64], v[48:72, 64:128]], axis=0)
        return jnp.concatenate([v[0:48], tail], axis=1)

    def arrive(m):
        def body(zz, c):
            slot = (1 - y) * 8 + (1 - x) * 4 + zz
            for half in range(2):
                done(R.at[slot, m, :, pl.ds(384 * half, 384)], at_r.at[slot, m, half])
            return c

        if m < 3:
            lax.fori_loop(0, 4, body, 0)

        def write(where, v):
            WN[m, where, :] = v

        from_slots(lambda s: R[s, m].astype(F32), write)

    early_own = (0, 1, 2, 3)

    def gather_start(n):
        buf = gathered[n]
        state["gather", n] = 0

        def give(dz):
            remote(buf.at[own], buf.at[own], ag_s.at[n], ag_z.at[n, z], dev(own + dz, core)).start()

        near(give)
        if n in early_own:
            for target in (slot_x, slot_y, slot_d):
                remote(buf.at[own], buf.at[own], ag_s.at[n], ag_p.at[n], dev(target, core)).start()

    def gather_forward(n):
        buf = gathered[n]
        state["gather", n] = 1

        def pass_on(dz):
            block = buf.at[own + dz]
            done(block, ag_z.at[n, z + dz])
            if n in early_own:
                for target in (slot_x, slot_y, slot_d):
                    remote(block, block, ag_s.at[n], ag_p.at[n], dev(target, core)).start()

        near(pass_on)
        if n not in early_own:
            block = buf.at[pl.ds(line, 4)]
            for target in (slot_x, slot_y, slot_d):
                remote(block, block, ag_s.at[n], ag_p.at[n], dev(target, core)).start()

    def gather_done(n):
        state["gather", n] = 2
        done(gathered[n].at[pl.ds(0, 12)], ag_p.at[n])

    def each_z(f):
        for d in range(3, -1, -1):
            for dz in (d, -d) if d else (0,):
                @pl.when(jnp.logical_and(z + dz >= 0, z + dz <= 3))
                def _():
                    f(dz)

    def sum_start(n):
        source, plane, unused, unused = summed[n]
        state["sum", n] = 0

        def give(dz):
            for target in (slot_x, slot_y, slot_d):
                remote(
                    source.at[target + dz], plane.at[line // 4, z + dz],
                    rs_s.at[n, 0], rs_p.at[n, z + dz], dev(target, core),
                ).start()

        each_z(give)
        plane[line // 4] = source[pl.ds(line, 4)]

    def sum_forward(n):
        unused, plane, along, final = summed[n]
        state["sum", n] = 1

        def give(dz):
            done(plane.at[pl.ds(0, 3), z + dz], rs_p.at[n, z + dz])
            total = jnp.sum(plane[:, z + dz].astype(F32), axis=0).astype(LOW)
            if dz == 0:
                final[z] = total
            else:
                along[z + dz] = total
                remote(
                    along.at[z + dz], final.at[z], rs_s.at[n, 1], rs_z.at[n], dev(own + dz, core)
                ).start()

        each_z(give)

    def sum_done(n):
        final = summed[n][3]
        state["sum", n] = 2
        done(final.at[pl.ds(0, 3)], rs_z.at[n])
        return jnp.sum(final[...].astype(F32), axis=0)

    def prepare_ffn():
        row = lax.broadcasted_iota(jnp.int32, (384, 512), 0)
        col = lax.broadcasted_iota(jnp.int32, (384, 512), 1)
        Emat[...] = jnp.where(col == 128 * (row // 96) + lax.rem(row, 96), 1.0, 0.0).astype(LOW)
        done(slabI.at[core], loc.at[2])
        pass_done(4)
        for g in range(4):
            halves = []
            for k in range(2):
                cols = slice(768 * g + 384 * k, 768 * g + 384 * k + 384)
                halves.append(jnp.concatenate([slabI[0, :, cols], slabI[1, :, cols]], axis=0))
            for i in range(4):
                lanes = slice(96 * i, 96 * i + 96)
                w1s_[4 * g + i] = pack(jnp.concatenate([half[:, lanes] for half in halves], axis=1))
        w1r[own] = w1s_[own]
        done(slabO.at[core], loc.at[3])
        pass_done(5)
        gap = jnp.zeros((64, 768), F32)
        W2[...] = jnp.concatenate([slabO[0], slabO[1], gap], axis=0).astype(LOW)

    def natural_small():
        direct_done(0)
        for g in range(8):
            parts = [
                smb[4 * (g // 2) + i].astype(F32)[8 * (g % 2) : 8 * (g % 2) + 8] for i in range(4)
            ]
            lines = [parts[0][0:1], parts[0][1:2]]
            for i in range(1, 4):
                lines += [parts[i - 1][2:3] + parts[i][0:1], parts[i][1:2]]
            lines += [parts[3][2:3]]
            sn[9 * g : 9 * g + 9, :] = jnp.concatenate(lines, axis=0)
        remote(sn, sno, sib_s.at[6], sib_r.at[6], sibling).start()
        state["pass", 6] = 0

    def vec(row, count=6, ref=sn):
        return jnp.concatenate([ref[row + i : row + i + 1, :] for i in range(count)], axis=1)

    relay_z(0)
    hop(0)
    pass_done(2)
    done(X.at[pl.ds(0, 512)], loc.at[1])
    pass_done(3)
    starts = jnp.concatenate([bndb[0, 0:8], bndb[1, 0:8] + 512.0], axis=0)[:, 0:1]
    ends = jnp.concatenate([bndb[0, 8:16], bndb[1, 8:16] + 512.0], axis=0)[:, 0:1]
    token = lax.broadcasted_iota(jnp.int32, (16, 1024), 1).astype(F32)
    inside = jnp.logical_and(token >= starts, token < ends)
    first = jnp.where(token == starts, 1.0, 0.0).astype(LOW)
    cls_in = dot_nn(first, X[...])
    cls_low = cls_in.astype(LOW)
    relay_z(1)
    relay_plane(0)
    natural_small()
    prepare_ffn()
    hop(1)
    relay_z(2)
    relay_plane(1)
    arrive(0)
    queries = (dot_nn(cls_low, WN[0]) + vec(0)).astype(LOW)
    Qb[own] = queries
    gather_start(1)
    hop(2)
    relay_plane(2)
    arrive(1)
    qsb[...] = (dot_nt(expand_heads(queries), WN[1]) * (HD**-0.5)).astype(LOW)
    ST[...] = dot_nt(qsb[...], X[...])

    def soften(h, c):
        at = pl.ds(pl.multiple_of(16 * h, 16), 16)
        s = jnp.where(inside, ST[at, :], -1000000000.0)
        e = jnp.exp(s - jnp.max(s, axis=1, keepdims=True))
        p = e / jnp.sum(e, axis=1, keepdims=True)
        Pf[at, :] = p
        Pb[at, :] = p.astype(LOW)
        return c

    lax.fori_loop(0, 12, soften, 0, unroll=12)
    ybf[...] = dot_nn(Pb[...], X[...]).astype(LOW)
    arrive(2)
    mixed = (pick_heads(dot_nn(ybf[...], WN[2])) + vec(6)).astype(LOW)
    hop(3)
    arrive(3)
    lifted = cls_in + dot_nn(mixed, WN[3]) + vec(12)
    centred = lifted - jnp.mean(lifted, axis=1, keepdims=True)
    rstd_one = lax.rsqrt(jnp.mean(centred * centred, axis=1, keepdims=True) + NORM_EPS)
    hat_one = centred * rstd_one
    normed = hat_one * vec(18) + vec(24)
    Yb[own] = normed.astype(LOW)
    gather_start(0)
    direct(1, lambda t: w1s_.at[t])

    early = jnp.concatenate(
        [ybf[...].astype(F32), cls_in, mixed.astype(F32), jnp.zeros((32, 768), F32)], axis=0
    )
    DX[0:768, 0:256] = early.T

    def write_m1(slot, v):
        m1s[slot] = v.astype(LOW)

    to_slots(lambda w: DX[w, 0:256], write_m1)
    m1r[own] = m1s[own]
    gather_forward(0)

    b1 = jnp.concatenate([vec(30 + 3 * g, 3) for g in range(8)], axis=0).astype(LOW)
    b1_wide = dot_nn(b1, Emat[...])
    for g in range(8):
        b1p[g] = jnp.broadcast_to(b1_wide[g : g + 1], (8, 512))
    group = pl.multiple_of(128 * z, 128)
    gy = 4 * y + 2 * x
    b1_row = jnp.concatenate(
        [
            b1p[gy, 0:1, pl.ds(group, 128)][:, 0:96], b1p[gy + 1, 0:1, pl.ds(group, 128)][:, 0:96],
            jnp.zeros((1, 64), F32),
        ], axis=1,
    )
    direct_done(1)

    def write_w1(where, v):
        W1[where, :] = v

    pad = jnp.zeros((48, 64), F32)
    from_slots(lambda s: jnp.concatenate([unpack(w1r[s]), pad], axis=1), write_w1)
    gather_done(0)
    all_y = Yb[...].reshape(256, 768)
    act = dot_nn(all_y, W1[...]) + b1_row
    Act[...] = act
    hidden, unused = gelu_parts(act)
    Gb[...] = hidden.astype(LOW)
    P2s[...] = dot_nn(Gb[...], W2[...]).astype(LOW).reshape(16, 16, 768)
    sum_start(0)
    sum_forward(0)
    hidden_sum = sum_done(0)
    second = normed + hidden_sum + vec(54)
    centred = second - jnp.mean(second, axis=1, keepdims=True)
    rstd_two = lax.rsqrt(jnp.mean(centred * centred, axis=1, keepdims=True) + NORM_EPS)
    hat_two = centred * rstd_two
    rstd_high, rstd_low = split_low(rstd_two)
    lane = lax.broadcasted_iota(jnp.int32, (16, 128), 1)
    positive = jnp.concatenate([bndb[0, 16:24], bndb[1, 16:24]], axis=0)
    extra = jnp.where(
        lane == 0, rstd_high.astype(F32),
        jnp.where(lane == 1, rstd_low.astype(F32), jnp.where(lane == 2, positive, 0.0)),
    )
    XH[core, own] = jnp.concatenate([hat_two, extra], axis=1).astype(LOW)
    gather_start(2)
    gather_forward(2)
    direct(3, lambda t: m1s.at[t])
    gather_forward(1)
    gather_done(2)
    remote(XH.at[core], XH.at[core], sib_s.at[7], sib_r.at[7], sibling).start()
    state["pass", 7] = 0
    pass_done(6)
    pass_done(7)

    def vec_of(encoder, row):
        return jnp.where(core == encoder, vec(row), vec(row, 6, sno))

    xq = XH[0].reshape(256, 896).astype(F32)
    xp = XH[1].reshape(256, 896).astype(F32)
    qc = (xq[:, 0:768] * vec_of(0, 60) + vec_of(0, 66)).astype(LOW)
    pc = (xp[:, 0:768] * vec_of(1, 60) + vec_of(1, 66)).astype(LOW)
    scale = 768 ** (-0.5)
    scores = dot_nt(qc, pc) * scale
    raised = jnp.exp(scores - jnp.max(scores, axis=1, keepdims=True))
    soft = raised / jnp.sum(raised, axis=1, keepdims=True)
    place = lax.broadcasted_iota(jnp.int32, (256, 256), 1)
    slot_of = place // 16
    owner_of = (
        16 * (slot_of // 8) + 8 * lax.rem(slot_of // 4, 2)
        + 4 * (lax.rem(place, 16) // 8) + lax.rem(slot_of, 4)
    )
    passage = (8 * owner_of + lax.rem(place, 8)).astype(F32)
    target = jnp.where(passage == xq[:, 770:771], 1.0, 0.0)
    grad_scores = (soft - target).astype(LOW)

    @pl.when(core == 0)
    def _():
        Dout[...] = dot_nn(grad_scores, pc) * scale

    @pl.when(core == 1)
    def _():
        Dout[...] = dot_tn(grad_scores, qc) * scale

    dout = Dout[...]
    block = XH[core].reshape(256, 896).astype(F32)
    hat = block[:, 0:768]
    rstd = block[:, 768:769] + block[:, 769:770]
    inner = dout * vec(60)
    grad_two = rstd * (
        inner - jnp.mean(inner, axis=1, keepdims=True)
        - hat * jnp.mean(inner * hat, axis=1, keepdims=True)
    )
    dg2 = jnp.sum(dout * hat, axis=0, keepdims=True)
    ds2 = jnp.sum(dout, axis=0, keepdims=True)
    Dout[...] = grad_two
    dZb[...] = grad_two.astype(LOW)
    db2 = jnp.sum(dZb[...].astype(F32), axis=0, keepdims=True)
    unused, slope = gelu_parts(Act[...])
    da = (dot_nt(dZb[...], W2[...]) * slope).astype(LOW)
    P3s[...] = dot_nt(da, W1[...]).astype(LOW).reshape(16, 16, 768)
    sum_start(1)
    DX[0:768, 0:256] = dot_tn(all_y, da)

    def write_dw(slot, v):
        dws[slot] = pack(v)

    to_slots(lambda w: DX[w, 0:256], write_dw)
    direct(5, lambda t: dws.at[t])
    sum_forward(1)
    dwr[own] = dws[own]
    db1 = jnp.sum(da.astype(F32), axis=0, keepdims=True)
    dw2 = dot_tn(Gb[...], dZb[...])
    GO[0] = dw2[0:96]
    GO[1] = dw2[96:192]
    pltpu.make_async_copy(GO.at[core], go_ref.at[core], out_l.at[0]).start()
    remote(GO.at[other], go_ref.at[core], out_s.at[0], out_r.at[0], sibling).start()
    state["out", 0] = 0
    own_rows = pl.ds(pl.multiple_of(16 * own, 16), 16)
    normed_sum = sum_done(1)

    grad_normed = Dout[own_rows, :] + normed_sum
    inner = grad_normed * vec(18)
    grad_one = rstd_one * (
        inner - jnp.mean(inner, axis=1, keepdims=True)
        - hat_one * jnp.mean(inner * hat_one, axis=1, keepdims=True)
    )
    grad_lift = grad_one.astype(LOW)
    grad_mixed = dot_nt(grad_lift, WN[3]).astype(LOW)
    dg1 = jnp.sum(grad_normed * hat_one, axis=0, keepdims=True)
    ds1 = jnp.sum(grad_normed, axis=0, keepdims=True)
    partial_sums = jnp.concatenate(
        [dg1[:, 128 * i : 128 * i + 128] for i in range(6)]
        + [ds1[:, 128 * i : 128 * i + 128] for i in range(6)]
        + [db1[:, 0:128], db1[:, 128:256], jnp.zeros((2, 128), F32)], axis=0,
    )
    dUb[own] = jnp.concatenate([grad_one, partial_sums], axis=1).astype(LOW)
    gather_start(3)
    spread = expand_heads(grad_mixed)
    vtb[...] = dot_nt(spread, WN[2]).astype(LOW)
    constant = jnp.sum(spread.astype(F32) * vec(6), axis=1, keepdims=True)
    ST[...] = dot_nt(vtb[...], X[...]) + constant

    def harden(h, c):
        at = pl.ds(pl.multiple_of(16 * h, 16), 16)
        p, dprob = Pf[at, :], ST[at, :]
        total = jnp.sum(p * dprob, axis=1, keepdims=True)
        DSb[at, :] = (p * (dprob - total)).astype(LOW)
        return c

    lax.fori_loop(0, 12, harden, 0, unroll=12)
    late = (dot_nn(DSb[...], X[...]) * (HD**-0.5)).astype(LOW)
    grad_query = pick_heads(dot_nn(late, WN[1])).astype(LOW)
    dQb[own] = grad_query
    gather_start(5)
    DX[0:768, 0:256] = jnp.concatenate(
        [late.astype(F32), jnp.zeros((64, 768), F32)], axis=0
    ).T

    def write_m2(slot, v):
        m2s[slot] = pack(v)

    to_slots(lambda w: DX[w, 0:256], write_m2)
    direct(6, lambda t: m2s.at[t])
    m2r[own] = m2s[own]
    gather_forward(3)

    grad_cls = grad_one + dot_nt(grad_query, WN[0])
    cls_high, cls_rest = split_low(grad_cls)
    right = jnp.concatenate([qsb[...], vtb[...], cls_high, cls_rest], axis=0)
    for k in range(2):
        part = slice(512 * k, 512 * k + 512)
        left = jnp.concatenate([DSb[:, part], Pb[:, part], first[:, part], first[:, part]], axis=0)
        DX[part, :] = dot_tn(left, right)
    gather_forward(5)
    other_rows = pl.ds(pl.multiple_of(512 * other, 512), 512)

    @pl.when(core == 0)
    def _():
        pltpu.make_async_copy(DX.at[rows], dxq_ref, out_l.at[1]).start()
        remote(DX.at[other_rows], dxq_ref, out_s.at[1], out_r.at[1], sibling).start()

    @pl.when(core == 1)
    def _():
        pltpu.make_async_copy(DX.at[rows], dxp_ref, out_l.at[1]).start()
        remote(DX.at[other_rows], dxp_ref, out_s.at[1], out_r.at[1], sibling).start()

    state["out", 1] = 0

    direct_done(5)
    for g in range(4):
        parts = [unpack(dwr[4 * g + i]) for i in range(4)]
        for k in range(2):
            block = jnp.concatenate([v[:, 96 * k : 96 * k + 96] for v in parts], axis=1)
            cols = slice(768 * g + 384 * k, 768 * g + 384 * k + 384)
            GI[0, :, cols] = block[0:24]
            GI[1, :, cols] = block[24:48]
    pltpu.make_async_copy(GI.at[core], gi_ref.at[core], out_l.at[2]).start()
    remote(GI.at[other], gi_ref.at[core], out_s.at[2], out_r.at[2], sibling).start()
    state["out", 2] = 0

    def put(m, v):
        GA[m // 2, 0, :, 768 * (m % 2) : 768 * (m % 2) + 768] = v[0:24]
        GA[m // 2, 1, :, 768 * (m % 2) : 768 * (m % 2) + 768] = v[24:48]

    def hand_out(half, n):
        part = ga_ref.at[core, :, pl.ds(1536 * half, 1536)]
        pltpu.make_async_copy(GA.at[half, core], part, out_l.at[n]).start()
        remote(GA.at[half, other], part, out_s.at[n], out_r.at[n], sibling).start()
        state["out", n] = 0

    def factor_sum(read, columns):
        def body(s, total):
            return total + dot_nn(read(s), expand_heads(columns[s]))

        return lax.fori_loop(0, 16, body, jnp.zeros((48, 768), F32), unroll=16)

    def columns_of(at):
        return jnp.concatenate(
            [m1r[s, :, at : at + 16].astype(F32) for s in range(16)], axis=1
        ).astype(LOW)

    gather_done(3)
    all_du = dUb[...].reshape(256, 896)[:, 0:768]
    all_da = dot_nt(all_du, WN[3]).astype(LOW)
    dAb[...] = all_da.reshape(16, 16, 768)
    direct_done(3)
    put(2, factor_sum(lambda s: m1r[s, :, 0:192], dAb))
    put(3, dot_nn(columns_of(208), all_du))
    hand_out(1, 5)
    cls_columns = columns_of(192)

    parts = [dUb[i, :, 768:896].astype(F32) for i in range(16)]
    sums = parts[0]
    for part in parts[1:]:
        sums = sums + part
    wide = [jnp.concatenate([part[12:13], part[13:14]], axis=1) for part in parts]
    narrow = jnp.concatenate(
        [
            jnp.concatenate(
                [wide[4 * (g // 2) + i][:, 96 * (g % 2) : 96 * (g % 2) + 96] for i in range(4)], axis=1
            )
            for g in range(8)
        ], axis=0,
    )

    def six(v):
        return [v[:, 128 * i : 128 * i + 128] for i in range(6)]

    lines = six(jnp.sum(all_da.astype(F32), axis=0, keepdims=True))
    lines += six(jnp.sum(all_du.astype(F32), axis=0, keepdims=True))
    lines += [sums[0:12]]
    for g in range(8):
        lines += [narrow[g : g + 1, 128 * i : 128 * i + 128] for i in range(3)]
    lines += six(db2) + six(dg2) + six(ds2) + [jnp.zeros((8, 128), F32)]
    GP[6:80] = jnp.concatenate(lines, axis=0)
    for g in range(8):
        for i in range(4):
            at = 9 * g + 9 * i // 4
            if at > 5:
                GS[g, i] = GP[at : at + 8]
    gather_done(1)
    settle(False)
    direct_done(6)
    put(1, factor_sum(lambda s: unpack(m2r[s]).astype(LOW), Qb))
    gather_done(5)
    all_dq = dQb[...].reshape(256, 768)
    put(0, dot_nn(cls_columns, all_dq))
    hand_out(0, 3)
    GP[0:6] = jnp.concatenate(six(jnp.sum(all_dq.astype(F32), axis=0, keepdims=True)), axis=0)
    for i in range(3):
        GS[0, i] = GP[9 * i // 4 : 9 * i // 4 + 8]
    for k in range(2):
        GSw[k] = GS[gy + k, z]
    pltpu.make_async_copy(GSw.at[core], gs_ref.at[core], out_l.at[4]).start()
    remote(GSw.at[other], gs_ref.at[core], out_s.at[4], out_r.at[4], sibling).start()
    state["out", 4] = 0
    finish()


def kernel_call(qt, pt, attn, ffi, ffo, small, lengths, positives):
    any_space = pl.BlockSpec(memory_space=pl.ANY)
    vmem = pl.BlockSpec(memory_space=pltpu.VMEM)
    V = pltpu.VMEM
    dma = pltpu.SemaphoreType.DMA
    scratch = [
        V((1024, 768), LOW), V((2, 24, 3072), F32), V((2, 24, 3072), F32), V((2, 96, 768), F32),
        V((2, 8, 128), F32), V((2, 8, 128), F32), V((16, 16, 128), LOW),
        V((24, 128), F32), V((2, 24, 128), F32), V((16, 4, 48, 768), LOW),
        V((4, 768, 768), LOW), V((72, 128), F32), V((72, 128), F32), V((192, 1024), F32),
        V((192, 1024), F32), V((192, 1024), LOW), V((192, 1024), LOW), V((384, 512), LOW),
        V((8, 8, 512), F32),
        V((16, 80, 128), LOW), V((16, 80, 128), LOW), V((768, 256), LOW), V((256, 768), LOW),
        V((16, 16, 768), LOW), V((16, 16, 768), LOW), V((4, 4, 16, 768), LOW),
        V((4, 16, 768), LOW), V((4, 16, 768), LOW),
        V((2, 16, 16, 896), LOW), V((256, 768), F32), V((256, 768), LOW), V((256, 256), LOW),
        V((256, 256), F32), V((16, 16, 768), LOW), V((4, 4, 16, 768), LOW),
        V((4, 16, 768), LOW), V((4, 16, 768), LOW), V((16, 16, 768), LOW),
        V((16, 16, 768), LOW), V((16, 16, 896), LOW), V((16, 16, 768), LOW),
        V((16, 48, 256), LOW), V((16, 48, 256), LOW), V((16, 80, 128), LOW), V((16, 80, 128), LOW),
        V((16, 80, 128), LOW), V((16, 80, 128), LOW),
        V((80, 128), F32), V((8, 4, 8, 128), F32), V((2, 8, 128), F32), V((2, 2, 24, 1536), F32), V((2, 24, 3072), F32),
        V((2, 96, 768), F32), V((1024, 768), F32), V((192, 768), LOW), V((192, 768), LOW),
        V((192, 768), LOW),
        dma((4,)), dma((8,)), dma((8,)), dma((4,)), dma((16, 4, 2)), dma((7,)), dma((7, 4)),
        dma((7,)), dma((7,)), dma((7,)), dma((2, 2)), dma((2, 4)), dma((2,)),
        dma((6,)), dma((6,)), dma((6,)),
    ]
    shapes = (
        (2, 24, 3072), (2, 24, 3072), (2, 96, 768), (2, 8, 128), (512, 768), (512, 768)
    )
    return pl.pallas_call(
        step_kernel,
        out_shape=[jax.ShapeDtypeStruct(s, F32) for s in shapes],
        in_specs=[any_space] * 5 + [vmem] * 3,
        out_specs=[any_space] * 6,
        scratch_shapes=scratch,
        compiler_params=pltpu.CompilerParams(
            collective_id=0, has_side_effects=True, vmem_limit_bytes=56 << 20
        ),
    )(qt, pt, attn, ffi, ffo, small, lengths, positives)


def update_kernel(*refs):
    ins, outs = refs[:18], refs[18:]
    for n in range(3):
        weight, first, second, grad = (r[...] for r in ins[4 * n : 4 * n + 4])
        new = adam_update(weight, first, second, grad, RATE_MATRIX, DECAY_MATRIX)
        for ref, value in zip(outs[3 * n : 3 * n + 3], new):
            ref[...] = value

    @pl.when(pl.program_id(0) == 0)
    def _():
        z = lax.axis_index("pair")
        weight, first, second, window = ins[12:16]
        lines = []
        for e in range(2):
            row = jnp.concatenate([window[e, i : i + 1, :] for i in range(3)], axis=1)
            picked = row[:, 0:288]
            for i in range(1, 4):
                picked = jnp.where(z == i, row[:, 32 * i : 32 * i + 288], picked)
            lines.append(picked)
        grad = jnp.concatenate(lines, axis=0)
        new = adam_update(weight[...], first[...], second[...], grad, RATE_SMALL, 0.0)
        for ref, value in zip(outs[9:12], new):
            ref[...] = value

    outs[12][...] = ins[16][...]
    outs[13][...] = ins[17][...]


def update_call(attn, inner, outer, small, grad_question, grad_passage):
    wide = pl.BlockSpec((1, 24, 3072), lambda i: (i, 0, 0))
    tall = pl.BlockSpec((1, 96, 768), lambda i: (i, 0, 0))
    vector = pl.BlockSpec((2, 288), lambda i: (0, 0))
    window = pl.BlockSpec((2, 8, 128), lambda i: (0, 0, 0))
    token = pl.BlockSpec((256, 768), lambda i: (i, 0))

    def like(a):
        return jax.ShapeDtypeStruct(a.shape, F32)

    return pl.pallas_call(
        update_kernel,
        grid=(2,),
        out_shape=[like(g[0]) for g in (attn, inner, outer, small) for _ in range(3)]
        + [like(grad_question), like(grad_passage)],
        in_specs=[wide] * 8 + [tall] * 4 + [vector] * 3 + [window, token, token],
        out_specs=[wide] * 6 + [tall] * 3 + [vector] * 3 + [token, token],
    )(*attn, *inner, *outer, *small, grad_question, grad_passage)


def local_kernel(
    question_tokens, passage_tokens, passage_lengths, positives,
    attn_weight, attn_first, attn_second, ffn_in_weight, ffn_in_first, ffn_in_second,
    ffn_out_weight, ffn_out_first, ffn_out_second, small_params, small_first, small_second,
):
    grads = kernel_call(
        question_tokens.reshape(512, 768), passage_tokens.reshape(512, 768),
        attn_weight, ffn_in_weight, ffn_out_weight, small_params,
        passage_lengths, positives.reshape(1, 8),
    )
    attn_sum, inner_sum, outer_sum, small_window, grad_question, grad_passage = grads
    results = update_call(
        (attn_weight, attn_first, attn_second, attn_sum),
        (ffn_in_weight, ffn_in_first, ffn_in_second, inner_sum),
        (ffn_out_weight, ffn_out_first, ffn_out_second, outer_sum),
        (small_params, small_first, small_second, small_window),
        grad_question, grad_passage,
    )
    return (
        *results[:12],
        results[12].reshape(question_tokens.shape),
        results[13].reshape(passage_tokens.shape),
    )


def fits_kernel(mesh):
    return mesh.shape["dp"] == 8 and mesh.shape["pair"] == 4


def solution(mesh):
    in_specs = (
        P(("dp", "pair"), None, None),
        P(("dp", "pair"), None, None),
        P(("dp", "pair"), None),
        P(("dp", "pair")),
        P(None, ("dp", "pair"), None),
        P(None, ("dp", "pair"), None),
        P(None, ("dp", "pair"), None),
        P(None, ("dp", "pair"), None),
        P(None, ("dp", "pair"), None),
        P(None, ("dp", "pair"), None),
        P(None, ("dp", "pair"), None),
        P(None, ("dp", "pair"), None),
        P(None, ("dp", "pair"), None),
        P(None, ("dp", "pair")),
        P(None, ("dp", "pair")),
        P(None, ("dp", "pair")),
    )
    out_specs = (
        P(None, ("dp", "pair"), None),
        P(None, ("dp", "pair"), None),
        P(None, ("dp", "pair"), None),
        P(None, ("dp", "pair"), None),
        P(None, ("dp", "pair"), None),
        P(None, ("dp", "pair"), None),
        P(None, ("dp", "pair"), None),
        P(None, ("dp", "pair"), None),
        P(None, ("dp", "pair"), None),
        P(None, ("dp", "pair")),
        P(None, ("dp", "pair")),
        P(None, ("dp", "pair")),
        P(("dp", "pair"), None, None),
        P(("dp", "pair"), None, None),
    )
    body = local_kernel if fits_kernel(mesh) else local
    return jax.shard_map(body, mesh=mesh, in_specs=in_specs, out_specs=out_specs, check_vma=False)
```

```python
import math

import jax
import jax.numpy as jnp
from jax import lax
from jax.experimental import pallas as pl
from jax.experimental.pallas import tpu as pltpu
from jax.sharding import PartitionSpec as P

HD = 64
STEP = 5


BETA_ONE = 0.9
BETA_TWO = 0.999
ADAM_EPS = 1e-08
NORM_EPS = 1e-06
RATE_MATRIX = 0.05
RATE_SMALL = 0.3
DECAY_MATRIX = 0.01


def layer_norm(values, norm_gain, norm_shift):
    row_mean = jnp.mean(values, axis=-1, keepdims=True)
    centred = values - row_mean
    spread = jnp.mean(centred * centred, axis=-1, keepdims=True)
    return centred * lax.rsqrt(spread + NORM_EPS) * norm_gain + norm_shift


def gelu_exact(values):
    return jax.nn.gelu(values, approximate=False)


def unpack(small_vec, model_width, hidden_width):
    widths = [model_width] * 5 + [hidden_width] + [model_width] * 3
    pieces = []
    offset = 0
    for length in widths:
        pieces.append(small_vec[offset : offset + length])
        offset = offset + length
    return pieces


def masked_scores(queries, key_rows, segment):
    scores = jnp.einsum(
        "blhe,bmhe->bhlm", queries, key_rows, preferred_element_type=jnp.float32
    ) * HD ** (-0.5)
    allowed = (segment[:, :, None] == segment[:, None, :])[:, None]
    return jnp.where(allowed, scores, -1000000000.0)


def encoder_forward(tokens, segment, attn_weights, inner_weight, outer_weight, small_vec):
    batch_size, length, model_width = tokens.shape
    head_count = model_width // HD
    flat_rows = tokens.reshape(batch_size * length, model_width)
    (
        bias_query,
        bias_value,
        bias_out,
        gain_one,
        shift_one,
        bias_inner,
        bias_outer,
        gain_two,
        shift_two,
    ) = unpack(small_vec, model_width, inner_weight.shape[1])
    bias_proj = jnp.concatenate([bias_query, jnp.zeros_like(bias_query), bias_value])
    projected = (
        jnp.dot(flat_rows, attn_weights[:, : 3 * model_width], preferred_element_type=jnp.float32)
        + bias_proj
    )
    projected = projected.astype(jnp.bfloat16).reshape(batch_size, length, 3, head_count, HD)
    queries = projected[:, :, 0]
    key_rows = projected[:, :, 1]
    value_rows = projected[:, :, 2]
    scores = masked_scores(queries, key_rows, segment)
    top_score = jnp.max(scores, axis=-1, keepdims=True)
    raised = jnp.exp(scores - top_score)
    totals = jnp.sum(raised, axis=-1, keepdims=True)
    attn_probs = (raised / totals).astype(jnp.bfloat16)
    log_total = top_score + jnp.log(totals)
    mixed_heads = jnp.einsum(
        "bhlm,bmhe->blhe", attn_probs, value_rows, preferred_element_type=jnp.float32
    )
    mixed_flat = mixed_heads.astype(jnp.bfloat16).reshape(batch_size * length, model_width)
    attn_out = (
        jnp.dot(mixed_flat, attn_weights[:, 3 * model_width :], preferred_element_type=jnp.float32)
        + bias_out
    )
    residual_one = flat_rows.astype(jnp.float32) + attn_out
    normed_one = layer_norm(residual_one, gain_one, shift_one)
    pre_act = (
        jnp.dot(normed_one.astype(jnp.bfloat16), inner_weight, preferred_element_type=jnp.float32)
        + bias_inner
    )
    activated = gelu_exact(pre_act).astype(jnp.bfloat16)
    branch = jnp.dot(activated, outer_weight, preferred_element_type=jnp.float32) + bias_outer
    residual_two = normed_one + branch
    result = layer_norm(residual_two, gain_two, shift_two).reshape(batch_size, length, model_width)
    kept_values = (
        queries,
        key_rows,
        value_rows,
        log_total,
        mixed_flat,
        residual_one,
        normed_one,
        pre_act,
        activated,
        residual_two,
    )
    return (result, kept_values)


def encoder_backward(
    tokens, segment, attn_weights, inner_weight, outer_weight, small_vec, kept_values, grad_result
):
    batch_size, length, model_width = tokens.shape
    head_count = model_width // HD
    flat_rows = tokens.reshape(batch_size * length, model_width)
    (
        queries,
        key_rows,
        value_rows,
        log_total,
        mixed_flat,
        residual_one,
        normed_one,
        pre_act,
        activated,
        residual_two,
    ) = kept_values
    (
        bias_query,
        bias_value,
        bias_out,
        gain_one,
        shift_one,
        bias_inner,
        bias_outer,
        gain_two,
        shift_two,
    ) = unpack(small_vec, model_width, inner_weight.shape[1])
    grad_flat = grad_result.reshape(batch_size * length, model_width)
    unused_two, norm_two_back = jax.vjp(layer_norm, residual_two, gain_two, shift_two)
    grad_two, grad_gain_two, grad_shift_two = norm_two_back(grad_flat)
    grad_branch = grad_two.astype(jnp.bfloat16)
    grad_bias_outer = jnp.sum(grad_branch, axis=0, dtype=jnp.float32)
    grad_outer = jnp.dot(activated.T, grad_branch, preferred_element_type=jnp.float32)
    grad_act = jnp.dot(grad_branch, outer_weight.T, preferred_element_type=jnp.float32)
    unused_act, gelu_back = jax.vjp(gelu_exact, pre_act)
    grad_pre = gelu_back(grad_act)[0].astype(jnp.bfloat16)
    grad_bias_inner = jnp.sum(grad_pre, axis=0, dtype=jnp.float32)
    grad_inner = jnp.dot(
        normed_one.astype(jnp.bfloat16).T, grad_pre, preferred_element_type=jnp.float32
    )
    grad_normed = grad_two + jnp.dot(grad_pre, inner_weight.T, preferred_element_type=jnp.float32)
    unused_one, norm_one_back = jax.vjp(layer_norm, residual_one, gain_one, shift_one)
    grad_one, grad_gain_one, grad_shift_one = norm_one_back(grad_normed)
    grad_attn_out = grad_one.astype(jnp.bfloat16)
    grad_bias_out = jnp.sum(grad_attn_out, axis=0, dtype=jnp.float32)
    grad_out_proj = jnp.dot(mixed_flat.T, grad_attn_out, preferred_element_type=jnp.float32)
    grad_mixed = jnp.dot(
        grad_attn_out, attn_weights[:, 3 * model_width :].T, preferred_element_type=jnp.float32
    )
    grad_mixed = grad_mixed.astype(jnp.bfloat16).reshape(batch_size, length, head_count, HD)
    scores = masked_scores(queries, key_rows, segment)
    attn_probs = jnp.exp(scores - log_total)
    grad_probs = jnp.einsum(
        "blhe,bmhe->bhlm", grad_mixed, value_rows, preferred_element_type=jnp.float32
    )
    inner_dot = jnp.sum(attn_probs * grad_probs, axis=-1, keepdims=True)
    grad_scores = (attn_probs * (grad_probs - inner_dot)).astype(jnp.bfloat16)
    grad_values = jnp.einsum(
        "bhlm,blhe->bmhe",
        attn_probs.astype(jnp.bfloat16),
        grad_mixed,
        preferred_element_type=jnp.float32,
    )
    grad_queries = jnp.einsum(
        "bhlm,bmhe->blhe", grad_scores, key_rows, preferred_element_type=jnp.float32
    ) * HD ** (-0.5)
    grad_keys = jnp.einsum(
        "bhlm,blhe->bmhe", grad_scores, queries, preferred_element_type=jnp.float32
    ) * HD ** (-0.5)
    row_total = batch_size * length
    grad_proj = jnp.concatenate(
        [
            grad_queries.reshape(row_total, model_width),
            grad_keys.reshape(row_total, model_width),
            grad_values.reshape(row_total, model_width),
        ],
        axis=1,
    ).astype(jnp.bfloat16)
    grad_bias_query = jnp.sum(grad_proj[:, :model_width], axis=0, dtype=jnp.float32)
    grad_bias_value = jnp.sum(grad_proj[:, 2 * model_width :], axis=0, dtype=jnp.float32)
    grad_proj_weight = jnp.dot(flat_rows.T, grad_proj, preferred_element_type=jnp.float32)
    grad_tokens = grad_one + jnp.dot(
        grad_proj, attn_weights[:, : 3 * model_width].T, preferred_element_type=jnp.float32
    )
    grad_attn = jnp.concatenate([grad_proj_weight, grad_out_proj], axis=1)
    grad_small = jnp.concatenate(
        [
            grad_bias_query,
            grad_bias_value,
            grad_bias_out,
            grad_gain_one,
            grad_shift_one,
            grad_bias_inner,
            grad_bias_outer,
            grad_gain_two,
            grad_shift_two,
        ]
    )
    return (
        grad_tokens.reshape(batch_size, length, model_width),
        grad_attn,
        grad_inner,
        grad_outer,
        grad_small,
    )


def rows_term(stacked, count):
    return jnp.moveaxis(stacked, 0, 1).reshape(count, -1)


def unfold_rows(summed, encoders):
    owned = summed.shape[0]
    return jnp.moveaxis(summed.reshape(owned, encoders, -1), 1, 0)


def adam_update(weight, first_moment, second, gradient, step_rate, decay_rate):
    first_new = BETA_ONE * first_moment + (1.0 - BETA_ONE) * gradient
    second_new = BETA_TWO * second + (1.0 - BETA_TWO) * gradient * gradient
    fix_one = 1.0 - BETA_ONE**STEP
    fix_two = 1.0 - BETA_TWO**STEP
    update = first_new / fix_one / (jnp.sqrt(second_new / fix_two) + ADAM_EPS)
    return (first_new, second_new, weight - step_rate * (update + decay_rate * weight))


def local(
    question_tokens,
    passage_tokens,
    passage_lengths,
    positives,
    attn_weight,
    attn_first,
    attn_second,
    ffn_in_weight,
    ffn_in_first,
    ffn_in_second,
    ffn_out_weight,
    ffn_out_first,
    ffn_out_second,
    small_params,
    small_first,
    small_second,
):
    gathered = (
        lax.all_gather(attn_weight.astype(jnp.bfloat16), ("dp", "pair"), axis=1, tiled=True),
        lax.all_gather(ffn_in_weight.astype(jnp.bfloat16), ("dp", "pair"), axis=1, tiled=True),
        lax.all_gather(ffn_out_weight.astype(jnp.bfloat16), ("dp", "pair"), axis=1, tiled=True),
        lax.all_gather(small_params.astype(jnp.bfloat16), ("dp", "pair"), axis=1, tiled=True),
    )
    attn_all, inner_all, outer_all, small_low = gathered
    small_all = small_low.astype(jnp.float32)
    question_count, question_len, model_width = question_tokens.shape
    row_count, row_len, unused_width = passage_tokens.shape
    attn_cols = attn_weight.shape[2]
    front_rows = attn_weight.shape[1]
    back_rows = ffn_out_weight.shape[1]
    seg_ends = jnp.cumsum(passage_lengths, axis=1)
    seg_starts = seg_ends - passage_lengths
    positions = jnp.arange(row_len, dtype=jnp.int32)
    passage_seg = jnp.sum(
        (positions[None, :, None] >= seg_ends[:, None, :]).astype(jnp.int32), axis=2
    )
    question_seg = jnp.zeros((question_count, question_len), jnp.int32)
    question_out, question_kept = encoder_forward(
        question_tokens, question_seg, attn_all[0], inner_all[0], outer_all[0], small_all[0]
    )
    passage_out, passage_kept = encoder_forward(
        passage_tokens, passage_seg, attn_all[1], inner_all[1], outer_all[1], small_all[1]
    )
    question_cls = question_out[:, 0].astype(jnp.bfloat16)
    passage_cls = (
        jnp.take_along_axis(passage_out, seg_starts[:, :, None], axis=1)
        .reshape(-1, model_width)
        .astype(jnp.bfloat16)
    )
    every_cls = lax.all_gather(passage_cls, ("dp", "pair"), axis=0, tiled=True)
    score_scale = model_width ** (-0.5)
    scores = jnp.dot(question_cls, every_cls.T, preferred_element_type=jnp.float32) * score_scale
    top_score = jnp.max(scores, axis=1, keepdims=True)
    raised = jnp.exp(scores - top_score)
    soft_scores = raised / jnp.sum(raised, axis=1, keepdims=True)
    columns = jnp.arange(every_cls.shape[0], dtype=jnp.int32)
    target = (columns[None, :] == positives[:, None]).astype(jnp.float32)
    grad_scores = (soft_scores - target).astype(jnp.bfloat16)
    grad_qcls = jnp.dot(grad_scores, every_cls, preferred_element_type=jnp.float32) * score_scale
    grad_pcls = lax.psum_scatter(
        jnp.dot(grad_scores.T, question_cls, preferred_element_type=jnp.float32) * score_scale,
        ("dp", "pair"),
        scatter_dimension=0,
        tiled=True,
    )
    grad_question_out = jnp.zeros_like(question_out).at[:, 0].set(grad_qcls)
    row_index = jnp.arange(row_count, dtype=jnp.int32)[:, None]
    grad_passage_out = (
        jnp.zeros_like(passage_out)
        .at[row_index, seg_starts]
        .set(grad_pcls.reshape(row_count, -1, model_width))
    )
    question_grad, q_attn, q_inner, q_outer, q_small = encoder_backward(
        question_tokens,
        question_seg,
        attn_all[0],
        inner_all[0],
        outer_all[0],
        small_all[0],
        question_kept,
        grad_question_out,
    )
    passage_grad, p_attn, p_inner, p_outer, p_small = encoder_backward(
        passage_tokens,
        passage_seg,
        attn_all[1],
        inner_all[1],
        outer_all[1],
        small_all[1],
        passage_kept,
        grad_passage_out,
    )
    front_stack = jnp.stack(
        [jnp.concatenate([q_attn, q_inner], axis=1), jnp.concatenate([p_attn, p_inner], axis=1)]
    )
    front_owned = lax.psum_scatter(
        rows_term(front_stack, front_rows * lax.axis_size(("dp", "pair"))),
        ("dp", "pair"),
        scatter_dimension=0,
        tiled=True,
    )
    back_owned = lax.psum_scatter(
        rows_term(jnp.stack([q_outer, p_outer]), back_rows * lax.axis_size(("dp", "pair"))),
        ("dp", "pair"),
        scatter_dimension=0,
        tiled=True,
    )
    small_sum = lax.psum_scatter(
        jnp.stack([q_small, p_small]), ("dp", "pair"), scatter_dimension=1, tiled=True
    )
    front_sum = unfold_rows(front_owned, 2)
    back_sum = unfold_rows(back_owned, 2)
    attn_sum = front_sum[:, :, :attn_cols]
    inner_sum = front_sum[:, :, attn_cols:]
    attn_m, attn_v, attn_w = adam_update(
        attn_weight, attn_first, attn_second, attn_sum, RATE_MATRIX, DECAY_MATRIX
    )
    inner_m, inner_v, inner_w = adam_update(
        ffn_in_weight, ffn_in_first, ffn_in_second, inner_sum, RATE_MATRIX, DECAY_MATRIX
    )
    outer_m, outer_v, outer_w = adam_update(
        ffn_out_weight, ffn_out_first, ffn_out_second, back_sum, RATE_MATRIX, DECAY_MATRIX
    )
    small_m, small_v, small_w = adam_update(
        small_params, small_first, small_second, small_sum, RATE_SMALL, 0.0
    )
    return (
        attn_m,
        attn_v,
        attn_w,
        inner_m,
        inner_v,
        inner_w,
        outer_m,
        outer_v,
        outer_w,
        small_m,
        small_v,
        small_w,
        question_grad,
        passage_grad,
    )


MESH_ID = pl.DeviceIdType.MESH
LOW = jnp.bfloat16
F32 = jnp.float32


def dot_nn(a, b):
    return jnp.dot(a, b, preferred_element_type=F32)


def dot_nt(a, b):
    return lax.dot_general(a, b, (((1,), (1,)), ((), ())), preferred_element_type=F32)


def dot_tn(a, b):
    return lax.dot_general(a, b, (((0,), (0,)), ((), ())), preferred_element_type=F32)


def expand_heads(rows):
    head_of = lax.broadcasted_iota(jnp.int32, rows.shape, 1) // HD
    heads = rows.shape[1] // HD
    return jnp.concatenate(
        [jnp.where(head_of == h, rows, jnp.zeros_like(rows)) for h in range(heads)], axis=0
    )


def pick_heads(stacked):
    width = stacked.shape[1]
    heads = width // HD
    head_of = lax.broadcasted_iota(jnp.int32, (16, width), 1) // HD
    total = jnp.zeros((16, width), F32)
    for h in range(heads):
        total = total + jnp.where(head_of == h, stacked[16 * h : 16 * h + 16], 0.0)
    return total


def split_low(values):
    high = values.astype(LOW)
    return high, (values - high.astype(F32)).astype(LOW)


def gelu_parts(values):
    cdf = 0.5 * (1.0 + lax.erf(values * (0.5**0.5)))
    density = jnp.exp(-0.5 * values * values) * (0.5 / math.pi) ** 0.5
    return values * cdf, cdf + values * density


def step_kernel(
    qt_ref, pt_ref, attn_ref, ffi_ref, ffo_ref, small_ref, len_ref, pos_ref,
    ga_ref, gi_ref, go_ref, gs_ref, dxq_ref, dxp_ref,
    X, slabA, slabI, slabO, smw, sm2, smb, bndo, bndb, R, WN, sn, sno, ST, Pf, Pb, DSb, Emat, b1p,
    w1s_, w1r, W1, W2, Yb, P2s, P2a, P2b, P2c, XH, Dout, dZb, Gb, Act, P3s, P3a, P3b, P3c, Qb, dAb, dUb, dQb,
    m1s, m1r, m2s, m2r, dws, dwr, GP, GS, GSw, GA, GI, GO, DX, qsb, vtb, ybf,
    loc, sib_s, sib_r, at_s, at_r, ag_s, ag_z, ag_p, aa_s, aa_r, rs_s, rs_p, rs_z, out_l, out_s, out_r,
):
    dp, z = lax.axis_index("dp"), lax.axis_index("pair")
    core = lax.rem(dp, 2)
    y, x = dp // 4, lax.rem(dp // 2, 2)
    own = y * 8 + x * 4 + z
    line = y * 8 + x * 4

    def dev(slot, k):
        return ((slot // 8) * 4 + lax.rem(slot // 4, 2) * 2 + k, lax.rem(slot, 4))

    sibling = dev(own, 1 - core)
    slot_x = y * 8 + (1 - x) * 4 + z
    slot_y = (1 - y) * 8 + x * 4 + z
    slot_d = (1 - y) * 8 + (1 - x) * 4 + z

    def remote(src, dst, ssem, rsem, target):
        return pltpu.make_async_remote_copy(
            src_ref=src, dst_ref=dst, send_sem=ssem, recv_sem=rsem,
            device_id=target, device_id_type=MESH_ID,
        )

    def done(ref, sem):
        pltpu.make_async_copy(ref, ref, sem).wait()

    barrier = pltpu.get_barrier_semaphore()
    other = 1 - core
    rows = pl.ds(pl.multiple_of(512 * core, 512), 512)
    pltpu.make_async_copy(attn_ref.at[core], slabA.at[core], loc.at[0]).start()

    def greet(r, c):
        pl.semaphore_signal(
            barrier, inc=1, device_id=dev(lax.rem(own + r, 16), core), device_id_type=MESH_ID
        )
        return c

    pl.semaphore_signal(barrier, inc=1, device_id=sibling, device_id_type=MESH_ID)
    lax.fori_loop(1, 16, greet, 0)

    @pl.when(core == 0)
    def _():
        pltpu.make_async_copy(qt_ref, X.at[rows], loc.at[1]).start()

    @pl.when(core == 1)
    def _():
        pltpu.make_async_copy(pt_ref, X.at[rows], loc.at[1]).start()

    pltpu.make_async_copy(ffi_ref.at[core], slabI.at[core], loc.at[2]).start()
    pltpu.make_async_copy(ffo_ref.at[core], slabO.at[core], loc.at[3]).start()

    narrow = small_ref[...].astype(LOW).astype(F32)
    window = jnp.zeros((2, 384), F32)
    for i in range(4):
        gaps = [jnp.zeros((2, n), F32) for n in (32 * i, 96 - 32 * i) if n]
        placed = jnp.concatenate(([gaps[0]] if i else []) + [narrow] + ([gaps[-1]] if i < 3 else []), axis=1)
        window = jnp.where(z == i, placed, window)
    for k in range(2):
        smw[k] = jnp.concatenate(
            [window[k : k + 1, 128 * i : 128 * i + 128] for i in range(3)]
            + [jnp.zeros((5, 128), F32)], axis=0,
        )
    sm2[core] = smw[core]

    lengths = len_ref[...].astype(F32)
    spans = jnp.concatenate(
        [jnp.broadcast_to(lengths[i : i + 1], (4, 4)) for i in range(2)], axis=0
    )
    at_row = lax.broadcasted_iota(jnp.int32, (8, 4), 0)
    at_lane = lax.broadcasted_iota(jnp.int32, (8, 4), 1)
    upto = at_lane <= lax.rem(at_row, 4)
    here = at_lane == lax.rem(at_row, 4)
    line_of = lax.broadcasted_iota(jnp.int32, (8, 1), 0)
    base = jnp.where(line_of >= 4, 256.0, 0.0)
    passage_end = jnp.sum(jnp.where(upto, spans, 0.0), axis=1, keepdims=True) + base
    passage_start = passage_end - jnp.sum(jnp.where(here, spans, 0.0), axis=1, keepdims=True)
    question_start = line_of.astype(F32) * 64.0
    eye = lax.broadcasted_iota(jnp.int32, (8, 8), 0) == lax.broadcasted_iota(jnp.int32, (8, 8), 1)
    goal = jnp.broadcast_to(pos_ref[...].astype(F32), (8, 8))
    goal = jnp.sum(jnp.where(eye, goal, 0.0), axis=1, keepdims=True)
    of_questions = jnp.concatenate([question_start, question_start + 64.0, goal], axis=0)
    of_passages = jnp.concatenate([passage_start, passage_end, goal], axis=0)
    bndb[core] = jnp.broadcast_to(jnp.where(core == 0, of_questions, of_passages), (24, 128))
    bndo[...] = jnp.broadcast_to(jnp.where(core == 0, of_passages, of_questions), (24, 128))
    pl.semaphore_wait(barrier, 16)

    remote(smw.at[other], sm2.at[core], sib_s.at[1], sib_r.at[1], sibling).start()
    remote(attn_ref.at[other], slabA.at[core], sib_s.at[0], sib_r.at[0], sibling).start()
    remote(bndo, bndb.at[core], sib_s.at[2], sib_r.at[2], sibling).start()

    @pl.when(core == 0)
    def _():
        remote(pt_ref, X.at[rows], sib_s.at[3], sib_r.at[3], sibling).start()

    @pl.when(core == 1)
    def _():
        remote(qt_ref, X.at[rows], sib_s.at[3], sib_r.at[3], sibling).start()

    remote(ffi_ref.at[other], slabI.at[core], sib_s.at[4], sib_r.at[4], sibling).start()
    remote(ffo_ref.at[other], slabO.at[core], sib_s.at[5], sib_r.at[5], sibling).start()

    done(sm2.at[other], sib_r.at[1])
    smb[own] = jnp.concatenate([sm2[0], sm2[1]], axis=0).astype(LOW)

    exchanged = (smb, w1r, None, m1r, None, dwr, m2r)
    gathered = (Yb, Qb, XH.at[core], dUb, None, dQb)
    summed = ((P2s, P2a, P2b, P2c), (P3s, P3a, P3b, P3c))
    passed = ((slabA.at[0], slabA.at[0]), (sm2.at[0], sm2.at[0]), (bndb.at[0], bndb.at[0]),
              (X.at[rows], X.at[rows]), (slabI.at[0], slabI.at[0]), (slabO.at[0], slabO.at[0]),
              (sn, sno), (XH.at[0], XH.at[0]))
    written = [[ref] * 3 for ref in (GO.at[0], DX.at[rows], GI.at[0], GA.at[0, 0], GSw.at[0], GA.at[0, 0])]
    state = {("pass", n): int(n < 2) for n in range(6)}
    state["attn", 0] = 1

    def direct(n, src_of):
        def body(r, c):
            target = lax.rem(own + r, 16)
            remote(src_of(target), exchanged[n].at[own], aa_s.at[n], aa_r.at[n], dev(target, core)).start()
            return c

        lax.fori_loop(1, 16, body, 0)
        state["direct", n] = 0

    def direct_done(n):
        done(exchanged[n].at[pl.ds(0, 15)], aa_r.at[n])
        state["direct", n] = 1

    def pass_done(n):
        done(passed[n][1], sib_r.at[n])
        state["pass", n] = 1

    direct(0, lambda t: smb.at[own])

    def push(slot, m, target):
        remote(R.at[slot, m], R.at[slot, m], at_s.at[m], at_r.at[slot, m, 0], dev(target, core)).start()

    def near(f, nearest=1):
        for d in range(nearest, 4):
            for dz in (d, -d) if d else (0,):
                @pl.when(jnp.logical_and(z + dz >= 0, z + dz <= 3))
                def _():
                    f(dz)

    def got(slot, m):
        done(R.at[slot, m], at_r.at[slot, m, 0])

    done(slabA.at[core], loc.at[0])
    done(slabA.at[other], sib_r.at[0])
    for m in (0, 3, 1, 2):
        cols = slice(768 * m, 768 * m + 768)
        R[own, m] = jnp.concatenate([slabA[0, :, cols], slabA[1, :, cols]], axis=0).astype(LOW)
        for target in (slot_x, slot_y) if m < 3 else (slot_x, slot_y, slot_d):
            push(own, m, target)
        if m < 3:
            near(lambda dz: push(own, m, own + dz))

    def hop(d):
        for i in range(4):
            slot = 4 * i + z
            if d == 0:
                @pl.when(4 * i != line)
                def _():
                    got(slot, 3)

                @pl.when(z < 3)
                def _():
                    push(slot, 3, own + 1)

                @pl.when(z > 0)
                def _():
                    push(slot, 3, own - 1)
            else:
                @pl.when(z - d >= 0)
                def _():
                    got(slot - d, 3)

                    @pl.when(z < 3)
                    def _():
                        push(slot - d, 3, own + 1)

                @pl.when(z + d <= 3)
                def _():
                    got(slot + d, 3)

                    @pl.when(z > 0)
                    def _():
                        push(slot + d, 3, own - 1)

    def settle(last=True):
        for kind, n in list(state):
            at = state[kind, n]
            if last and kind == "gather" and at == 0:
                gather_forward(n)
            if last and kind == "gather" and at < 2:
                gather_done(n)
            if last and kind == "sum" and at == 0:
                sum_forward(n)
            if last and kind == "sum" and at < 2:
                sum_done(n)
            if last and kind == "direct" and at == 0:
                direct_done(n)
            if last and kind == "pass" and at == 0:
                pass_done(n)
            if kind == "gather" and (last or at == 2):
                done(gathered[n].at[pl.ds(0, 15)], ag_s.at[n])
            elif kind == "direct" and (last or at == 1):
                done(exchanged[n].at[pl.ds(0, 15)], aa_s.at[n])
            elif kind == "sum" and (last or at == 2):
                done(summed[n][1].at[pl.ds(0, 3)], rs_s.at[n, 0])
                done(summed[n][3].at[pl.ds(0, 3)], rs_s.at[n, 1])
            elif kind == "pass" and (last or at == 1):
                done(passed[n][0], sib_s.at[n])
            elif kind == "out" and last:
                for ref, sem in zip(written[n], (out_l, out_s, out_r)):
                    done(ref, sem.at[n])
            elif kind == "attn":
                for m in range(3):
                    done(R.at[pl.ds(0, 15), m], at_s.at[m])
                done(R.at[pl.ds(0, 7), 3], at_s.at[3])

                @pl.when(jnp.logical_and(z > 0, z < 3))
                def _():
                    done(R.at[pl.ds(0, 16), 3], at_s.at[3])
            else:
                continue
            del state[kind, n]

    def finish():
        settle()

    def relay_z(m):
        def give(dz):
            got(own + dz, m)
            for target in (slot_x, slot_y):
                push(own + dz, m, target)

        near(give)

    def relay_plane(m):
        def give(dz):
            for slot, target, half in ((slot_x + dz, slot_y, 0), (slot_y + dz, slot_x, 1)):
                got(slot, m)
                part = R.at[slot, m, :, pl.ds(384 * half, 384)]
                remote(part, part, at_s.at[m], at_r.at[slot, m, half], dev(target, core)).start()

        near(give, 0)

    def from_slots(read, write):
        def body(g, c):
            got = [read(4 * g + i) for i in range(4)]
            natural = jnp.concatenate([v[0:24] for v in got] + [v[24:48] for v in got], axis=0)
            write(pl.ds(pl.multiple_of(192 * g, 64), 192), natural.astype(LOW))
            return c

        lax.fori_loop(0, 4, body, 0)

    def to_slots(read, write):
        def body(g, c):
            v = read(pl.ds(pl.multiple_of(192 * g, 64), 192))
            for i in range(4):
                part = jnp.concatenate(
                    [v[24 * i : 24 * i + 24], v[96 + 24 * i : 96 + 24 * i + 24]], axis=0
                )
                write(4 * g + i, part)
            return c

        lax.fori_loop(0, 4, body, 0)

    def pack(v):
        tail = jnp.concatenate([v[0:24, 128:192], v[24:48, 128:192]], axis=1)
        return jnp.concatenate([v[:, 0:128], tail, jnp.zeros((8, 128), F32)], axis=0).astype(LOW)

    def unpack(packed):
        v = packed.astype(F32)
        tail = jnp.concatenate([v[48:72, 0:64], v[48:72, 64:128]], axis=0)
        return jnp.concatenate([v[0:48], tail], axis=1)

    def arrive(m):
        def body(zz, c):
            slot = (1 - y) * 8 + (1 - x) * 4 + zz
            for half in range(2):
                done(R.at[slot, m, :, pl.ds(384 * half, 384)], at_r.at[slot, m, half])
            return c

        if m < 3:
            lax.fori_loop(0, 4, body, 0)

        def write(where, v):
            WN[m, where, :] = v

        from_slots(lambda s: R[s, m].astype(F32), write)

    early_own = (0, 1, 2, 3)

    def gather_start(n):
        buf = gathered[n]
        state["gather", n] = 0

        def give(dz):
            remote(buf.at[own], buf.at[own], ag_s.at[n], ag_z.at[n, z], dev(own + dz, core)).start()

        near(give)
        if n in early_own:
            for target in (slot_x, slot_y, slot_d):
                remote(buf.at[own], buf.at[own], ag_s.at[n], ag_p.at[n], dev(target, core)).start()

    def gather_forward(n):
        buf = gathered[n]
        state["gather", n] = 1

        def pass_on(dz):
            block = buf.at[own + dz]
            done(block, ag_z.at[n, z + dz])
            if n in early_own:
                for target in (slot_x, slot_y, slot_d):
                    remote(block, block, ag_s.at[n], ag_p.at[n], dev(target, core)).start()

        near(pass_on)
        if n not in early_own:
            block = buf.at[pl.ds(line, 4)]
            for target in (slot_x, slot_y, slot_d):
                remote(block, block, ag_s.at[n], ag_p.at[n], dev(target, core)).start()

    def gather_done(n):
        state["gather", n] = 2
        done(gathered[n].at[pl.ds(0, 12)], ag_p.at[n])

    def each_z(f):
        for d in range(3, -1, -1):
            for dz in (d, -d) if d else (0,):
                @pl.when(jnp.logical_and(z + dz >= 0, z + dz <= 3))
                def _():
                    f(dz)

    def sum_start(n):
        source, plane, unused, unused = summed[n]
        state["sum", n] = 0

        def give(dz):
            for target in (slot_x, slot_y, slot_d):
                remote(
                    source.at[target + dz], plane.at[line // 4, z + dz],
                    rs_s.at[n, 0], rs_p.at[n, z + dz], dev(target, core),
                ).start()

        each_z(give)
        plane[line // 4] = source[pl.ds(line, 4)]

    def sum_forward(n):
        unused, plane, along, final = summed[n]
        state["sum", n] = 1

        def give(dz):
            done(plane.at[pl.ds(0, 3), z + dz], rs_p.at[n, z + dz])
            total = jnp.sum(plane[:, z + dz].astype(F32), axis=0).astype(LOW)
            if dz == 0:
                final[z] = total
            else:
                along[z + dz] = total
                remote(
                    along.at[z + dz], final.at[z], rs_s.at[n, 1], rs_z.at[n], dev(own + dz, core)
                ).start()

        each_z(give)

    def sum_done(n):
        final = summed[n][3]
        state["sum", n] = 2
        done(final.at[pl.ds(0, 3)], rs_z.at[n])
        return jnp.sum(final[...].astype(F32), axis=0)

    def prepare_ffn():
        row = lax.broadcasted_iota(jnp.int32, (384, 512), 0)
        col = lax.broadcasted_iota(jnp.int32, (384, 512), 1)
        Emat[...] = jnp.where(col == 128 * (row // 96) + lax.rem(row, 96), 1.0, 0.0).astype(LOW)
        done(slabI.at[core], loc.at[2])
        pass_done(4)
        for g in range(4):
            halves = []
            for k in range(2):
                cols = slice(768 * g + 384 * k, 768 * g + 384 * k + 384)
                halves.append(jnp.concatenate([slabI[0, :, cols], slabI[1, :, cols]], axis=0))
            for i in range(4):
                lanes = slice(96 * i, 96 * i + 96)
                w1s_[4 * g + i] = pack(jnp.concatenate([half[:, lanes] for half in halves], axis=1))
        w1r[own] = w1s_[own]
        done(slabO.at[core], loc.at[3])
        pass_done(5)
        gap = jnp.zeros((64, 768), F32)
        W2[...] = jnp.concatenate([slabO[0], slabO[1], gap], axis=0).astype(LOW)

    def natural_small():
        direct_done(0)
        for g in range(8):
            parts = [
                smb[4 * (g // 2) + i].astype(F32)[8 * (g % 2) : 8 * (g % 2) + 8] for i in range(4)
            ]
            lines = [parts[0][0:1], parts[0][1:2]]
            for i in range(1, 4):
                lines += [parts[i - 1][2:3] + parts[i][0:1], parts[i][1:2]]
            lines += [parts[3][2:3]]
            sn[9 * g : 9 * g + 9, :] = jnp.concatenate(lines, axis=0)
        remote(sn, sno, sib_s.at[6], sib_r.at[6], sibling).start()
        state["pass", 6] = 0

    def vec(row, count=6, ref=sn):
        return jnp.concatenate([ref[row + i : row + i + 1, :] for i in range(count)], axis=1)

    relay_z(0)
    hop(0)
    pass_done(2)
    done(X.at[pl.ds(0, 512)], loc.at[1])
    pass_done(3)
    starts = jnp.concatenate([bndb[0, 0:8], bndb[1, 0:8] + 512.0], axis=0)[:, 0:1]
    ends = jnp.concatenate([bndb[0, 8:16], bndb[1, 8:16] + 512.0], axis=0)[:, 0:1]
    token = lax.broadcasted_iota(jnp.int32, (16, 1024), 1).astype(F32)
    inside = jnp.logical_and(token >= starts, token < ends)
    first = jnp.where(token == starts, 1.0, 0.0).astype(LOW)
    cls_in = dot_nn(first, X[...])
    cls_low = cls_in.astype(LOW)
    relay_z(1)
    relay_plane(0)
    natural_small()
    prepare_ffn()
    hop(1)
    relay_z(2)
    relay_plane(1)
    arrive(0)
    queries = (dot_nn(cls_low, WN[0]) + vec(0)).astype(LOW)
    Qb[own] = queries
    gather_start(1)
    hop(2)
    relay_plane(2)
    arrive(1)
    qsb[...] = (dot_nt(expand_heads(queries), WN[1]) * (HD**-0.5)).astype(LOW)
    ST[...] = dot_nt(qsb[...], X[...])

    def soften(h, c):
        at = pl.ds(pl.multiple_of(16 * h, 16), 16)
        s = jnp.where(inside, ST[at, :], -1000000000.0)
        e = jnp.exp(s - jnp.max(s, axis=1, keepdims=True))
        p = e / jnp.sum(e, axis=1, keepdims=True)
        Pf[at, :] = p
        Pb[at, :] = p.astype(LOW)
        return c

    lax.fori_loop(0, 12, soften, 0, unroll=12)
    ybf[...] = dot_nn(Pb[...], X[...]).astype(LOW)
    arrive(2)
    mixed = (pick_heads(dot_nn(ybf[...], WN[2])) + vec(6)).astype(LOW)
    hop(3)
    arrive(3)
    lifted = cls_in + dot_nn(mixed, WN[3]) + vec(12)
    centred = lifted - jnp.mean(lifted, axis=1, keepdims=True)
    rstd_one = lax.rsqrt(jnp.mean(centred * centred, axis=1, keepdims=True) + NORM_EPS)
    hat_one = centred * rstd_one
    normed = hat_one * vec(18) + vec(24)
    Yb[own] = normed.astype(LOW)
    gather_start(0)
    direct(1, lambda t: w1s_.at[t])

    early = jnp.concatenate(
        [ybf[...].astype(F32), cls_in, mixed.astype(F32), jnp.zeros((32, 768), F32)], axis=0
    )
    DX[0:768, 0:256] = early.T

    def write_m1(slot, v):
        m1s[slot] = v.astype(LOW)

    to_slots(lambda w: DX[w, 0:256], write_m1)
    m1r[own] = m1s[own]
    gather_forward(0)

    b1 = jnp.concatenate([vec(30 + 3 * g, 3) for g in range(8)], axis=0).astype(LOW)
    b1_wide = dot_nn(b1, Emat[...])
    for g in range(8):
        b1p[g] = jnp.broadcast_to(b1_wide[g : g + 1], (8, 512))
    group = pl.multiple_of(128 * z, 128)
    gy = 4 * y + 2 * x
    b1_row = jnp.concatenate(
        [
            b1p[gy, 0:1, pl.ds(group, 128)][:, 0:96], b1p[gy + 1, 0:1, pl.ds(group, 128)][:, 0:96],
            jnp.zeros((1, 64), F32),
        ], axis=1,
    )
    direct_done(1)

    def write_w1(where, v):
        W1[where, :] = v

    pad = jnp.zeros((48, 64), F32)
    from_slots(lambda s: jnp.concatenate([unpack(w1r[s]), pad], axis=1), write_w1)
    gather_done(0)
    all_y = Yb[...].reshape(256, 768)
    act = dot_nn(all_y, W1[...]) + b1_row
    Act[...] = act
    hidden, unused = gelu_parts(act)
    Gb[...] = hidden.astype(LOW)
    P2s[...] = dot_nn(Gb[...], W2[...]).astype(LOW).reshape(16, 16, 768)
    sum_start(0)
    sum_forward(0)
    hidden_sum = sum_done(0)
    second = normed + hidden_sum + vec(54)
    centred = second - jnp.mean(second, axis=1, keepdims=True)
    rstd_two = lax.rsqrt(jnp.mean(centred * centred, axis=1, keepdims=True) + NORM_EPS)
    hat_two = centred * rstd_two
    rstd_high, rstd_low = split_low(rstd_two)
    lane = lax.broadcasted_iota(jnp.int32, (16, 128), 1)
    positive = jnp.concatenate([bndb[0, 16:24], bndb[1, 16:24]], axis=0)
    extra = jnp.where(
        lane == 0, rstd_high.astype(F32),
        jnp.where(lane == 1, rstd_low.astype(F32), jnp.where(lane == 2, positive, 0.0)),
    )
    XH[core, own] = jnp.concatenate([hat_two, extra], axis=1).astype(LOW)
    gather_start(2)
    gather_forward(2)
    direct(3, lambda t: m1s.at[t])
    gather_forward(1)
    gather_done(2)
    remote(XH.at[core], XH.at[core], sib_s.at[7], sib_r.at[7], sibling).start()
    state["pass", 7] = 0
    pass_done(6)
    pass_done(7)

    def vec_of(encoder, row):
        return jnp.where(core == encoder, vec(row), vec(row, 6, sno))

    xq = XH[0].reshape(256, 896).astype(F32)
    xp = XH[1].reshape(256, 896).astype(F32)
    qc = (xq[:, 0:768] * vec_of(0, 60) + vec_of(0, 66)).astype(LOW)
    pc = (xp[:, 0:768] * vec_of(1, 60) + vec_of(1, 66)).astype(LOW)
    scale = 768 ** (-0.5)
    scores = dot_nt(qc, pc) * scale
    raised = jnp.exp(scores - jnp.max(scores, axis=1, keepdims=True))
    soft = raised / jnp.sum(raised, axis=1, keepdims=True)
    place = lax.broadcasted_iota(jnp.int32, (256, 256), 1)
    slot_of = place // 16
    owner_of = (
        16 * (slot_of // 8) + 8 * lax.rem(slot_of // 4, 2)
        + 4 * (lax.rem(place, 16) // 8) + lax.rem(slot_of, 4)
    )
    passage = (8 * owner_of + lax.rem(place, 8)).astype(F32)
    target = jnp.where(passage == xq[:, 770:771], 1.0, 0.0)
    grad_scores = (soft - target).astype(LOW)

    @pl.when(core == 0)
    def _():
        Dout[...] = dot_nn(grad_scores, pc) * scale

    @pl.when(core == 1)
    def _():
        Dout[...] = dot_tn(grad_scores, qc) * scale

    dout = Dout[...]
    block = XH[core].reshape(256, 896).astype(F32)
    hat = block[:, 0:768]
    rstd = block[:, 768:769] + block[:, 769:770]
    inner = dout * vec(60)
    grad_two = rstd * (
        inner - jnp.mean(inner, axis=1, keepdims=True)
        - hat * jnp.mean(inner * hat, axis=1, keepdims=True)
    )
    dg2 = jnp.sum(dout * hat, axis=0, keepdims=True)
    ds2 = jnp.sum(dout, axis=0, keepdims=True)
    Dout[...] = grad_two
    dZb[...] = grad_two.astype(LOW)
    db2 = jnp.sum(dZb[...].astype(F32), axis=0, keepdims=True)
    unused, slope = gelu_parts(Act[...])
    da = (dot_nt(dZb[...], W2[...]) * slope).astype(LOW)
    P3s[...] = dot_nt(da, W1[...]).astype(LOW).reshape(16, 16, 768)
    sum_start(1)
    DX[0:768, 0:256] = dot_tn(all_y, da)

    def write_dw(slot, v):
        dws[slot] = pack(v)

    to_slots(lambda w: DX[w, 0:256], write_dw)
    direct(5, lambda t: dws.at[t])
    sum_forward(1)
    dwr[own] = dws[own]
    db1 = jnp.sum(da.astype(F32), axis=0, keepdims=True)
    dw2 = dot_tn(Gb[...], dZb[...])
    GO[0] = dw2[0:96]
    GO[1] = dw2[96:192]
    pltpu.make_async_copy(GO.at[core], go_ref.at[core], out_l.at[0]).start()
    remote(GO.at[other], go_ref.at[core], out_s.at[0], out_r.at[0], sibling).start()
    state["out", 0] = 0
    own_rows = pl.ds(pl.multiple_of(16 * own, 16), 16)
    normed_sum = sum_done(1)

    grad_normed = Dout[own_rows, :] + normed_sum
    inner = grad_normed * vec(18)
    grad_one = rstd_one * (
        inner - jnp.mean(inner, axis=1, keepdims=True)
        - hat_one * jnp.mean(inner * hat_one, axis=1, keepdims=True)
    )
    grad_lift = grad_one.astype(LOW)
    grad_mixed = dot_nt(grad_lift, WN[3]).astype(LOW)
    dg1 = jnp.sum(grad_normed * hat_one, axis=0, keepdims=True)
    ds1 = jnp.sum(grad_normed, axis=0, keepdims=True)
    partial_sums = jnp.concatenate(
        [dg1[:, 128 * i : 128 * i + 128] for i in range(6)]
        + [ds1[:, 128 * i : 128 * i + 128] for i in range(6)]
        + [db1[:, 0:128], db1[:, 128:256], jnp.zeros((2, 128), F32)], axis=0,
    )
    dUb[own] = jnp.concatenate([grad_one, partial_sums], axis=1).astype(LOW)
    gather_start(3)
    spread = expand_heads(grad_mixed)
    vtb[...] = dot_nt(spread, WN[2]).astype(LOW)
    constant = jnp.sum(spread.astype(F32) * vec(6), axis=1, keepdims=True)
    ST[...] = dot_nt(vtb[...], X[...]) + constant

    def harden(h, c):
        at = pl.ds(pl.multiple_of(16 * h, 16), 16)
        p, dprob = Pf[at, :], ST[at, :]
        total = jnp.sum(p * dprob, axis=1, keepdims=True)
        DSb[at, :] = (p * (dprob - total)).astype(LOW)
        return c

    lax.fori_loop(0, 12, harden, 0, unroll=12)
    late = (dot_nn(DSb[...], X[...]) * (HD**-0.5)).astype(LOW)
    grad_query = pick_heads(dot_nn(late, WN[1])).astype(LOW)
    dQb[own] = grad_query
    gather_start(5)
    DX[0:768, 0:256] = jnp.concatenate(
        [late.astype(F32), jnp.zeros((64, 768), F32)], axis=0
    ).T

    def write_m2(slot, v):
        m2s[slot] = pack(v)

    to_slots(lambda w: DX[w, 0:256], write_m2)
    gather_forward(3)
    direct(6, lambda t: m2s.at[t])
    m2r[own] = m2s[own]

    grad_cls = grad_one + dot_nt(grad_query, WN[0])
    cls_high, cls_rest = split_low(grad_cls)
    right = jnp.concatenate([qsb[...], vtb[...], cls_high, cls_rest], axis=0)
    for k in range(2):
        part = slice(512 * k, 512 * k + 512)
        left = jnp.concatenate([DSb[:, part], Pb[:, part], first[:, part], first[:, part]], axis=0)
        DX[part, :] = dot_tn(left, right)
    gather_forward(5)
    other_rows = pl.ds(pl.multiple_of(512 * other, 512), 512)

    @pl.when(core == 0)
    def _():
        pltpu.make_async_copy(DX.at[rows], dxq_ref, out_l.at[1]).start()
        remote(DX.at[other_rows], dxq_ref, out_s.at[1], out_r.at[1], sibling).start()

    @pl.when(core == 1)
    def _():
        pltpu.make_async_copy(DX.at[rows], dxp_ref, out_l.at[1]).start()
        remote(DX.at[other_rows], dxp_ref, out_s.at[1], out_r.at[1], sibling).start()

    state["out", 1] = 0

    direct_done(5)
    for g in range(4):
        parts = [unpack(dwr[4 * g + i]) for i in range(4)]
        for k in range(2):
            block = jnp.concatenate([v[:, 96 * k : 96 * k + 96] for v in parts], axis=1)
            cols = slice(768 * g + 384 * k, 768 * g + 384 * k + 384)
            GI[0, :, cols] = block[0:24]
            GI[1, :, cols] = block[24:48]
    pltpu.make_async_copy(GI.at[core], gi_ref.at[core], out_l.at[2]).start()
    remote(GI.at[other], gi_ref.at[core], out_s.at[2], out_r.at[2], sibling).start()
    state["out", 2] = 0

    def put(m, v):
        GA[m // 2, 0, :, 768 * (m % 2) : 768 * (m % 2) + 768] = v[0:24]
        GA[m // 2, 1, :, 768 * (m % 2) : 768 * (m % 2) + 768] = v[24:48]

    def hand_out(half, n):
        part = ga_ref.at[core, :, pl.ds(1536 * half, 1536)]
        pltpu.make_async_copy(GA.at[half, core], part, out_l.at[n]).start()
        remote(GA.at[half, other], part, out_s.at[n], out_r.at[n], sibling).start()
        state["out", n] = 0

    def factor_sum(read, columns):
        def body(s, total):
            return total + dot_nn(read(s), expand_heads(columns[s]))

        return lax.fori_loop(0, 16, body, jnp.zeros((48, 768), F32), unroll=16)

    def columns_of(at):
        return jnp.concatenate(
            [m1r[s, :, at : at + 16].astype(F32) for s in range(16)], axis=1
        ).astype(LOW)

    gather_done(3)
    all_du = dUb[...].reshape(256, 896)[:, 0:768]
    all_da = dot_nt(all_du, WN[3]).astype(LOW)
    dAb[...] = all_da.reshape(16, 16, 768)
    direct_done(3)
    put(2, factor_sum(lambda s: m1r[s, :, 0:192], dAb))
    put(3, dot_nn(columns_of(208), all_du))
    hand_out(1, 5)
    cls_columns = columns_of(192)

    parts = [dUb[i, :, 768:896].astype(F32) for i in range(16)]
    sums = parts[0]
    for part in parts[1:]:
        sums = sums + part
    wide = [jnp.concatenate([part[12:13], part[13:14]], axis=1) for part in parts]
    narrow = jnp.concatenate(
        [
            jnp.concatenate(
                [wide[4 * (g // 2) + i][:, 96 * (g % 2) : 96 * (g % 2) + 96] for i in range(4)], axis=1
            )
            for g in range(8)
        ], axis=0,
    )

    def six(v):
        return [v[:, 128 * i : 128 * i + 128] for i in range(6)]

    lines = six(jnp.sum(all_da.astype(F32), axis=0, keepdims=True))
    lines += six(jnp.sum(all_du.astype(F32), axis=0, keepdims=True))
    lines += [sums[0:12]]
    for g in range(8):
        lines += [narrow[g : g + 1, 128 * i : 128 * i + 128] for i in range(3)]
    lines += six(db2) + six(dg2) + six(ds2) + [jnp.zeros((8, 128), F32)]
    GP[6:80] = jnp.concatenate(lines, axis=0)
    for g in range(8):
        for i in range(4):
            at = 9 * g + 9 * i // 4
            if at > 5:
                GS[g, i] = GP[at : at + 8]
    gather_done(1)
    settle(False)
    direct_done(6)
    put(1, factor_sum(lambda s: unpack(m2r[s]).astype(LOW), Qb))
    gather_done(5)
    all_dq = dQb[...].reshape(256, 768)
    put(0, dot_nn(cls_columns, all_dq))
    hand_out(0, 3)
    GP[0:6] = jnp.concatenate(six(jnp.sum(all_dq.astype(F32), axis=0, keepdims=True)), axis=0)
    for i in range(3):
        GS[0, i] = GP[9 * i // 4 : 9 * i // 4 + 8]
    for k in range(2):
        GSw[k] = GS[gy + k, z]
    pltpu.make_async_copy(GSw.at[core], gs_ref.at[core], out_l.at[4]).start()
    remote(GSw.at[other], gs_ref.at[core], out_s.at[4], out_r.at[4], sibling).start()
    state["out", 4] = 0
    finish()


def kernel_call(qt, pt, attn, ffi, ffo, small, lengths, positives):
    any_space = pl.BlockSpec(memory_space=pl.ANY)
    vmem = pl.BlockSpec(memory_space=pltpu.VMEM)
    V = pltpu.VMEM
    dma = pltpu.SemaphoreType.DMA
    scratch = [
        V((1024, 768), LOW), V((2, 24, 3072), F32), V((2, 24, 3072), F32), V((2, 96, 768), F32),
        V((2, 8, 128), F32), V((2, 8, 128), F32), V((16, 16, 128), LOW),
        V((24, 128), F32), V((2, 24, 128), F32), V((16, 4, 48, 768), LOW),
        V((4, 768, 768), LOW), V((72, 128), F32), V((72, 128), F32), V((192, 1024), F32),
        V((192, 1024), F32), V((192, 1024), LOW), V((192, 1024), LOW), V((384, 512), LOW),
        V((8, 8, 512), F32),
        V((16, 80, 128), LOW), V((16, 80, 128), LOW), V((768, 256), LOW), V((256, 768), LOW),
        V((16, 16, 768), LOW), V((16, 16, 768), LOW), V((4, 4, 16, 768), LOW),
        V((4, 16, 768), LOW), V((4, 16, 768), LOW),
        V((2, 16, 16, 896), LOW), V((256, 768), F32), V((256, 768), LOW), V((256, 256), LOW),
        V((256, 256), F32), V((16, 16, 768), LOW), V((4, 4, 16, 768), LOW),
        V((4, 16, 768), LOW), V((4, 16, 768), LOW), V((16, 16, 768), LOW),
        V((16, 16, 768), LOW), V((16, 16, 896), LOW), V((16, 16, 768), LOW),
        V((16, 48, 256), LOW), V((16, 48, 256), LOW), V((16, 80, 128), LOW), V((16, 80, 128), LOW),
        V((16, 80, 128), LOW), V((16, 80, 128), LOW),
        V((80, 128), F32), V((8, 4, 8, 128), F32), V((2, 8, 128), F32), V((2, 2, 24, 1536), F32), V((2, 24, 3072), F32),
        V((2, 96, 768), F32), V((1024, 768), F32), V((192, 768), LOW), V((192, 768), LOW),
        V((192, 768), LOW),
        dma((4,)), dma((8,)), dma((8,)), dma((4,)), dma((16, 4, 2)), dma((7,)), dma((7, 4)),
        dma((7,)), dma((7,)), dma((7,)), dma((2, 2)), dma((2, 4)), dma((2,)),
        dma((6,)), dma((6,)), dma((6,)),
    ]
    shapes = (
        (2, 24, 3072), (2, 24, 3072), (2, 96, 768), (2, 8, 128), (512, 768), (512, 768)
    )
    return pl.pallas_call(
        step_kernel,
        out_shape=[jax.ShapeDtypeStruct(s, F32) for s in shapes],
        in_specs=[any_space] * 5 + [vmem] * 3,
        out_specs=[any_space] * 6,
        scratch_shapes=scratch,
        compiler_params=pltpu.CompilerParams(
            collective_id=0, has_side_effects=True, vmem_limit_bytes=56 << 20
        ),
    )(qt, pt, attn, ffi, ffo, small, lengths, positives)


def update_kernel(*refs):
    ins, outs = refs[:18], refs[18:]
    for n in range(3):
        weight, first, second, grad = (r[...] for r in ins[4 * n : 4 * n + 4])
        new = adam_update(weight, first, second, grad, RATE_MATRIX, DECAY_MATRIX)
        for ref, value in zip(outs[3 * n : 3 * n + 3], new):
            ref[...] = value

    @pl.when(pl.program_id(0) == 0)
    def _():
        z = lax.axis_index("pair")
        weight, first, second, window = ins[12:16]
        lines = []
        for e in range(2):
            row = jnp.concatenate([window[e, i : i + 1, :] for i in range(3)], axis=1)
            picked = row[:, 0:288]
            for i in range(1, 4):
                picked = jnp.where(z == i, row[:, 32 * i : 32 * i + 288], picked)
            lines.append(picked)
        grad = jnp.concatenate(lines, axis=0)
        new = adam_update(weight[...], first[...], second[...], grad, RATE_SMALL, 0.0)
        for ref, value in zip(outs[9:12], new):
            ref[...] = value

    outs[12][...] = ins[16][...]
    outs[13][...] = ins[17][...]


def update_call(attn, inner, outer, small, grad_question, grad_passage):
    wide = pl.BlockSpec((1, 24, 3072), lambda i: (i, 0, 0))
    tall = pl.BlockSpec((1, 96, 768), lambda i: (i, 0, 0))
    vector = pl.BlockSpec((2, 288), lambda i: (0, 0))
    window = pl.BlockSpec((2, 8, 128), lambda i: (0, 0, 0))
    token = pl.BlockSpec((256, 768), lambda i: (i, 0))

    def like(a):
        return jax.ShapeDtypeStruct(a.shape, F32)

    return pl.pallas_call(
        update_kernel,
        grid=(2,),
        out_shape=[like(g[0]) for g in (attn, inner, outer, small) for _ in range(3)]
        + [like(grad_question), like(grad_passage)],
        in_specs=[wide] * 8 + [tall] * 4 + [vector] * 3 + [window, token, token],
        out_specs=[wide] * 6 + [tall] * 3 + [vector] * 3 + [token, token],
    )(*attn, *inner, *outer, *small, grad_question, grad_passage)


def local_kernel(
    question_tokens, passage_tokens, passage_lengths, positives,
    attn_weight, attn_first, attn_second, ffn_in_weight, ffn_in_first, ffn_in_second,
    ffn_out_weight, ffn_out_first, ffn_out_second, small_params, small_first, small_second,
):
    grads = kernel_call(
        question_tokens.reshape(512, 768), passage_tokens.reshape(512, 768),
        attn_weight, ffn_in_weight, ffn_out_weight, small_params,
        passage_lengths, positives.reshape(1, 8),
    )
    attn_sum, inner_sum, outer_sum, small_window, grad_question, grad_passage = grads
    results = update_call(
        (attn_weight, attn_first, attn_second, attn_sum),
        (ffn_in_weight, ffn_in_first, ffn_in_second, inner_sum),
        (ffn_out_weight, ffn_out_first, ffn_out_second, outer_sum),
        (small_params, small_first, small_second, small_window),
        grad_question, grad_passage,
    )
    return (
        *results[:12],
        results[12].reshape(question_tokens.shape),
        results[13].reshape(passage_tokens.shape),
    )


def fits_kernel(mesh):
    return mesh.shape["dp"] == 8 and mesh.shape["pair"] == 4


def solution(mesh):
    in_specs = (
        P(("dp", "pair"), None, None),
        P(("dp", "pair"), None, None),
        P(("dp", "pair"), None),
        P(("dp", "pair")),
        P(None, ("dp", "pair"), None),
        P(None, ("dp", "pair"), None),
        P(None, ("dp", "pair"), None),
        P(None, ("dp", "pair"), None),
        P(None, ("dp", "pair"), None),
        P(None, ("dp", "pair"), None),
        P(None, ("dp", "pair"), None),
        P(None, ("dp", "pair"), None),
        P(None, ("dp", "pair"), None),
        P(None, ("dp", "pair")),
        P(None, ("dp", "pair")),
        P(None, ("dp", "pair")),
    )
    out_specs = (
        P(None, ("dp", "pair"), None),
        P(None, ("dp", "pair"), None),
        P(None, ("dp", "pair"), None),
        P(None, ("dp", "pair"), None),
        P(None, ("dp", "pair"), None),
        P(None, ("dp", "pair"), None),
        P(None, ("dp", "pair"), None),
        P(None, ("dp", "pair"), None),
        P(None, ("dp", "pair"), None),
        P(None, ("dp", "pair")),
        P(None, ("dp", "pair")),
        P(None, ("dp", "pair")),
        P(("dp", "pair"), None, None),
        P(("dp", "pair"), None, None),
    )
    body = local_kernel if fits_kernel(mesh) else local
    return jax.shard_map(body, mesh=mesh, in_specs=in_specs, out_specs=out_specs, check_vma=False)
```
